32 devices in a mesh: groups: 2 (over y), seq: 8 (over z, x), branch: 2 (over core).
Axes of the slice: x: 2, y: 2, z: 4, core: 2. Of those that a mesh axis runs over, the one named last changes fastest.
Arguments:
- queries: bfloat16 [2, 256, 1536], P('branch', ('groups', 'seq')), parts along dimension 1, may hold values from -8 to 8
- key_rows: bfloat16 [2, 256, 1536], P('branch', ('groups', 'seq')), parts along dimension 1, may hold values from -8 to 8
- value_rows: bfloat16 [2, 256, 1536], P('branch', ('groups', 'seq')), parts along dimension 1, may hold values from -40 to 40
- counts: int32 [16], P('groups'), parts along dimension 0, may hold values from 1 to 16, 112 in all
- head_of: int32 [8, 2], replicated, may hold values from 0 to 11, as said below
- out_weight: bfloat16 [1536, 1536], P(None, 'branch'), may hold values from -0.15625 to 0.15625
Outputs:
- projected: bfloat16 [256, 1536], P(('groups', 'seq'), 'branch'), parts along dimension 0
- saved_logsumexp: float32 [2, 16, 2, 16, 8], P('branch', ('groups', 'seq')), parts along dimension 1
The draws below stay inside these ranges and needn't reach their ends.
There are 2 independent parts, one for each index of `groups`. The reference program is written for one: setup_inputs(seed, part) draws one part's arguments, and reference() takes and returns one part's arrays. A program takes and returns all parts, laid end to end along the dimension named above; an argument that names none is the same for every part. Nothing has to cross between parts.
Inputs may be any that keep to these rules, and one draw needn't show every extreme that they name: `head_of`: each of the 12 heads is named by at least 1 entries, and one head by exactly 1.
All inputs are finite; a program needn't handle non-finite values. Where the reference program divides by a largest or mean magnitude, that divisor is 1e-20 or more.
Results may differ from the reference program's by a relative error of at most 0.0063.
Values may be sent and summed in bfloat16 or wider, within the bound.
No kernel may reach another device: no remote copies, remote signals or barrier semaphores. Data moves between devices by JAX's collectives and lax.ppermute only.
A program may use at most 64 MiB of HBM per device.

```python
import math
import jax
import jax.numpy as jnp
import numpy as np
from jax import lax

HEADS = 12
HDIM = 128
DOUT = 1536
TOK_DEV = 16
TOKENS = 128
VALID = 112
HSLOT = 2
MINSERVE = 1
QROWS = 16
N_SEQ = 8


def draw_pair(key):
    seed_query = jax.random.fold_in(key, 101)
    seed_keys = jax.random.fold_in(key, 102)
    dims_all = (2, TOKENS, HEADS * HDIM)
    query_draw = jnp.clip(jax.random.normal(seed_query, dims_all, jnp.float32), -8.0, 8.0)
    keys_draw = jnp.clip(jax.random.normal(seed_keys, dims_all, jnp.float32), -8.0, 8.0)
    return (query_draw, keys_draw)


def draw_queries(key, part):
    return draw_pair(key)[0].astype(jnp.bfloat16)


def draw_key_rows(key, part):
    return draw_pair(key)[1].astype(jnp.bfloat16)


def draw_value_rows(key, part):
    seed_base = jax.random.fold_in(key, 201)
    seed_scale = jax.random.fold_in(key, 202)
    column_scale = jnp.exp(jax.random.uniform(seed_scale, (HEADS * HDIM,), jnp.float32, 0.0, math.log(10.0)))
    base_draw = jax.random.normal(seed_base, (2, TOKENS, HEADS * HDIM), jnp.float32)
    return jnp.clip(base_draw * column_scale[None, None, :], -40.0, 40.0).astype(jnp.bfloat16)


def draw_head_of(key, part):
    slot_total = N_SEQ * HSLOT
    spare = slot_total - HEADS * MINSERVE
    seed_lean = jax.random.fold_in(key, 301)
    seed_pick = jax.random.fold_in(key, 302)
    seed_perm = jax.random.fold_in(key, 303)
    lean_head = jax.random.randint(seed_lean, (), 0, HEADS)
    base_rows = jnp.repeat(jnp.arange(HEADS, dtype=jnp.int32), MINSERVE)
    picked = jax.random.randint(seed_pick, (spare,), 0, HEADS - 1)
    picked = picked + (picked >= lean_head).astype(jnp.int32)
    serving = jnp.concatenate([base_rows, picked.astype(jnp.int32)])
    serving = jax.random.permutation(seed_perm, serving)
    return serving.reshape(N_SEQ, HSLOT).astype(jnp.int32)


def levels(stream_key, dims, split, smallest, high):
    loudness = 1.0
    for axis_at, parts in split:
        draws = jax.random.uniform(jax.random.fold_in(jax.random.fold_in(stream_key, 6), axis_at), (parts,), jnp.float32, smallest / len(split), high / len(split))
        loudness = loudness * jnp.repeat(jnp.exp(draws), dims[axis_at] // parts).reshape((-1,) + (1,) * (len(dims) - 1 - axis_at))
    return loudness


def profile(count, total, limit, slope):
    weights = [(1 << 20) // math.isqrt(rank ** slope) + 1 for rank in range(2, count + 1)]
    spare, given = total - limit - (count - 1), [1] * (count - 1)
    while spare > 0:
        free = [i for i in range(count - 1) if given[i] < limit]
        mass, budget = sum([weights[i] for i in free]), spare
        for i in free:
            more = min(limit - given[i], max(1, budget * weights[i] // mass), spare)
            given[i] = given[i] + more
            spare = spare - more
    return np.array([limit] + given)


def uneven_parts(own_key, number_of, total, bound, skew):
    if number_of == 2:
        one = jax.random.randint(own_key, (), max(1, total - bound), min(bound, total - 1) + 1)
        return jnp.stack([one, total - one])
    sizes = jnp.asarray(profile(number_of, total, bound, skew), jnp.int32)
    couples = (number_of - 1) // 2
    giver, sink = sizes[1:1 + 2 * couples:2], sizes[2:2 + 2 * couples:2]
    margin = jnp.minimum(giver - 1, bound - sink)
    shifted = jax.random.randint(jax.random.fold_in(own_key, 1), (couples,), 0, 1 << 20) % (margin + 1)
    sizes = sizes.at[1:1 + 2 * couples:2].set(giver - shifted).at[2:2 + 2 * couples:2].set(sink + shifted)
    return sizes[jax.random.permutation(jax.random.fold_in(own_key, 2), number_of)]


def centred(key, dims, deviation, most, cuts=(), held_as=jnp.bfloat16):
    factor_of = levels(key, dims, cuts, -0.22, 0.18) if cuts else 1.0
    entries = jax.random.normal(key, dims, jnp.float32) * deviation * factor_of
    return jnp.minimum(jnp.maximum(entries, -most), most).astype(held_as)


def setup_inputs(seed: int = 0, part: int = 0) -> dict:
    streams_of = jax.random.split(jax.random.key(seed), 7)
    part_keys = jax.random.split(jax.random.fold_in(streams_of[6], part), 7)
    queries = draw_queries(jax.random.fold_in(jax.random.fold_in(streams_of[6], part), 71), part)
    key_rows = draw_key_rows(jax.random.fold_in(jax.random.fold_in(streams_of[6], part), 71), part)
    value_rows = draw_value_rows(jax.random.fold_in(jax.random.fold_in(streams_of[6], part), 71), part)
    counts = uneven_parts(part_keys[3], N_SEQ, VALID, TOK_DEV, 2).astype(jnp.int32)
    head_of = draw_head_of(jax.random.fold_in(streams_of[6], 71), part)
    out_weight = centred(streams_of[5], (HEADS * HDIM, DOUT), (HEADS * HDIM) ** -0.5, 0.15625, ((1, 2),))
    return dict(queries=queries, key_rows=key_rows, value_rows=value_rows, counts=counts, head_of=head_of, out_weight=out_weight)


GUIDE_SCALE = 3.0
EPSILON = 1e-06

def slot_layout(head_of):
    flat_heads = head_of.reshape(-1)
    slot_order = jnp.arange(flat_heads.shape[0], dtype=jnp.int32)
    same_head = flat_heads[:, None] == flat_heads[None, :]
    group_size = lax.optimization_barrier(jnp.sum(same_head.astype(jnp.int32), axis=1))
    earlier = same_head & (slot_order[None, :] < slot_order[:, None])
    group_rank = lax.optimization_barrier(jnp.sum(earlier.astype(jnp.int32), axis=1))
    return (flat_heads, group_size, group_rank)

def branch_attention(query_all, key_all, value_all, key_valid):
    scale_factor = 1.0 / math.sqrt(HDIM)
    key_float = key_all.reshape(TOKENS, HEADS, HDIM).astype(jnp.float32)
    value_float = value_all.reshape(TOKENS, HEADS, HDIM).astype(jnp.float32)
    query_tiles = query_all.reshape(N_SEQ, TOK_DEV, HEADS, HDIM)

    def one_tile(query_tile):
        scores = jnp.einsum('qhd,khd->hqk', query_tile.astype(jnp.float32), key_float) * scale_factor
        scores = jnp.where(key_valid[None, None, :], scores, -jnp.inf)
        top_score = lax.optimization_barrier(jnp.max(scores, axis=2, keepdims=True))
        weights = jnp.exp(scores - top_score)
        weight_sum = lax.optimization_barrier(jnp.sum(weights, axis=2))
        rounded = lax.optimization_barrier(weights.astype(jnp.bfloat16))
        mixed = jnp.einsum('hqk,khd->qhd', rounded.astype(jnp.float32), value_float)
        attended = mixed / jnp.transpose(weight_sum)[:, :, None]
        logsum = top_score[:, :, 0] + jnp.log(weight_sum)
        return (attended, logsum)
    return lax.map(one_tile, query_tiles)

def reference(queries, key_rows, value_rows, counts, head_of, out_weight):
    positions = jnp.arange(TOK_DEV, dtype=jnp.int32)
    valid_grid = positions[None, :] < counts[:, None]
    key_valid = valid_grid.reshape(-1)
    flat_heads, group_size, group_rank = slot_layout(head_of)
    row_steps = jnp.arange(QROWS, dtype=jnp.int32)
    served_rows = group_rank[:, None] + group_size[:, None] * row_steps[None, :]
    served_ok = served_rows[:, :, None] < counts[None, None, :]
    clipped = jnp.minimum(served_rows, TOK_DEV - 1)
    attended_all = []
    saved_all = []
    for branch_id in range(2):
        attended, logsum = branch_attention(queries[branch_id], key_rows[branch_id], value_rows[branch_id], key_valid)
        attended = jnp.where(valid_grid[:, :, None, None], attended, 0.0)
        attended_all.append(attended.reshape(TOKENS, HEADS * HDIM).astype(jnp.bfloat16))
        by_head = jnp.transpose(logsum, (1, 2, 0))
        picked = by_head[flat_heads[:, None], clipped]
        saved_rows = jnp.where(served_ok, picked, 0.0).reshape(N_SEQ, HSLOT, QROWS, N_SEQ)
        saved_all.append(saved_rows)
    positive = lax.optimization_barrier(attended_all[0]).astype(jnp.float32)
    negative = lax.optimization_barrier(attended_all[1]).astype(jnp.float32)
    guided = GUIDE_SCALE * positive - (GUIDE_SCALE - 1.0) * negative
    magnitude = lax.optimization_barrier(jnp.mean(jnp.abs(guided), axis=1, keepdims=True))
    normed = (guided / (magnitude + EPSILON)).astype(jnp.bfloat16)
    projected = jnp.dot(normed, out_weight, preferred_element_type=jnp.float32).astype(jnp.bfloat16)
    return (projected, jnp.stack(saved_all))
```

```python
import functools
import math

import jax
import jax.numpy as jnp
from jax import lax
from jax.experimental import pallas as pl
from jax.experimental.pallas import tpu as pltpu
from jax.sharding import PartitionSpec as P

HEADS = 12
HDIM = 128


GUIDE_SCALE = 3.0
EPSILON = 1e-06


def partner_2(array, axis, stride):
    return lax.ppermute(array, axis, [(i, i ^ 1 << stride) for i in range(lax.axis_size(axis))])


def slot_layout(head_of):
    flat_heads = head_of.reshape(-1)
    slot_order = jnp.arange(flat_heads.shape[0], dtype=jnp.int32)
    same_head = flat_heads[:, None] == flat_heads[None, :]
    group_size = jnp.sum(same_head.astype(jnp.int32), axis=1)
    earlier = same_head & (slot_order[None, :] < slot_order[:, None])
    group_rank = jnp.sum(earlier.astype(jnp.int32), axis=1)
    return (flat_heads, group_size, group_rank)


def key_grouping(seq_count, tok_dev):
    shard_limit = max(1, 2048 // tok_dev)
    grouping = 1
    for attempt in range(16):
        if grouping * 2 <= shard_limit and seq_count % (grouping * 2) == 0:
            grouping = grouping * 2
    return grouping


def attend_rows(query_block, key_slot, value_slot, key_valid, key_block):
    row_count = query_block.shape[0]
    head_size = query_block.shape[1]
    block_count = key_slot.shape[0] // key_block
    scale_factor = 1.0 / math.sqrt(head_size)

    def fold_block(block_id, state_in):
        top_score, weight_sum, summed = state_in
        scores = (
            jnp.einsum("qd,kd->qk", query_block, key_slot, preferred_element_type=jnp.float32)
            * scale_factor
        )
        scores = jnp.where(key_valid[None, :], scores, -jnp.inf)
        new_top = jnp.maximum(top_score, jnp.max(scores, axis=1))
        fading = jnp.exp(top_score - new_top)
        weights = jnp.exp(scores - new_top[:, None])
        weight_sum = weight_sum * fading + jnp.sum(weights, axis=1)
        summed = summed * fading[:, None] + jnp.dot(
            weights.astype(jnp.bfloat16), value_slot, preferred_element_type=jnp.float32
        )
        return (new_top, weight_sum, summed)

    start_state = (
        jnp.full((row_count,), -jnp.inf, jnp.float32),
        jnp.zeros((row_count,), jnp.float32),
        jnp.zeros((row_count, head_size), jnp.float32),
    )
    top_score, weight_sum, summed = lax.fori_loop(0, block_count, fold_block, start_state)
    return (summed / weight_sum[:, None], top_score + jnp.log(weight_sum))


def serve_slots(query_items, mask_items, key_recv, value_recv, key_valid, key_block):
    source_count, slot_count, item_count, head_size = query_items.shape
    all_tokens = key_recv.shape[0] * key_recv.shape[2]
    per_block = max(1, 512 // source_count)
    slot_outputs = []
    slot_logsum = []
    for slot_id in range(slot_count):
        key_slot = key_recv[:, slot_id].reshape(all_tokens, head_size)
        value_slot = value_recv[:, slot_id].reshape(all_tokens, head_size)
        taken_items = min(per_block, item_count)
        query_block = query_items[:, slot_id, 0:taken_items].reshape(
            source_count * taken_items, head_size
        )
        attended, logsum = attend_rows(query_block, key_slot, value_slot, key_valid, key_block)
        pieces_out = attended.reshape(source_count, taken_items, head_size)
        pieces_sum = logsum.reshape(source_count, taken_items)
        slot_outputs.append(pieces_out)
        slot_logsum.append(pieces_sum)
    attended = jnp.stack(slot_outputs, axis=1)
    logsum = jnp.stack(slot_logsum, axis=1)
    keep_rows = mask_items > 0
    attended = jnp.where(keep_rows[:, :, :, None], attended, 0.0).astype(jnp.bfloat16)
    logsum = jnp.where(keep_rows, logsum, 0.0)
    return (attended, logsum)


def per_device_exchange(queries, key_rows, value_rows, counts, head_of, out_weight):
    seq_count = lax.axis_size("seq")
    tok_dev = queries.shape[1]
    slot_count = head_of.shape[1]
    fewest = max(1, seq_count * slot_count // (2 * HEADS))
    row_cap = (tok_dev + fewest - 1) // fewest
    my_index = lax.axis_index("seq")
    flat_heads, group_size, group_rank = slot_layout(head_of)
    row_steps = jnp.arange(row_cap, dtype=jnp.int32)
    served_rows = group_rank[:, None] + group_size[:, None] * row_steps[None, :]
    my_count = counts[my_index]
    clipped = jnp.minimum(served_rows, tok_dev - 1)
    query_grid = queries[0].reshape(tok_dev, HEADS, HDIM)
    row_live = served_rows < my_count
    query_send = query_grid[clipped, flat_heads[:, None]]
    query_send = jnp.where(row_live[:, :, None], query_send, jnp.zeros((), jnp.bfloat16)).reshape(
        seq_count, slot_count, row_cap, HDIM
    )
    mask_send = row_live.astype(jnp.bfloat16).reshape(seq_count, slot_count, row_cap)
    token_ids = jnp.arange(tok_dev, dtype=jnp.int32)
    key_grid = key_rows[0].reshape(tok_dev, HEADS, HDIM)
    value_grid = value_rows[0].reshape(tok_dev, HEADS, HDIM)
    key_send = key_grid[token_ids[None, :], flat_heads[:, None]].reshape(
        seq_count, slot_count, tok_dev, HDIM
    )
    value_send = value_grid[token_ids[None, :], flat_heads[:, None]].reshape(
        seq_count, slot_count, tok_dev, HDIM
    )
    key_valid = (token_ids[None, :] < counts[:, None]).reshape(-1)
    key_block = tok_dev * key_grouping(seq_count, tok_dev)
    query_recv, mask_recv, key_recv, value_recv = (
        lax.all_to_all(query_send, "seq", split_axis=0, concat_axis=0, tiled=True),
        lax.all_to_all(mask_send, "seq", split_axis=0, concat_axis=0, tiled=True),
        lax.all_to_all(key_send, "seq", split_axis=0, concat_axis=0, tiled=True),
        lax.all_to_all(value_send, "seq", split_axis=0, concat_axis=0, tiled=True),
    )
    attended, logsum = serve_slots(
        query_recv, mask_recv, key_recv, value_recv, key_valid, key_block
    )
    returned = lax.all_to_all(attended, "seq", split_axis=0, concat_axis=0, tiled=True)
    head_ids = jnp.arange(HEADS, dtype=jnp.int32)
    head_group = jnp.sum((flat_heads[None, :] == head_ids[:, None]).astype(jnp.int32), axis=1)
    row_rank = token_ids[:, None] % head_group[None, :]
    row_step = token_ids[:, None] // head_group[None, :]
    slot_ids = jnp.arange(flat_heads.shape[0], dtype=jnp.int32)
    matched = (flat_heads[None, None, :] == head_ids[None, :, None]) & (
        group_rank[None, None, :] == row_rank[:, :, None]
    )
    owner_slot = jnp.sum(jnp.where(matched, slot_ids[None, None, :], 0), axis=2)
    flat_index = owner_slot * row_cap + row_step
    returned_rows = returned.reshape(-1, HDIM)
    attended_home = returned_rows[flat_index].reshape(tok_dev, HEADS * HDIM)
    partner = partner_2(attended_home, "branch", 0)
    on_positive = lax.axis_index("branch") == 0
    own_value = attended_home.astype(jnp.float32)
    partner_value = partner.astype(jnp.float32)
    positive = jnp.where(on_positive, own_value, partner_value)
    negative = jnp.where(on_positive, partner_value, own_value)
    guided = GUIDE_SCALE * positive - (GUIDE_SCALE - 1.0) * negative
    magnitude = jnp.mean(jnp.abs(guided), axis=1, keepdims=True)
    normed = (guided / (magnitude + EPSILON)).astype(jnp.bfloat16)
    projected = jnp.dot(normed, out_weight, preferred_element_type=jnp.float32).astype(jnp.bfloat16)
    saved_rows = jnp.transpose(logsum, (1, 2, 0)).reshape(1, 1, slot_count, row_cap, seq_count)
    return (projected, saved_rows)


CLIP_AXES = ("seq", "branch")
KERNEL_PARAMS = pltpu.CompilerParams(vmem_limit_bytes=16 * 1024 * 1024)


def clip_position():
    return lax.axis_index("seq"), lax.axis_index("branch")


def swap_with(array, offset, device_count):
    return lax.ppermute(array, CLIP_AXES, [(i, i ^ offset) for i in range(device_count)])


def pack_kernel(device_count, head_ref, query_ref, key_ref, value_ref, *message_refs):
    shard, core = clip_position()
    tok_dev = query_ref.shape[1]
    for offset in range(device_count):
        head = head_ref[core ^ (offset % 2), shard ^ (offset // 2)]
        columns = pl.ds(pl.multiple_of(head * HDIM, HDIM), HDIM)
        for part, source_ref in enumerate((query_ref, key_ref, value_ref)):
            message_refs[offset][pl.ds(part * tok_dev, tok_dev), :] = source_ref[0, :, columns]


def attend_kernel(device_count, head_ref, counts_ref, *refs):
    message_refs = refs[:device_count]
    guided_refs = refs[device_count : device_count + device_count // 2]
    own_tile_ref, other_tile_ref = refs[device_count + device_count // 2 :]
    shard_count = device_count // 2
    shard, core = clip_position()
    tok_dev = message_refs[0].shape[0] // 3
    tokens = shard_count * tok_dev
    row_cap = own_tile_ref.shape[1]
    shard_tokens = [counts_ref[shard ^ block] for block in range(shard_count)]

    lane = lax.broadcasted_iota(jnp.int32, (1, tokens), 1)
    lane_block = lane // tok_dev
    lane_limit = jnp.zeros((1, tokens), jnp.int32)
    for block in range(shard_count):
        lane_limit = jnp.where(lane_block == block, shard_tokens[block], lane_limit)
    key_valid = lane - lane_block * tok_dev < lane_limit

    scale_factor = 1.0 / math.sqrt(HDIM)
    attended = []
    logsums = []
    for side in range(2):
        sides = [message_refs[2 * block + side] for block in range(shard_count)]

        def gathered(part):
            return jnp.concatenate(
                [ref[pl.ds(part * tok_dev, tok_dev), :] for ref in sides], axis=0
            )

        scores = (
            lax.dot_general(
                gathered(0),
                gathered(1),
                (((1,), (1,)), ((), ())),
                preferred_element_type=jnp.float32,
            )
            * scale_factor
        )
        scores = jnp.where(key_valid, scores, -jnp.inf)
        top_score = jnp.max(scores, axis=1, keepdims=True)
        weights = jnp.exp(scores - top_score)
        weight_sum = jnp.sum(weights, axis=1, keepdims=True)
        mixed = jnp.dot(
            weights.astype(jnp.bfloat16), gathered(2), preferred_element_type=jnp.float32
        )
        attended.append((mixed / weight_sum).astype(jnp.bfloat16).astype(jnp.float32))
        logsums.append(top_score + jnp.log(weight_sum))

    own_scale = jnp.where(core == 0, GUIDE_SCALE, 1.0 - GUIDE_SCALE)
    other_scale = jnp.where(core == 0, 1.0 - GUIDE_SCALE, GUIDE_SCALE)
    guided = own_scale * attended[0] + other_scale * attended[1]
    row = lax.broadcasted_iota(jnp.int32, (tok_dev, HDIM), 0)
    for block in range(shard_count):
        rows = guided[block * tok_dev : (block + 1) * tok_dev]
        rows = jnp.where(row < shard_tokens[block], rows, 0.0)
        guided_refs[block][...] = rows.astype(jnp.bfloat16)

    my_head = head_ref[core, shard]
    group_size = jnp.int32(0)
    group_rank = jnp.int32(0)
    for other_shard in range(head_ref.shape[1]):
        for other_core in range(head_ref.shape[0]):
            same = (head_ref[other_core, other_shard] == my_head).astype(jnp.int32)
            earlier = (other_shard * 2 + other_core < shard * 2 + core).astype(jnp.int32)
            group_size = group_size + same
            group_rank = group_rank + same * earlier
    token = lax.broadcasted_iota(jnp.int32, (tok_dev, row_cap), 0)
    step = lax.broadcasted_iota(jnp.int32, (tok_dev, row_cap), 1)
    served = group_rank + group_size * step
    for side, tile_ref in enumerate((own_tile_ref, other_tile_ref)):
        for block in range(shard_count):
            taken = (token == served) & (served < shard_tokens[block])
            column = logsums[side][block * tok_dev : (block + 1) * tok_dev]
            line = jnp.sum(jnp.where(taken, column, 0.0), axis=0, keepdims=True)
            tile_ref[pl.ds(shard ^ block, 1), :] = line


def project_kernel(device_count, head_ref, weight_ref, own_tile_ref, other_tile_ref, *refs):
    message_refs = refs[:device_count]
    projected_ref, saved_ref, guided_ref = refs[device_count:]
    shard, core = clip_position()
    saved_ref[core] = own_tile_ref[...]
    saved_ref[1 - core] = other_tile_ref[...]
    for offset in range(device_count):
        head = head_ref[core ^ (offset % 2), shard ^ (offset // 2)]
        columns = pl.ds(pl.multiple_of(head * HDIM, HDIM), HDIM)
        guided_ref[:, columns] = message_refs[offset][...]
    guided = guided_ref[...]
    magnitude = jnp.mean(jnp.abs(guided.astype(jnp.float32)), axis=1, keepdims=True)
    total = jnp.dot(guided, weight_ref[...], preferred_element_type=jnp.float32)
    projected_ref[...] = (total / (magnitude + EPSILON)).astype(jnp.bfloat16)


def per_device_direct(queries, key_rows, value_rows, counts, head_of, out_weight):
    seq_count = lax.axis_size("seq")
    device_count = seq_count * lax.axis_size("branch")
    tok_dev = queries.shape[1]
    slot_count = head_of.shape[1]
    fewest = max(1, seq_count * slot_count // (2 * HEADS))
    row_cap = (tok_dev + fewest - 1) // fewest
    head_table = jnp.transpose(head_of)
    smem = pl.BlockSpec(memory_space=pltpu.SMEM)
    vmem = pl.BlockSpec(memory_space=pltpu.VMEM)

    def held(array):
        return pltpu.with_memory_space_constraint(array, pltpu.VMEM)

    messages = pl.pallas_call(
        functools.partial(pack_kernel, device_count),
        out_shape=[pltpu.VMEM((3 * tok_dev, HDIM), jnp.bfloat16)] * device_count,
        in_specs=[smem] + [vmem] * 3,
        out_specs=[vmem] * device_count,
        compiler_params=KERNEL_PARAMS,
        name="pack",
    )(head_table, queries, key_rows, value_rows)
    arrived = [messages[0]] + [
        swap_with(messages[offset], offset, device_count) for offset in range(1, device_count)
    ]
    results = pl.pallas_call(
        functools.partial(attend_kernel, device_count),
        out_shape=[pltpu.VMEM((tok_dev, HDIM), jnp.bfloat16)] * seq_count
        + [pltpu.VMEM((seq_count, row_cap), jnp.float32)] * 2,
        in_specs=[smem] * 2 + [vmem] * device_count,
        out_specs=[vmem] * (seq_count + 2),
        compiler_params=KERNEL_PARAMS,
        name="attend",
    )(head_table, counts, *[held(message) for message in arrived])
    guided = results[:seq_count]
    own_tile, lent_tile = results[seq_count:]
    returned = [guided[0]] + [
        swap_with(guided[offset // 2], offset, device_count) for offset in range(1, device_count)
    ]
    other_tile = swap_with(lent_tile, 1, device_count)
    projected, saved = pl.pallas_call(
        functools.partial(project_kernel, device_count),
        out_shape=[
            jax.ShapeDtypeStruct((tok_dev, out_weight.shape[1]), jnp.bfloat16),
            jax.ShapeDtypeStruct((slot_count, seq_count, row_cap), jnp.float32),
        ],
        in_specs=[smem] + [vmem] * (3 + device_count),
        out_specs=[vmem] * 2,
        scratch_shapes=[pltpu.VMEM((tok_dev, HEADS * HDIM), jnp.bfloat16)],
        compiler_params=KERNEL_PARAMS,
        name="project",
    )(head_table, held(out_weight), held(own_tile), held(other_tile), *[held(r) for r in returned])
    saved = jnp.transpose(saved, (0, 2, 1))
    return (projected, saved.reshape(1, 1, slot_count, row_cap, seq_count))


def solution(mesh):
    seq_count = mesh.shape["seq"]
    few_devices = seq_count & (seq_count - 1) == 0 and seq_count <= HEADS
    return jax.shard_map(
        per_device_direct if few_devices else per_device_exchange,
        mesh=mesh,
        in_specs=(
            P("branch", ("groups", "seq"), None),
            P("branch", ("groups", "seq"), None),
            P("branch", ("groups", "seq"), None),
            P("groups"),
            P(),
            P(None, "branch"),
        ),
        out_specs=(
            P(("groups", "seq"), "branch"),
            P("branch", ("groups", "seq"), None, None, None),
        ),
        check_vma=False,
    )
```

```python
import functools
import math

import jax
import jax.numpy as jnp
from jax import lax
from jax.experimental import pallas as pl
from jax.experimental.pallas import tpu as pltpu
from jax.sharding import PartitionSpec as P

HEADS = 12
HDIM = 128


GUIDE_SCALE = 3.0
EPSILON = 1e-06


def partner_2(array, axis, stride):
    return lax.ppermute(array, axis, [(i, i ^ 1 << stride) for i in range(lax.axis_size(axis))])


def slot_layout(head_of):
    flat_heads = head_of.reshape(-1)
    slot_order = jnp.arange(flat_heads.shape[0], dtype=jnp.int32)
    same_head = flat_heads[:, None] == flat_heads[None, :]
    group_size = jnp.sum(same_head.astype(jnp.int32), axis=1)
    earlier = same_head & (slot_order[None, :] < slot_order[:, None])
    group_rank = jnp.sum(earlier.astype(jnp.int32), axis=1)
    return (flat_heads, group_size, group_rank)


def key_grouping(seq_count, tok_dev):
    shard_limit = max(1, 2048 // tok_dev)
    grouping = 1
    for attempt in range(16):
        if grouping * 2 <= shard_limit and seq_count % (grouping * 2) == 0:
            grouping = grouping * 2
    return grouping


def attend_rows(query_block, key_slot, value_slot, key_valid, key_block):
    row_count = query_block.shape[0]
    head_size = query_block.shape[1]
    block_count = key_slot.shape[0] // key_block
    scale_factor = 1.0 / math.sqrt(head_size)

    def fold_block(block_id, state_in):
        top_score, weight_sum, summed = state_in
        scores = (
            jnp.einsum("qd,kd->qk", query_block, key_slot, preferred_element_type=jnp.float32)
            * scale_factor
        )
        scores = jnp.where(key_valid[None, :], scores, -jnp.inf)
        new_top = jnp.maximum(top_score, jnp.max(scores, axis=1))
        fading = jnp.exp(top_score - new_top)
        weights = jnp.exp(scores - new_top[:, None])
        weight_sum = weight_sum * fading + jnp.sum(weights, axis=1)
        summed = summed * fading[:, None] + jnp.dot(
            weights.astype(jnp.bfloat16), value_slot, preferred_element_type=jnp.float32
        )
        return (new_top, weight_sum, summed)

    start_state = (
        jnp.full((row_count,), -jnp.inf, jnp.float32),
        jnp.zeros((row_count,), jnp.float32),
        jnp.zeros((row_count, head_size), jnp.float32),
    )
    top_score, weight_sum, summed = lax.fori_loop(0, block_count, fold_block, start_state)
    return (summed / weight_sum[:, None], top_score + jnp.log(weight_sum))


def serve_slots(query_items, mask_items, key_recv, value_recv, key_valid, key_block):
    source_count, slot_count, item_count, head_size = query_items.shape
    all_tokens = key_recv.shape[0] * key_recv.shape[2]
    per_block = max(1, 512 // source_count)
    slot_outputs = []
    slot_logsum = []
    for slot_id in range(slot_count):
        key_slot = key_recv[:, slot_id].reshape(all_tokens, head_size)
        value_slot = value_recv[:, slot_id].reshape(all_tokens, head_size)
        taken_items = min(per_block, item_count)
        query_block = query_items[:, slot_id, 0:taken_items].reshape(
            source_count * taken_items, head_size
        )
        attended, logsum = attend_rows(query_block, key_slot, value_slot, key_valid, key_block)
        pieces_out = attended.reshape(source_count, taken_items, head_size)
        pieces_sum = logsum.reshape(source_count, taken_items)
        slot_outputs.append(pieces_out)
        slot_logsum.append(pieces_sum)
    attended = jnp.stack(slot_outputs, axis=1)
    logsum = jnp.stack(slot_logsum, axis=1)
    keep_rows = mask_items > 0
    attended = jnp.where(keep_rows[:, :, :, None], attended, 0.0).astype(jnp.bfloat16)
    logsum = jnp.where(keep_rows, logsum, 0.0)
    return (attended, logsum)


def per_device_exchange(queries, key_rows, value_rows, counts, head_of, out_weight):
    seq_count = lax.axis_size("seq")
    tok_dev = queries.shape[1]
    slot_count = head_of.shape[1]
    fewest = max(1, seq_count * slot_count // (2 * HEADS))
    row_cap = (tok_dev + fewest - 1) // fewest
    my_index = lax.axis_index("seq")
    flat_heads, group_size, group_rank = slot_layout(head_of)
    row_steps = jnp.arange(row_cap, dtype=jnp.int32)
    served_rows = group_rank[:, None] + group_size[:, None] * row_steps[None, :]
    my_count = counts[my_index]
    clipped = jnp.minimum(served_rows, tok_dev - 1)
    query_grid = queries[0].reshape(tok_dev, HEADS, HDIM)
    row_live = served_rows < my_count
    query_send = query_grid[clipped, flat_heads[:, None]]
    query_send = jnp.where(row_live[:, :, None], query_send, jnp.zeros((), jnp.bfloat16)).reshape(
        seq_count, slot_count, row_cap, HDIM
    )
    mask_send = row_live.astype(jnp.bfloat16).reshape(seq_count, slot_count, row_cap)
    token_ids = jnp.arange(tok_dev, dtype=jnp.int32)
    key_grid = key_rows[0].reshape(tok_dev, HEADS, HDIM)
    value_grid = value_rows[0].reshape(tok_dev, HEADS, HDIM)
    key_send = key_grid[token_ids[None, :], flat_heads[:, None]].reshape(
        seq_count, slot_count, tok_dev, HDIM
    )
    value_send = value_grid[token_ids[None, :], flat_heads[:, None]].reshape(
        seq_count, slot_count, tok_dev, HDIM
    )
    key_valid = (token_ids[None, :] < counts[:, None]).reshape(-1)
    key_block = tok_dev * key_grouping(seq_count, tok_dev)
    query_recv, mask_recv, key_recv, value_recv = (
        lax.all_to_all(query_send, "seq", split_axis=0, concat_axis=0, tiled=True),
        lax.all_to_all(mask_send, "seq", split_axis=0, concat_axis=0, tiled=True),
        lax.all_to_all(key_send, "seq", split_axis=0, concat_axis=0, tiled=True),
        lax.all_to_all(value_send, "seq", split_axis=0, concat_axis=0, tiled=True),
    )
    attended, logsum = serve_slots(
        query_recv, mask_recv, key_recv, value_recv, key_valid, key_block
    )
    returned = lax.all_to_all(attended, "seq", split_axis=0, concat_axis=0, tiled=True)
    head_ids = jnp.arange(HEADS, dtype=jnp.int32)
    head_group = jnp.sum((flat_heads[None, :] == head_ids[:, None]).astype(jnp.int32), axis=1)
    row_rank = token_ids[:, None] % head_group[None, :]
    row_step = token_ids[:, None] // head_group[None, :]
    slot_ids = jnp.arange(flat_heads.shape[0], dtype=jnp.int32)
    matched = (flat_heads[None, None, :] == head_ids[None, :, None]) & (
        group_rank[None, None, :] == row_rank[:, :, None]
    )
    owner_slot = jnp.sum(jnp.where(matched, slot_ids[None, None, :], 0), axis=2)
    flat_index = owner_slot * row_cap + row_step
    returned_rows = returned.reshape(-1, HDIM)
    attended_home = returned_rows[flat_index].reshape(tok_dev, HEADS * HDIM)
    partner = partner_2(attended_home, "branch", 0)
    on_positive = lax.axis_index("branch") == 0
    own_value = attended_home.astype(jnp.float32)
    partner_value = partner.astype(jnp.float32)
    positive = jnp.where(on_positive, own_value, partner_value)
    negative = jnp.where(on_positive, partner_value, own_value)
    guided = GUIDE_SCALE * positive - (GUIDE_SCALE - 1.0) * negative
    magnitude = jnp.mean(jnp.abs(guided), axis=1, keepdims=True)
    normed = (guided / (magnitude + EPSILON)).astype(jnp.bfloat16)
    projected = jnp.dot(normed, out_weight, preferred_element_type=jnp.float32).astype(jnp.bfloat16)
    saved_rows = jnp.transpose(logsum, (1, 2, 0)).reshape(1, 1, slot_count, row_cap, seq_count)
    return (projected, saved_rows)


KERNEL_PARAMS = pltpu.CompilerParams(vmem_limit_bytes=16 * 1024 * 1024)


def softmax_parts(query_rows, key_all, key_valid):
    scores = (
        lax.dot_general(
            query_rows, key_all, (((1,), (1,)), ((), ())), preferred_element_type=jnp.float32
        )
        * (1.0 / math.sqrt(HDIM))
    )
    scores = jnp.where(key_valid, scores, -jnp.inf)
    top_score = jnp.max(scores, axis=1, keepdims=True)
    weights = jnp.exp(scores - top_score)
    weight_sum = jnp.sum(weights, axis=1, keepdims=True)
    return top_score, weights, weight_sum


def attend_kernel(
    head_hbm,
    counts_hbm,
    query_hbm,
    key_all_hbm,
    value_all_hbm,
    query_all_hbm,
    weight_hbm,
    attended_ref,
    weight_out_ref,
    saved_ref,
    head_ref,
    counts_ref,
    query_ref,
    key_all_ref,
    value_all_ref,
    query_all_ref,
    copy_sems,
):
    copies = [
        pltpu.make_async_copy(source, target, copy_sems.at[number])
        for number, (source, target) in enumerate(
            (
                (counts_hbm, counts_ref),
                (head_hbm, head_ref),
                (query_hbm, query_ref),
                (key_all_hbm, key_all_ref),
                (value_all_hbm, value_all_ref),
                (query_all_hbm, query_all_ref),
                (weight_hbm, weight_out_ref),
            )
        )
    ]
    for copy in copies:
        copy.start()
    for copy in copies[:5]:
        copy.wait()
    shard = lax.axis_index("seq")
    tokens = key_all_ref.shape[0]
    tok_dev = query_ref.shape[1]
    shard_count = tokens // tok_dev
    slot_count, _, row_cap = saved_ref.shape
    shard_tokens = [counts_ref[block] for block in range(shard_count)]

    lane = lax.broadcasted_iota(jnp.int32, (1, tokens), 1)
    lane_block = lane // tok_dev
    lane_limit = jnp.zeros((1, tokens), jnp.int32)
    for block in range(shard_count):
        lane_limit = jnp.where(lane_block == block, shard_tokens[block], lane_limit)
    key_valid = lane - lane_block * tok_dev < lane_limit

    row_valid = lax.broadcasted_iota(jnp.int32, (tok_dev, HDIM), 0) < counts_ref[shard]
    for head in range(HEADS):
        columns = pl.ds(head * HDIM, HDIM)
        _, weights, weight_sum = softmax_parts(
            query_ref[0, :, columns], key_all_ref[:, columns], key_valid
        )
        mixed = jnp.dot(
            weights.astype(jnp.bfloat16),
            value_all_ref[:, columns],
            preferred_element_type=jnp.float32,
        )
        rows = jnp.where(row_valid, mixed / weight_sum, 0.0)
        attended_ref[:, columns] = rows.astype(jnp.bfloat16)

    copies[5].wait()
    token = lax.broadcasted_iota(jnp.int32, (tok_dev, row_cap), 0)
    step = lax.broadcasted_iota(jnp.int32, (tok_dev, row_cap), 1)
    for slot in range(slot_count):
        head = head_ref[slot, shard]
        group_size = jnp.int32(0)
        group_rank = jnp.int32(0)
        for other_shard in range(shard_count):
            for other_slot in range(slot_count):
                same = (head_ref[other_slot, other_shard] == head).astype(jnp.int32)
                before = other_shard * slot_count + other_slot < shard * slot_count + slot
                group_size = group_size + same
                group_rank = group_rank + same * before.astype(jnp.int32)
        columns = pl.ds(pl.multiple_of(head * HDIM, HDIM), HDIM)
        top_score, _, weight_sum = softmax_parts(
            query_all_ref[:, columns], key_all_ref[:, columns], key_valid
        )
        logsum = top_score + jnp.log(weight_sum)
        served = group_rank + group_size * step
        for block in range(shard_count):
            taken = (token == served) & (served < shard_tokens[block])
            column = logsum[block * tok_dev : (block + 1) * tok_dev]
            saved_ref[slot, pl.ds(block, 1), :] = jnp.sum(
                jnp.where(taken, column, 0.0), axis=0, keepdims=True
            )
    copies[6].wait()


def project_kernel(own_ref, partner_ref, weight_ref, projected_ref):
    on_positive = lax.axis_index("branch") == 0
    own_scale = jnp.where(on_positive, GUIDE_SCALE, 1.0 - GUIDE_SCALE)
    partner_scale = jnp.where(on_positive, 1.0 - GUIDE_SCALE, GUIDE_SCALE)
    guided = own_scale * own_ref[...].astype(jnp.float32) + partner_scale * partner_ref[
        ...
    ].astype(jnp.float32)
    magnitude = jnp.mean(jnp.abs(guided), axis=1, keepdims=True)
    normed = (guided / (magnitude + EPSILON)).astype(jnp.bfloat16)
    projected_ref[...] = jnp.dot(
        normed, weight_ref[...], preferred_element_type=jnp.float32
    ).astype(jnp.bfloat16)


def per_device_gathered(queries, key_rows, value_rows, counts, head_of, out_weight):
    seq_count = lax.axis_size("seq")
    tok_dev = queries.shape[1]
    tokens = seq_count * tok_dev
    width = HEADS * HDIM
    slot_count = head_of.shape[1]
    fewest = max(1, seq_count * slot_count // (2 * HEADS))
    row_cap = (tok_dev + fewest - 1) // fewest
    vmem = pl.BlockSpec(memory_space=pltpu.VMEM)

    query_all, key_all, value_all = [
        lax.all_gather(array[0], "seq", axis=0, tiled=True)
        for array in (queries, key_rows, value_rows)
    ]
    attended, weight_held, saved = pl.pallas_call(
        attend_kernel,
        out_shape=[
            pltpu.VMEM((tok_dev, width), jnp.bfloat16),
            pltpu.VMEM(out_weight.shape, jnp.bfloat16),
            jax.ShapeDtypeStruct((slot_count, seq_count, row_cap), jnp.float32),
        ],
        in_specs=[pl.BlockSpec(memory_space=pl.ANY)] * 7,
        out_specs=[vmem] * 3,
        scratch_shapes=[
            pltpu.SMEM((slot_count, seq_count), jnp.int32),
            pltpu.SMEM((seq_count,), jnp.int32),
            pltpu.VMEM((1, tok_dev, width), jnp.bfloat16),
        ]
        + [pltpu.VMEM((tokens, width), jnp.bfloat16)] * 3
        + [pltpu.SemaphoreType.DMA((7,))],
        compiler_params=KERNEL_PARAMS,
        name="attend",
    )(
        *[
            pltpu.with_memory_space_constraint(array, pltpu.HBM)
            for array in (
                jnp.transpose(head_of),
                counts,
                queries,
                key_all,
                value_all,
                query_all,
                out_weight,
            )
        ]
    )
    partner = partner_2(attended, "branch", 0)
    projected = pl.pallas_call(
        project_kernel,
        out_shape=jax.ShapeDtypeStruct((tok_dev, out_weight.shape[1]), jnp.bfloat16),
        in_specs=[vmem] * 3,
        out_specs=vmem,
        compiler_params=KERNEL_PARAMS,
        name="project",
    )(*[pltpu.with_memory_space_constraint(x, pltpu.VMEM) for x in (attended, partner, weight_held)])
    saved = jnp.transpose(saved, (0, 2, 1))
    return (projected, saved.reshape(1, 1, slot_count, row_cap, seq_count))


def solution(mesh):
    per_device = per_device_gathered if mesh.shape["seq"] <= HEADS else per_device_exchange
    return jax.shard_map(
        per_device,
        mesh=mesh,
        in_specs=(
            P("branch", ("groups", "seq"), None),
            P("branch", ("groups", "seq"), None),
            P("branch", ("groups", "seq"), None),
            P("groups"),
            P(),
            P(None, "branch"),
        ),
        out_specs=(
            P(("groups", "seq"), "branch"),
            P("branch", ("groups", "seq"), None, None, None),
        ),
        check_vma=False,
    )
```

```python
import functools
import math

import jax
import jax.numpy as jnp
from jax import lax
from jax.experimental import pallas as pl
from jax.experimental.pallas import tpu as pltpu
from jax.sharding import PartitionSpec as P

HEADS = 12
HDIM = 128


GUIDE_SCALE = 3.0
EPSILON = 1e-06


def partner_2(array, axis, stride):
    return lax.ppermute(array, axis, [(i, i ^ 1 << stride) for i in range(lax.axis_size(axis))])


def slot_layout(head_of):
    flat_heads = head_of.reshape(-1)
    slot_order = jnp.arange(flat_heads.shape[0], dtype=jnp.int32)
    same_head = flat_heads[:, None] == flat_heads[None, :]
    group_size = jnp.sum(same_head.astype(jnp.int32), axis=1)
    earlier = same_head & (slot_order[None, :] < slot_order[:, None])
    group_rank = jnp.sum(earlier.astype(jnp.int32), axis=1)
    return (flat_heads, group_size, group_rank)


def key_grouping(seq_count, tok_dev):
    shard_limit = max(1, 2048 // tok_dev)
    grouping = 1
    for attempt in range(16):
        if grouping * 2 <= shard_limit and seq_count % (grouping * 2) == 0:
            grouping = grouping * 2
    return grouping


def attend_rows(query_block, key_slot, value_slot, key_valid, key_block):
    row_count = query_block.shape[0]
    head_size = query_block.shape[1]
    block_count = key_slot.shape[0] // key_block
    scale_factor = 1.0 / math.sqrt(head_size)

    def fold_block(block_id, state_in):
        top_score, weight_sum, summed = state_in
        scores = (
            jnp.einsum("qd,kd->qk", query_block, key_slot, preferred_element_type=jnp.float32)
            * scale_factor
        )
        scores = jnp.where(key_valid[None, :], scores, -jnp.inf)
        new_top = jnp.maximum(top_score, jnp.max(scores, axis=1))
        fading = jnp.exp(top_score - new_top)
        weights = jnp.exp(scores - new_top[:, None])
        weight_sum = weight_sum * fading + jnp.sum(weights, axis=1)
        summed = summed * fading[:, None] + jnp.dot(
            weights.astype(jnp.bfloat16), value_slot, preferred_element_type=jnp.float32
        )
        return (new_top, weight_sum, summed)

    start_state = (
        jnp.full((row_count,), -jnp.inf, jnp.float32),
        jnp.zeros((row_count,), jnp.float32),
        jnp.zeros((row_count, head_size), jnp.float32),
    )
    top_score, weight_sum, summed = lax.fori_loop(0, block_count, fold_block, start_state)
    return (summed / weight_sum[:, None], top_score + jnp.log(weight_sum))


def serve_slots(query_items, mask_items, key_recv, value_recv, key_valid, key_block):
    source_count, slot_count, item_count, head_size = query_items.shape
    all_tokens = key_recv.shape[0] * key_recv.shape[2]
    per_block = max(1, 512 // source_count)
    slot_outputs = []
    slot_logsum = []
    for slot_id in range(slot_count):
        key_slot = key_recv[:, slot_id].reshape(all_tokens, head_size)
        value_slot = value_recv[:, slot_id].reshape(all_tokens, head_size)
        taken_items = min(per_block, item_count)
        query_block = query_items[:, slot_id, 0:taken_items].reshape(
            source_count * taken_items, head_size
        )
        attended, logsum = attend_rows(query_block, key_slot, value_slot, key_valid, key_block)
        pieces_out = attended.reshape(source_count, taken_items, head_size)
        pieces_sum = logsum.reshape(source_count, taken_items)
        slot_outputs.append(pieces_out)
        slot_logsum.append(pieces_sum)
    attended = jnp.stack(slot_outputs, axis=1)
    logsum = jnp.stack(slot_logsum, axis=1)
    keep_rows = mask_items > 0
    attended = jnp.where(keep_rows[:, :, :, None], attended, 0.0).astype(jnp.bfloat16)
    logsum = jnp.where(keep_rows, logsum, 0.0)
    return (attended, logsum)


def per_device_exchange(queries, key_rows, value_rows, counts, head_of, out_weight):
    seq_count = lax.axis_size("seq")
    tok_dev = queries.shape[1]
    slot_count = head_of.shape[1]
    fewest = max(1, seq_count * slot_count // (2 * HEADS))
    row_cap = (tok_dev + fewest - 1) // fewest
    my_index = lax.axis_index("seq")
    flat_heads, group_size, group_rank = slot_layout(head_of)
    row_steps = jnp.arange(row_cap, dtype=jnp.int32)
    served_rows = group_rank[:, None] + group_size[:, None] * row_steps[None, :]
    my_count = counts[my_index]
    clipped = jnp.minimum(served_rows, tok_dev - 1)
    query_grid = queries[0].reshape(tok_dev, HEADS, HDIM)
    row_live = served_rows < my_count
    query_send = query_grid[clipped, flat_heads[:, None]]
    query_send = jnp.where(row_live[:, :, None], query_send, jnp.zeros((), jnp.bfloat16)).reshape(
        seq_count, slot_count, row_cap, HDIM
    )
    mask_send = row_live.astype(jnp.bfloat16).reshape(seq_count, slot_count, row_cap)
    token_ids = jnp.arange(tok_dev, dtype=jnp.int32)
    key_grid = key_rows[0].reshape(tok_dev, HEADS, HDIM)
    value_grid = value_rows[0].reshape(tok_dev, HEADS, HDIM)
    key_send = key_grid[token_ids[None, :], flat_heads[:, None]].reshape(
        seq_count, slot_count, tok_dev, HDIM
    )
    value_send = value_grid[token_ids[None, :], flat_heads[:, None]].reshape(
        seq_count, slot_count, tok_dev, HDIM
    )
    key_valid = (token_ids[None, :] < counts[:, None]).reshape(-1)
    key_block = tok_dev * key_grouping(seq_count, tok_dev)
    query_recv, mask_recv, key_recv, value_recv = (
        lax.all_to_all(query_send, "seq", split_axis=0, concat_axis=0, tiled=True),
        lax.all_to_all(mask_send, "seq", split_axis=0, concat_axis=0, tiled=True),
        lax.all_to_all(key_send, "seq", split_axis=0, concat_axis=0, tiled=True),
        lax.all_to_all(value_send, "seq", split_axis=0, concat_axis=0, tiled=True),
    )
    attended, logsum = serve_slots(
        query_recv, mask_recv, key_recv, value_recv, key_valid, key_block
    )
    returned = lax.all_to_all(attended, "seq", split_axis=0, concat_axis=0, tiled=True)
    head_ids = jnp.arange(HEADS, dtype=jnp.int32)
    head_group = jnp.sum((flat_heads[None, :] == head_ids[:, None]).astype(jnp.int32), axis=1)
    row_rank = token_ids[:, None] % head_group[None, :]
    row_step = token_ids[:, None] // head_group[None, :]
    slot_ids = jnp.arange(flat_heads.shape[0], dtype=jnp.int32)
    matched = (flat_heads[None, None, :] == head_ids[None, :, None]) & (
        group_rank[None, None, :] == row_rank[:, :, None]
    )
    owner_slot = jnp.sum(jnp.where(matched, slot_ids[None, None, :], 0), axis=2)
    flat_index = owner_slot * row_cap + row_step
    returned_rows = returned.reshape(-1, HDIM)
    attended_home = returned_rows[flat_index].reshape(tok_dev, HEADS * HDIM)
    partner = partner_2(attended_home, "branch", 0)
    on_positive = lax.axis_index("branch") == 0
    own_value = attended_home.astype(jnp.float32)
    partner_value = partner.astype(jnp.float32)
    positive = jnp.where(on_positive, own_value, partner_value)
    negative = jnp.where(on_positive, partner_value, own_value)
    guided = GUIDE_SCALE * positive - (GUIDE_SCALE - 1.0) * negative
    magnitude = jnp.mean(jnp.abs(guided), axis=1, keepdims=True)
    normed = (guided / (magnitude + EPSILON)).astype(jnp.bfloat16)
    projected = jnp.dot(normed, out_weight, preferred_element_type=jnp.float32).astype(jnp.bfloat16)
    saved_rows = jnp.transpose(logsum, (1, 2, 0)).reshape(1, 1, slot_count, row_cap, seq_count)
    return (projected, saved_rows)


KERNEL_PARAMS = pltpu.CompilerParams(vmem_limit_bytes=16 * 1024 * 1024)


def swap_shards(array, offset):
    pairs = [(i, i ^ offset) for i in range(lax.axis_size("seq"))]
    return lax.ppermute(array, "seq", pairs)


def split_offset(shard_count):
    return 2 if shard_count > 2 else 1


def gather_offsets(shard_count):
    split = split_offset(shard_count)
    offsets = [1 << bit for bit in range(shard_count.bit_length() - 1)]
    return [offset for offset in reversed(offsets) if offset != split]


def set_order(shard_count):
    order = [0, split_offset(shard_count)]
    for offset in gather_offsets(shard_count):
        order = order + [member ^ offset for member in order]
    return order


def pack_kernel(
    query_hbm,
    key_hbm,
    value_hbm,
    counts_hbm,
    head_hbm,
    kv_own_ref,
    query_own_ref,
    kv_send_ref,
    query_send_ref,
    limits_ref,
    pick_ref,
    slot_head_ref,
    counts_ref,
    head_ref,
    copy_sems,
):
    tok_dev, half_width = query_own_ref.shape
    slot_count, shard_count = head_ref.shape
    shard = lax.axis_index("seq")
    half = (shard // split_offset(shard_count)) % 2
    mine = pl.ds(pl.multiple_of(half * half_width, half_width), half_width)
    others = pl.ds(pl.multiple_of((1 - half) * half_width, half_width), half_width)
    key_rows, value_rows = pl.ds(0, tok_dev), pl.ds(tok_dev, tok_dev)
    copies = [
        pltpu.make_async_copy(source, target, copy_sems.at[number])
        for number, (source, target) in enumerate(
            (
                (counts_hbm, counts_ref),
                (head_hbm, head_ref),
                (key_hbm.at[0, :, others], kv_send_ref.at[key_rows, :]),
                (value_hbm.at[0, :, others], kv_send_ref.at[value_rows, :]),
                (key_hbm.at[0, :, mine], kv_own_ref.at[key_rows, :]),
                (value_hbm.at[0, :, mine], kv_own_ref.at[value_rows, :]),
                (query_hbm.at[0, :, others], query_send_ref),
                (query_hbm.at[0, :, mine], query_own_ref),
            )
        )
    ]
    for copy in copies:
        copy.start()
    copies[0].wait()
    copies[1].wait()

    lane = lax.broadcasted_iota(jnp.int32, (1, limits_ref.shape[1]), 1)
    lane_limit = jnp.zeros(lane.shape, jnp.int32)
    for place, offset in enumerate(set_order(shard_count)):
        lane_limit = jnp.where(lane // tok_dev == place, counts_ref[shard ^ offset], lane_limit)
    limits_ref[0:1, :] = (lane % tok_dev < lane_limit).astype(jnp.int32)
    limits_ref[1:2, :] = jnp.full(lane.shape, counts_ref[shard], jnp.int32)
    split = split_offset(shard_count)
    limits_ref[2:3, :] = jnp.full(lane.shape, counts_ref[shard ^ split], jnp.int32)

    step = lax.broadcasted_iota(jnp.int32, (1, pick_ref.shape[2]), 1)
    for slot in range(slot_count):
        head = head_ref[slot, shard]
        group_size = jnp.int32(0)
        group_rank = jnp.int32(0)
        for other_shard in range(shard_count):
            for other_slot in range(slot_count):
                same = (head_ref[other_slot, other_shard] == head).astype(jnp.int32)
                before = other_shard * slot_count + other_slot < shard * slot_count + slot
                group_size = group_size + same
                group_rank = group_rank + same * before.astype(jnp.int32)
        served = group_rank + group_size * step
        for source in range(shard_count):
            pick_ref[slot, source : source + 1, :] = jnp.where(
                served < counts_ref[source], served + source * tok_dev, -1
            )
        slot_head_ref[slot] = jnp.full(slot_head_ref.shape[1:], head, jnp.int32)
    for copy in copies[2:]:
        copy.wait()


def attend_kernel(set_count, limits_ref, query_own_ref, query_split_ref, *refs):
    set_refs = refs[:set_count]
    weight_hbm, keep_ref, send_ref, table_ref, weight_ref, lines_ref, weight_sem = refs[set_count:]
    weight_copy = pltpu.make_async_copy(weight_hbm, weight_ref, weight_sem)
    weight_copy.start()
    tok_dev, half_width = query_own_ref.shape
    half_heads = half_width // HDIM
    split = split_offset(set_count)
    shard = lax.axis_index("seq")
    first_head = (shard // split) % 2 * half_heads
    key_valid = limits_ref[0:1, :] > 0
    row = lax.broadcasted_iota(jnp.int32, (tok_dev, HDIM), 0)
    own_valid = row < limits_ref[1:2, :HDIM]
    split_valid = row < limits_ref[2:3, :HDIM]
    lane = lax.broadcasted_iota(jnp.int32, (2 * tok_dev, lines_ref.shape[1]), 1)
    lines = jnp.zeros(lane.shape, jnp.float32)
    for head in range(half_heads):
        columns = pl.ds(head * HDIM, HDIM)
        query_rows = jnp.concatenate([query_own_ref[:, columns], query_split_ref[:, columns]], axis=0)
        key_all = jnp.concatenate([ref[pl.ds(0, tok_dev), columns] for ref in set_refs], axis=0)
        value_all = jnp.concatenate(
            [ref[pl.ds(tok_dev, tok_dev), columns] for ref in set_refs], axis=0
        )
        scores = (
            lax.dot_general(
                query_rows, key_all, (((1,), (1,)), ((), ())), preferred_element_type=jnp.float32
            )
            * (1.0 / math.sqrt(HDIM))
        )
        scores = jnp.where(key_valid, scores, -jnp.inf)
        top_score = jnp.max(scores, axis=1, keepdims=True)
        weights = jnp.exp(scores - top_score)
        weight_sum = jnp.sum(weights, axis=1, keepdims=True)
        mixed = jnp.dot(
            weights.astype(jnp.bfloat16), value_all, preferred_element_type=jnp.float32
        )
        attended = mixed / weight_sum
        keep_ref[:, columns] = jnp.where(own_valid, attended[:tok_dev], 0.0).astype(jnp.bfloat16)
        send_ref[:, columns] = jnp.where(split_valid, attended[tok_dev:], 0.0).astype(jnp.bfloat16)
        lines = jnp.where(lane == first_head + head, top_score + jnp.log(weight_sum), lines)
    lines_ref[...] = jnp.zeros(lines_ref.shape, jnp.float32)
    own_rows = pl.ds(pl.multiple_of(shard * tok_dev, tok_dev), tok_dev)
    split_rows = pl.ds(pl.multiple_of((shard ^ split) * tok_dev, tok_dev), tok_dev)
    lines_ref[own_rows, :] = lines[:tok_dev]
    lines_ref[split_rows, :] = lines[tok_dev:]
    table_ref[...] = jnp.transpose(lines_ref[...])[: table_ref.shape[0]]
    weight_copy.wait()


def project_kernel(
    keep_ref, back_ref, partner_keep_ref, partner_back_ref, weight_ref, projected_ref
):
    half_width = keep_ref.shape[1]
    half = (lax.axis_index("seq") // split_offset(lax.axis_size("seq"))) % 2
    on_positive = lax.axis_index("branch") == 0
    own_scale = jnp.where(on_positive, GUIDE_SCALE, 1.0 - GUIDE_SCALE)
    partner_scale = jnp.where(on_positive, 1.0 - GUIDE_SCALE, GUIDE_SCALE)
    parts = [
        own_scale * own_ref[...].astype(jnp.float32)
        + partner_scale * partner_ref[...].astype(jnp.float32)
        for own_ref, partner_ref in ((keep_ref, partner_keep_ref), (back_ref, partner_back_ref))
    ]
    magnitude = jnp.sum(
        jnp.abs(parts[0]) + jnp.abs(parts[1]), axis=1, keepdims=True
    ) / (2 * half_width)
    total = jnp.zeros(projected_ref.shape, jnp.float32)
    for part, place in zip(parts, (half, 1 - half)):
        normed = (part / (magnitude + EPSILON)).astype(jnp.bfloat16)
        rows = pl.ds(pl.multiple_of(place * half_width, half_width), half_width)
        total = total + jnp.dot(normed, weight_ref[rows, :], preferred_element_type=jnp.float32)
    projected_ref[...] = total.astype(jnp.bfloat16)


def serve_kernel(table_ref, pick_ref, slot_head_ref, saved_ref):
    table = table_ref[...]
    head = lax.broadcasted_iota(jnp.int32, table.shape, 0)
    for slot in range(saved_ref.shape[0]):
        line = jnp.sum(
            jnp.where(head == slot_head_ref[slot, 0:1, :], table, 0.0), axis=0, keepdims=True
        )
        pick = pick_ref[slot]
        spread = jnp.broadcast_to(line, pick.shape)
        taken = jnp.take_along_axis(spread, jnp.maximum(pick, 0), axis=1)
        saved_ref[slot] = jnp.where(pick >= 0, taken, 0.0)[:, : saved_ref.shape[2]]


def per_device_halves(queries, key_rows, value_rows, counts, head_of, out_weight):
    seq_count = lax.axis_size("seq")
    tok_dev, width = queries.shape[1:]
    half_width = width // 2
    tokens = seq_count * tok_dev
    slot_count = head_of.shape[1]
    fewest = max(1, seq_count * slot_count // (2 * HEADS))
    row_cap = (tok_dev + fewest - 1) // fewest
    split = split_offset(seq_count)
    table_rows = (HEADS + 7) // 8 * 8
    any_spec = pl.BlockSpec(memory_space=pl.ANY)
    vmem = pl.BlockSpec(memory_space=pltpu.VMEM)

    def held(*arrays):
        return [pltpu.with_memory_space_constraint(array, pltpu.VMEM) for array in arrays]

    def far(*arrays):
        return [pltpu.with_memory_space_constraint(array, pltpu.HBM) for array in arrays]

    kv_own, query_own, kv_send, query_send, limits, pick, slot_head = pl.pallas_call(
        pack_kernel,
        out_shape=[
            pltpu.VMEM((2 * tok_dev, half_width), jnp.bfloat16),
            pltpu.VMEM((tok_dev, half_width), jnp.bfloat16),
            pltpu.VMEM((2 * tok_dev, half_width), jnp.bfloat16),
            pltpu.VMEM((tok_dev, half_width), jnp.bfloat16),
            pltpu.VMEM((8, tokens), jnp.int32),
            pltpu.VMEM((slot_count, seq_count, tokens), jnp.int32),
            pltpu.VMEM((slot_count, 8, tokens), jnp.int32),
        ],
        in_specs=[any_spec] * 5,
        out_specs=[vmem] * 7,
        scratch_shapes=[
            pltpu.SMEM((seq_count,), jnp.int32),
            pltpu.SMEM((slot_count, seq_count), jnp.int32),
            pltpu.SemaphoreType.DMA((8,)),
        ],
        compiler_params=KERNEL_PARAMS,
        name="pack",
    )(*far(queries, key_rows, value_rows, counts, jnp.transpose(head_of)))

    sets = {0: kv_own, split: swap_shards(kv_send, split)}
    for offset in gather_offsets(seq_count):
        for member in list(sets):
            sets[member ^ offset] = swap_shards(sets[member], offset)
    query_split = swap_shards(query_send, split)
    keep, send, table, weight_held = pl.pallas_call(
        functools.partial(attend_kernel, seq_count),
        out_shape=[
            pltpu.VMEM((tok_dev, half_width), jnp.bfloat16),
            pltpu.VMEM((tok_dev, half_width), jnp.bfloat16),
            pltpu.VMEM((table_rows, tokens), jnp.float32),
            pltpu.VMEM(out_weight.shape, jnp.bfloat16),
        ],
        in_specs=[vmem] * (3 + seq_count) + [any_spec],
        out_specs=[vmem] * 4,
        scratch_shapes=[pltpu.VMEM((tokens, HDIM), jnp.float32), pltpu.SemaphoreType.DMA],
        compiler_params=KERNEL_PARAMS,
        name="attend",
    )(
        *held(limits, query_own, query_split, *[sets[member] for member in set_order(seq_count)]),
        *far(out_weight),
    )

    for offset in gather_offsets(seq_count) + [split]:
        table = table + swap_shards(table, offset)
    across = [(2 * i + b, 2 * (i ^ split) + 1 - b) for i in range(seq_count) for b in range(2)]
    partner_back = lax.ppermute(send, ("seq", "branch"), across)
    back = swap_shards(send, split)
    partner_keep = partner_2(keep, "branch", 0)
    projected = pl.pallas_call(
        project_kernel,
        out_shape=jax.ShapeDtypeStruct((tok_dev, out_weight.shape[1]), jnp.bfloat16),
        in_specs=[vmem] * 5,
        out_specs=vmem,
        compiler_params=KERNEL_PARAMS,
        name="project",
    )(*held(keep, back, partner_keep, partner_back, weight_held))
    saved = pl.pallas_call(
        serve_kernel,
        out_shape=jax.ShapeDtypeStruct((slot_count, seq_count, row_cap), jnp.float32),
        in_specs=[vmem] * 3,
        out_specs=vmem,
        compiler_params=KERNEL_PARAMS,
        name="serve",
    )(*held(table, pick, slot_head))
    saved = jnp.transpose(saved, (0, 2, 1))
    return (projected, saved.reshape(1, 1, slot_count, row_cap, seq_count))


def solution(mesh):
    seq_count = mesh.shape["seq"]
    hypercube = seq_count > 1 and seq_count & (seq_count - 1) == 0
    small = hypercube and seq_count <= HEADS
    return jax.shard_map(
        per_device_halves if small else per_device_exchange,
        mesh=mesh,
        in_specs=(
            P("branch", ("groups", "seq"), None),
            P("branch", ("groups", "seq"), None),
            P("branch", ("groups", "seq"), None),
            P("groups"),
            P(),
            P(None, "branch"),
        ),
        out_specs=(
            P(("groups", "seq"), "branch"),
            P("branch", ("groups", "seq"), None, None, None),
        ),
        check_vma=False,
    )
```

```python
import functools
import math

import jax
import jax.numpy as jnp
from jax import lax
from jax.experimental import pallas as pl
from jax.experimental.pallas import tpu as pltpu
from jax.sharding import PartitionSpec as P

HEADS = 12
HDIM = 128


GUIDE_SCALE = 3.0
EPSILON = 1e-06


def partner_2(array, axis, stride):
    return lax.ppermute(array, axis, [(i, i ^ 1 << stride) for i in range(lax.axis_size(axis))])


def slot_layout(head_of):
    flat_heads = head_of.reshape(-1)
    slot_order = jnp.arange(flat_heads.shape[0], dtype=jnp.int32)
    same_head = flat_heads[:, None] == flat_heads[None, :]
    group_size = jnp.sum(same_head.astype(jnp.int32), axis=1)
    earlier = same_head & (slot_order[None, :] < slot_order[:, None])
    group_rank = jnp.sum(earlier.astype(jnp.int32), axis=1)
    return (flat_heads, group_size, group_rank)


def key_grouping(seq_count, tok_dev):
    shard_limit = max(1, 2048 // tok_dev)
    grouping = 1
    for attempt in range(16):
        if grouping * 2 <= shard_limit and seq_count % (grouping * 2) == 0:
            grouping = grouping * 2
    return grouping


def attend_rows(query_block, key_slot, value_slot, key_valid, key_block):
    row_count = query_block.shape[0]
    head_size = query_block.shape[1]
    block_count = key_slot.shape[0] // key_block
    scale_factor = 1.0 / math.sqrt(head_size)

    def fold_block(block_id, state_in):
        top_score, weight_sum, summed = state_in
        scores = (
            jnp.einsum("qd,kd->qk", query_block, key_slot, preferred_element_type=jnp.float32)
            * scale_factor
        )
        scores = jnp.where(key_valid[None, :], scores, -jnp.inf)
        new_top = jnp.maximum(top_score, jnp.max(scores, axis=1))
        fading = jnp.exp(top_score - new_top)
        weights = jnp.exp(scores - new_top[:, None])
        weight_sum = weight_sum * fading + jnp.sum(weights, axis=1)
        summed = summed * fading[:, None] + jnp.dot(
            weights.astype(jnp.bfloat16), value_slot, preferred_element_type=jnp.float32
        )
        return (new_top, weight_sum, summed)

    start_state = (
        jnp.full((row_count,), -jnp.inf, jnp.float32),
        jnp.zeros((row_count,), jnp.float32),
        jnp.zeros((row_count, head_size), jnp.float32),
    )
    top_score, weight_sum, summed = lax.fori_loop(0, block_count, fold_block, start_state)
    return (summed / weight_sum[:, None], top_score + jnp.log(weight_sum))


def serve_slots(query_items, mask_items, key_recv, value_recv, key_valid, key_block):
    source_count, slot_count, item_count, head_size = query_items.shape
    all_tokens = key_recv.shape[0] * key_recv.shape[2]
    per_block = max(1, 512 // source_count)
    slot_outputs = []
    slot_logsum = []
    for slot_id in range(slot_count):
        key_slot = key_recv[:, slot_id].reshape(all_tokens, head_size)
        value_slot = value_recv[:, slot_id].reshape(all_tokens, head_size)
        taken_items = min(per_block, item_count)
        query_block = query_items[:, slot_id, 0:taken_items].reshape(
            source_count * taken_items, head_size
        )
        attended, logsum = attend_rows(query_block, key_slot, value_slot, key_valid, key_block)
        pieces_out = attended.reshape(source_count, taken_items, head_size)
        pieces_sum = logsum.reshape(source_count, taken_items)
        slot_outputs.append(pieces_out)
        slot_logsum.append(pieces_sum)
    attended = jnp.stack(slot_outputs, axis=1)
    logsum = jnp.stack(slot_logsum, axis=1)
    keep_rows = mask_items > 0
    attended = jnp.where(keep_rows[:, :, :, None], attended, 0.0).astype(jnp.bfloat16)
    logsum = jnp.where(keep_rows, logsum, 0.0)
    return (attended, logsum)


def per_device_exchange(queries, key_rows, value_rows, counts, head_of, out_weight):
    seq_count = lax.axis_size("seq")
    tok_dev = queries.shape[1]
    slot_count = head_of.shape[1]
    fewest = max(1, seq_count * slot_count // (2 * HEADS))
    row_cap = (tok_dev + fewest - 1) // fewest
    my_index = lax.axis_index("seq")
    flat_heads, group_size, group_rank = slot_layout(head_of)
    row_steps = jnp.arange(row_cap, dtype=jnp.int32)
    served_rows = group_rank[:, None] + group_size[:, None] * row_steps[None, :]
    my_count = counts[my_index]
    clipped = jnp.minimum(served_rows, tok_dev - 1)
    query_grid = queries[0].reshape(tok_dev, HEADS, HDIM)
    row_live = served_rows < my_count
    query_send = query_grid[clipped, flat_heads[:, None]]
    query_send = jnp.where(row_live[:, :, None], query_send, jnp.zeros((), jnp.bfloat16)).reshape(
        seq_count, slot_count, row_cap, HDIM
    )
    mask_send = row_live.astype(jnp.bfloat16).reshape(seq_count, slot_count, row_cap)
    token_ids = jnp.arange(tok_dev, dtype=jnp.int32)
    key_grid = key_rows[0].reshape(tok_dev, HEADS, HDIM)
    value_grid = value_rows[0].reshape(tok_dev, HEADS, HDIM)
    key_send = key_grid[token_ids[None, :], flat_heads[:, None]].reshape(
        seq_count, slot_count, tok_dev, HDIM
    )
    value_send = value_grid[token_ids[None, :], flat_heads[:, None]].reshape(
        seq_count, slot_count, tok_dev, HDIM
    )
    key_valid = (token_ids[None, :] < counts[:, None]).reshape(-1)
    key_block = tok_dev * key_grouping(seq_count, tok_dev)
    query_recv, mask_recv, key_recv, value_recv = (
        lax.all_to_all(query_send, "seq", split_axis=0, concat_axis=0, tiled=True),
        lax.all_to_all(mask_send, "seq", split_axis=0, concat_axis=0, tiled=True),
        lax.all_to_all(key_send, "seq", split_axis=0, concat_axis=0, tiled=True),
        lax.all_to_all(value_send, "seq", split_axis=0, concat_axis=0, tiled=True),
    )
    attended, logsum = serve_slots(
        query_recv, mask_recv, key_recv, value_recv, key_valid, key_block
    )
    returned = lax.all_to_all(attended, "seq", split_axis=0, concat_axis=0, tiled=True)
    head_ids = jnp.arange(HEADS, dtype=jnp.int32)
    head_group = jnp.sum((flat_heads[None, :] == head_ids[:, None]).astype(jnp.int32), axis=1)
    row_rank = token_ids[:, None] % head_group[None, :]
    row_step = token_ids[:, None] // head_group[None, :]
    slot_ids = jnp.arange(flat_heads.shape[0], dtype=jnp.int32)
    matched = (flat_heads[None, None, :] == head_ids[None, :, None]) & (
        group_rank[None, None, :] == row_rank[:, :, None]
    )
    owner_slot = jnp.sum(jnp.where(matched, slot_ids[None, None, :], 0), axis=2)
    flat_index = owner_slot * row_cap + row_step
    returned_rows = returned.reshape(-1, HDIM)
    attended_home = returned_rows[flat_index].reshape(tok_dev, HEADS * HDIM)
    partner = partner_2(attended_home, "branch", 0)
    on_positive = lax.axis_index("branch") == 0
    own_value = attended_home.astype(jnp.float32)
    partner_value = partner.astype(jnp.float32)
    positive = jnp.where(on_positive, own_value, partner_value)
    negative = jnp.where(on_positive, partner_value, own_value)
    guided = GUIDE_SCALE * positive - (GUIDE_SCALE - 1.0) * negative
    magnitude = jnp.mean(jnp.abs(guided), axis=1, keepdims=True)
    normed = (guided / (magnitude + EPSILON)).astype(jnp.bfloat16)
    projected = jnp.dot(normed, out_weight, preferred_element_type=jnp.float32).astype(jnp.bfloat16)
    saved_rows = jnp.transpose(logsum, (1, 2, 0)).reshape(1, 1, slot_count, row_cap, seq_count)
    return (projected, saved_rows)


KERNEL_PARAMS = pltpu.CompilerParams(vmem_limit_bytes=16 * 1024 * 1024)


SPLIT = 2


def swap_shards(array, offset):
    pairs = [(i, i ^ offset) for i in range(lax.axis_size("seq"))]
    return lax.ppermute(array, "seq", pairs)


def set_order(shard_count):
    line = list(range(0, shard_count, SPLIT))
    return line + [offset + 1 for offset in line]


def pack_kernel(
    query_hbm,
    key_hbm,
    value_hbm,
    counts_hbm,
    head_hbm,
    own_ref,
    other_ref,
    limits_ref,
    pick_ref,
    slot_head_ref,
    counts_ref,
    head_ref,
    copy_sems,
):
    tok_dev = own_ref.shape[0] // 3
    half_width = own_ref.shape[1]
    slot_count, shard_count = head_ref.shape
    shard = lax.axis_index("seq")
    half = (shard // SPLIT) % 2
    copies = [
        pltpu.make_async_copy(counts_hbm, counts_ref, copy_sems.at[0]),
        pltpu.make_async_copy(head_hbm, head_ref, copy_sems.at[1]),
    ]
    for target, place in ((other_ref, 1 - half), (own_ref, half)):
        columns = pl.ds(pl.multiple_of(place * half_width, half_width), half_width)
        for part, source in enumerate((key_hbm, value_hbm, query_hbm)):
            rows = pl.ds(part * tok_dev, tok_dev)
            copies.append(
                pltpu.make_async_copy(
                    source.at[0, :, columns], target.at[rows, :], copy_sems.at[len(copies)]
                )
            )
    for copy in copies:
        copy.start()
    copies[0].wait()
    copies[1].wait()

    lane = lax.broadcasted_iota(jnp.int32, (1, limits_ref.shape[1]), 1)
    lane_limit = jnp.zeros(lane.shape, jnp.int32)
    for place, offset in enumerate(set_order(shard_count)):
        lane_limit = jnp.where(lane // tok_dev == place, counts_ref[shard ^ offset], lane_limit)
    limits_ref[0:1, :] = (lane % tok_dev < lane_limit).astype(jnp.int32)
    limits_ref[1:2, :] = jnp.full(lane.shape, counts_ref[shard], jnp.int32)
    limits_ref[2:3, :] = jnp.full(lane.shape, counts_ref[shard ^ SPLIT], jnp.int32)

    step = lax.broadcasted_iota(jnp.int32, (1, pick_ref.shape[2]), 1)
    for slot in range(slot_count):
        head = head_ref[slot, shard]
        group_size = jnp.int32(0)
        group_rank = jnp.int32(0)
        for other_shard in range(shard_count):
            for other_slot in range(slot_count):
                same = (head_ref[other_slot, other_shard] == head).astype(jnp.int32)
                before = other_shard * slot_count + other_slot < shard * slot_count + slot
                group_size = group_size + same
                group_rank = group_rank + same * before.astype(jnp.int32)
        served = group_rank + group_size * step
        for source in range(shard_count):
            pick_ref[slot, source : source + 1, :] = jnp.where(
                served < counts_ref[source], served + source * tok_dev, -1
            )
        slot_head_ref[slot] = jnp.full(slot_head_ref.shape[1:], head, jnp.int32)
    for copy in copies[2:]:
        copy.wait()


def gathered(set_refs, part, columns):
    tok_dev = set_refs[0].shape[0] // 3
    rows = pl.ds(part * tok_dev, tok_dev)
    return jnp.concatenate([ref[rows, columns] for ref in set_refs], axis=0)


def head_scores(query_rows, key_all):
    return lax.dot_general(
        query_rows, key_all, (((1,), (1,)), ((), ())), preferred_element_type=jnp.float32
    )


def attend_kernel(set_count, limits_ref, *refs):
    set_refs = refs[:set_count]
    weight_hbm, keep_ref, send_ref, weight_ref, weight_sem = refs[set_count:]
    weight_copy = pltpu.make_async_copy(weight_hbm, weight_ref, weight_sem)
    weight_copy.start()
    tok_dev, half_width = keep_ref.shape
    heads = [pl.ds(start, HDIM) for start in range(0, half_width, HDIM)]
    scores = jnp.concatenate(
        [
            head_scores(gathered(set_refs[:2], 2, columns), gathered(set_refs, 0, columns))
            for columns in heads
        ],
        axis=0,
    ) * (1.0 / math.sqrt(HDIM))
    scores = jnp.where(limits_ref[0:1, :] > 0, scores, -jnp.inf)
    weights = jnp.exp(scores - jnp.max(scores, axis=1, keepdims=True))
    weight_sum = jnp.sum(weights, axis=1, keepdims=True)
    rounded = weights.astype(jnp.bfloat16)
    row = lax.broadcasted_iota(jnp.int32, (tok_dev, HDIM), 0)
    for number, columns in enumerate(heads):
        first = 2 * tok_dev * number
        mixed = jnp.dot(
            rounded[first : first + 2 * tok_dev],
            gathered(set_refs, 1, columns),
            preferred_element_type=jnp.float32,
        )
        attended = mixed / weight_sum[first : first + 2 * tok_dev]
        for target, rows, limit in (
            (keep_ref, attended[:tok_dev], limits_ref[1:2, :HDIM]),
            (send_ref, attended[tok_dev:], limits_ref[2:3, :HDIM]),
        ):
            target[:, columns] = jnp.where(row < limit, rows, 0.0).astype(jnp.bfloat16)
    weight_copy.wait()


def logsum_kernel(set_count, limits_ref, *refs):
    set_refs = refs[:set_count]
    table_ref, lines_ref = refs[set_count:]
    tok_dev = set_refs[0].shape[0] // 3
    half_heads = set_refs[0].shape[1] // HDIM
    shard = lax.axis_index("seq")
    first_head = (shard // SPLIT) % 2 * half_heads
    key_valid = limits_ref[0:1, :] > 0
    lane = lax.broadcasted_iota(jnp.int32, lines_ref.shape, 1)
    lines = jnp.zeros(lines_ref.shape, jnp.float32)
    for head in range(half_heads):
        columns = pl.ds(head * HDIM, HDIM)
        scores = head_scores(gathered(set_refs, 2, columns), gathered(set_refs, 0, columns))
        scores = jnp.where(key_valid, scores * (1.0 / math.sqrt(HDIM)), -jnp.inf)
        top_score = jnp.max(scores, axis=1, keepdims=True)
        weight_sum = jnp.sum(jnp.exp(scores - top_score), axis=1, keepdims=True)
        lines = jnp.where(lane == first_head + head, top_score + jnp.log(weight_sum), lines)
    for place, offset in enumerate(set_order(set_count)):
        rows = pl.ds(pl.multiple_of((shard ^ offset) * tok_dev, tok_dev), tok_dev)
        lines_ref[rows, :] = lines[place * tok_dev : (place + 1) * tok_dev]
    table_ref[...] = jnp.transpose(lines_ref[...])[: table_ref.shape[0]]


def project_kernel(
    keep_ref, back_ref, partner_keep_ref, partner_back_ref, weight_ref, projected_ref
):
    half_width = keep_ref.shape[1]
    half = (lax.axis_index("seq") // SPLIT) % 2
    on_positive = lax.axis_index("branch") == 0
    own_scale = jnp.where(on_positive, GUIDE_SCALE, 1.0 - GUIDE_SCALE)
    partner_scale = jnp.where(on_positive, 1.0 - GUIDE_SCALE, GUIDE_SCALE)
    parts = [
        own_scale * own_ref[...].astype(jnp.float32)
        + partner_scale * partner_ref[...].astype(jnp.float32)
        for own_ref, partner_ref in ((keep_ref, partner_keep_ref), (back_ref, partner_back_ref))
    ]
    magnitude = jnp.sum(
        jnp.abs(parts[0]) + jnp.abs(parts[1]), axis=1, keepdims=True
    ) / (2 * half_width)
    total = jnp.zeros(projected_ref.shape, jnp.float32)
    for part, place in zip(parts, (half, 1 - half)):
        normed = (part / (magnitude + EPSILON)).astype(jnp.bfloat16)
        rows = pl.ds(pl.multiple_of(place * half_width, half_width), half_width)
        total = total + jnp.dot(normed, weight_ref[rows, :], preferred_element_type=jnp.float32)
    projected_ref[...] = total.astype(jnp.bfloat16)


def serve_kernel(table_ref, other_table_ref, pick_ref, slot_head_ref, saved_ref):
    table = table_ref[...] + other_table_ref[...]
    head = lax.broadcasted_iota(jnp.int32, table.shape, 0)
    for slot in range(saved_ref.shape[0]):
        line = jnp.sum(
            jnp.where(head == slot_head_ref[slot, 0:1, :], table, 0.0), axis=0, keepdims=True
        )
        pick = pick_ref[slot]
        spread = jnp.broadcast_to(line, pick.shape)
        taken = jnp.take_along_axis(spread, jnp.maximum(pick, 0), axis=1)
        saved_ref[slot] = jnp.where(pick >= 0, taken, 0.0)[:, : saved_ref.shape[2]]


def per_device_halves(queries, key_rows, value_rows, counts, head_of, out_weight):
    seq_count = lax.axis_size("seq")
    tok_dev, width = queries.shape[1:]
    half_width = width // 2
    tokens = seq_count * tok_dev
    slot_count = head_of.shape[1]
    fewest = max(1, seq_count * slot_count // (2 * HEADS))
    row_cap = (tok_dev + fewest - 1) // fewest
    table_rows = (HEADS + 7) // 8 * 8
    any_spec = pl.BlockSpec(memory_space=pl.ANY)
    vmem = pl.BlockSpec(memory_space=pltpu.VMEM)

    def held(*arrays):
        return [pltpu.with_memory_space_constraint(array, pltpu.VMEM) for array in arrays]

    def far(*arrays):
        return [pltpu.with_memory_space_constraint(array, pltpu.HBM) for array in arrays]

    own, other, limits, pick, slot_head = pl.pallas_call(
        pack_kernel,
        out_shape=[
            pltpu.VMEM((3 * tok_dev, half_width), jnp.bfloat16),
            pltpu.VMEM((3 * tok_dev, half_width), jnp.bfloat16),
            pltpu.VMEM((8, tokens), jnp.int32),
            pltpu.VMEM((slot_count, seq_count, tokens), jnp.int32),
            pltpu.VMEM((slot_count, 8, tokens), jnp.int32),
        ],
        in_specs=[any_spec] * 5,
        out_specs=[vmem] * 5,
        scratch_shapes=[
            pltpu.SMEM((seq_count,), jnp.int32),
            pltpu.SMEM((slot_count, seq_count), jnp.int32),
            pltpu.SemaphoreType.DMA((8,)),
        ],
        compiler_params=KERNEL_PARAMS,
        name="pack",
    )(*far(queries, key_rows, value_rows, counts, jnp.transpose(head_of)))

    sets = {0: own}
    for offset in reversed(range(SPLIT, seq_count, SPLIT)):
        sets[offset] = swap_shards(other if offset & SPLIT else own, offset)
    for offset in range(0, seq_count, SPLIT):
        sets[offset + 1] = swap_shards(sets[offset], 1)
    set_list = held(*[sets[offset] for offset in set_order(seq_count)])
    limits = held(limits)[0]
    keep, send, weight_held = pl.pallas_call(
        functools.partial(attend_kernel, seq_count),
        out_shape=[
            pltpu.VMEM((tok_dev, half_width), jnp.bfloat16),
            pltpu.VMEM((tok_dev, half_width), jnp.bfloat16),
            pltpu.VMEM(out_weight.shape, jnp.bfloat16),
        ],
        in_specs=[vmem] * (1 + seq_count) + [any_spec],
        out_specs=[vmem] * 3,
        scratch_shapes=[pltpu.SemaphoreType.DMA],
        compiler_params=KERNEL_PARAMS,
        name="attend",
    )(limits, *set_list, *far(out_weight))
    across = [(2 * i + b, 2 * (i ^ SPLIT) + 1 - b) for i in range(seq_count) for b in range(2)]
    partner_back = lax.ppermute(send, ("seq", "branch"), across)
    back = swap_shards(send, SPLIT)
    table = pl.pallas_call(
        functools.partial(logsum_kernel, seq_count),
        out_shape=pltpu.VMEM((table_rows, tokens), jnp.float32),
        in_specs=[vmem] * (1 + seq_count),
        out_specs=vmem,
        scratch_shapes=[pltpu.VMEM((tokens, HDIM), jnp.float32)],
        compiler_params=KERNEL_PARAMS,
        name="logsum",
    )(limits, *set_list)
    other_table = swap_shards(table, SPLIT)
    partner_keep = partner_2(keep, "branch", 0)
    projected = pl.pallas_call(
        project_kernel,
        out_shape=jax.ShapeDtypeStruct((tok_dev, out_weight.shape[1]), jnp.bfloat16),
        in_specs=[vmem] * 5,
        out_specs=vmem,
        compiler_params=KERNEL_PARAMS,
        name="project",
    )(*held(keep, back, partner_keep, partner_back, weight_held))
    saved = pl.pallas_call(
        serve_kernel,
        out_shape=jax.ShapeDtypeStruct((slot_count, seq_count, row_cap), jnp.float32),
        in_specs=[vmem] * 4,
        out_specs=vmem,
        compiler_params=KERNEL_PARAMS,
        name="serve",
    )(*held(table, other_table, pick, slot_head))
    saved = jnp.transpose(saved, (0, 2, 1))
    return (projected, saved.reshape(1, 1, slot_count, row_cap, seq_count))


def solution(mesh):
    seq_count = mesh.shape["seq"]
    hypercube = seq_count > SPLIT and seq_count & (seq_count - 1) == 0
    small = hypercube and seq_count <= HEADS
    return jax.shard_map(
        per_device_halves if small else per_device_exchange,
        mesh=mesh,
        in_specs=(
            P("branch", ("groups", "seq"), None),
            P("branch", ("groups", "seq"), None),
            P("branch", ("groups", "seq"), None),
            P("groups"),
            P(),
            P(None, "branch"),
        ),
        out_specs=(
            P(("groups", "seq"), "branch"),
            P("branch", ("groups", "seq"), None, None, None),
        ),
        check_vma=False,
    )
```

```python
import functools
import math

import jax
import jax.numpy as jnp
from jax import lax
from jax.experimental import pallas as pl
from jax.experimental.pallas import tpu as pltpu
from jax.sharding import PartitionSpec as P

HEADS = 12
HDIM = 128


GUIDE_SCALE = 3.0
EPSILON = 1e-06


def partner_2(array, axis, stride):
    return lax.ppermute(array, axis, [(i, i ^ 1 << stride) for i in range(lax.axis_size(axis))])


def slot_layout(head_of):
    flat_heads = head_of.reshape(-1)
    slot_order = jnp.arange(flat_heads.shape[0], dtype=jnp.int32)
    same_head = flat_heads[:, None] == flat_heads[None, :]
    group_size = jnp.sum(same_head.astype(jnp.int32), axis=1)
    earlier = same_head & (slot_order[None, :] < slot_order[:, None])
    group_rank = jnp.sum(earlier.astype(jnp.int32), axis=1)
    return (flat_heads, group_size, group_rank)


def key_grouping(seq_count, tok_dev):
    shard_limit = max(1, 2048 // tok_dev)
    grouping = 1
    for attempt in range(16):
        if grouping * 2 <= shard_limit and seq_count % (grouping * 2) == 0:
            grouping = grouping * 2
    return grouping


def attend_rows(query_block, key_slot, value_slot, key_valid, key_block):
    row_count = query_block.shape[0]
    head_size = query_block.shape[1]
    block_count = key_slot.shape[0] // key_block
    scale_factor = 1.0 / math.sqrt(head_size)

    def fold_block(block_id, state_in):
        top_score, weight_sum, summed = state_in
        scores = (
            jnp.einsum("qd,kd->qk", query_block, key_slot, preferred_element_type=jnp.float32)
            * scale_factor
        )
        scores = jnp.where(key_valid[None, :], scores, -jnp.inf)
        new_top = jnp.maximum(top_score, jnp.max(scores, axis=1))
        fading = jnp.exp(top_score - new_top)
        weights = jnp.exp(scores - new_top[:, None])
        weight_sum = weight_sum * fading + jnp.sum(weights, axis=1)
        summed = summed * fading[:, None] + jnp.dot(
            weights.astype(jnp.bfloat16), value_slot, preferred_element_type=jnp.float32
        )
        return (new_top, weight_sum, summed)

    start_state = (
        jnp.full((row_count,), -jnp.inf, jnp.float32),
        jnp.zeros((row_count,), jnp.float32),
        jnp.zeros((row_count, head_size), jnp.float32),
    )
    top_score, weight_sum, summed = lax.fori_loop(0, block_count, fold_block, start_state)
    return (summed / weight_sum[:, None], top_score + jnp.log(weight_sum))


def serve_slots(query_items, mask_items, key_recv, value_recv, key_valid, key_block):
    source_count, slot_count, item_count, head_size = query_items.shape
    all_tokens = key_recv.shape[0] * key_recv.shape[2]
    per_block = max(1, 512 // source_count)
    slot_outputs = []
    slot_logsum = []
    for slot_id in range(slot_count):
        key_slot = key_recv[:, slot_id].reshape(all_tokens, head_size)
        value_slot = value_recv[:, slot_id].reshape(all_tokens, head_size)
        taken_items = min(per_block, item_count)
        query_block = query_items[:, slot_id, 0:taken_items].reshape(
            source_count * taken_items, head_size
        )
        attended, logsum = attend_rows(query_block, key_slot, value_slot, key_valid, key_block)
        pieces_out = attended.reshape(source_count, taken_items, head_size)
        pieces_sum = logsum.reshape(source_count, taken_items)
        slot_outputs.append(pieces_out)
        slot_logsum.append(pieces_sum)
    attended = jnp.stack(slot_outputs, axis=1)
    logsum = jnp.stack(slot_logsum, axis=1)
    keep_rows = mask_items > 0
    attended = jnp.where(keep_rows[:, :, :, None], attended, 0.0).astype(jnp.bfloat16)
    logsum = jnp.where(keep_rows, logsum, 0.0)
    return (attended, logsum)


def per_device_exchange(queries, key_rows, value_rows, counts, head_of, out_weight):
    seq_count = lax.axis_size("seq")
    tok_dev = queries.shape[1]
    slot_count = head_of.shape[1]
    fewest = max(1, seq_count * slot_count // (2 * HEADS))
    row_cap = (tok_dev + fewest - 1) // fewest
    my_index = lax.axis_index("seq")
    flat_heads, group_size, group_rank = slot_layout(head_of)
    row_steps = jnp.arange(row_cap, dtype=jnp.int32)
    served_rows = group_rank[:, None] + group_size[:, None] * row_steps[None, :]
    my_count = counts[my_index]
    clipped = jnp.minimum(served_rows, tok_dev - 1)
    query_grid = queries[0].reshape(tok_dev, HEADS, HDIM)
    row_live = served_rows < my_count
    query_send = query_grid[clipped, flat_heads[:, None]]
    query_send = jnp.where(row_live[:, :, None], query_send, jnp.zeros((), jnp.bfloat16)).reshape(
        seq_count, slot_count, row_cap, HDIM
    )
    mask_send = row_live.astype(jnp.bfloat16).reshape(seq_count, slot_count, row_cap)
    token_ids = jnp.arange(tok_dev, dtype=jnp.int32)
    key_grid = key_rows[0].reshape(tok_dev, HEADS, HDIM)
    value_grid = value_rows[0].reshape(tok_dev, HEADS, HDIM)
    key_send = key_grid[token_ids[None, :], flat_heads[:, None]].reshape(
        seq_count, slot_count, tok_dev, HDIM
    )
    value_send = value_grid[token_ids[None, :], flat_heads[:, None]].reshape(
        seq_count, slot_count, tok_dev, HDIM
    )
    key_valid = (token_ids[None, :] < counts[:, None]).reshape(-1)
    key_block = tok_dev * key_grouping(seq_count, tok_dev)
    query_recv, mask_recv, key_recv, value_recv = (
        lax.all_to_all(query_send, "seq", split_axis=0, concat_axis=0, tiled=True),
        lax.all_to_all(mask_send, "seq", split_axis=0, concat_axis=0, tiled=True),
        lax.all_to_all(key_send, "seq", split_axis=0, concat_axis=0, tiled=True),
        lax.all_to_all(value_send, "seq", split_axis=0, concat_axis=0, tiled=True),
    )
    attended, logsum = serve_slots(
        query_recv, mask_recv, key_recv, value_recv, key_valid, key_block
    )
    returned = lax.all_to_all(attended, "seq", split_axis=0, concat_axis=0, tiled=True)
    head_ids = jnp.arange(HEADS, dtype=jnp.int32)
    head_group = jnp.sum((flat_heads[None, :] == head_ids[:, None]).astype(jnp.int32), axis=1)
    row_rank = token_ids[:, None] % head_group[None, :]
    row_step = token_ids[:, None] // head_group[None, :]
    slot_ids = jnp.arange(flat_heads.shape[0], dtype=jnp.int32)
    matched = (flat_heads[None, None, :] == head_ids[None, :, None]) & (
        group_rank[None, None, :] == row_rank[:, :, None]
    )
    owner_slot = jnp.sum(jnp.where(matched, slot_ids[None, None, :], 0), axis=2)
    flat_index = owner_slot * row_cap + row_step
    returned_rows = returned.reshape(-1, HDIM)
    attended_home = returned_rows[flat_index].reshape(tok_dev, HEADS * HDIM)
    partner = partner_2(attended_home, "branch", 0)
    on_positive = lax.axis_index("branch") == 0
    own_value = attended_home.astype(jnp.float32)
    partner_value = partner.astype(jnp.float32)
    positive = jnp.where(on_positive, own_value, partner_value)
    negative = jnp.where(on_positive, partner_value, own_value)
    guided = GUIDE_SCALE * positive - (GUIDE_SCALE - 1.0) * negative
    magnitude = jnp.mean(jnp.abs(guided), axis=1, keepdims=True)
    normed = (guided / (magnitude + EPSILON)).astype(jnp.bfloat16)
    projected = jnp.dot(normed, out_weight, preferred_element_type=jnp.float32).astype(jnp.bfloat16)
    saved_rows = jnp.transpose(logsum, (1, 2, 0)).reshape(1, 1, slot_count, row_cap, seq_count)
    return (projected, saved_rows)


KERNEL_PARAMS = pltpu.CompilerParams(vmem_limit_bytes=16 * 1024 * 1024)


SPLIT = 2
TABLE_PIECES = 3
SPLITTER = 65537.0


def swap_shards(array, offset):
    pairs = [(i, i ^ offset) for i in range(lax.axis_size("seq"))]
    return lax.ppermute(array, "seq", pairs)


def set_order(shard_count):
    line = list(range(0, shard_count, SPLIT))
    return line + [offset + 1 for offset in line]


def pack_kernel(
    query_hbm,
    key_hbm,
    value_hbm,
    counts_hbm,
    head_hbm,
    own_ref,
    other_ref,
    line_copy_ref,
    limits_ref,
    pick_ref,
    slot_head_ref,
    counts_ref,
    head_ref,
    copy_sems,
):
    tok_dev = own_ref.shape[0] // 3
    half_width = own_ref.shape[1]
    slot_count, shard_count = head_ref.shape
    shard = lax.axis_index("seq")
    half = (shard // SPLIT) % 2
    copies = [
        pltpu.make_async_copy(counts_hbm, counts_ref, copy_sems.at[0]),
        pltpu.make_async_copy(head_hbm, head_ref, copy_sems.at[1]),
    ]
    for target, place in ((line_copy_ref, half), (other_ref, 1 - half), (own_ref, half)):
        columns = pl.ds(pl.multiple_of(place * half_width, half_width), half_width)
        for part, source in enumerate((key_hbm, value_hbm, query_hbm)):
            rows = pl.ds(part * tok_dev, tok_dev)
            copies.append(
                pltpu.make_async_copy(
                    source.at[0, :, columns], target.at[rows, :], copy_sems.at[len(copies)]
                )
            )
    for copy in copies:
        copy.start()
    copies[0].wait()
    copies[1].wait()

    lane = lax.broadcasted_iota(jnp.int32, (1, limits_ref.shape[1]), 1)
    lane_limit = jnp.zeros(lane.shape, jnp.int32)
    for place, offset in enumerate(set_order(shard_count)):
        lane_limit = jnp.where(lane // tok_dev == place, counts_ref[shard ^ offset], lane_limit)
    limits_ref[0:1, :] = (lane % tok_dev < lane_limit).astype(jnp.int32)
    limits_ref[1:2, :] = jnp.full(lane.shape, counts_ref[shard], jnp.int32)
    limits_ref[2:3, :] = jnp.full(lane.shape, counts_ref[shard ^ SPLIT], jnp.int32)

    step = lax.broadcasted_iota(jnp.int32, (1, pick_ref.shape[2]), 1)
    for slot in range(slot_count):
        head = head_ref[slot, shard]
        group_size = jnp.int32(0)
        group_rank = jnp.int32(0)
        for other_shard in range(shard_count):
            for other_slot in range(slot_count):
                same = (head_ref[other_slot, other_shard] == head).astype(jnp.int32)
                before = other_shard * slot_count + other_slot < shard * slot_count + slot
                group_size = group_size + same
                group_rank = group_rank + same * before.astype(jnp.int32)
        served = group_rank + group_size * step
        for source in range(shard_count):
            pick_ref[slot, source : source + 1, :] = jnp.where(
                served < counts_ref[source], served + source * tok_dev, -1
            )
        slot_head_ref[slot] = jnp.full(slot_head_ref.shape[1:], head, jnp.int32)
    for copy in copies[2:]:
        copy.wait()


def hold_kernel(weight_hbm, after_ref, weight_ref, weight_sem):
    copy = pltpu.make_async_copy(weight_hbm, weight_ref, weight_sem)
    copy.start()
    copy.wait()


def gathered(set_refs, part, columns):
    tok_dev = set_refs[0].shape[0] // 3
    rows = pl.ds(part * tok_dev, tok_dev)
    return jnp.concatenate([ref[rows, columns] for ref in set_refs], axis=0)


def head_scores(query_rows, key_all):
    return lax.dot_general(
        query_rows, key_all, (((1,), (1,)), ((), ())), preferred_element_type=jnp.float32
    )


def attend_kernel(set_count, limits_ref, *refs):
    set_refs = refs[:set_count]
    keep_ref, send_ref = refs[set_count:]
    tok_dev, half_width = keep_ref.shape
    heads = [pl.ds(start, HDIM) for start in range(0, half_width, HDIM)]
    scores = jnp.concatenate(
        [
            head_scores(gathered(set_refs[:2], 2, columns), gathered(set_refs, 0, columns))
            for columns in heads
        ],
        axis=0,
    ) * (1.0 / math.sqrt(HDIM))
    scores = jnp.where(limits_ref[0:1, :] > 0, scores, -jnp.inf)
    weights = jnp.exp(scores - jnp.max(scores, axis=1, keepdims=True))
    weight_sum = jnp.sum(weights, axis=1, keepdims=True)
    rounded = weights.astype(jnp.bfloat16)
    row = lax.broadcasted_iota(jnp.int32, (tok_dev, HDIM), 0)
    for number, columns in enumerate(heads):
        first = 2 * tok_dev * number
        mixed = jnp.dot(
            rounded[first : first + 2 * tok_dev],
            gathered(set_refs, 1, columns),
            preferred_element_type=jnp.float32,
        )
        attended = mixed / weight_sum[first : first + 2 * tok_dev]
        for target, rows, limit in (
            (keep_ref, attended[:tok_dev], limits_ref[1:2, :HDIM]),
            (send_ref, attended[tok_dev:], limits_ref[2:3, :HDIM]),
        ):
            target[:, columns] = jnp.where(row < limit, rows, 0.0).astype(jnp.bfloat16)


def logsum_kernel(set_count, limits_ref, send_ref, *refs):
    set_refs = refs[:set_count]
    message_ref, table_ref, lines_ref = refs[set_count:]
    tok_dev, half_width = send_ref.shape
    half_heads = half_width // HDIM
    shard = lax.axis_index("seq")
    message_ref[pl.ds(0, tok_dev), :] = send_ref[...]
    key_valid = limits_ref[0:1, :] > 0
    lane = lax.broadcasted_iota(jnp.int32, (set_count * tok_dev, HDIM), 1)
    lines = jnp.zeros(lane.shape, jnp.float32)
    for head in range(half_heads):
        columns = pl.ds(head * HDIM, HDIM)
        scores = head_scores(gathered(set_refs, 2, columns), gathered(set_refs, 0, columns))
        scores = jnp.where(key_valid, scores * (1.0 / math.sqrt(HDIM)), -jnp.inf)
        top_score = jnp.max(scores, axis=1, keepdims=True)
        weight_sum = jnp.sum(jnp.exp(scores - top_score), axis=1, keepdims=True)
        lines = jnp.where(lane == head, top_score + jnp.log(weight_sum), lines)
    for place, offset in enumerate(set_order(set_count)):
        rows = pl.ds(pl.multiple_of((shard ^ offset) * tok_dev, tok_dev), tok_dev)
        lines_ref[rows, :] = lines[place * tok_dev : (place + 1) * tok_dev]
    table = jnp.transpose(lines_ref[...])[: table_ref.shape[0]]
    table_ref[...] = table
    row = lax.broadcasted_iota(jnp.int32, (tok_dev, lines.shape[0]), 0)
    for head in range(half_heads):
        rest = jnp.broadcast_to(table[head : head + 1], row.shape)
        block = jnp.zeros(row.shape, jnp.float32)
        for piece in range(TABLE_PIECES):
            scaled = rest * SPLITTER
            part = scaled - (scaled - rest)
            block = jnp.where(row == piece, part, block)
            rest = rest - part
        columns = pl.ds(head * lines.shape[0], lines.shape[0])
        message_ref[pl.ds(tok_dev, tok_dev), columns] = block.astype(jnp.bfloat16)


def project_kernel(
    keep_ref,
    message_ref,
    partner_keep_ref,
    partner_back_ref,
    weight_ref,
    table_ref,
    pick_ref,
    slot_head_ref,
    projected_ref,
    saved_ref,
):
    tok_dev, half_width = keep_ref.shape
    half_heads = half_width // HDIM
    tokens = table_ref.shape[1]
    half = (lax.axis_index("seq") // SPLIT) % 2
    on_positive = lax.axis_index("branch") == 0
    own_scale = jnp.where(on_positive, GUIDE_SCALE, 1.0 - GUIDE_SCALE)
    partner_scale = jnp.where(on_positive, 1.0 - GUIDE_SCALE, GUIDE_SCALE)
    parts = [
        own_scale * own.astype(jnp.float32) + partner_scale * partner.astype(jnp.float32)
        for own, partner in (
            (keep_ref[...], partner_keep_ref[...]),
            (message_ref[pl.ds(0, tok_dev), :], partner_back_ref[...]),
        )
    ]
    magnitude = jnp.sum(
        jnp.abs(parts[0]) + jnp.abs(parts[1]), axis=1, keepdims=True
    ) / (2 * half_width)
    total = jnp.zeros(projected_ref.shape, jnp.float32)
    for part, place in zip(parts, (half, 1 - half)):
        normed = (part / (magnitude + EPSILON)).astype(jnp.bfloat16)
        rows = pl.ds(pl.multiple_of(place * half_width, half_width), half_width)
        total = total + jnp.dot(normed, weight_ref[rows, :], preferred_element_type=jnp.float32)
    projected_ref[...] = total.astype(jnp.bfloat16)

    for slot in range(saved_ref.shape[0]):
        slot_head = slot_head_ref[slot, 0:1, :]
        line = jnp.zeros((1, tokens), jnp.float32)
        for head in range(half_heads):
            pieces = message_ref[pl.ds(tok_dev, tok_dev), pl.ds(head * tokens, tokens)]
            pieces = pieces.astype(jnp.float32)
            other = pieces[0:1]
            for piece in range(1, TABLE_PIECES):
                other = other + pieces[piece : piece + 1]
            line = jnp.where(slot_head == half * half_heads + head, table_ref[head : head + 1], line)
            line = jnp.where(slot_head == (1 - half) * half_heads + head, other, line)
        pick = pick_ref[slot]
        spread = jnp.broadcast_to(line, pick.shape)
        taken = jnp.take_along_axis(spread, jnp.maximum(pick, 0), axis=1)
        saved_ref[slot] = jnp.where(pick >= 0, taken, 0.0)[:, : saved_ref.shape[2]]


def per_device_halves(queries, key_rows, value_rows, counts, head_of, out_weight):
    seq_count = lax.axis_size("seq")
    tok_dev, width = queries.shape[1:]
    half_width = width // 2
    tokens = seq_count * tok_dev
    slot_count = head_of.shape[1]
    fewest = max(1, seq_count * slot_count // (2 * HEADS))
    row_cap = (tok_dev + fewest - 1) // fewest
    any_spec = pl.BlockSpec(memory_space=pl.ANY)
    vmem = pl.BlockSpec(memory_space=pltpu.VMEM)

    def held(*arrays):
        return [pltpu.with_memory_space_constraint(array, pltpu.VMEM) for array in arrays]

    def far(*arrays):
        return [pltpu.with_memory_space_constraint(array, pltpu.HBM) for array in arrays]

    own, other, line_copy, limits, pick, slot_head = pl.pallas_call(
        pack_kernel,
        out_shape=[
            pltpu.VMEM((3 * tok_dev, half_width), jnp.bfloat16),
            pltpu.VMEM((3 * tok_dev, half_width), jnp.bfloat16),
            pltpu.VMEM((3 * tok_dev, half_width), jnp.bfloat16),
            pltpu.VMEM((8, tokens), jnp.int32),
            pltpu.VMEM((slot_count, seq_count, tokens), jnp.int32),
            pltpu.VMEM((slot_count, 8, tokens), jnp.int32),
        ],
        in_specs=[any_spec] * 5,
        out_specs=[vmem] * 6,
        scratch_shapes=[
            pltpu.SMEM((seq_count,), jnp.int32),
            pltpu.SMEM((slot_count, seq_count), jnp.int32),
            pltpu.SemaphoreType.DMA((11,)),
        ],
        compiler_params=KERNEL_PARAMS,
        name="pack",
    )(*far(queries, key_rows, value_rows, counts, jnp.transpose(head_of)))

    sets = {0: own}
    for offset in range(SPLIT, seq_count, SPLIT):
        sets[offset] = swap_shards(other if offset & SPLIT else line_copy, offset)
    for offset in range(0, seq_count, SPLIT):
        sets[offset + 1] = swap_shards(sets[offset], 1)
    set_list = held(*[sets[offset] for offset in set_order(seq_count)])
    limits = held(limits)[0]
    keep, send = pl.pallas_call(
        functools.partial(attend_kernel, seq_count),
        out_shape=[pltpu.VMEM((tok_dev, half_width), jnp.bfloat16)] * 2,
        in_specs=[vmem] * (1 + seq_count),
        out_specs=[vmem] * 2,
        compiler_params=KERNEL_PARAMS,
        name="attend",
    )(limits, *set_list)
    across = [(2 * i + b, 2 * (i ^ SPLIT) + 1 - b) for i in range(seq_count) for b in range(2)]
    partner_back = lax.ppermute(send, ("seq", "branch"), across)
    partner_keep = partner_2(keep, "branch", 0)
    message, table = pl.pallas_call(
        functools.partial(logsum_kernel, seq_count),
        out_shape=[
            pltpu.VMEM((2 * tok_dev, half_width), jnp.bfloat16),
            pltpu.VMEM((half_width // HDIM + 7 & -8, tokens), jnp.float32),
        ],
        in_specs=[vmem] * (2 + seq_count),
        out_specs=[vmem] * 2,
        scratch_shapes=[pltpu.VMEM((tokens, HDIM), jnp.float32)],
        compiler_params=KERNEL_PARAMS,
        name="logsum",
    )(limits, *held(send), *set_list)
    weight_held = pl.pallas_call(
        hold_kernel,
        out_shape=pltpu.VMEM(out_weight.shape, jnp.bfloat16),
        in_specs=[any_spec, vmem],
        out_specs=vmem,
        scratch_shapes=[pltpu.SemaphoreType.DMA],
        compiler_params=KERNEL_PARAMS,
        cost_estimate=pl.CostEstimate(
            flops=0, bytes_accessed=4 * out_weight.size, transcendentals=0
        ),
        name="hold",
    )(*far(out_weight), *held(table))
    back = swap_shards(message, SPLIT)
    projected, saved = pl.pallas_call(
        project_kernel,
        out_shape=[
            jax.ShapeDtypeStruct((tok_dev, out_weight.shape[1]), jnp.bfloat16),
            jax.ShapeDtypeStruct((slot_count, seq_count, row_cap), jnp.float32),
        ],
        in_specs=[vmem] * 8,
        out_specs=[vmem] * 2,
        compiler_params=KERNEL_PARAMS,
        name="project",
    )(*held(keep, back, partner_keep, partner_back, weight_held, table, pick, slot_head))
    saved = jnp.transpose(saved, (0, 2, 1))
    return (projected, saved.reshape(1, 1, slot_count, row_cap, seq_count))


def solution(mesh):
    seq_count = mesh.shape["seq"]
    hypercube = seq_count > SPLIT and seq_count & (seq_count - 1) == 0
    small = hypercube and seq_count <= HEADS
    return jax.shard_map(
        per_device_halves if small else per_device_exchange,
        mesh=mesh,
        in_specs=(
            P("branch", ("groups", "seq"), None),
            P("branch", ("groups", "seq"), None),
            P("branch", ("groups", "seq"), None),
            P("groups"),
            P(),
            P(None, "branch"),
        ),
        out_specs=(
            P(("groups", "seq"), "branch"),
            P("branch", ("groups", "seq"), None, None, None),
        ),
        check_vma=False,
    )
```

```python
import functools
import math

import jax
import jax.numpy as jnp
from jax import lax
from jax.experimental import pallas as pl
from jax.experimental.pallas import tpu as pltpu
from jax.sharding import PartitionSpec as P

HEADS = 12
HDIM = 128


GUIDE_SCALE = 3.0
EPSILON = 1e-06


def partner_2(array, axis, stride):
    return lax.ppermute(array, axis, [(i, i ^ 1 << stride) for i in range(lax.axis_size(axis))])


def slot_layout(head_of):
    flat_heads = head_of.reshape(-1)
    slot_order = jnp.arange(flat_heads.shape[0], dtype=jnp.int32)
    same_head = flat_heads[:, None] == flat_heads[None, :]
    group_size = jnp.sum(same_head.astype(jnp.int32), axis=1)
    earlier = same_head & (slot_order[None, :] < slot_order[:, None])
    group_rank = jnp.sum(earlier.astype(jnp.int32), axis=1)
    return (flat_heads, group_size, group_rank)


def key_grouping(seq_count, tok_dev):
    shard_limit = max(1, 2048 // tok_dev)
    grouping = 1
    for attempt in range(16):
        if grouping * 2 <= shard_limit and seq_count % (grouping * 2) == 0:
            grouping = grouping * 2
    return grouping


def attend_rows(query_block, key_slot, value_slot, key_valid, key_block):
    row_count = query_block.shape[0]
    head_size = query_block.shape[1]
    block_count = key_slot.shape[0] // key_block
    scale_factor = 1.0 / math.sqrt(head_size)

    def fold_block(block_id, state_in):
        top_score, weight_sum, summed = state_in
        scores = (
            jnp.einsum("qd,kd->qk", query_block, key_slot, preferred_element_type=jnp.float32)
            * scale_factor
        )
        scores = jnp.where(key_valid[None, :], scores, -jnp.inf)
        new_top = jnp.maximum(top_score, jnp.max(scores, axis=1))
        fading = jnp.exp(top_score - new_top)
        weights = jnp.exp(scores - new_top[:, None])
        weight_sum = weight_sum * fading + jnp.sum(weights, axis=1)
        summed = summed * fading[:, None] + jnp.dot(
            weights.astype(jnp.bfloat16), value_slot, preferred_element_type=jnp.float32
        )
        return (new_top, weight_sum, summed)

    start_state = (
        jnp.full((row_count,), -jnp.inf, jnp.float32),
        jnp.zeros((row_count,), jnp.float32),
        jnp.zeros((row_count, head_size), jnp.float32),
    )
    top_score, weight_sum, summed = lax.fori_loop(0, block_count, fold_block, start_state)
    return (summed / weight_sum[:, None], top_score + jnp.log(weight_sum))


def serve_slots(query_items, mask_items, key_recv, value_recv, key_valid, key_block):
    source_count, slot_count, item_count, head_size = query_items.shape
    all_tokens = key_recv.shape[0] * key_recv.shape[2]
    per_block = max(1, 512 // source_count)
    slot_outputs = []
    slot_logsum = []
    for slot_id in range(slot_count):
        key_slot = key_recv[:, slot_id].reshape(all_tokens, head_size)
        value_slot = value_recv[:, slot_id].reshape(all_tokens, head_size)
        taken_items = min(per_block, item_count)
        query_block = query_items[:, slot_id, 0:taken_items].reshape(
            source_count * taken_items, head_size
        )
        attended, logsum = attend_rows(query_block, key_slot, value_slot, key_valid, key_block)
        pieces_out = attended.reshape(source_count, taken_items, head_size)
        pieces_sum = logsum.reshape(source_count, taken_items)
        slot_outputs.append(pieces_out)
        slot_logsum.append(pieces_sum)
    attended = jnp.stack(slot_outputs, axis=1)
    logsum = jnp.stack(slot_logsum, axis=1)
    keep_rows = mask_items > 0
    attended = jnp.where(keep_rows[:, :, :, None], attended, 0.0).astype(jnp.bfloat16)
    logsum = jnp.where(keep_rows, logsum, 0.0)
    return (attended, logsum)


def per_device_exchange(queries, key_rows, value_rows, counts, head_of, out_weight):
    seq_count = lax.axis_size("seq")
    tok_dev = queries.shape[1]
    slot_count = head_of.shape[1]
    fewest = max(1, seq_count * slot_count // (2 * HEADS))
    row_cap = (tok_dev + fewest - 1) // fewest
    my_index = lax.axis_index("seq")
    flat_heads, group_size, group_rank = slot_layout(head_of)
    row_steps = jnp.arange(row_cap, dtype=jnp.int32)
    served_rows = group_rank[:, None] + group_size[:, None] * row_steps[None, :]
    my_count = counts[my_index]
    clipped = jnp.minimum(served_rows, tok_dev - 1)
    query_grid = queries[0].reshape(tok_dev, HEADS, HDIM)
    row_live = served_rows < my_count
    query_send = query_grid[clipped, flat_heads[:, None]]
    query_send = jnp.where(row_live[:, :, None], query_send, jnp.zeros((), jnp.bfloat16)).reshape(
        seq_count, slot_count, row_cap, HDIM
    )
    mask_send = row_live.astype(jnp.bfloat16).reshape(seq_count, slot_count, row_cap)
    token_ids = jnp.arange(tok_dev, dtype=jnp.int32)
    key_grid = key_rows[0].reshape(tok_dev, HEADS, HDIM)
    value_grid = value_rows[0].reshape(tok_dev, HEADS, HDIM)
    key_send = key_grid[token_ids[None, :], flat_heads[:, None]].reshape(
        seq_count, slot_count, tok_dev, HDIM
    )
    value_send = value_grid[token_ids[None, :], flat_heads[:, None]].reshape(
        seq_count, slot_count, tok_dev, HDIM
    )
    key_valid = (token_ids[None, :] < counts[:, None]).reshape(-1)
    key_block = tok_dev * key_grouping(seq_count, tok_dev)
    query_recv, mask_recv, key_recv, value_recv = (
        lax.all_to_all(query_send, "seq", split_axis=0, concat_axis=0, tiled=True),
        lax.all_to_all(mask_send, "seq", split_axis=0, concat_axis=0, tiled=True),
        lax.all_to_all(key_send, "seq", split_axis=0, concat_axis=0, tiled=True),
        lax.all_to_all(value_send, "seq", split_axis=0, concat_axis=0, tiled=True),
    )
    attended, logsum = serve_slots(
        query_recv, mask_recv, key_recv, value_recv, key_valid, key_block
    )
    returned = lax.all_to_all(attended, "seq", split_axis=0, concat_axis=0, tiled=True)
    head_ids = jnp.arange(HEADS, dtype=jnp.int32)
    head_group = jnp.sum((flat_heads[None, :] == head_ids[:, None]).astype(jnp.int32), axis=1)
    row_rank = token_ids[:, None] % head_group[None, :]
    row_step = token_ids[:, None] // head_group[None, :]
    slot_ids = jnp.arange(flat_heads.shape[0], dtype=jnp.int32)
    matched = (flat_heads[None, None, :] == head_ids[None, :, None]) & (
        group_rank[None, None, :] == row_rank[:, :, None]
    )
    owner_slot = jnp.sum(jnp.where(matched, slot_ids[None, None, :], 0), axis=2)
    flat_index = owner_slot * row_cap + row_step
    returned_rows = returned.reshape(-1, HDIM)
    attended_home = returned_rows[flat_index].reshape(tok_dev, HEADS * HDIM)
    partner = partner_2(attended_home, "branch", 0)
    on_positive = lax.axis_index("branch") == 0
    own_value = attended_home.astype(jnp.float32)
    partner_value = partner.astype(jnp.float32)
    positive = jnp.where(on_positive, own_value, partner_value)
    negative = jnp.where(on_positive, partner_value, own_value)
    guided = GUIDE_SCALE * positive - (GUIDE_SCALE - 1.0) * negative
    magnitude = jnp.mean(jnp.abs(guided), axis=1, keepdims=True)
    normed = (guided / (magnitude + EPSILON)).astype(jnp.bfloat16)
    projected = jnp.dot(normed, out_weight, preferred_element_type=jnp.float32).astype(jnp.bfloat16)
    saved_rows = jnp.transpose(logsum, (1, 2, 0)).reshape(1, 1, slot_count, row_cap, seq_count)
    return (projected, saved_rows)


KERNEL_PARAMS = pltpu.CompilerParams(vmem_limit_bytes=16 * 1024 * 1024)


SPLIT = 2
HOLD_COPIES = 4
TABLE_PIECES = 3
SPLITTER = 65537.0


def swap_shards(array, offset):
    pairs = [(i, i ^ offset) for i in range(lax.axis_size("seq"))]
    return lax.ppermute(array, "seq", pairs)


def set_order(shard_count):
    line = list(range(0, shard_count, SPLIT))
    return line + [offset + 1 for offset in line]


def pack_kernel(
    query_hbm,
    key_hbm,
    value_hbm,
    counts_hbm,
    head_hbm,
    own_ref,
    other_ref,
    limits_ref,
    pick_ref,
    slot_head_ref,
    counts_ref,
    head_ref,
    copy_sems,
):
    tok_dev = own_ref.shape[0] // 3
    half_width = own_ref.shape[1]
    slot_count, shard_count = head_ref.shape
    shard = lax.axis_index("seq")
    half = (shard // SPLIT) % 2
    copies = [
        pltpu.make_async_copy(counts_hbm, counts_ref, copy_sems.at[0]),
        pltpu.make_async_copy(head_hbm, head_ref, copy_sems.at[1]),
    ]
    for target, place in ((other_ref, 1 - half), (own_ref, half)):
        columns = pl.ds(pl.multiple_of(place * half_width, half_width), half_width)
        for part, source in enumerate((key_hbm, value_hbm, query_hbm)):
            rows = pl.ds(part * tok_dev, tok_dev)
            copies.append(
                pltpu.make_async_copy(
                    source.at[0, :, columns], target.at[rows, :], copy_sems.at[len(copies)]
                )
            )
    for copy in copies:
        copy.start()
    copies[0].wait()
    copies[1].wait()

    lane = lax.broadcasted_iota(jnp.int32, (1, limits_ref.shape[1]), 1)
    lane_limit = jnp.zeros(lane.shape, jnp.int32)
    for place, offset in enumerate(set_order(shard_count)):
        lane_limit = jnp.where(lane // tok_dev == place, counts_ref[shard ^ offset], lane_limit)
    limits_ref[0:1, :] = (lane % tok_dev < lane_limit).astype(jnp.int32)
    limits_ref[1:2, :] = jnp.full(lane.shape, counts_ref[shard], jnp.int32)
    limits_ref[2:3, :] = jnp.full(lane.shape, counts_ref[shard ^ SPLIT], jnp.int32)

    step = lax.broadcasted_iota(jnp.int32, (1, pick_ref.shape[2]), 1)
    for slot in range(slot_count):
        head = head_ref[slot, shard]
        group_size = jnp.int32(0)
        group_rank = jnp.int32(0)
        for other_shard in range(shard_count):
            for other_slot in range(slot_count):
                same = (head_ref[other_slot, other_shard] == head).astype(jnp.int32)
                before = other_shard * slot_count + other_slot < shard * slot_count + slot
                group_size = group_size + same
                group_rank = group_rank + same * before.astype(jnp.int32)
        served = group_rank + group_size * step
        for source in range(shard_count):
            pick_ref[slot, source : source + 1, :] = jnp.where(
                served < counts_ref[source], served + source * tok_dev, -1
            )
        slot_head_ref[slot] = jnp.full(slot_head_ref.shape[1:], head, jnp.int32)
    for copy in copies[2:]:
        copy.wait()


def hold_kernel(weight_hbm, after_ref, weight_ref, copy_sems):
    share = weight_ref.shape[0] // HOLD_COPIES
    copies = []
    for number in range(HOLD_COPIES):
        rows = pl.ds(number * share, share)
        copies.append(
            pltpu.make_async_copy(
                weight_hbm.at[rows, :], weight_ref.at[rows, :], copy_sems.at[number]
            )
        )
    for copy in copies:
        copy.start()
    for copy in copies:
        copy.wait()


def gathered(set_refs, part, columns):
    tok_dev = set_refs[0].shape[0] // 3
    rows = pl.ds(part * tok_dev, tok_dev)
    return jnp.concatenate([ref[rows, columns] for ref in set_refs], axis=0)


def head_scores(query_rows, key_all):
    return lax.dot_general(
        query_rows, key_all, (((1,), (1,)), ((), ())), preferred_element_type=jnp.float32
    )


def attend_kernel(set_count, limits_ref, *refs):
    set_refs = refs[:set_count]
    keep_ref, send_ref = refs[set_count:]
    tok_dev, half_width = keep_ref.shape
    heads = [pl.ds(start, HDIM) for start in range(0, half_width, HDIM)]
    scores = jnp.concatenate(
        [
            head_scores(gathered(set_refs[:2], 2, columns), gathered(set_refs, 0, columns))
            for columns in heads
        ],
        axis=0,
    ) * (1.0 / math.sqrt(HDIM))
    scores = jnp.where(limits_ref[0:1, :] > 0, scores, -jnp.inf)
    weights = jnp.exp(scores - jnp.max(scores, axis=1, keepdims=True))
    weight_sum = jnp.sum(weights, axis=1, keepdims=True)
    rounded = weights.astype(jnp.bfloat16)
    row = lax.broadcasted_iota(jnp.int32, (tok_dev, HDIM), 0)
    for number, columns in enumerate(heads):
        first = 2 * tok_dev * number
        mixed = jnp.dot(
            rounded[first : first + 2 * tok_dev],
            gathered(set_refs, 1, columns),
            preferred_element_type=jnp.float32,
        )
        attended = mixed / weight_sum[first : first + 2 * tok_dev]
        for target, rows, limit in (
            (keep_ref, attended[:tok_dev], limits_ref[1:2, :HDIM]),
            (send_ref, attended[tok_dev:], limits_ref[2:3, :HDIM]),
        ):
            target[:, columns] = jnp.where(row < limit, rows, 0.0).astype(jnp.bfloat16)


def logsum_kernel(set_count, limits_ref, send_ref, *refs):
    set_refs = refs[:set_count]
    message_ref, table_ref, lines_ref = refs[set_count:]
    tok_dev, half_width = send_ref.shape
    half_heads = half_width // HDIM
    shard = lax.axis_index("seq")
    message_ref[pl.ds(0, tok_dev), :] = send_ref[...]
    key_valid = limits_ref[0:1, :] > 0
    lane = lax.broadcasted_iota(jnp.int32, (set_count * tok_dev, HDIM), 1)
    lines = jnp.zeros(lane.shape, jnp.float32)
    for head in range(half_heads):
        columns = pl.ds(head * HDIM, HDIM)
        scores = head_scores(gathered(set_refs, 2, columns), gathered(set_refs, 0, columns))
        scores = jnp.where(key_valid, scores * (1.0 / math.sqrt(HDIM)), -jnp.inf)
        top_score = jnp.max(scores, axis=1, keepdims=True)
        weight_sum = jnp.sum(jnp.exp(scores - top_score), axis=1, keepdims=True)
        lines = jnp.where(lane == head, top_score + jnp.log(weight_sum), lines)
    for place, offset in enumerate(set_order(set_count)):
        rows = pl.ds(pl.multiple_of((shard ^ offset) * tok_dev, tok_dev), tok_dev)
        lines_ref[rows, :] = lines[place * tok_dev : (place + 1) * tok_dev]
    table = jnp.transpose(lines_ref[...])[: table_ref.shape[0]]
    table_ref[...] = table
    row = lax.broadcasted_iota(jnp.int32, (tok_dev, lines.shape[0]), 0)
    for head in range(half_heads):
        rest = jnp.broadcast_to(table[head : head + 1], row.shape)
        block = jnp.zeros(row.shape, jnp.float32)
        for piece in range(TABLE_PIECES):
            scaled = rest * SPLITTER
            part = scaled - (scaled - rest)
            block = jnp.where(row == piece, part, block)
            rest = rest - part
        columns = pl.ds(head * lines.shape[0], lines.shape[0])
        message_ref[pl.ds(tok_dev, tok_dev), columns] = block.astype(jnp.bfloat16)


def guidance(own, partner):
    on_positive = lax.axis_index("branch") == 0
    own_scale = jnp.where(on_positive, GUIDE_SCALE, 1.0 - GUIDE_SCALE)
    partner_scale = jnp.where(on_positive, 1.0 - GUIDE_SCALE, GUIDE_SCALE)
    return own_scale * own.astype(jnp.float32) + partner_scale * partner.astype(jnp.float32)


def half_product(guided, weight_ref, place):
    half_width = guided.shape[1]
    rows = pl.ds(pl.multiple_of(place * half_width, half_width), half_width)
    return jnp.dot(
        guided.astype(jnp.bfloat16), weight_ref[rows, :], preferred_element_type=jnp.float32
    )


def keep_kernel(keep_ref, partner_keep_ref, weight_ref, total_ref, size_ref):
    half = (lax.axis_index("seq") // SPLIT) % 2
    guided = guidance(keep_ref[...], partner_keep_ref[...])
    size = jnp.sum(jnp.abs(guided), axis=1, keepdims=True)
    size_ref[...] = jnp.broadcast_to(size, size_ref.shape)
    total_ref[...] = half_product(guided, weight_ref, half)


def project_kernel(
    total_ref,
    size_ref,
    message_ref,
    partner_back_ref,
    weight_ref,
    table_ref,
    pick_ref,
    slot_head_ref,
    projected_ref,
    saved_ref,
):
    tok_dev, half_width = partner_back_ref.shape
    half_heads = half_width // HDIM
    tokens = table_ref.shape[1]
    half = (lax.axis_index("seq") // SPLIT) % 2
    guided = guidance(message_ref[pl.ds(0, tok_dev), :], partner_back_ref[...])
    size = size_ref[:, 0:1] + jnp.sum(jnp.abs(guided), axis=1, keepdims=True)
    magnitude = size / (2 * half_width)
    total = total_ref[...] + half_product(guided, weight_ref, 1 - half)
    projected_ref[...] = (total / (magnitude + EPSILON)).astype(jnp.bfloat16)

    for slot in range(saved_ref.shape[0]):
        slot_head = slot_head_ref[slot, 0:1, :]
        line = jnp.zeros((1, tokens), jnp.float32)
        for head in range(half_heads):
            pieces = message_ref[pl.ds(tok_dev, tok_dev), pl.ds(head * tokens, tokens)]
            pieces = pieces.astype(jnp.float32)
            other = pieces[0:1]
            for piece in range(1, TABLE_PIECES):
                other = other + pieces[piece : piece + 1]
            line = jnp.where(slot_head == half * half_heads + head, table_ref[head : head + 1], line)
            line = jnp.where(slot_head == (1 - half) * half_heads + head, other, line)
        pick = pick_ref[slot]
        spread = jnp.broadcast_to(line, pick.shape)
        taken = jnp.take_along_axis(spread, jnp.maximum(pick, 0), axis=1)
        saved_ref[slot] = jnp.where(pick >= 0, taken, 0.0)[:, : saved_ref.shape[2]]


def per_device_halves(queries, key_rows, value_rows, counts, head_of, out_weight):
    seq_count = lax.axis_size("seq")
    tok_dev, width = queries.shape[1:]
    half_width = width // 2
    tokens = seq_count * tok_dev
    slot_count = head_of.shape[1]
    fewest = max(1, seq_count * slot_count // (2 * HEADS))
    row_cap = (tok_dev + fewest - 1) // fewest
    any_spec = pl.BlockSpec(memory_space=pl.ANY)
    vmem = pl.BlockSpec(memory_space=pltpu.VMEM)

    def held(*arrays):
        return [pltpu.with_memory_space_constraint(array, pltpu.VMEM) for array in arrays]

    def far(*arrays):
        return [pltpu.with_memory_space_constraint(array, pltpu.HBM) for array in arrays]

    own, other, limits, pick, slot_head = pl.pallas_call(
        pack_kernel,
        out_shape=[
            pltpu.VMEM((3 * tok_dev, half_width), jnp.bfloat16),
            pltpu.VMEM((3 * tok_dev, half_width), jnp.bfloat16),
            pltpu.VMEM((8, tokens), jnp.int32),
            pltpu.VMEM((slot_count, seq_count, tokens), jnp.int32),
            pltpu.VMEM((slot_count, 8, tokens), jnp.int32),
        ],
        in_specs=[any_spec] * 5,
        out_specs=[vmem] * 5,
        scratch_shapes=[
            pltpu.SMEM((seq_count,), jnp.int32),
            pltpu.SMEM((slot_count, seq_count), jnp.int32),
            pltpu.SemaphoreType.DMA((8,)),
        ],
        compiler_params=KERNEL_PARAMS,
        name="pack",
    )(*far(queries, key_rows, value_rows, counts, jnp.transpose(head_of)))

    weight_held = pl.pallas_call(
        hold_kernel,
        out_shape=pltpu.VMEM(out_weight.shape, jnp.bfloat16),
        in_specs=[any_spec, vmem],
        out_specs=vmem,
        scratch_shapes=[pltpu.SemaphoreType.DMA((HOLD_COPIES,))],
        compiler_params=KERNEL_PARAMS,
        cost_estimate=pl.CostEstimate(
            flops=0, bytes_accessed=4 * out_weight.size, transcendentals=0
        ),
        name="hold",
    )(*far(out_weight), *held(limits))
    sets = {0: own}
    for offset in range(SPLIT, seq_count, SPLIT):
        sets[offset] = swap_shards(other if offset & SPLIT else own, offset)
    for offset in range(0, seq_count, SPLIT):
        sets[offset + 1] = swap_shards(sets[offset], 1)
    set_list = held(*[sets[offset] for offset in set_order(seq_count)])
    limits, weight_held = lax.optimization_barrier((limits, weight_held))
    limits = held(limits)[0]
    keep, send = pl.pallas_call(
        functools.partial(attend_kernel, seq_count),
        out_shape=[pltpu.VMEM((tok_dev, half_width), jnp.bfloat16)] * 2,
        in_specs=[vmem] * (1 + seq_count),
        out_specs=[vmem] * 2,
        compiler_params=KERNEL_PARAMS,
        name="attend",
    )(limits, *set_list)
    across = [(2 * i + b, 2 * (i ^ SPLIT) + 1 - b) for i in range(seq_count) for b in range(2)]
    partner_back = lax.ppermute(send, ("seq", "branch"), across)
    partner_keep = partner_2(keep, "branch", 0)
    message, table = pl.pallas_call(
        functools.partial(logsum_kernel, seq_count),
        out_shape=[
            pltpu.VMEM((2 * tok_dev, half_width), jnp.bfloat16),
            pltpu.VMEM((half_width // HDIM + 7 & -8, tokens), jnp.float32),
        ],
        in_specs=[vmem] * (2 + seq_count),
        out_specs=[vmem] * 2,
        scratch_shapes=[pltpu.VMEM((tokens, HDIM), jnp.float32)],
        compiler_params=KERNEL_PARAMS,
        name="logsum",
    )(limits, *held(send), *set_list)
    back = swap_shards(message, SPLIT)
    total, size = pl.pallas_call(
        keep_kernel,
        out_shape=[
            pltpu.VMEM((tok_dev, out_weight.shape[1]), jnp.float32),
            pltpu.VMEM((tok_dev, HDIM), jnp.float32),
        ],
        in_specs=[vmem] * 3,
        out_specs=[vmem] * 2,
        compiler_params=KERNEL_PARAMS,
        name="keep",
    )(*held(keep, partner_keep, weight_held))
    projected, saved = pl.pallas_call(
        project_kernel,
        out_shape=[
            jax.ShapeDtypeStruct((tok_dev, out_weight.shape[1]), jnp.bfloat16),
            jax.ShapeDtypeStruct((slot_count, seq_count, row_cap), jnp.float32),
        ],
        in_specs=[vmem] * 8,
        out_specs=[vmem] * 2,
        compiler_params=KERNEL_PARAMS,
        name="project",
    )(*held(total, size, back, partner_back, weight_held, table, pick, slot_head))
    saved = jnp.transpose(saved, (0, 2, 1))
    return (projected, saved.reshape(1, 1, slot_count, row_cap, seq_count))


def solution(mesh):
    seq_count = mesh.shape["seq"]
    hypercube = seq_count > SPLIT and seq_count & (seq_count - 1) == 0
    small = hypercube and seq_count <= HEADS
    return jax.shard_map(
        per_device_halves if small else per_device_exchange,
        mesh=mesh,
        in_specs=(
            P("branch", ("groups", "seq"), None),
            P("branch", ("groups", "seq"), None),
            P("branch", ("groups", "seq"), None),
            P("groups"),
            P(),
            P(None, "branch"),
        ),
        out_specs=(
            P(("groups", "seq"), "branch"),
            P("branch", ("groups", "seq"), None, None, None),
        ),
        check_vma=False,
    )
```

```python
import functools
import math

import jax
import jax.numpy as jnp
from jax import lax
from jax.experimental import pallas as pl
from jax.experimental.pallas import tpu as pltpu
from jax.sharding import PartitionSpec as P

HEADS = 12
HDIM = 128


GUIDE_SCALE = 3.0
EPSILON = 1e-06


def partner_2(array, axis, stride):
    return lax.ppermute(array, axis, [(i, i ^ 1 << stride) for i in range(lax.axis_size(axis))])


def slot_layout(head_of):
    flat_heads = head_of.reshape(-1)
    slot_order = jnp.arange(flat_heads.shape[0], dtype=jnp.int32)
    same_head = flat_heads[:, None] == flat_heads[None, :]
    group_size = jnp.sum(same_head.astype(jnp.int32), axis=1)
    earlier = same_head & (slot_order[None, :] < slot_order[:, None])
    group_rank = jnp.sum(earlier.astype(jnp.int32), axis=1)
    return (flat_heads, group_size, group_rank)


def key_grouping(seq_count, tok_dev):
    shard_limit = max(1, 2048 // tok_dev)
    grouping = 1
    for attempt in range(16):
        if grouping * 2 <= shard_limit and seq_count % (grouping * 2) == 0:
            grouping = grouping * 2
    return grouping


def attend_rows(query_block, key_slot, value_slot, key_valid, key_block):
    row_count = query_block.shape[0]
    head_size = query_block.shape[1]
    block_count = key_slot.shape[0] // key_block
    scale_factor = 1.0 / math.sqrt(head_size)

    def fold_block(block_id, state_in):
        top_score, weight_sum, summed = state_in
        scores = (
            jnp.einsum("qd,kd->qk", query_block, key_slot, preferred_element_type=jnp.float32)
            * scale_factor
        )
        scores = jnp.where(key_valid[None, :], scores, -jnp.inf)
        new_top = jnp.maximum(top_score, jnp.max(scores, axis=1))
        fading = jnp.exp(top_score - new_top)
        weights = jnp.exp(scores - new_top[:, None])
        weight_sum = weight_sum * fading + jnp.sum(weights, axis=1)
        summed = summed * fading[:, None] + jnp.dot(
            weights.astype(jnp.bfloat16), value_slot, preferred_element_type=jnp.float32
        )
        return (new_top, weight_sum, summed)

    start_state = (
        jnp.full((row_count,), -jnp.inf, jnp.float32),
        jnp.zeros((row_count,), jnp.float32),
        jnp.zeros((row_count, head_size), jnp.float32),
    )
    top_score, weight_sum, summed = lax.fori_loop(0, block_count, fold_block, start_state)
    return (summed / weight_sum[:, None], top_score + jnp.log(weight_sum))


def serve_slots(query_items, mask_items, key_recv, value_recv, key_valid, key_block):
    source_count, slot_count, item_count, head_size = query_items.shape
    all_tokens = key_recv.shape[0] * key_recv.shape[2]
    per_block = max(1, 512 // source_count)
    slot_outputs = []
    slot_logsum = []
    for slot_id in range(slot_count):
        key_slot = key_recv[:, slot_id].reshape(all_tokens, head_size)
        value_slot = value_recv[:, slot_id].reshape(all_tokens, head_size)
        taken_items = min(per_block, item_count)
        query_block = query_items[:, slot_id, 0:taken_items].reshape(
            source_count * taken_items, head_size
        )
        attended, logsum = attend_rows(query_block, key_slot, value_slot, key_valid, key_block)
        pieces_out = attended.reshape(source_count, taken_items, head_size)
        pieces_sum = logsum.reshape(source_count, taken_items)
        slot_outputs.append(pieces_out)
        slot_logsum.append(pieces_sum)
    attended = jnp.stack(slot_outputs, axis=1)
    logsum = jnp.stack(slot_logsum, axis=1)
    keep_rows = mask_items > 0
    attended = jnp.where(keep_rows[:, :, :, None], attended, 0.0).astype(jnp.bfloat16)
    logsum = jnp.where(keep_rows, logsum, 0.0)
    return (attended, logsum)


def per_device_exchange(queries, key_rows, value_rows, counts, head_of, out_weight):
    seq_count = lax.axis_size("seq")
    tok_dev = queries.shape[1]
    slot_count = head_of.shape[1]
    fewest = max(1, seq_count * slot_count // (2 * HEADS))
    row_cap = (tok_dev + fewest - 1) // fewest
    my_index = lax.axis_index("seq")
    flat_heads, group_size, group_rank = slot_layout(head_of)
    row_steps = jnp.arange(row_cap, dtype=jnp.int32)
    served_rows = group_rank[:, None] + group_size[:, None] * row_steps[None, :]
    my_count = counts[my_index]
    clipped = jnp.minimum(served_rows, tok_dev - 1)
    query_grid = queries[0].reshape(tok_dev, HEADS, HDIM)
    row_live = served_rows < my_count
    query_send = query_grid[clipped, flat_heads[:, None]]
    query_send = jnp.where(row_live[:, :, None], query_send, jnp.zeros((), jnp.bfloat16)).reshape(
        seq_count, slot_count, row_cap, HDIM
    )
    mask_send = row_live.astype(jnp.bfloat16).reshape(seq_count, slot_count, row_cap)
    token_ids = jnp.arange(tok_dev, dtype=jnp.int32)
    key_grid = key_rows[0].reshape(tok_dev, HEADS, HDIM)
    value_grid = value_rows[0].reshape(tok_dev, HEADS, HDIM)
    key_send = key_grid[token_ids[None, :], flat_heads[:, None]].reshape(
        seq_count, slot_count, tok_dev, HDIM
    )
    value_send = value_grid[token_ids[None, :], flat_heads[:, None]].reshape(
        seq_count, slot_count, tok_dev, HDIM
    )
    key_valid = (token_ids[None, :] < counts[:, None]).reshape(-1)
    key_block = tok_dev * key_grouping(seq_count, tok_dev)
    query_recv, mask_recv, key_recv, value_recv = (
        lax.all_to_all(query_send, "seq", split_axis=0, concat_axis=0, tiled=True),
        lax.all_to_all(mask_send, "seq", split_axis=0, concat_axis=0, tiled=True),
        lax.all_to_all(key_send, "seq", split_axis=0, concat_axis=0, tiled=True),
        lax.all_to_all(value_send, "seq", split_axis=0, concat_axis=0, tiled=True),
    )
    attended, logsum = serve_slots(
        query_recv, mask_recv, key_recv, value_recv, key_valid, key_block
    )
    returned = lax.all_to_all(attended, "seq", split_axis=0, concat_axis=0, tiled=True)
    head_ids = jnp.arange(HEADS, dtype=jnp.int32)
    head_group = jnp.sum((flat_heads[None, :] == head_ids[:, None]).astype(jnp.int32), axis=1)
    row_rank = token_ids[:, None] % head_group[None, :]
    row_step = token_ids[:, None] // head_group[None, :]
    slot_ids = jnp.arange(flat_heads.shape[0], dtype=jnp.int32)
    matched = (flat_heads[None, None, :] == head_ids[None, :, None]) & (
        group_rank[None, None, :] == row_rank[:, :, None]
    )
    owner_slot = jnp.sum(jnp.where(matched, slot_ids[None, None, :], 0), axis=2)
    flat_index = owner_slot * row_cap + row_step
    returned_rows = returned.reshape(-1, HDIM)
    attended_home = returned_rows[flat_index].reshape(tok_dev, HEADS * HDIM)
    partner = partner_2(attended_home, "branch", 0)
    on_positive = lax.axis_index("branch") == 0
    own_value = attended_home.astype(jnp.float32)
    partner_value = partner.astype(jnp.float32)
    positive = jnp.where(on_positive, own_value, partner_value)
    negative = jnp.where(on_positive, partner_value, own_value)
    guided = GUIDE_SCALE * positive - (GUIDE_SCALE - 1.0) * negative
    magnitude = jnp.mean(jnp.abs(guided), axis=1, keepdims=True)
    normed = (guided / (magnitude + EPSILON)).astype(jnp.bfloat16)
    projected = jnp.dot(normed, out_weight, preferred_element_type=jnp.float32).astype(jnp.bfloat16)
    saved_rows = jnp.transpose(logsum, (1, 2, 0)).reshape(1, 1, slot_count, row_cap, seq_count)
    return (projected, saved_rows)


KERNEL_PARAMS = pltpu.CompilerParams(vmem_limit_bytes=16 * 1024 * 1024)


SPLIT = 2
FAR = 4
HOLD_COPIES = 4
TABLE_PIECES = 3
SPLITTER = 65537.0


def swap_shards(array, offset):
    pairs = [(i, i ^ offset) for i in range(lax.axis_size("seq"))]
    return lax.ppermute(array, "seq", pairs)


def swap_by_core(array, offsets):
    pairs = [
        (2 * i + core, 2 * (i ^ offsets[core]) + core)
        for i in range(lax.axis_size("seq"))
        for core in range(2)
    ]
    return lax.ppermute(array, ("seq", "branch"), pairs)


FIRST = (SPLIT, SPLIT + FAR)
SECOND = (SPLIT + FAR, SPLIT)
THIRD = (1, FAR)
FOURTH = (FAR, 1)


def place_offsets():
    received = [(0, 0), FIRST, SECOND, THIRD, FOURTH]
    passed_on = [(a + 1, b + 1) for a, b in (FIRST, SECOND, (FAR, FAR))]
    core = lax.axis_index("branch")
    return [jnp.where(core == 0, a, b) for a, b in received + passed_on]


def pack_kernel(
    query_hbm,
    key_hbm,
    value_hbm,
    counts_hbm,
    head_hbm,
    own_ref,
    other_ref,
    limits_ref,
    pick_ref,
    slot_head_ref,
    counts_ref,
    head_ref,
    copy_sems,
):
    tok_dev = own_ref.shape[0] // 3
    half_width = own_ref.shape[1]
    slot_count, shard_count = head_ref.shape
    shard = lax.axis_index("seq")
    half = (shard // SPLIT) % 2
    copies = [
        pltpu.make_async_copy(counts_hbm, counts_ref, copy_sems.at[0]),
        pltpu.make_async_copy(head_hbm, head_ref, copy_sems.at[1]),
    ]
    for target, place in ((other_ref, 1 - half), (own_ref, half)):
        columns = pl.ds(pl.multiple_of(place * half_width, half_width), half_width)
        for part, source in enumerate((key_hbm, value_hbm, query_hbm)):
            rows = pl.ds(part * tok_dev, tok_dev)
            copies.append(
                pltpu.make_async_copy(
                    source.at[0, :, columns], target.at[rows, :], copy_sems.at[len(copies)]
                )
            )
    for copy in copies:
        copy.start()
    copies[0].wait()
    copies[1].wait()

    lane = lax.broadcasted_iota(jnp.int32, (1, limits_ref.shape[1]), 1)
    lane_limit = jnp.zeros(lane.shape, jnp.int32)
    for place, offset in enumerate(place_offsets()):
        lane_limit = jnp.where(lane // tok_dev == place, counts_ref[shard ^ offset], lane_limit)
    limits_ref[0:1, :] = (lane % tok_dev < lane_limit).astype(jnp.int32)
    limits_ref[1:2, :] = jnp.full(lane.shape, counts_ref[shard], jnp.int32)
    limits_ref[2:3, :] = jnp.full(lane.shape, counts_ref[shard ^ SPLIT], jnp.int32)

    step = lax.broadcasted_iota(jnp.int32, (1, pick_ref.shape[2]), 1)
    for slot in range(slot_count):
        head = head_ref[slot, shard]
        group_size = jnp.int32(0)
        group_rank = jnp.int32(0)
        for other_shard in range(shard_count):
            for other_slot in range(slot_count):
                same = (head_ref[other_slot, other_shard] == head).astype(jnp.int32)
                before = other_shard * slot_count + other_slot < shard * slot_count + slot
                group_size = group_size + same
                group_rank = group_rank + same * before.astype(jnp.int32)
        served = group_rank + group_size * step
        for source in range(shard_count):
            pick_ref[slot, source : source + 1, :] = jnp.where(
                served < counts_ref[source], served + source * tok_dev, -1
            )
        slot_head_ref[slot] = jnp.full(slot_head_ref.shape[1:], head, jnp.int32)
    for copy in copies[2:]:
        copy.wait()


def hold_kernel(weight_hbm, after_ref, weight_ref, copy_sems):
    share = weight_ref.shape[0] // HOLD_COPIES
    copies = []
    for number in range(HOLD_COPIES):
        rows = pl.ds(number * share, share)
        copies.append(
            pltpu.make_async_copy(
                weight_hbm.at[rows, :], weight_ref.at[rows, :], copy_sems.at[number]
            )
        )
    for copy in copies:
        copy.start()
    for copy in copies:
        copy.wait()


def gathered(set_refs, part, columns):
    tok_dev = set_refs[0].shape[0] // 3
    rows = pl.ds(part * tok_dev, tok_dev)
    return jnp.concatenate([ref[rows, columns] for ref in set_refs], axis=0)


def head_scores(query_rows, key_all):
    return lax.dot_general(
        query_rows, key_all, (((1,), (1,)), ((), ())), preferred_element_type=jnp.float32
    )


def attend_kernel(set_count, limits_ref, *refs):
    set_refs = refs[:set_count]
    keep_ref, send_ref, message_ref, table_ref, lines_ref = refs[set_count:]
    tok_dev, half_width = keep_ref.shape
    half_heads = half_width // HDIM
    on_first_core = lax.axis_index("branch") == 0
    shard = lax.axis_index("seq")
    head_columns = [pl.ds(head * HDIM, HDIM) for head in range(half_heads)]
    key_valid = limits_ref[0:1, :] > 0

    def served_rows(array):
        near = jnp.where(
            on_first_core, array[tok_dev : 2 * tok_dev], array[2 * tok_dev : 3 * tok_dev]
        )
        return jnp.concatenate([array[:tok_dev], near], axis=0)

    all_scores = [
        head_scores(gathered(set_refs, 2, columns), gathered(set_refs, 0, columns))
        for columns in head_columns
    ]
    lane = lax.broadcasted_iota(jnp.int32, all_scores[0].shape, 1)
    lines = jnp.zeros(lane.shape, jnp.float32)
    served = []
    for head, scores in enumerate(all_scores):
        scores = jnp.where(key_valid, scores * (1.0 / math.sqrt(HDIM)), -jnp.inf)
        top_score = jnp.max(scores, axis=1, keepdims=True)
        weights = jnp.exp(scores - top_score)
        weight_sum = jnp.sum(weights, axis=1, keepdims=True)
        lines = jnp.where(lane == head, top_score + jnp.log(weight_sum), lines)
        served.append((served_rows(weights).astype(jnp.bfloat16), served_rows(weight_sum)))
    row = lax.broadcasted_iota(jnp.int32, (tok_dev, HDIM), 0)
    for columns, (rounded, weight_sum) in zip(head_columns, served):
        mixed = jnp.dot(
            rounded, gathered(set_refs, 1, columns), preferred_element_type=jnp.float32
        )
        attended = mixed / weight_sum
        kept = jnp.where(row < limits_ref[1:2, :HDIM], attended[:tok_dev], 0.0)
        sent = jnp.where(row < limits_ref[2:3, :HDIM], attended[tok_dev:], 0.0)
        keep_ref[:, columns] = kept.astype(jnp.bfloat16)
        send_ref[:, columns] = sent.astype(jnp.bfloat16)
        message_ref[pl.ds(0, tok_dev), columns] = sent.astype(jnp.bfloat16)

    for place, offset in enumerate(place_offsets()):
        rows = pl.ds(pl.multiple_of((shard ^ offset) * tok_dev, tok_dev), tok_dev)
        lines_ref[rows, :] = lines[place * tok_dev : (place + 1) * tok_dev]
    table = jnp.transpose(lines_ref[...])[: table_ref.shape[0]]
    table_ref[...] = table
    row = lax.broadcasted_iota(jnp.int32, (tok_dev, lines.shape[0]), 0)
    for head in range(half_heads):
        rest = jnp.broadcast_to(table[head : head + 1], row.shape)
        block = jnp.zeros(row.shape, jnp.float32)
        for piece in range(TABLE_PIECES):
            scaled = rest * SPLITTER
            part = scaled - (scaled - rest)
            block = jnp.where(row == piece, part, block)
            rest = rest - part
        columns = pl.ds(head * lines.shape[0], lines.shape[0])
        message_ref[pl.ds(tok_dev, tok_dev), columns] = block.astype(jnp.bfloat16)


def guidance(own, partner):
    on_positive = lax.axis_index("branch") == 0
    own_scale = jnp.where(on_positive, GUIDE_SCALE, 1.0 - GUIDE_SCALE)
    partner_scale = jnp.where(on_positive, 1.0 - GUIDE_SCALE, GUIDE_SCALE)
    return own_scale * own.astype(jnp.float32) + partner_scale * partner.astype(jnp.float32)


def half_product(guided, weight_ref, place):
    half_width = guided.shape[1]
    rows = pl.ds(pl.multiple_of(place * half_width, half_width), half_width)
    return jnp.dot(
        guided.astype(jnp.bfloat16), weight_ref[rows, :], preferred_element_type=jnp.float32
    )


def keep_kernel(keep_ref, partner_keep_ref, weight_ref, total_ref, size_ref):
    half = (lax.axis_index("seq") // SPLIT) % 2
    guided = guidance(keep_ref[...], partner_keep_ref[...])
    size = jnp.sum(jnp.abs(guided), axis=1, keepdims=True)
    size_ref[...] = jnp.broadcast_to(size, size_ref.shape)
    total_ref[...] = half_product(guided, weight_ref, half)


def project_kernel(
    total_ref,
    size_ref,
    message_ref,
    partner_back_ref,
    weight_ref,
    table_ref,
    pick_ref,
    slot_head_ref,
    projected_ref,
    saved_ref,
):
    tok_dev, half_width = partner_back_ref.shape
    half_heads = half_width // HDIM
    tokens = table_ref.shape[1]
    half = (lax.axis_index("seq") // SPLIT) % 2
    guided = guidance(message_ref[pl.ds(0, tok_dev), :], partner_back_ref[...])
    size = size_ref[:, 0:1] + jnp.sum(jnp.abs(guided), axis=1, keepdims=True)
    magnitude = size / (2 * half_width)
    total = total_ref[...] + half_product(guided, weight_ref, 1 - half)
    projected_ref[...] = (total / (magnitude + EPSILON)).astype(jnp.bfloat16)

    for slot in range(saved_ref.shape[0]):
        slot_head = slot_head_ref[slot, 0:1, :]
        line = jnp.zeros((1, tokens), jnp.float32)
        for head in range(half_heads):
            pieces = message_ref[pl.ds(tok_dev, tok_dev), pl.ds(head * tokens, tokens)]
            pieces = pieces.astype(jnp.float32)
            other = pieces[0:1]
            for piece in range(1, TABLE_PIECES):
                other = other + pieces[piece : piece + 1]
            line = jnp.where(slot_head == half * half_heads + head, table_ref[head : head + 1], line)
            line = jnp.where(slot_head == (1 - half) * half_heads + head, other, line)
        pick = pick_ref[slot]
        spread = jnp.broadcast_to(line, pick.shape)
        taken = jnp.take_along_axis(spread, jnp.maximum(pick, 0), axis=1)
        saved_ref[slot] = jnp.where(pick >= 0, taken, 0.0)[:, : saved_ref.shape[2]]


def per_device_halves(queries, key_rows, value_rows, counts, head_of, out_weight):
    seq_count = lax.axis_size("seq")
    tok_dev, width = queries.shape[1:]
    half_width = width // 2
    tokens = seq_count * tok_dev
    slot_count = head_of.shape[1]
    fewest = max(1, seq_count * slot_count // (2 * HEADS))
    row_cap = (tok_dev + fewest - 1) // fewest
    any_spec = pl.BlockSpec(memory_space=pl.ANY)
    vmem = pl.BlockSpec(memory_space=pltpu.VMEM)

    def held(*arrays):
        return [pltpu.with_memory_space_constraint(array, pltpu.VMEM) for array in arrays]

    def distant(*arrays):
        return [pltpu.with_memory_space_constraint(array, pltpu.HBM) for array in arrays]

    own, other, limits, pick, slot_head = pl.pallas_call(
        pack_kernel,
        out_shape=[
            pltpu.VMEM((3 * tok_dev, half_width), jnp.bfloat16),
            pltpu.VMEM((3 * tok_dev, half_width), jnp.bfloat16),
            pltpu.VMEM((8, tokens), jnp.int32),
            pltpu.VMEM((slot_count, seq_count, tokens), jnp.int32),
            pltpu.VMEM((slot_count, 8, tokens), jnp.int32),
        ],
        in_specs=[any_spec] * 5,
        out_specs=[vmem] * 5,
        scratch_shapes=[
            pltpu.SMEM((seq_count,), jnp.int32),
            pltpu.SMEM((slot_count, seq_count), jnp.int32),
            pltpu.SemaphoreType.DMA((8,)),
        ],
        compiler_params=KERNEL_PARAMS,
        name="pack",
    )(*distant(queries, key_rows, value_rows, counts, jnp.transpose(head_of)))

    weight_held = pl.pallas_call(
        hold_kernel,
        out_shape=pltpu.VMEM(out_weight.shape, jnp.bfloat16),
        in_specs=[any_spec, vmem],
        out_specs=vmem,
        scratch_shapes=[pltpu.SemaphoreType.DMA((HOLD_COPIES,))],
        compiler_params=KERNEL_PARAMS,
        cost_estimate=pl.CostEstimate(
            flops=0, bytes_accessed=4 * out_weight.size, transcendentals=0
        ),
        name="hold",
    )(*distant(out_weight), *held(limits))
    first = swap_by_core(other, FIRST)
    second = swap_by_core(other, SECOND)
    third = swap_by_core(own, THIRD)
    fourth = swap_by_core(own, FOURTH)
    far = jnp.where(lax.axis_index("branch") == 0, fourth, third)
    passed_on = [swap_shards(array, 1) for array in (first, second, far)]
    sets = [own, first, second, third, fourth] + passed_on
    limits, weight_held = lax.optimization_barrier((limits, weight_held))
    keep, send, message, table = pl.pallas_call(
        functools.partial(attend_kernel, len(sets)),
        out_shape=[pltpu.VMEM((tok_dev, half_width), jnp.bfloat16)] * 2
        + [
            pltpu.VMEM((2 * tok_dev, half_width), jnp.bfloat16),
            pltpu.VMEM((half_width // HDIM + 7 & -8, tokens), jnp.float32),
        ],
        in_specs=[vmem] * (1 + len(sets)),
        out_specs=[vmem] * 4,
        scratch_shapes=[pltpu.VMEM((tokens, HDIM), jnp.float32)],
        compiler_params=KERNEL_PARAMS,
        name="attend",
    )(*held(limits, *sets))
    across = [(2 * i + b, 2 * (i ^ SPLIT) + 1 - b) for i in range(seq_count) for b in range(2)]
    partner_back = lax.ppermute(send, ("seq", "branch"), across)
    partner_keep = partner_2(keep, "branch", 0)
    back = swap_shards(message, SPLIT)
    total, size = pl.pallas_call(
        keep_kernel,
        out_shape=[
            pltpu.VMEM((tok_dev, out_weight.shape[1]), jnp.float32),
            pltpu.VMEM((tok_dev, HDIM), jnp.float32),
        ],
        in_specs=[vmem] * 3,
        out_specs=[vmem] * 2,
        compiler_params=KERNEL_PARAMS,
        name="keep",
    )(*held(keep, partner_keep, weight_held))
    projected, saved = pl.pallas_call(
        project_kernel,
        out_shape=[
            jax.ShapeDtypeStruct((tok_dev, out_weight.shape[1]), jnp.bfloat16),
            jax.ShapeDtypeStruct((slot_count, seq_count, row_cap), jnp.float32),
        ],
        in_specs=[vmem] * 8,
        out_specs=[vmem] * 2,
        compiler_params=KERNEL_PARAMS,
        name="project",
    )(*held(total, size, back, partner_back, weight_held, table, pick, slot_head))
    saved = jnp.transpose(saved, (0, 2, 1))
    return (projected, saved.reshape(1, 1, slot_count, row_cap, seq_count))


def solution(mesh):
    seq_count = mesh.shape["seq"]
    small = seq_count == 2 * FAR
    return jax.shard_map(
        per_device_halves if small else per_device_exchange,
        mesh=mesh,
        in_specs=(
            P("branch", ("groups", "seq"), None),
            P("branch", ("groups", "seq"), None),
            P("branch", ("groups", "seq"), None),
            P("groups"),
            P(),
            P(None, "branch"),
        ),
        out_specs=(
            P(("groups", "seq"), "branch"),
            P("branch", ("groups", "seq"), None, None, None),
        ),
        check_vma=False,
    )
```

```python
import functools
import math

import jax
import jax.numpy as jnp
from jax import lax
from jax.experimental import pallas as pl
from jax.experimental.pallas import tpu as pltpu
from jax.sharding import PartitionSpec as P

HEADS = 12
HDIM = 128


GUIDE_SCALE = 3.0
EPSILON = 1e-06


def partner_2(array, axis, stride):
    return lax.ppermute(array, axis, [(i, i ^ 1 << stride) for i in range(lax.axis_size(axis))])


def slot_layout(head_of):
    flat_heads = head_of.reshape(-1)
    slot_order = jnp.arange(flat_heads.shape[0], dtype=jnp.int32)
    same_head = flat_heads[:, None] == flat_heads[None, :]
    group_size = jnp.sum(same_head.astype(jnp.int32), axis=1)
    earlier = same_head & (slot_order[None, :] < slot_order[:, None])
    group_rank = jnp.sum(earlier.astype(jnp.int32), axis=1)
    return (flat_heads, group_size, group_rank)


def key_grouping(seq_count, tok_dev):
    shard_limit = max(1, 2048 // tok_dev)
    grouping = 1
    for attempt in range(16):
        if grouping * 2 <= shard_limit and seq_count % (grouping * 2) == 0:
            grouping = grouping * 2
    return grouping


def attend_rows(query_block, key_slot, value_slot, key_valid, key_block):
    row_count = query_block.shape[0]
    head_size = query_block.shape[1]
    block_count = key_slot.shape[0] // key_block
    scale_factor = 1.0 / math.sqrt(head_size)

    def fold_block(block_id, state_in):
        top_score, weight_sum, summed = state_in
        scores = (
            jnp.einsum("qd,kd->qk", query_block, key_slot, preferred_element_type=jnp.float32)
            * scale_factor
        )
        scores = jnp.where(key_valid[None, :], scores, -jnp.inf)
        new_top = jnp.maximum(top_score, jnp.max(scores, axis=1))
        fading = jnp.exp(top_score - new_top)
        weights = jnp.exp(scores - new_top[:, None])
        weight_sum = weight_sum * fading + jnp.sum(weights, axis=1)
        summed = summed * fading[:, None] + jnp.dot(
            weights.astype(jnp.bfloat16), value_slot, preferred_element_type=jnp.float32
        )
        return (new_top, weight_sum, summed)

    start_state = (
        jnp.full((row_count,), -jnp.inf, jnp.float32),
        jnp.zeros((row_count,), jnp.float32),
        jnp.zeros((row_count, head_size), jnp.float32),
    )
    top_score, weight_sum, summed = lax.fori_loop(0, block_count, fold_block, start_state)
    return (summed / weight_sum[:, None], top_score + jnp.log(weight_sum))


def serve_slots(query_items, mask_items, key_recv, value_recv, key_valid, key_block):
    source_count, slot_count, item_count, head_size = query_items.shape
    all_tokens = key_recv.shape[0] * key_recv.shape[2]
    per_block = max(1, 512 // source_count)
    slot_outputs = []
    slot_logsum = []
    for slot_id in range(slot_count):
        key_slot = key_recv[:, slot_id].reshape(all_tokens, head_size)
        value_slot = value_recv[:, slot_id].reshape(all_tokens, head_size)
        taken_items = min(per_block, item_count)
        query_block = query_items[:, slot_id, 0:taken_items].reshape(
            source_count * taken_items, head_size
        )
        attended, logsum = attend_rows(query_block, key_slot, value_slot, key_valid, key_block)
        pieces_out = attended.reshape(source_count, taken_items, head_size)
        pieces_sum = logsum.reshape(source_count, taken_items)
        slot_outputs.append(pieces_out)
        slot_logsum.append(pieces_sum)
    attended = jnp.stack(slot_outputs, axis=1)
    logsum = jnp.stack(slot_logsum, axis=1)
    keep_rows = mask_items > 0
    attended = jnp.where(keep_rows[:, :, :, None], attended, 0.0).astype(jnp.bfloat16)
    logsum = jnp.where(keep_rows, logsum, 0.0)
    return (attended, logsum)


def per_device_exchange(queries, key_rows, value_rows, counts, head_of, out_weight):
    seq_count = lax.axis_size("seq")
    tok_dev = queries.shape[1]
    slot_count = head_of.shape[1]
    fewest = max(1, seq_count * slot_count // (2 * HEADS))
    row_cap = (tok_dev + fewest - 1) // fewest
    my_index = lax.axis_index("seq")
    flat_heads, group_size, group_rank = slot_layout(head_of)
    row_steps = jnp.arange(row_cap, dtype=jnp.int32)
    served_rows = group_rank[:, None] + group_size[:, None] * row_steps[None, :]
    my_count = counts[my_index]
    clipped = jnp.minimum(served_rows, tok_dev - 1)
    query_grid = queries[0].reshape(tok_dev, HEADS, HDIM)
    row_live = served_rows < my_count
    query_send = query_grid[clipped, flat_heads[:, None]]
    query_send = jnp.where(row_live[:, :, None], query_send, jnp.zeros((), jnp.bfloat16)).reshape(
        seq_count, slot_count, row_cap, HDIM
    )
    mask_send = row_live.astype(jnp.bfloat16).reshape(seq_count, slot_count, row_cap)
    token_ids = jnp.arange(tok_dev, dtype=jnp.int32)
    key_grid = key_rows[0].reshape(tok_dev, HEADS, HDIM)
    value_grid = value_rows[0].reshape(tok_dev, HEADS, HDIM)
    key_send = key_grid[token_ids[None, :], flat_heads[:, None]].reshape(
        seq_count, slot_count, tok_dev, HDIM
    )
    value_send = value_grid[token_ids[None, :], flat_heads[:, None]].reshape(
        seq_count, slot_count, tok_dev, HDIM
    )
    key_valid = (token_ids[None, :] < counts[:, None]).reshape(-1)
    key_block = tok_dev * key_grouping(seq_count, tok_dev)
    query_recv, mask_recv, key_recv, value_recv = (
        lax.all_to_all(query_send, "seq", split_axis=0, concat_axis=0, tiled=True),
        lax.all_to_all(mask_send, "seq", split_axis=0, concat_axis=0, tiled=True),
        lax.all_to_all(key_send, "seq", split_axis=0, concat_axis=0, tiled=True),
        lax.all_to_all(value_send, "seq", split_axis=0, concat_axis=0, tiled=True),
    )
    attended, logsum = serve_slots(
        query_recv, mask_recv, key_recv, value_recv, key_valid, key_block
    )
    returned = lax.all_to_all(attended, "seq", split_axis=0, concat_axis=0, tiled=True)
    head_ids = jnp.arange(HEADS, dtype=jnp.int32)
    head_group = jnp.sum((flat_heads[None, :] == head_ids[:, None]).astype(jnp.int32), axis=1)
    row_rank = token_ids[:, None] % head_group[None, :]
    row_step = token_ids[:, None] // head_group[None, :]
    slot_ids = jnp.arange(flat_heads.shape[0], dtype=jnp.int32)
    matched = (flat_heads[None, None, :] == head_ids[None, :, None]) & (
        group_rank[None, None, :] == row_rank[:, :, None]
    )
    owner_slot = jnp.sum(jnp.where(matched, slot_ids[None, None, :], 0), axis=2)
    flat_index = owner_slot * row_cap + row_step
    returned_rows = returned.reshape(-1, HDIM)
    attended_home = returned_rows[flat_index].reshape(tok_dev, HEADS * HDIM)
    partner = partner_2(attended_home, "branch", 0)
    on_positive = lax.axis_index("branch") == 0
    own_value = attended_home.astype(jnp.float32)
    partner_value = partner.astype(jnp.float32)
    positive = jnp.where(on_positive, own_value, partner_value)
    negative = jnp.where(on_positive, partner_value, own_value)
    guided = GUIDE_SCALE * positive - (GUIDE_SCALE - 1.0) * negative
    magnitude = jnp.mean(jnp.abs(guided), axis=1, keepdims=True)
    normed = (guided / (magnitude + EPSILON)).astype(jnp.bfloat16)
    projected = jnp.dot(normed, out_weight, preferred_element_type=jnp.float32).astype(jnp.bfloat16)
    saved_rows = jnp.transpose(logsum, (1, 2, 0)).reshape(1, 1, slot_count, row_cap, seq_count)
    return (projected, saved_rows)


KERNEL_PARAMS = pltpu.CompilerParams(vmem_limit_bytes=16 * 1024 * 1024)


SPLIT = 2
HOLD_COPIES = 4
TABLE_PIECES = 3
SPLITTER = 65537.0


def swap_shards(array, offset):
    pairs = [(i, i ^ offset) for i in range(lax.axis_size("seq"))]
    return lax.ppermute(array, "seq", pairs)


def place_offsets(shard_count):
    line = list(range(0, shard_count, SPLIT))
    return line + [offset + 1 for offset in line]


def pack_kernel(
    query_hbm,
    key_hbm,
    value_hbm,
    counts_hbm,
    head_hbm,
    own_ref,
    other_ref,
    limits_ref,
    pick_ref,
    slot_head_ref,
    counts_ref,
    head_ref,
    copy_sems,
):
    tok_dev = own_ref.shape[0] // 3
    half_width = own_ref.shape[1]
    slot_count, shard_count = head_ref.shape
    shard = lax.axis_index("seq")
    half = (shard // SPLIT) % 2
    copies = [
        pltpu.make_async_copy(counts_hbm, counts_ref, copy_sems.at[0]),
        pltpu.make_async_copy(head_hbm, head_ref, copy_sems.at[1]),
    ]
    for target, place in ((other_ref, 1 - half), (own_ref, half)):
        columns = pl.ds(pl.multiple_of(place * half_width, half_width), half_width)
        for part, source in enumerate((key_hbm, value_hbm, query_hbm)):
            rows = pl.ds(part * tok_dev, tok_dev)
            copies.append(
                pltpu.make_async_copy(
                    source.at[0, :, columns], target.at[rows, :], copy_sems.at[len(copies)]
                )
            )
    for copy in copies:
        copy.start()
    copies[0].wait()
    copies[1].wait()

    lane = lax.broadcasted_iota(jnp.int32, (1, limits_ref.shape[1]), 1)
    lane_limit = jnp.zeros(lane.shape, jnp.int32)
    for place, offset in enumerate(place_offsets(shard_count)):
        lane_limit = jnp.where(lane // tok_dev == place, counts_ref[shard ^ offset], lane_limit)
    limits_ref[0:1, :] = (lane % tok_dev < lane_limit).astype(jnp.int32)
    limits_ref[1:2, :] = jnp.full(lane.shape, counts_ref[shard], jnp.int32)
    limits_ref[2:3, :] = jnp.full(lane.shape, counts_ref[shard ^ SPLIT], jnp.int32)

    step = lax.broadcasted_iota(jnp.int32, (1, pick_ref.shape[2]), 1)
    for slot in range(slot_count):
        head = head_ref[slot, shard]
        group_size = jnp.int32(0)
        group_rank = jnp.int32(0)
        for other_shard in range(shard_count):
            for other_slot in range(slot_count):
                same = (head_ref[other_slot, other_shard] == head).astype(jnp.int32)
                before = other_shard * slot_count + other_slot < shard * slot_count + slot
                group_size = group_size + same
                group_rank = group_rank + same * before.astype(jnp.int32)
        served = group_rank + group_size * step
        for source in range(shard_count):
            pick_ref[slot, source : source + 1, :] = jnp.where(
                served < counts_ref[source], served + source * tok_dev, -1
            )
        slot_head_ref[slot] = jnp.full(slot_head_ref.shape[1:], head, jnp.int32)
    for copy in copies[2:]:
        copy.wait()


def hold_kernel(weight_hbm, after_ref, weight_ref, copy_sems):
    share = weight_ref.shape[0] // HOLD_COPIES
    copies = []
    for number in range(HOLD_COPIES):
        rows = pl.ds(number * share, share)
        copies.append(
            pltpu.make_async_copy(
                weight_hbm.at[rows, :], weight_ref.at[rows, :], copy_sems.at[number]
            )
        )
    for copy in copies:
        copy.start()
    for copy in copies:
        copy.wait()


def gathered(set_refs, part, columns):
    tok_dev = set_refs[0].shape[0] // 3
    rows = pl.ds(part * tok_dev, tok_dev)
    return jnp.concatenate([ref[rows, columns] for ref in set_refs], axis=0)


def head_scores(query_rows, key_all):
    return lax.dot_general(
        query_rows, key_all, (((1,), (1,)), ((), ())), preferred_element_type=jnp.float32
    )


def attend_kernel(set_count, limits_ref, *refs):
    set_refs = refs[:set_count]
    keep_ref, send_ref, message_ref, table_ref, lines_ref = refs[set_count:]
    tok_dev, half_width = keep_ref.shape
    half_heads = half_width // HDIM
    shard = lax.axis_index("seq")
    head_columns = [pl.ds(head * HDIM, HDIM) for head in range(half_heads)]
    key_valid = limits_ref[0:1, :] > 0

    all_scores = [
        head_scores(gathered(set_refs, 2, columns), gathered(set_refs, 0, columns))
        for columns in head_columns
    ]
    lane = lax.broadcasted_iota(jnp.int32, all_scores[0].shape, 1)
    lines = jnp.zeros(lane.shape, jnp.float32)
    served = []
    for head, scores in enumerate(all_scores):
        scores = jnp.where(key_valid, scores * (1.0 / math.sqrt(HDIM)), -jnp.inf)
        top_score = jnp.max(scores, axis=1, keepdims=True)
        weights = jnp.exp(scores - top_score)
        weight_sum = jnp.sum(weights, axis=1, keepdims=True)
        lines = jnp.where(lane == head, top_score + jnp.log(weight_sum), lines)
        served.append((weights[: 2 * tok_dev].astype(jnp.bfloat16), weight_sum[: 2 * tok_dev]))
    row = lax.broadcasted_iota(jnp.int32, (tok_dev, HDIM), 0)
    for columns, (rounded, weight_sum) in zip(head_columns, served):
        mixed = jnp.dot(
            rounded, gathered(set_refs, 1, columns), preferred_element_type=jnp.float32
        )
        attended = mixed / weight_sum
        kept = jnp.where(row < limits_ref[1:2, :HDIM], attended[:tok_dev], 0.0)
        sent = jnp.where(row < limits_ref[2:3, :HDIM], attended[tok_dev:], 0.0)
        keep_ref[:, columns] = kept.astype(jnp.bfloat16)
        send_ref[:, columns] = sent.astype(jnp.bfloat16)
        message_ref[pl.ds(0, tok_dev), columns] = sent.astype(jnp.bfloat16)

    for place, offset in enumerate(place_offsets(set_count)):
        rows = pl.ds(pl.multiple_of((shard ^ offset) * tok_dev, tok_dev), tok_dev)
        lines_ref[rows, :] = lines[place * tok_dev : (place + 1) * tok_dev]
    table = jnp.transpose(lines_ref[...])[: table_ref.shape[0]]
    table_ref[...] = table
    row = lax.broadcasted_iota(jnp.int32, (tok_dev, lines.shape[0]), 0)
    for head in range(half_heads):
        rest = jnp.broadcast_to(table[head : head + 1], row.shape)
        block = jnp.zeros(row.shape, jnp.float32)
        for piece in range(TABLE_PIECES):
            scaled = rest * SPLITTER
            part = scaled - (scaled - rest)
            block = jnp.where(row == piece, part, block)
            rest = rest - part
        columns = pl.ds(head * lines.shape[0], lines.shape[0])
        message_ref[pl.ds(tok_dev, tok_dev), columns] = block.astype(jnp.bfloat16)


def guidance(own, partner):
    on_positive = lax.axis_index("branch") == 0
    own_scale = jnp.where(on_positive, GUIDE_SCALE, 1.0 - GUIDE_SCALE)
    partner_scale = jnp.where(on_positive, 1.0 - GUIDE_SCALE, GUIDE_SCALE)
    return own_scale * own.astype(jnp.float32) + partner_scale * partner.astype(jnp.float32)


def half_product(guided, weight_ref, place):
    half_width = guided.shape[1]
    rows = pl.ds(pl.multiple_of(place * half_width, half_width), half_width)
    return jnp.dot(
        guided.astype(jnp.bfloat16), weight_ref[rows, :], preferred_element_type=jnp.float32
    )


def keep_kernel(keep_ref, partner_keep_ref, weight_ref, total_ref, size_ref):
    half = (lax.axis_index("seq") // SPLIT) % 2
    guided = guidance(keep_ref[...], partner_keep_ref[...])
    size = jnp.sum(jnp.abs(guided), axis=1, keepdims=True)
    size_ref[...] = jnp.broadcast_to(size, size_ref.shape)
    total_ref[...] = half_product(guided, weight_ref, half)


def project_kernel(
    total_ref,
    size_ref,
    message_ref,
    partner_back_ref,
    weight_ref,
    table_ref,
    pick_ref,
    slot_head_ref,
    projected_ref,
    saved_ref,
):
    tok_dev, half_width = partner_back_ref.shape
    half_heads = half_width // HDIM
    tokens = table_ref.shape[1]
    half = (lax.axis_index("seq") // SPLIT) % 2
    guided = guidance(message_ref[pl.ds(0, tok_dev), :], partner_back_ref[...])
    size = size_ref[:, 0:1] + jnp.sum(jnp.abs(guided), axis=1, keepdims=True)
    magnitude = size / (2 * half_width)
    total = total_ref[...] + half_product(guided, weight_ref, 1 - half)
    projected_ref[...] = (total / (magnitude + EPSILON)).astype(jnp.bfloat16)

    for slot in range(saved_ref.shape[0]):
        slot_head = slot_head_ref[slot, 0:1, :]
        line = jnp.zeros((1, tokens), jnp.float32)
        for head in range(half_heads):
            pieces = message_ref[pl.ds(tok_dev, tok_dev), pl.ds(head * tokens, tokens)]
            pieces = pieces.astype(jnp.float32)
            other = pieces[0:1]
            for piece in range(1, TABLE_PIECES):
                other = other + pieces[piece : piece + 1]
            line = jnp.where(slot_head == half * half_heads + head, table_ref[head : head + 1], line)
            line = jnp.where(slot_head == (1 - half) * half_heads + head, other, line)
        pick = pick_ref[slot]
        spread = jnp.broadcast_to(line, pick.shape)
        taken = jnp.take_along_axis(spread, jnp.maximum(pick, 0), axis=1)
        saved_ref[slot] = jnp.where(pick >= 0, taken, 0.0)[:, : saved_ref.shape[2]]


def per_device_halves(queries, key_rows, value_rows, counts, head_of, out_weight):
    seq_count = lax.axis_size("seq")
    tok_dev, width = queries.shape[1:]
    half_width = width // 2
    tokens = seq_count * tok_dev
    slot_count = head_of.shape[1]
    fewest = max(1, seq_count * slot_count // (2 * HEADS))
    row_cap = (tok_dev + fewest - 1) // fewest
    any_spec = pl.BlockSpec(memory_space=pl.ANY)
    vmem = pl.BlockSpec(memory_space=pltpu.VMEM)

    def held(*arrays):
        return [pltpu.with_memory_space_constraint(array, pltpu.VMEM) for array in arrays]

    def distant(*arrays):
        return [pltpu.with_memory_space_constraint(array, pltpu.HBM) for array in arrays]

    own, other, limits, pick, slot_head = pl.pallas_call(
        pack_kernel,
        out_shape=[
            pltpu.VMEM((3 * tok_dev, half_width), jnp.bfloat16),
            pltpu.VMEM((3 * tok_dev, half_width), jnp.bfloat16),
            pltpu.VMEM((8, tokens), jnp.int32),
            pltpu.VMEM((slot_count, seq_count, tokens), jnp.int32),
            pltpu.VMEM((slot_count, 8, tokens), jnp.int32),
        ],
        in_specs=[any_spec] * 5,
        out_specs=[vmem] * 5,
        scratch_shapes=[
            pltpu.SMEM((seq_count,), jnp.int32),
            pltpu.SMEM((slot_count, seq_count), jnp.int32),
            pltpu.SemaphoreType.DMA((8,)),
        ],
        compiler_params=KERNEL_PARAMS,
        name="pack",
    )(*distant(queries, key_rows, value_rows, counts, jnp.transpose(head_of)))

    weight_held = pl.pallas_call(
        hold_kernel,
        out_shape=pltpu.VMEM(out_weight.shape, jnp.bfloat16),
        in_specs=[any_spec, vmem],
        out_specs=vmem,
        scratch_shapes=[pltpu.SemaphoreType.DMA((HOLD_COPIES,))],
        compiler_params=KERNEL_PARAMS,
        cost_estimate=pl.CostEstimate(
            flops=0, bytes_accessed=4 * out_weight.size, transcendentals=0
        ),
        name="hold",
    )(*distant(out_weight), *held(limits))
    line = [own] + [
        swap_shards(other if offset & SPLIT else own, offset)
        for offset in range(SPLIT, seq_count, SPLIT)
    ]
    sets = line + [swap_shards(array, 1) for array in line]
    limits, weight_held = lax.optimization_barrier((limits, weight_held))
    keep, send, message, table = pl.pallas_call(
        functools.partial(attend_kernel, len(sets)),
        out_shape=[pltpu.VMEM((tok_dev, half_width), jnp.bfloat16)] * 2
        + [
            pltpu.VMEM((2 * tok_dev, half_width), jnp.bfloat16),
            pltpu.VMEM((half_width // HDIM + 7 & -8, tokens), jnp.float32),
        ],
        in_specs=[vmem] * (1 + len(sets)),
        out_specs=[vmem] * 4,
        scratch_shapes=[pltpu.VMEM((tokens, HDIM), jnp.float32)],
        compiler_params=KERNEL_PARAMS,
        name="attend",
    )(*held(limits, *sets))
    across = [(2 * i + b, 2 * (i ^ SPLIT) + 1 - b) for i in range(seq_count) for b in range(2)]
    partner_back = lax.ppermute(send, ("seq", "branch"), across)
    partner_keep = partner_2(keep, "branch", 0)
    back = swap_shards(message, SPLIT)
    total, size = pl.pallas_call(
        keep_kernel,
        out_shape=[
            pltpu.VMEM((tok_dev, out_weight.shape[1]), jnp.float32),
            pltpu.VMEM((tok_dev, HDIM), jnp.float32),
        ],
        in_specs=[vmem] * 3,
        out_specs=[vmem] * 2,
        compiler_params=KERNEL_PARAMS,
        name="keep",
    )(*held(keep, partner_keep, weight_held))
    projected, saved = pl.pallas_call(
        project_kernel,
        out_shape=[
            jax.ShapeDtypeStruct((tok_dev, out_weight.shape[1]), jnp.bfloat16),
            jax.ShapeDtypeStruct((slot_count, seq_count, row_cap), jnp.float32),
        ],
        in_specs=[vmem] * 8,
        out_specs=[vmem] * 2,
        compiler_params=KERNEL_PARAMS,
        name="project",
    )(*held(total, size, back, partner_back, weight_held, table, pick, slot_head))
    saved = jnp.transpose(saved, (0, 2, 1))
    return (projected, saved.reshape(1, 1, slot_count, row_cap, seq_count))


def solution(mesh):
    seq_count = mesh.shape["seq"]
    hypercube = seq_count > SPLIT and seq_count & (seq_count - 1) == 0
    small = hypercube and seq_count <= HEADS
    return jax.shard_map(
        per_device_halves if small else per_device_exchange,
        mesh=mesh,
        in_specs=(
            P("branch", ("groups", "seq"), None),
            P("branch", ("groups", "seq"), None),
            P("branch", ("groups", "seq"), None),
            P("groups"),
            P(),
            P(None, "branch"),
        ),
        out_specs=(
            P(("groups", "seq"), "branch"),
            P("branch", ("groups", "seq"), None, None, None),
        ),
        check_vma=False,
    )
```

```python
import functools
import math

import jax
import jax.numpy as jnp
from jax import lax
from jax.experimental import pallas as pl
from jax.experimental.pallas import tpu as pltpu
from jax.sharding import PartitionSpec as P

HEADS = 12
HDIM = 128


GUIDE_SCALE = 3.0
EPSILON = 1e-06


def partner_2(array, axis, stride):
    return lax.ppermute(array, axis, [(i, i ^ 1 << stride) for i in range(lax.axis_size(axis))])


def slot_layout(head_of):
    flat_heads = head_of.reshape(-1)
    slot_order = jnp.arange(flat_heads.shape[0], dtype=jnp.int32)
    same_head = flat_heads[:, None] == flat_heads[None, :]
    group_size = jnp.sum(same_head.astype(jnp.int32), axis=1)
    earlier = same_head & (slot_order[None, :] < slot_order[:, None])
    group_rank = jnp.sum(earlier.astype(jnp.int32), axis=1)
    return (flat_heads, group_size, group_rank)


def key_grouping(seq_count, tok_dev):
    shard_limit = max(1, 2048 // tok_dev)
    grouping = 1
    for attempt in range(16):
        if grouping * 2 <= shard_limit and seq_count % (grouping * 2) == 0:
            grouping = grouping * 2
    return grouping


def attend_rows(query_block, key_slot, value_slot, key_valid, key_block):
    row_count = query_block.shape[0]
    head_size = query_block.shape[1]
    block_count = key_slot.shape[0] // key_block
    scale_factor = 1.0 / math.sqrt(head_size)

    def fold_block(block_id, state_in):
        top_score, weight_sum, summed = state_in
        scores = (
            jnp.einsum("qd,kd->qk", query_block, key_slot, preferred_element_type=jnp.float32)
            * scale_factor
        )
        scores = jnp.where(key_valid[None, :], scores, -jnp.inf)
        new_top = jnp.maximum(top_score, jnp.max(scores, axis=1))
        fading = jnp.exp(top_score - new_top)
        weights = jnp.exp(scores - new_top[:, None])
        weight_sum = weight_sum * fading + jnp.sum(weights, axis=1)
        summed = summed * fading[:, None] + jnp.dot(
            weights.astype(jnp.bfloat16), value_slot, preferred_element_type=jnp.float32
        )
        return (new_top, weight_sum, summed)

    start_state = (
        jnp.full((row_count,), -jnp.inf, jnp.float32),
        jnp.zeros((row_count,), jnp.float32),
        jnp.zeros((row_count, head_size), jnp.float32),
    )
    top_score, weight_sum, summed = lax.fori_loop(0, block_count, fold_block, start_state)
    return (summed / weight_sum[:, None], top_score + jnp.log(weight_sum))


def serve_slots(query_items, mask_items, key_recv, value_recv, key_valid, key_block):
    source_count, slot_count, item_count, head_size = query_items.shape
    all_tokens = key_recv.shape[0] * key_recv.shape[2]
    per_block = max(1, 512 // source_count)
    slot_outputs = []
    slot_logsum = []
    for slot_id in range(slot_count):
        key_slot = key_recv[:, slot_id].reshape(all_tokens, head_size)
        value_slot = value_recv[:, slot_id].reshape(all_tokens, head_size)
        taken_items = min(per_block, item_count)
        query_block = query_items[:, slot_id, 0:taken_items].reshape(
            source_count * taken_items, head_size
        )
        attended, logsum = attend_rows(query_block, key_slot, value_slot, key_valid, key_block)
        pieces_out = attended.reshape(source_count, taken_items, head_size)
        pieces_sum = logsum.reshape(source_count, taken_items)
        slot_outputs.append(pieces_out)
        slot_logsum.append(pieces_sum)
    attended = jnp.stack(slot_outputs, axis=1)
    logsum = jnp.stack(slot_logsum, axis=1)
    keep_rows = mask_items > 0
    attended = jnp.where(keep_rows[:, :, :, None], attended, 0.0).astype(jnp.bfloat16)
    logsum = jnp.where(keep_rows, logsum, 0.0)
    return (attended, logsum)


def per_device_exchange(queries, key_rows, value_rows, counts, head_of, out_weight):
    seq_count = lax.axis_size("seq")
    tok_dev = queries.shape[1]
    slot_count = head_of.shape[1]
    fewest = max(1, seq_count * slot_count // (2 * HEADS))
    row_cap = (tok_dev + fewest - 1) // fewest
    my_index = lax.axis_index("seq")
    flat_heads, group_size, group_rank = slot_layout(head_of)
    row_steps = jnp.arange(row_cap, dtype=jnp.int32)
    served_rows = group_rank[:, None] + group_size[:, None] * row_steps[None, :]
    my_count = counts[my_index]
    clipped = jnp.minimum(served_rows, tok_dev - 1)
    query_grid = queries[0].reshape(tok_dev, HEADS, HDIM)
    row_live = served_rows < my_count
    query_send = query_grid[clipped, flat_heads[:, None]]
    query_send = jnp.where(row_live[:, :, None], query_send, jnp.zeros((), jnp.bfloat16)).reshape(
        seq_count, slot_count, row_cap, HDIM
    )
    mask_send = row_live.astype(jnp.bfloat16).reshape(seq_count, slot_count, row_cap)
    token_ids = jnp.arange(tok_dev, dtype=jnp.int32)
    key_grid = key_rows[0].reshape(tok_dev, HEADS, HDIM)
    value_grid = value_rows[0].reshape(tok_dev, HEADS, HDIM)
    key_send = key_grid[token_ids[None, :], flat_heads[:, None]].reshape(
        seq_count, slot_count, tok_dev, HDIM
    )
    value_send = value_grid[token_ids[None, :], flat_heads[:, None]].reshape(
        seq_count, slot_count, tok_dev, HDIM
    )
    key_valid = (token_ids[None, :] < counts[:, None]).reshape(-1)
    key_block = tok_dev * key_grouping(seq_count, tok_dev)
    query_recv, mask_recv, key_recv, value_recv = (
        lax.all_to_all(query_send, "seq", split_axis=0, concat_axis=0, tiled=True),
        lax.all_to_all(mask_send, "seq", split_axis=0, concat_axis=0, tiled=True),
        lax.all_to_all(key_send, "seq", split_axis=0, concat_axis=0, tiled=True),
        lax.all_to_all(value_send, "seq", split_axis=0, concat_axis=0, tiled=True),
    )
    attended, logsum = serve_slots(
        query_recv, mask_recv, key_recv, value_recv, key_valid, key_block
    )
    returned = lax.all_to_all(attended, "seq", split_axis=0, concat_axis=0, tiled=True)
    head_ids = jnp.arange(HEADS, dtype=jnp.int32)
    head_group = jnp.sum((flat_heads[None, :] == head_ids[:, None]).astype(jnp.int32), axis=1)
    row_rank = token_ids[:, None] % head_group[None, :]
    row_step = token_ids[:, None] // head_group[None, :]
    slot_ids = jnp.arange(flat_heads.shape[0], dtype=jnp.int32)
    matched = (flat_heads[None, None, :] == head_ids[None, :, None]) & (
        group_rank[None, None, :] == row_rank[:, :, None]
    )
    owner_slot = jnp.sum(jnp.where(matched, slot_ids[None, None, :], 0), axis=2)
    flat_index = owner_slot * row_cap + row_step
    returned_rows = returned.reshape(-1, HDIM)
    attended_home = returned_rows[flat_index].reshape(tok_dev, HEADS * HDIM)
    partner = partner_2(attended_home, "branch", 0)
    on_positive = lax.axis_index("branch") == 0
    own_value = attended_home.astype(jnp.float32)
    partner_value = partner.astype(jnp.float32)
    positive = jnp.where(on_positive, own_value, partner_value)
    negative = jnp.where(on_positive, partner_value, own_value)
    guided = GUIDE_SCALE * positive - (GUIDE_SCALE - 1.0) * negative
    magnitude = jnp.mean(jnp.abs(guided), axis=1, keepdims=True)
    normed = (guided / (magnitude + EPSILON)).astype(jnp.bfloat16)
    projected = jnp.dot(normed, out_weight, preferred_element_type=jnp.float32).astype(jnp.bfloat16)
    saved_rows = jnp.transpose(logsum, (1, 2, 0)).reshape(1, 1, slot_count, row_cap, seq_count)
    return (projected, saved_rows)


KERNEL_PARAMS = pltpu.CompilerParams(vmem_limit_bytes=16 * 1024 * 1024)


SPLIT = 2
HOLD_COPIES = 4
TABLE_PIECES = 3
SPLITTER = 65537.0


def swap_shards(array, offset):
    pairs = [(i, i ^ offset) for i in range(lax.axis_size("seq"))]
    return lax.ppermute(array, "seq", pairs)


def place_offsets(shard_count):
    line = list(range(0, shard_count, SPLIT))
    return line + [offset + 1 for offset in line]


def pack_kernel(
    query_hbm,
    key_hbm,
    value_hbm,
    counts_hbm,
    head_hbm,
    own_ref,
    other_ref,
    limits_ref,
    pick_ref,
    slot_head_ref,
    counts_ref,
    head_ref,
    copy_sems,
):
    tok_dev = own_ref.shape[0] // 3
    half_width = own_ref.shape[1]
    slot_count, shard_count = head_ref.shape
    shard = lax.axis_index("seq")
    half = (shard // SPLIT) % 2
    copies = [
        pltpu.make_async_copy(counts_hbm, counts_ref, copy_sems.at[0]),
        pltpu.make_async_copy(head_hbm, head_ref, copy_sems.at[1]),
    ]
    for target, place in ((other_ref, 1 - half), (own_ref, half)):
        columns = pl.ds(pl.multiple_of(place * half_width, half_width), half_width)
        for part, source in enumerate((key_hbm, value_hbm, query_hbm)):
            rows = pl.ds(part * tok_dev, tok_dev)
            copies.append(
                pltpu.make_async_copy(
                    source.at[0, :, columns], target.at[rows, :], copy_sems.at[len(copies)]
                )
            )
    for copy in copies:
        copy.start()
    copies[0].wait()
    copies[1].wait()

    lane = lax.broadcasted_iota(jnp.int32, (1, limits_ref.shape[1]), 1)
    lane_limit = jnp.zeros(lane.shape, jnp.int32)
    for place, offset in enumerate(place_offsets(shard_count)):
        lane_limit = jnp.where(lane // tok_dev == place, counts_ref[shard ^ offset], lane_limit)
    limits_ref[0:1, :] = (lane % tok_dev < lane_limit).astype(jnp.int32)
    limits_ref[1:2, :] = jnp.full(lane.shape, counts_ref[shard], jnp.int32)
    limits_ref[2:3, :] = jnp.full(lane.shape, counts_ref[shard ^ SPLIT], jnp.int32)

    step = lax.broadcasted_iota(jnp.int32, (1, pick_ref.shape[2]), 1)
    for slot in range(slot_count):
        head = head_ref[slot, shard]
        group_size = jnp.int32(0)
        group_rank = jnp.int32(0)
        for other_shard in range(shard_count):
            for other_slot in range(slot_count):
                same = (head_ref[other_slot, other_shard] == head).astype(jnp.int32)
                before = other_shard * slot_count + other_slot < shard * slot_count + slot
                group_size = group_size + same
                group_rank = group_rank + same * before.astype(jnp.int32)
        served = group_rank + group_size * step
        for source in range(shard_count):
            pick_ref[slot, source : source + 1, :] = jnp.where(
                served < counts_ref[source], served + source * tok_dev, -1
            )
        slot_head_ref[slot] = jnp.full(slot_head_ref.shape[1:], head, jnp.int32)
    for copy in copies[2:]:
        copy.wait()


def hold_kernel(weight_hbm, after_ref, weight_ref, copy_sems):
    share = weight_ref.shape[0] // HOLD_COPIES
    copies = []
    for number in range(HOLD_COPIES):
        rows = pl.ds(number * share, share)
        copies.append(
            pltpu.make_async_copy(
                weight_hbm.at[rows, :], weight_ref.at[rows, :], copy_sems.at[number]
            )
        )
    for copy in copies:
        copy.start()
    for copy in copies:
        copy.wait()


def part_blocks(half_heads, tok_dev):
    return -(-half_heads * TABLE_PIECES // tok_dev)


def gathered(set_refs, part, columns):
    tok_dev = set_refs[0].shape[0] // 3
    rows = pl.ds(part * tok_dev, tok_dev)
    return jnp.concatenate([ref[rows, columns] for ref in set_refs], axis=0)


def head_scores(query_rows, key_all):
    return lax.dot_general(
        query_rows, key_all, (((1,), (1,)), ((), ())), preferred_element_type=jnp.float32
    )


def attend_kernel(set_count, limits_ref, *refs):
    set_refs = refs[:set_count]
    keep_ref, message_ref, table_ref, lines_ref = refs[set_count:]
    tok_dev, half_width = keep_ref.shape
    half_heads = half_width // HDIM
    shard = lax.axis_index("seq")
    head_columns = [pl.ds(head * HDIM, HDIM) for head in range(half_heads)]
    key_valid = limits_ref[0:1, :] > 0

    all_scores = [
        head_scores(gathered(set_refs, 2, columns), gathered(set_refs, 0, columns))
        for columns in head_columns
    ]
    lane = lax.broadcasted_iota(jnp.int32, all_scores[0].shape, 1)
    lines = jnp.zeros(lane.shape, jnp.float32)
    served = []
    for head, scores in enumerate(all_scores):
        scores = jnp.where(key_valid, scores * (1.0 / math.sqrt(HDIM)), -jnp.inf)
        top_score = jnp.max(scores, axis=1, keepdims=True)
        weights = jnp.exp(scores - top_score)
        weight_sum = jnp.sum(weights, axis=1, keepdims=True)
        lines = jnp.where(lane == head, top_score + jnp.log(weight_sum), lines)
        served.append((weights[: 2 * tok_dev].astype(jnp.bfloat16), weight_sum[: 2 * tok_dev]))
    row = lax.broadcasted_iota(jnp.int32, (tok_dev, HDIM), 0)
    for columns, (rounded, weight_sum) in zip(head_columns, served):
        mixed = jnp.dot(
            rounded, gathered(set_refs, 1, columns), preferred_element_type=jnp.float32
        )
        attended = mixed / weight_sum
        kept = jnp.where(row < limits_ref[1:2, :HDIM], attended[:tok_dev], 0.0)
        sent = jnp.where(row < limits_ref[2:3, :HDIM], attended[tok_dev:], 0.0)
        keep_ref[:, columns] = kept.astype(jnp.bfloat16)
        message_ref[:, columns] = sent.astype(jnp.bfloat16)

    for place, offset in enumerate(place_offsets(set_count)):
        rows = pl.ds(pl.multiple_of((shard ^ offset) * tok_dev, tok_dev), tok_dev)
        lines_ref[rows, :] = lines[place * tok_dev : (place + 1) * tok_dev]
    table = jnp.transpose(lines_ref[...])[: table_ref.shape[0]]
    table_ref[...] = table
    row = lax.broadcasted_iota(jnp.int32, (tok_dev, lines.shape[0]), 0)
    blocks = [jnp.zeros(row.shape, jnp.float32) for _ in range(part_blocks(half_heads, tok_dev))]
    for head in range(half_heads):
        rest = jnp.broadcast_to(table[head : head + 1], row.shape)
        for piece in range(TABLE_PIECES):
            scaled = rest * SPLITTER
            part = scaled - (scaled - rest)
            block, at_row = divmod(head * TABLE_PIECES + piece, tok_dev)
            blocks[block] = jnp.where(row == at_row, part, blocks[block])
            rest = rest - part
    message_ref[:, pl.ds(half_width, len(blocks) * lines.shape[0])] = jnp.concatenate(
        blocks, axis=1
    ).astype(jnp.bfloat16)


def guidance(own, partner):
    on_positive = lax.axis_index("branch") == 0
    own_scale = jnp.where(on_positive, GUIDE_SCALE, 1.0 - GUIDE_SCALE)
    partner_scale = jnp.where(on_positive, 1.0 - GUIDE_SCALE, GUIDE_SCALE)
    return own_scale * own.astype(jnp.float32) + partner_scale * partner.astype(jnp.float32)


def half_product(guided, weight_ref, place):
    half_width = guided.shape[1]
    rows = pl.ds(pl.multiple_of(place * half_width, half_width), half_width)
    return jnp.dot(
        guided.astype(jnp.bfloat16), weight_ref[rows, :], preferred_element_type=jnp.float32
    )


def keep_kernel(keep_ref, partner_keep_ref, weight_ref, total_ref, size_ref):
    half = (lax.axis_index("seq") // SPLIT) % 2
    guided = guidance(keep_ref[...], partner_keep_ref[...])
    size = jnp.sum(jnp.abs(guided), axis=1, keepdims=True)
    size_ref[...] = jnp.broadcast_to(size, size_ref.shape)
    total_ref[...] = half_product(guided, weight_ref, half)


def project_kernel(
    total_ref,
    size_ref,
    partner_back_ref,
    message_ref,
    weight_ref,
    table_ref,
    pick_ref,
    slot_head_ref,
    projected_ref,
    saved_ref,
):
    tok_dev = message_ref.shape[0]
    half_width = weight_ref.shape[0] // 2
    half_heads = half_width // HDIM
    tokens = table_ref.shape[1]
    half = (lax.axis_index("seq") // SPLIT) % 2
    rows = pl.ds(0, half_width)
    guided = guidance(message_ref[:, rows], partner_back_ref[:, rows])
    size = size_ref[:, 0:1] + jnp.sum(jnp.abs(guided), axis=1, keepdims=True)
    magnitude = size / (2 * half_width)
    total = total_ref[...] + half_product(guided, weight_ref, 1 - half)
    projected_ref[...] = (total / (magnitude + EPSILON)).astype(jnp.bfloat16)

    parts = message_ref[:, pl.ds(half_width, message_ref.shape[1] - half_width)].astype(jnp.float32)
    others = []
    for head in range(half_heads):
        other = jnp.zeros((1, tokens), jnp.float32)
        for piece in range(TABLE_PIECES):
            block, at_row = divmod(head * TABLE_PIECES + piece, tok_dev)
            other = other + parts[at_row : at_row + 1, block * tokens : (block + 1) * tokens]
        others.append(other)
    for slot in range(saved_ref.shape[0]):
        slot_head = slot_head_ref[slot, 0:1, :]
        line = jnp.zeros((1, tokens), jnp.float32)
        for head in range(half_heads):
            line = jnp.where(slot_head == half * half_heads + head, table_ref[head : head + 1], line)
            line = jnp.where(slot_head == (1 - half) * half_heads + head, others[head], line)
        pick = pick_ref[slot]
        spread = jnp.broadcast_to(line, pick.shape)
        taken = jnp.take_along_axis(spread, jnp.maximum(pick, 0), axis=1)
        saved_ref[slot] = jnp.where(pick >= 0, taken, 0.0)[:, : saved_ref.shape[2]]


def per_device_halves(queries, key_rows, value_rows, counts, head_of, out_weight):
    seq_count = lax.axis_size("seq")
    tok_dev, width = queries.shape[1:]
    half_width = width // 2
    tokens = seq_count * tok_dev
    slot_count = head_of.shape[1]
    fewest = max(1, seq_count * slot_count // (2 * HEADS))
    row_cap = (tok_dev + fewest - 1) // fewest
    message_width = half_width + part_blocks(half_width // HDIM, tok_dev) * tokens
    any_spec = pl.BlockSpec(memory_space=pl.ANY)
    vmem = pl.BlockSpec(memory_space=pltpu.VMEM)

    def held(*arrays):
        return [pltpu.with_memory_space_constraint(array, pltpu.VMEM) for array in arrays]

    def distant(*arrays):
        return [pltpu.with_memory_space_constraint(array, pltpu.HBM) for array in arrays]

    own, other, limits, pick, slot_head = pl.pallas_call(
        pack_kernel,
        out_shape=[
            pltpu.VMEM((3 * tok_dev, half_width), jnp.bfloat16),
            pltpu.VMEM((3 * tok_dev, half_width), jnp.bfloat16),
            pltpu.VMEM((8, tokens), jnp.int32),
            pltpu.VMEM((slot_count, seq_count, tokens), jnp.int32),
            pltpu.VMEM((slot_count, 8, tokens), jnp.int32),
        ],
        in_specs=[any_spec] * 5,
        out_specs=[vmem] * 5,
        scratch_shapes=[
            pltpu.SMEM((seq_count,), jnp.int32),
            pltpu.SMEM((slot_count, seq_count), jnp.int32),
            pltpu.SemaphoreType.DMA((8,)),
        ],
        compiler_params=KERNEL_PARAMS,
        name="pack",
    )(*distant(queries, key_rows, value_rows, counts, jnp.transpose(head_of)))

    weight_held = pl.pallas_call(
        hold_kernel,
        out_shape=pltpu.VMEM(out_weight.shape, jnp.bfloat16),
        in_specs=[any_spec, vmem],
        out_specs=vmem,
        scratch_shapes=[pltpu.SemaphoreType.DMA((HOLD_COPIES,))],
        compiler_params=KERNEL_PARAMS,
        cost_estimate=pl.CostEstimate(
            flops=0, bytes_accessed=4 * out_weight.size, transcendentals=0
        ),
        name="hold",
    )(*distant(out_weight), *held(limits))
    line = [own] + [
        swap_shards(other if offset & SPLIT else own, offset)
        for offset in range(SPLIT, seq_count, SPLIT)
    ]
    sets = line + [swap_shards(array, 1) for array in line]
    limits, weight_held = lax.optimization_barrier((limits, weight_held))
    keep, message, table = pl.pallas_call(
        functools.partial(attend_kernel, len(sets)),
        out_shape=[
            pltpu.VMEM((tok_dev, half_width), jnp.bfloat16),
            pltpu.VMEM((tok_dev, message_width), jnp.bfloat16),
            pltpu.VMEM((half_width // HDIM + 7 & -8, tokens), jnp.float32),
        ],
        in_specs=[vmem] * (1 + len(sets)),
        out_specs=[vmem] * 3,
        scratch_shapes=[pltpu.VMEM((tokens, HDIM), jnp.float32)],
        compiler_params=KERNEL_PARAMS,
        name="attend",
    )(*held(limits, *sets))
    across = [(2 * i + b, 2 * (i ^ SPLIT) + 1 - b) for i in range(seq_count) for b in range(2)]
    partner_back = lax.ppermute(message, ("seq", "branch"), across)
    partner_keep = partner_2(keep, "branch", 0)
    back = swap_shards(message, SPLIT)
    total, size = pl.pallas_call(
        keep_kernel,
        out_shape=[
            pltpu.VMEM((tok_dev, out_weight.shape[1]), jnp.float32),
            pltpu.VMEM((tok_dev, HDIM), jnp.float32),
        ],
        in_specs=[vmem] * 3,
        out_specs=[vmem] * 2,
        compiler_params=KERNEL_PARAMS,
        name="keep",
    )(*held(keep, partner_keep, weight_held))
    projected, saved = pl.pallas_call(
        project_kernel,
        out_shape=[
            jax.ShapeDtypeStruct((tok_dev, out_weight.shape[1]), jnp.bfloat16),
            jax.ShapeDtypeStruct((slot_count, seq_count, row_cap), jnp.float32),
        ],
        in_specs=[vmem] * 8,
        out_specs=[vmem] * 2,
        compiler_params=KERNEL_PARAMS,
        name="project",
    )(*held(total, size, partner_back, back, weight_held, table, pick, slot_head))
    saved = jnp.transpose(saved, (0, 2, 1))
    return (projected, saved.reshape(1, 1, slot_count, row_cap, seq_count))


def solution(mesh):
    seq_count = mesh.shape["seq"]
    hypercube = seq_count > SPLIT and seq_count & (seq_count - 1) == 0
    small = hypercube and seq_count <= HEADS
    return jax.shard_map(
        per_device_halves if small else per_device_exchange,
        mesh=mesh,
        in_specs=(
            P("branch", ("groups", "seq"), None),
            P("branch", ("groups", "seq"), None),
            P("branch", ("groups", "seq"), None),
            P("groups"),
            P(),
            P(None, "branch"),
        ),
        out_specs=(
            P(("groups", "seq"), "branch"),
            P("branch", ("groups", "seq"), None, None, None),
        ),
        check_vma=False,
    )
```

```python
import functools
import math

import jax
import jax.numpy as jnp
from jax import lax
from jax.experimental import pallas as pl
from jax.experimental.pallas import tpu as pltpu
from jax.sharding import PartitionSpec as P

HEADS = 12
HDIM = 128


GUIDE_SCALE = 3.0
EPSILON = 1e-06


def partner_2(array, axis, stride):
    return lax.ppermute(array, axis, [(i, i ^ 1 << stride) for i in range(lax.axis_size(axis))])


def slot_layout(head_of):
    flat_heads = head_of.reshape(-1)
    slot_order = jnp.arange(flat_heads.shape[0], dtype=jnp.int32)
    same_head = flat_heads[:, None] == flat_heads[None, :]
    group_size = jnp.sum(same_head.astype(jnp.int32), axis=1)
    earlier = same_head & (slot_order[None, :] < slot_order[:, None])
    group_rank = jnp.sum(earlier.astype(jnp.int32), axis=1)
    return (flat_heads, group_size, group_rank)


def key_grouping(seq_count, tok_dev):
    shard_limit = max(1, 2048 // tok_dev)
    grouping = 1
    for attempt in range(16):
        if grouping * 2 <= shard_limit and seq_count % (grouping * 2) == 0:
            grouping = grouping * 2
    return grouping


def attend_rows(query_block, key_slot, value_slot, key_valid, key_block):
    row_count = query_block.shape[0]
    head_size = query_block.shape[1]
    block_count = key_slot.shape[0] // key_block
    scale_factor = 1.0 / math.sqrt(head_size)

    def fold_block(block_id, state_in):
        top_score, weight_sum, summed = state_in
        scores = (
            jnp.einsum("qd,kd->qk", query_block, key_slot, preferred_element_type=jnp.float32)
            * scale_factor
        )
        scores = jnp.where(key_valid[None, :], scores, -jnp.inf)
        new_top = jnp.maximum(top_score, jnp.max(scores, axis=1))
        fading = jnp.exp(top_score - new_top)
        weights = jnp.exp(scores - new_top[:, None])
        weight_sum = weight_sum * fading + jnp.sum(weights, axis=1)
        summed = summed * fading[:, None] + jnp.dot(
            weights.astype(jnp.bfloat16), value_slot, preferred_element_type=jnp.float32
        )
        return (new_top, weight_sum, summed)

    start_state = (
        jnp.full((row_count,), -jnp.inf, jnp.float32),
        jnp.zeros((row_count,), jnp.float32),
        jnp.zeros((row_count, head_size), jnp.float32),
    )
    top_score, weight_sum, summed = lax.fori_loop(0, block_count, fold_block, start_state)
    return (summed / weight_sum[:, None], top_score + jnp.log(weight_sum))


def serve_slots(query_items, mask_items, key_recv, value_recv, key_valid, key_block):
    source_count, slot_count, item_count, head_size = query_items.shape
    all_tokens = key_recv.shape[0] * key_recv.shape[2]
    per_block = max(1, 512 // source_count)
    slot_outputs = []
    slot_logsum = []
    for slot_id in range(slot_count):
        key_slot = key_recv[:, slot_id].reshape(all_tokens, head_size)
        value_slot = value_recv[:, slot_id].reshape(all_tokens, head_size)
        taken_items = min(per_block, item_count)
        query_block = query_items[:, slot_id, 0:taken_items].reshape(
            source_count * taken_items, head_size
        )
        attended, logsum = attend_rows(query_block, key_slot, value_slot, key_valid, key_block)
        pieces_out = attended.reshape(source_count, taken_items, head_size)
        pieces_sum = logsum.reshape(source_count, taken_items)
        slot_outputs.append(pieces_out)
        slot_logsum.append(pieces_sum)
    attended = jnp.stack(slot_outputs, axis=1)
    logsum = jnp.stack(slot_logsum, axis=1)
    keep_rows = mask_items > 0
    attended = jnp.where(keep_rows[:, :, :, None], attended, 0.0).astype(jnp.bfloat16)
    logsum = jnp.where(keep_rows, logsum, 0.0)
    return (attended, logsum)


def per_device_exchange(queries, key_rows, value_rows, counts, head_of, out_weight):
    seq_count = lax.axis_size("seq")
    tok_dev = queries.shape[1]
    slot_count = head_of.shape[1]
    fewest = max(1, seq_count * slot_count // (2 * HEADS))
    row_cap = (tok_dev + fewest - 1) // fewest
    my_index = lax.axis_index("seq")
    flat_heads, group_size, group_rank = slot_layout(head_of)
    row_steps = jnp.arange(row_cap, dtype=jnp.int32)
    served_rows = group_rank[:, None] + group_size[:, None] * row_steps[None, :]
    my_count = counts[my_index]
    clipped = jnp.minimum(served_rows, tok_dev - 1)
    query_grid = queries[0].reshape(tok_dev, HEADS, HDIM)
    row_live = served_rows < my_count
    query_send = query_grid[clipped, flat_heads[:, None]]
    query_send = jnp.where(row_live[:, :, None], query_send, jnp.zeros((), jnp.bfloat16)).reshape(
        seq_count, slot_count, row_cap, HDIM
    )
    mask_send = row_live.astype(jnp.bfloat16).reshape(seq_count, slot_count, row_cap)
    token_ids = jnp.arange(tok_dev, dtype=jnp.int32)
    key_grid = key_rows[0].reshape(tok_dev, HEADS, HDIM)
    value_grid = value_rows[0].reshape(tok_dev, HEADS, HDIM)
    key_send = key_grid[token_ids[None, :], flat_heads[:, None]].reshape(
        seq_count, slot_count, tok_dev, HDIM
    )
    value_send = value_grid[token_ids[None, :], flat_heads[:, None]].reshape(
        seq_count, slot_count, tok_dev, HDIM
    )
    key_valid = (token_ids[None, :] < counts[:, None]).reshape(-1)
    key_block = tok_dev * key_grouping(seq_count, tok_dev)
    query_recv, mask_recv, key_recv, value_recv = (
        lax.all_to_all(query_send, "seq", split_axis=0, concat_axis=0, tiled=True),
        lax.all_to_all(mask_send, "seq", split_axis=0, concat_axis=0, tiled=True),
        lax.all_to_all(key_send, "seq", split_axis=0, concat_axis=0, tiled=True),
        lax.all_to_all(value_send, "seq", split_axis=0, concat_axis=0, tiled=True),
    )
    attended, logsum = serve_slots(
        query_recv, mask_recv, key_recv, value_recv, key_valid, key_block
    )
    returned = lax.all_to_all(attended, "seq", split_axis=0, concat_axis=0, tiled=True)
    head_ids = jnp.arange(HEADS, dtype=jnp.int32)
    head_group = jnp.sum((flat_heads[None, :] == head_ids[:, None]).astype(jnp.int32), axis=1)
    row_rank = token_ids[:, None] % head_group[None, :]
    row_step = token_ids[:, None] // head_group[None, :]
    slot_ids = jnp.arange(flat_heads.shape[0], dtype=jnp.int32)
    matched = (flat_heads[None, None, :] == head_ids[None, :, None]) & (
        group_rank[None, None, :] == row_rank[:, :, None]
    )
    owner_slot = jnp.sum(jnp.where(matched, slot_ids[None, None, :], 0), axis=2)
    flat_index = owner_slot * row_cap + row_step
    returned_rows = returned.reshape(-1, HDIM)
    attended_home = returned_rows[flat_index].reshape(tok_dev, HEADS * HDIM)
    partner = partner_2(attended_home, "branch", 0)
    on_positive = lax.axis_index("branch") == 0
    own_value = attended_home.astype(jnp.float32)
    partner_value = partner.astype(jnp.float32)
    positive = jnp.where(on_positive, own_value, partner_value)
    negative = jnp.where(on_positive, partner_value, own_value)
    guided = GUIDE_SCALE * positive - (GUIDE_SCALE - 1.0) * negative
    magnitude = jnp.mean(jnp.abs(guided), axis=1, keepdims=True)
    normed = (guided / (magnitude + EPSILON)).astype(jnp.bfloat16)
    projected = jnp.dot(normed, out_weight, preferred_element_type=jnp.float32).astype(jnp.bfloat16)
    saved_rows = jnp.transpose(logsum, (1, 2, 0)).reshape(1, 1, slot_count, row_cap, seq_count)
    return (projected, saved_rows)


KERNEL_PARAMS = pltpu.CompilerParams(vmem_limit_bytes=16 * 1024 * 1024)


SPLIT = 2
HOLD_COPIES = 4
TABLE_PIECES = 3
SPLITTER = 65537.0


def swap_shards(array, offset):
    pairs = [(i, i ^ offset) for i in range(lax.axis_size("seq"))]
    return lax.ppermute(array, "seq", pairs)


def place_offsets(shard_count):
    line = list(range(0, shard_count, SPLIT))
    return line + [offset + 1 for offset in line]


def pack_kernel(
    query_hbm,
    key_hbm,
    value_hbm,
    counts_hbm,
    head_hbm,
    own_ref,
    other_ref,
    limits_ref,
    pick_ref,
    slot_head_ref,
    counts_ref,
    head_ref,
    copy_sems,
):
    tok_dev = own_ref.shape[0] // 3
    half_width = own_ref.shape[1]
    slot_count, shard_count = head_ref.shape
    shard = lax.axis_index("seq")
    half = (shard // SPLIT) % 2
    copies = [
        pltpu.make_async_copy(counts_hbm, counts_ref, copy_sems.at[0]),
        pltpu.make_async_copy(head_hbm, head_ref, copy_sems.at[1]),
    ]
    for target, place in ((other_ref, 1 - half), (own_ref, half)):
        columns = pl.ds(pl.multiple_of(place * half_width, half_width), half_width)
        for part, source in enumerate((key_hbm, value_hbm, query_hbm)):
            rows = pl.ds(part * tok_dev, tok_dev)
            copies.append(
                pltpu.make_async_copy(
                    source.at[0, :, columns], target.at[rows, :], copy_sems.at[len(copies)]
                )
            )
    for copy in copies:
        copy.start()
    copies[0].wait()
    copies[1].wait()

    lane = lax.broadcasted_iota(jnp.int32, (1, limits_ref.shape[1]), 1)
    lane_limit = jnp.zeros(lane.shape, jnp.int32)
    for place, offset in enumerate(place_offsets(shard_count)):
        lane_limit = jnp.where(lane // tok_dev == place, counts_ref[shard ^ offset], lane_limit)
    limits_ref[0:1, :] = (lane % tok_dev < lane_limit).astype(jnp.int32)
    limits_ref[1:2, :] = jnp.full(lane.shape, counts_ref[shard], jnp.int32)
    limits_ref[2:3, :] = jnp.full(lane.shape, counts_ref[shard ^ SPLIT], jnp.int32)

    step = lax.broadcasted_iota(jnp.int32, (1, pick_ref.shape[2]), 1)
    for slot in range(slot_count):
        head = head_ref[slot, shard]
        group_size = jnp.int32(0)
        group_rank = jnp.int32(0)
        for other_shard in range(shard_count):
            for other_slot in range(slot_count):
                same = (head_ref[other_slot, other_shard] == head).astype(jnp.int32)
                before = other_shard * slot_count + other_slot < shard * slot_count + slot
                group_size = group_size + same
                group_rank = group_rank + same * before.astype(jnp.int32)
        served = group_rank + group_size * step
        for source in range(shard_count):
            pick_ref[slot, source : source + 1, :] = jnp.where(
                served < counts_ref[source], served + source * tok_dev, -1
            )
        slot_head_ref[slot] = jnp.full(slot_head_ref.shape[1:], head, jnp.int32)
    for copy in copies[2:]:
        copy.wait()


def hold_kernel(weight_hbm, after_ref, weight_ref, copy_sems):
    share = weight_ref.shape[0] // HOLD_COPIES
    copies = []
    for number in range(HOLD_COPIES):
        rows = pl.ds(number * share, share)
        copies.append(
            pltpu.make_async_copy(
                weight_hbm.at[rows, :], weight_ref.at[rows, :], copy_sems.at[number]
            )
        )
    for copy in copies:
        copy.start()
    for copy in copies:
        copy.wait()


def part_blocks(half_heads, tok_dev):
    return -(-half_heads * TABLE_PIECES // tok_dev)


def gathered(set_refs, part, columns):
    tok_dev = set_refs[0].shape[0] // 3
    rows = pl.ds(part * tok_dev, tok_dev)
    return jnp.concatenate([ref[rows, columns] for ref in set_refs], axis=0)


def head_scores(query_rows, key_all):
    return lax.dot_general(
        query_rows, key_all, (((1,), (1,)), ((), ())), preferred_element_type=jnp.float32
    )


def attend_kernel(set_count, limits_ref, *refs):
    set_refs = refs[:set_count]
    keep_ref, message_ref, table_ref, lines_ref = refs[set_count:]
    tok_dev, half_width = keep_ref.shape
    half_heads = half_width // HDIM
    shard = lax.axis_index("seq")
    head_columns = [pl.ds(head * HDIM, HDIM) for head in range(half_heads)]
    key_valid = limits_ref[0:1, :] > 0

    all_scores = [
        head_scores(gathered(set_refs, 2, columns), gathered(set_refs, 0, columns))
        for columns in head_columns
    ]
    lane = lax.broadcasted_iota(jnp.int32, all_scores[0].shape, 1)
    lines = jnp.zeros(lane.shape, jnp.float32)
    served = []
    for head, scores in enumerate(all_scores):
        scores = jnp.where(key_valid, scores * (1.0 / math.sqrt(HDIM)), -jnp.inf)
        top_score = jnp.max(scores, axis=1, keepdims=True)
        weights = jnp.exp(scores - top_score)
        weight_sum = jnp.sum(weights, axis=1, keepdims=True)
        lines = jnp.where(lane == head, top_score + jnp.log(weight_sum), lines)
        served.append((weights[: 2 * tok_dev].astype(jnp.bfloat16), weight_sum[: 2 * tok_dev]))
    row = lax.broadcasted_iota(jnp.int32, (tok_dev, HDIM), 0)
    for columns, (rounded, weight_sum) in zip(head_columns, served):
        mixed = jnp.dot(
            rounded, gathered(set_refs, 1, columns), preferred_element_type=jnp.float32
        )
        attended = mixed / weight_sum
        kept = jnp.where(row < limits_ref[1:2, :HDIM], attended[:tok_dev], 0.0)
        sent = jnp.where(row < limits_ref[2:3, :HDIM], attended[tok_dev:], 0.0)
        keep_ref[:, columns] = kept.astype(jnp.bfloat16)
        message_ref[:, columns] = sent.astype(jnp.bfloat16)

    for place, offset in enumerate(place_offsets(set_count)):
        rows = pl.ds(pl.multiple_of((shard ^ offset) * tok_dev, tok_dev), tok_dev)
        lines_ref[rows, :] = lines[place * tok_dev : (place + 1) * tok_dev]
    table = jnp.transpose(lines_ref[...])[: table_ref.shape[0]]
    table_ref[...] = table
    row = lax.broadcasted_iota(jnp.int32, (tok_dev, lines.shape[0]), 0)
    blocks = [jnp.zeros(row.shape, jnp.float32) for _ in range(part_blocks(half_heads, tok_dev))]
    for head in range(half_heads):
        rest = jnp.broadcast_to(table[head : head + 1], row.shape)
        for piece in range(TABLE_PIECES):
            scaled = rest * SPLITTER
            part = scaled - (scaled - rest)
            block, at_row = divmod(head * TABLE_PIECES + piece, tok_dev)
            blocks[block] = jnp.where(row == at_row, part, blocks[block])
            rest = rest - part
    message_ref[:, pl.ds(half_width, len(blocks) * lines.shape[0])] = jnp.concatenate(
        blocks, axis=1
    ).astype(jnp.bfloat16)


def guidance(own, partner):
    on_positive = lax.axis_index("branch") == 0
    own_scale = jnp.where(on_positive, GUIDE_SCALE, 1.0 - GUIDE_SCALE)
    partner_scale = jnp.where(on_positive, 1.0 - GUIDE_SCALE, GUIDE_SCALE)
    return own_scale * own.astype(jnp.float32) + partner_scale * partner.astype(jnp.float32)


def half_product(guided, weight_ref, place):
    half_width = guided.shape[1]
    rows = pl.ds(pl.multiple_of(place * half_width, half_width), half_width)
    return jnp.dot(
        guided.astype(jnp.bfloat16), weight_ref[rows, :], preferred_element_type=jnp.float32
    )


def keep_kernel(keep_ref, partner_keep_ref, weight_ref, total_ref, size_ref):
    half = (lax.axis_index("seq") // SPLIT) % 2
    guided = guidance(keep_ref[...], partner_keep_ref[...])
    size = jnp.sum(jnp.abs(guided), axis=1, keepdims=True)
    size_ref[...] = jnp.broadcast_to(size, size_ref.shape)
    total_ref[...] = half_product(guided, weight_ref, half)


def project_kernel(
    total_ref,
    size_ref,
    message_ref,
    partner_back_ref,
    weight_ref,
    table_ref,
    pick_ref,
    slot_head_ref,
    projected_ref,
    saved_ref,
):
    tok_dev = message_ref.shape[0]
    half_width = weight_ref.shape[0] // 2
    half_heads = half_width // HDIM
    tokens = table_ref.shape[1]
    half = (lax.axis_index("seq") // SPLIT) % 2
    rows = pl.ds(0, half_width)
    guided = guidance(message_ref[:, rows], partner_back_ref[:, rows])
    size = size_ref[:, 0:1] + jnp.sum(jnp.abs(guided), axis=1, keepdims=True)
    magnitude = size / (2 * half_width)
    total = total_ref[...] + half_product(guided, weight_ref, 1 - half)
    projected_ref[...] = (total / (magnitude + EPSILON)).astype(jnp.bfloat16)

    parts = message_ref[:, pl.ds(half_width, message_ref.shape[1] - half_width)].astype(jnp.float32)
    others = []
    for head in range(half_heads):
        other = jnp.zeros((1, tokens), jnp.float32)
        for piece in range(TABLE_PIECES):
            block, at_row = divmod(head * TABLE_PIECES + piece, tok_dev)
            other = other + parts[at_row : at_row + 1, block * tokens : (block + 1) * tokens]
        others.append(other)
    for slot in range(saved_ref.shape[0]):
        slot_head = slot_head_ref[slot, 0:1, :]
        line = jnp.zeros((1, tokens), jnp.float32)
        for head in range(half_heads):
            line = jnp.where(slot_head == half * half_heads + head, table_ref[head : head + 1], line)
            line = jnp.where(slot_head == (1 - half) * half_heads + head, others[head], line)
        pick = pick_ref[slot]
        spread = jnp.broadcast_to(line, pick.shape)
        taken = jnp.take_along_axis(spread, jnp.maximum(pick, 0), axis=1)
        saved_ref[slot] = jnp.where(pick >= 0, taken, 0.0)[:, : saved_ref.shape[2]]


def per_device_halves(queries, key_rows, value_rows, counts, head_of, out_weight):
    seq_count = lax.axis_size("seq")
    tok_dev, width = queries.shape[1:]
    half_width = width // 2
    tokens = seq_count * tok_dev
    slot_count = head_of.shape[1]
    fewest = max(1, seq_count * slot_count // (2 * HEADS))
    row_cap = (tok_dev + fewest - 1) // fewest
    message_width = half_width + part_blocks(half_width // HDIM, tok_dev) * tokens
    any_spec = pl.BlockSpec(memory_space=pl.ANY)
    vmem = pl.BlockSpec(memory_space=pltpu.VMEM)

    def held(*arrays):
        return [pltpu.with_memory_space_constraint(array, pltpu.VMEM) for array in arrays]

    def distant(*arrays):
        return [pltpu.with_memory_space_constraint(array, pltpu.HBM) for array in arrays]

    own, other, limits, pick, slot_head = pl.pallas_call(
        pack_kernel,
        out_shape=[
            pltpu.VMEM((3 * tok_dev, half_width), jnp.bfloat16),
            pltpu.VMEM((3 * tok_dev, half_width), jnp.bfloat16),
            pltpu.VMEM((8, tokens), jnp.int32),
            pltpu.VMEM((slot_count, seq_count, tokens), jnp.int32),
            pltpu.VMEM((slot_count, 8, tokens), jnp.int32),
        ],
        in_specs=[any_spec] * 5,
        out_specs=[vmem] * 5,
        scratch_shapes=[
            pltpu.SMEM((seq_count,), jnp.int32),
            pltpu.SMEM((slot_count, seq_count), jnp.int32),
            pltpu.SemaphoreType.DMA((8,)),
        ],
        compiler_params=KERNEL_PARAMS,
        name="pack",
    )(*distant(queries, key_rows, value_rows, counts, jnp.transpose(head_of)))

    weight_held = pl.pallas_call(
        hold_kernel,
        out_shape=pltpu.VMEM(out_weight.shape, jnp.bfloat16),
        in_specs=[any_spec, vmem],
        out_specs=vmem,
        scratch_shapes=[pltpu.SemaphoreType.DMA((HOLD_COPIES,))],
        compiler_params=KERNEL_PARAMS,
        cost_estimate=pl.CostEstimate(
            flops=0, bytes_accessed=4 * out_weight.size, transcendentals=0
        ),
        name="hold",
    )(*distant(out_weight), *held(limits))
    line = [own] + [
        swap_shards(other if offset & SPLIT else own, offset)
        for offset in range(SPLIT, seq_count, SPLIT)
    ]
    sets = line + [swap_shards(array, 1) for array in line]
    limits, weight_held = lax.optimization_barrier((limits, weight_held))
    keep, message, table = pl.pallas_call(
        functools.partial(attend_kernel, len(sets)),
        out_shape=[
            pltpu.VMEM((tok_dev, half_width), jnp.bfloat16),
            pltpu.VMEM((tok_dev, message_width), jnp.bfloat16),
            pltpu.VMEM((half_width // HDIM + 7 & -8, tokens), jnp.float32),
        ],
        in_specs=[vmem] * (1 + len(sets)),
        out_specs=[vmem] * 3,
        scratch_shapes=[pltpu.VMEM((tokens, HDIM), jnp.float32)],
        compiler_params=KERNEL_PARAMS,
        name="attend",
    )(*held(limits, *sets))
    partner_keep = partner_2(keep, "branch", 0)
    back = swap_shards(message, SPLIT)
    partner_back = partner_2(back, "branch", 0)
    total, size = pl.pallas_call(
        keep_kernel,
        out_shape=[
            pltpu.VMEM((tok_dev, out_weight.shape[1]), jnp.float32),
            pltpu.VMEM((tok_dev, HDIM), jnp.float32),
        ],
        in_specs=[vmem] * 3,
        out_specs=[vmem] * 2,
        compiler_params=KERNEL_PARAMS,
        name="keep",
    )(*held(keep, partner_keep, weight_held))
    projected, saved = pl.pallas_call(
        project_kernel,
        out_shape=[
            jax.ShapeDtypeStruct((tok_dev, out_weight.shape[1]), jnp.bfloat16),
            jax.ShapeDtypeStruct((slot_count, seq_count, row_cap), jnp.float32),
        ],
        in_specs=[vmem] * 8,
        out_specs=[vmem] * 2,
        compiler_params=KERNEL_PARAMS,
        name="project",
    )(*held(total, size, back, partner_back, weight_held, table, pick, slot_head))
    saved = jnp.transpose(saved, (0, 2, 1))
    return (projected, saved.reshape(1, 1, slot_count, row_cap, seq_count))


def solution(mesh):
    seq_count = mesh.shape["seq"]
    hypercube = seq_count > SPLIT and seq_count & (seq_count - 1) == 0
    small = hypercube and seq_count <= HEADS
    return jax.shard_map(
        per_device_halves if small else per_device_exchange,
        mesh=mesh,
        in_specs=(
            P("branch", ("groups", "seq"), None),
            P("branch", ("groups", "seq"), None),
            P("branch", ("groups", "seq"), None),
            P("groups"),
            P(),
            P(None, "branch"),
        ),
        out_specs=(
            P(("groups", "seq"), "branch"),
            P("branch", ("groups", "seq"), None, None, None),
        ),
        check_vma=False,
    )
```

```python
import functools
import math

import jax
import jax.numpy as jnp
from jax import lax
from jax.experimental import pallas as pl
from jax.experimental.pallas import tpu as pltpu
from jax.sharding import PartitionSpec as P

HEADS = 12
HDIM = 128


GUIDE_SCALE = 3.0
EPSILON = 1e-06


def partner_2(array, axis, stride):
    return lax.ppermute(array, axis, [(i, i ^ 1 << stride) for i in range(lax.axis_size(axis))])


def slot_layout(head_of):
    flat_heads = head_of.reshape(-1)
    slot_order = jnp.arange(flat_heads.shape[0], dtype=jnp.int32)
    same_head = flat_heads[:, None] == flat_heads[None, :]
    group_size = jnp.sum(same_head.astype(jnp.int32), axis=1)
    earlier = same_head & (slot_order[None, :] < slot_order[:, None])
    group_rank = jnp.sum(earlier.astype(jnp.int32), axis=1)
    return (flat_heads, group_size, group_rank)


def key_grouping(seq_count, tok_dev):
    shard_limit = max(1, 2048 // tok_dev)
    grouping = 1
    for attempt in range(16):
        if grouping * 2 <= shard_limit and seq_count % (grouping * 2) == 0:
            grouping = grouping * 2
    return grouping


def attend_rows(query_block, key_slot, value_slot, key_valid, key_block):
    row_count = query_block.shape[0]
    head_size = query_block.shape[1]
    block_count = key_slot.shape[0] // key_block
    scale_factor = 1.0 / math.sqrt(head_size)

    def fold_block(block_id, state_in):
        top_score, weight_sum, summed = state_in
        scores = (
            jnp.einsum("qd,kd->qk", query_block, key_slot, preferred_element_type=jnp.float32)
            * scale_factor
        )
        scores = jnp.where(key_valid[None, :], scores, -jnp.inf)
        new_top = jnp.maximum(top_score, jnp.max(scores, axis=1))
        fading = jnp.exp(top_score - new_top)
        weights = jnp.exp(scores - new_top[:, None])
        weight_sum = weight_sum * fading + jnp.sum(weights, axis=1)
        summed = summed * fading[:, None] + jnp.dot(
            weights.astype(jnp.bfloat16), value_slot, preferred_element_type=jnp.float32
        )
        return (new_top, weight_sum, summed)

    start_state = (
        jnp.full((row_count,), -jnp.inf, jnp.float32),
        jnp.zeros((row_count,), jnp.float32),
        jnp.zeros((row_count, head_size), jnp.float32),
    )
    top_score, weight_sum, summed = lax.fori_loop(0, block_count, fold_block, start_state)
    return (summed / weight_sum[:, None], top_score + jnp.log(weight_sum))


def serve_slots(query_items, mask_items, key_recv, value_recv, key_valid, key_block):
    source_count, slot_count, item_count, head_size = query_items.shape
    all_tokens = key_recv.shape[0] * key_recv.shape[2]
    per_block = max(1, 512 // source_count)
    slot_outputs = []
    slot_logsum = []
    for slot_id in range(slot_count):
        key_slot = key_recv[:, slot_id].reshape(all_tokens, head_size)
        value_slot = value_recv[:, slot_id].reshape(all_tokens, head_size)
        taken_items = min(per_block, item_count)
        query_block = query_items[:, slot_id, 0:taken_items].reshape(
            source_count * taken_items, head_size
        )
        attended, logsum = attend_rows(query_block, key_slot, value_slot, key_valid, key_block)
        pieces_out = attended.reshape(source_count, taken_items, head_size)
        pieces_sum = logsum.reshape(source_count, taken_items)
        slot_outputs.append(pieces_out)
        slot_logsum.append(pieces_sum)
    attended = jnp.stack(slot_outputs, axis=1)
    logsum = jnp.stack(slot_logsum, axis=1)
    keep_rows = mask_items > 0
    attended = jnp.where(keep_rows[:, :, :, None], attended, 0.0).astype(jnp.bfloat16)
    logsum = jnp.where(keep_rows, logsum, 0.0)
    return (attended, logsum)


def per_device_exchange(queries, key_rows, value_rows, counts, head_of, out_weight):
    seq_count = lax.axis_size("seq")
    tok_dev = queries.shape[1]
    slot_count = head_of.shape[1]
    fewest = max(1, seq_count * slot_count // (2 * HEADS))
    row_cap = (tok_dev + fewest - 1) // fewest
    my_index = lax.axis_index("seq")
    flat_heads, group_size, group_rank = slot_layout(head_of)
    row_steps = jnp.arange(row_cap, dtype=jnp.int32)
    served_rows = group_rank[:, None] + group_size[:, None] * row_steps[None, :]
    my_count = counts[my_index]
    clipped = jnp.minimum(served_rows, tok_dev - 1)
    query_grid = queries[0].reshape(tok_dev, HEADS, HDIM)
    row_live = served_rows < my_count
    query_send = query_grid[clipped, flat_heads[:, None]]
    query_send = jnp.where(row_live[:, :, None], query_send, jnp.zeros((), jnp.bfloat16)).reshape(
        seq_count, slot_count, row_cap, HDIM
    )
    mask_send = row_live.astype(jnp.bfloat16).reshape(seq_count, slot_count, row_cap)
    token_ids = jnp.arange(tok_dev, dtype=jnp.int32)
    key_grid = key_rows[0].reshape(tok_dev, HEADS, HDIM)
    value_grid = value_rows[0].reshape(tok_dev, HEADS, HDIM)
    key_send = key_grid[token_ids[None, :], flat_heads[:, None]].reshape(
        seq_count, slot_count, tok_dev, HDIM
    )
    value_send = value_grid[token_ids[None, :], flat_heads[:, None]].reshape(
        seq_count, slot_count, tok_dev, HDIM
    )
    key_valid = (token_ids[None, :] < counts[:, None]).reshape(-1)
    key_block = tok_dev * key_grouping(seq_count, tok_dev)
    query_recv, mask_recv, key_recv, value_recv = (
        lax.all_to_all(query_send, "seq", split_axis=0, concat_axis=0, tiled=True),
        lax.all_to_all(mask_send, "seq", split_axis=0, concat_axis=0, tiled=True),
        lax.all_to_all(key_send, "seq", split_axis=0, concat_axis=0, tiled=True),
        lax.all_to_all(value_send, "seq", split_axis=0, concat_axis=0, tiled=True),
    )
    attended, logsum = serve_slots(
        query_recv, mask_recv, key_recv, value_recv, key_valid, key_block
    )
    returned = lax.all_to_all(attended, "seq", split_axis=0, concat_axis=0, tiled=True)
    head_ids = jnp.arange(HEADS, dtype=jnp.int32)
    head_group = jnp.sum((flat_heads[None, :] == head_ids[:, None]).astype(jnp.int32), axis=1)
    row_rank = token_ids[:, None] % head_group[None, :]
    row_step = token_ids[:, None] // head_group[None, :]
    slot_ids = jnp.arange(flat_heads.shape[0], dtype=jnp.int32)
    matched = (flat_heads[None, None, :] == head_ids[None, :, None]) & (
        group_rank[None, None, :] == row_rank[:, :, None]
    )
    owner_slot = jnp.sum(jnp.where(matched, slot_ids[None, None, :], 0), axis=2)
    flat_index = owner_slot * row_cap + row_step
    returned_rows = returned.reshape(-1, HDIM)
    attended_home = returned_rows[flat_index].reshape(tok_dev, HEADS * HDIM)
    partner = partner_2(attended_home, "branch", 0)
    on_positive = lax.axis_index("branch") == 0
    own_value = attended_home.astype(jnp.float32)
    partner_value = partner.astype(jnp.float32)
    positive = jnp.where(on_positive, own_value, partner_value)
    negative = jnp.where(on_positive, partner_value, own_value)
    guided = GUIDE_SCALE * positive - (GUIDE_SCALE - 1.0) * negative
    magnitude = jnp.mean(jnp.abs(guided), axis=1, keepdims=True)
    normed = (guided / (magnitude + EPSILON)).astype(jnp.bfloat16)
    projected = jnp.dot(normed, out_weight, preferred_element_type=jnp.float32).astype(jnp.bfloat16)
    saved_rows = jnp.transpose(logsum, (1, 2, 0)).reshape(1, 1, slot_count, row_cap, seq_count)
    return (projected, saved_rows)


KERNEL_PARAMS = pltpu.CompilerParams(vmem_limit_bytes=16 * 1024 * 1024)


SPLIT = 2
HOLD_COPIES = 4
TABLE_PIECES = 3
SPLITTER = 65537.0


def swap_shards(array, offset):
    pairs = [(i, i ^ offset) for i in range(lax.axis_size("seq"))]
    return lax.ppermute(array, "seq", pairs)


def place_offsets(shard_count):
    line = list(range(0, shard_count, SPLIT))
    return line + [offset + 1 for offset in line]


def pack_kernel(
    query_hbm,
    key_hbm,
    value_hbm,
    counts_hbm,
    head_hbm,
    own_ref,
    other_ref,
    limits_ref,
    pick_ref,
    slot_head_ref,
    counts_ref,
    head_ref,
    copy_sems,
):
    tok_dev = own_ref.shape[0] // 3
    half_width = own_ref.shape[1]
    slot_count, shard_count = head_ref.shape
    shard = lax.axis_index("seq")
    half = (shard // SPLIT) % 2
    copies = [
        pltpu.make_async_copy(counts_hbm, counts_ref, copy_sems.at[0]),
        pltpu.make_async_copy(head_hbm, head_ref, copy_sems.at[1]),
    ]
    for target, place in ((other_ref, 1 - half), (own_ref, half)):
        columns = pl.ds(pl.multiple_of(place * half_width, half_width), half_width)
        for part, source in enumerate((key_hbm, value_hbm, query_hbm)):
            rows = pl.ds(part * tok_dev, tok_dev)
            copies.append(
                pltpu.make_async_copy(
                    source.at[0, :, columns], target.at[rows, :], copy_sems.at[len(copies)]
                )
            )
    for copy in copies:
        copy.start()
    copies[0].wait()
    copies[1].wait()

    lane = lax.broadcasted_iota(jnp.int32, (1, limits_ref.shape[1]), 1)
    lane_limit = jnp.zeros(lane.shape, jnp.int32)
    for place, offset in enumerate(place_offsets(shard_count)):
        lane_limit = jnp.where(lane // tok_dev == place, counts_ref[shard ^ offset], lane_limit)
    limits_ref[0:1, :] = (lane % tok_dev < lane_limit).astype(jnp.int32)
    limits_ref[1:2, :] = jnp.full(lane.shape, counts_ref[shard], jnp.int32)
    limits_ref[2:3, :] = jnp.full(lane.shape, counts_ref[shard ^ SPLIT], jnp.int32)

    step = lax.broadcasted_iota(jnp.int32, (1, pick_ref.shape[2]), 1)
    for slot in range(slot_count):
        head = head_ref[slot, shard]
        group_size = jnp.int32(0)
        group_rank = jnp.int32(0)
        for other_shard in range(shard_count):
            for other_slot in range(slot_count):
                same = (head_ref[other_slot, other_shard] == head).astype(jnp.int32)
                before = other_shard * slot_count + other_slot < shard * slot_count + slot
                group_size = group_size + same
                group_rank = group_rank + same * before.astype(jnp.int32)
        served = group_rank + group_size * step
        for source in range(shard_count):
            pick_ref[slot, source : source + 1, :] = jnp.where(
                served < counts_ref[source], served + source * tok_dev, -1
            )
        slot_head_ref[slot] = jnp.full(slot_head_ref.shape[1:], head, jnp.int32)
    for copy in copies[2:]:
        copy.wait()


def hold_kernel(weight_hbm, after_ref, weight_ref, copy_sems):
    share = weight_ref.shape[0] // HOLD_COPIES
    copies = []
    for number in range(HOLD_COPIES):
        rows = pl.ds(number * share, share)
        copies.append(
            pltpu.make_async_copy(
                weight_hbm.at[rows, :], weight_ref.at[rows, :], copy_sems.at[number]
            )
        )
    for copy in copies:
        copy.start()
    for copy in copies:
        copy.wait()


def part_blocks(half_heads, tok_dev):
    return -(-half_heads * TABLE_PIECES // tok_dev)


def gathered(set_refs, part, columns):
    tok_dev = set_refs[0].shape[0] // 3
    rows = pl.ds(part * tok_dev, tok_dev)
    return jnp.concatenate([ref[rows, columns] for ref in set_refs], axis=0)


def head_scores(query_rows, key_all):
    return lax.dot_general(
        query_rows, key_all, (((1,), (1,)), ((), ())), preferred_element_type=jnp.float32
    )


def attend_kernel(set_count, limits_ref, *refs):
    set_refs = refs[:set_count]
    keep_ref, message_ref, table_ref, lines_ref = refs[set_count:]
    tok_dev, half_width = keep_ref.shape
    half_heads = half_width // HDIM
    shard = lax.axis_index("seq")
    head_columns = [pl.ds(head * HDIM, HDIM) for head in range(half_heads)]
    key_valid = limits_ref[0:1, :] > 0

    all_scores = [
        head_scores(gathered(set_refs, 2, columns), gathered(set_refs, 0, columns))
        for columns in head_columns
    ]
    lane = lax.broadcasted_iota(jnp.int32, all_scores[0].shape, 1)
    lines = jnp.zeros(lane.shape, jnp.float32)
    served = []
    for head, scores in enumerate(all_scores):
        scores = jnp.where(key_valid, scores * (1.0 / math.sqrt(HDIM)), -jnp.inf)
        top_score = jnp.max(scores, axis=1, keepdims=True)
        weights = jnp.exp(scores - top_score)
        weight_sum = jnp.sum(weights, axis=1, keepdims=True)
        lines = jnp.where(lane == head, top_score + jnp.log(weight_sum), lines)
        served.append((weights[: 2 * tok_dev].astype(jnp.bfloat16), weight_sum[: 2 * tok_dev]))
    row = lax.broadcasted_iota(jnp.int32, (tok_dev, HDIM), 0)
    for columns, (rounded, weight_sum) in zip(head_columns, served):
        mixed = jnp.dot(
            rounded, gathered(set_refs, 1, columns), preferred_element_type=jnp.float32
        )
        attended = mixed / weight_sum
        kept = jnp.where(row < limits_ref[1:2, :HDIM], attended[:tok_dev], 0.0)
        sent = jnp.where(row < limits_ref[2:3, :HDIM], attended[tok_dev:], 0.0)
        keep_ref[:, columns] = kept.astype(jnp.bfloat16)
        message_ref[:, columns] = sent.astype(jnp.bfloat16)

    for place, offset in enumerate(place_offsets(set_count)):
        rows = pl.ds(pl.multiple_of((shard ^ offset) * tok_dev, tok_dev), tok_dev)
        lines_ref[rows, :] = lines[place * tok_dev : (place + 1) * tok_dev]
    table = jnp.transpose(lines_ref[...])[: table_ref.shape[0]]
    table_ref[...] = table
    row = lax.broadcasted_iota(jnp.int32, (tok_dev, lines.shape[0]), 0)
    blocks = [jnp.zeros(row.shape, jnp.float32) for _ in range(part_blocks(half_heads, tok_dev))]
    for head in range(half_heads):
        rest = jnp.broadcast_to(table[head : head + 1], row.shape)
        for piece in range(TABLE_PIECES):
            scaled = rest * SPLITTER
            part = scaled - (scaled - rest)
            block, at_row = divmod(head * TABLE_PIECES + piece, tok_dev)
            blocks[block] = jnp.where(row == at_row, part, blocks[block])
            rest = rest - part
    message_ref[:, pl.ds(half_width, len(blocks) * lines.shape[0])] = jnp.concatenate(
        blocks, axis=1
    ).astype(jnp.bfloat16)


def guidance(own, partner):
    on_positive = lax.axis_index("branch") == 0
    own_scale = jnp.where(on_positive, GUIDE_SCALE, 1.0 - GUIDE_SCALE)
    partner_scale = jnp.where(on_positive, 1.0 - GUIDE_SCALE, GUIDE_SCALE)
    return own_scale * own.astype(jnp.float32) + partner_scale * partner.astype(jnp.float32)


def half_product(guided, weight_ref, place):
    half_width = guided.shape[1]
    rows = pl.ds(pl.multiple_of(place * half_width, half_width), half_width)
    return jnp.dot(
        guided.astype(jnp.bfloat16), weight_ref[rows, :], preferred_element_type=jnp.float32
    )


def keep_kernel(keep_ref, partner_keep_ref, weight_ref, total_ref, size_ref):
    half = (lax.axis_index("seq") // SPLIT) % 2
    guided = guidance(keep_ref[...], partner_keep_ref[...])
    size = jnp.sum(jnp.abs(guided), axis=1, keepdims=True)
    size_ref[...] = jnp.broadcast_to(size, size_ref.shape)
    total_ref[...] = half_product(guided, weight_ref, half)


def project_kernel(
    total_ref,
    size_ref,
    message_ref,
    partner_back_ref,
    weight_ref,
    table_ref,
    pick_ref,
    slot_head_ref,
    projected_ref,
    saved_ref,
):
    tok_dev = message_ref.shape[0]
    half_width = weight_ref.shape[0] // 2
    half_heads = half_width // HDIM
    tokens = table_ref.shape[1]
    half = (lax.axis_index("seq") // SPLIT) % 2
    rows = pl.ds(0, half_width)
    guided = guidance(message_ref[:, rows], partner_back_ref[:, rows])
    size = size_ref[:, 0:1] + jnp.sum(jnp.abs(guided), axis=1, keepdims=True)
    magnitude = size / (2 * half_width)
    total = total_ref[...] + half_product(guided, weight_ref, 1 - half)
    projected_ref[...] = (total / (magnitude + EPSILON)).astype(jnp.bfloat16)

    parts = message_ref[:, pl.ds(half_width, message_ref.shape[1] - half_width)].astype(jnp.float32)
    others = []
    for head in range(half_heads):
        other = jnp.zeros((1, tokens), jnp.float32)
        for piece in range(TABLE_PIECES):
            block, at_row = divmod(head * TABLE_PIECES + piece, tok_dev)
            other = other + parts[at_row : at_row + 1, block * tokens : (block + 1) * tokens]
        others.append(other)
    for slot in range(saved_ref.shape[0]):
        slot_head = slot_head_ref[slot, 0:1, :]
        line = jnp.zeros((1, tokens), jnp.float32)
        for head in range(half_heads):
            line = jnp.where(slot_head == half * half_heads + head, table_ref[head : head + 1], line)
            line = jnp.where(slot_head == (1 - half) * half_heads + head, others[head], line)
        pick = pick_ref[slot]
        spread = jnp.broadcast_to(line, pick.shape)
        taken = jnp.take_along_axis(spread, jnp.maximum(pick, 0), axis=1)
        saved_ref[slot] = jnp.where(pick >= 0, taken, 0.0)[:, : saved_ref.shape[2]]


def per_device_halves(queries, key_rows, value_rows, counts, head_of, out_weight):
    seq_count = lax.axis_size("seq")
    tok_dev, width = queries.shape[1:]
    half_width = width // 2
    tokens = seq_count * tok_dev
    slot_count = head_of.shape[1]
    fewest = max(1, seq_count * slot_count // (2 * HEADS))
    row_cap = (tok_dev + fewest - 1) // fewest
    message_width = half_width + part_blocks(half_width // HDIM, tok_dev) * tokens
    any_spec = pl.BlockSpec(memory_space=pl.ANY)
    vmem = pl.BlockSpec(memory_space=pltpu.VMEM)

    def held(*arrays):
        return [pltpu.with_memory_space_constraint(array, pltpu.VMEM) for array in arrays]

    def distant(*arrays):
        return [pltpu.with_memory_space_constraint(array, pltpu.HBM) for array in arrays]

    own, other, limits, pick, slot_head = pl.pallas_call(
        pack_kernel,
        out_shape=[
            pltpu.VMEM((3 * tok_dev, half_width), jnp.bfloat16),
            pltpu.VMEM((3 * tok_dev, half_width), jnp.bfloat16),
            pltpu.VMEM((8, tokens), jnp.int32),
            pltpu.VMEM((slot_count, seq_count, tokens), jnp.int32),
            pltpu.VMEM((slot_count, 8, tokens), jnp.int32),
        ],
        in_specs=[any_spec] * 5,
        out_specs=[vmem] * 5,
        scratch_shapes=[
            pltpu.SMEM((seq_count,), jnp.int32),
            pltpu.SMEM((slot_count, seq_count), jnp.int32),
            pltpu.SemaphoreType.DMA((8,)),
        ],
        compiler_params=KERNEL_PARAMS,
        name="pack",
    )(*distant(queries, key_rows, value_rows, counts, jnp.transpose(head_of)))

    weight_held = pl.pallas_call(
        hold_kernel,
        out_shape=pltpu.VMEM(out_weight.shape, jnp.bfloat16),
        in_specs=[any_spec, vmem],
        out_specs=vmem,
        scratch_shapes=[pltpu.SemaphoreType.DMA((HOLD_COPIES,))],
        compiler_params=KERNEL_PARAMS,
        cost_estimate=pl.CostEstimate(
            flops=0, bytes_accessed=4 * out_weight.size, transcendentals=0
        ),
        name="hold",
    )(*distant(out_weight), *held(limits))
    line = [own] + [
        swap_shards(other if offset & SPLIT else own, offset)
        for offset in range(SPLIT, seq_count, SPLIT)
    ]
    sets = line + [swap_shards(array, 1) for array in line]
    limits, weight_held = lax.optimization_barrier((limits, weight_held))
    keep, message, table = pl.pallas_call(
        functools.partial(attend_kernel, len(sets)),
        out_shape=[
            pltpu.VMEM((tok_dev, half_width), jnp.bfloat16),
            pltpu.VMEM((tok_dev, message_width), jnp.bfloat16),
            pltpu.VMEM((half_width // HDIM + 7 & -8, tokens), jnp.float32),
        ],
        in_specs=[vmem] * (1 + len(sets)),
        out_specs=[vmem] * 3,
        scratch_shapes=[pltpu.VMEM((tokens, HDIM), jnp.float32)],
        compiler_params=KERNEL_PARAMS,
        name="attend",
    )(*held(limits, *sets))
    partner_keep = partner_2(keep, "branch", 0)
    back = swap_shards(message, SPLIT)
    total, size = pl.pallas_call(
        keep_kernel,
        out_shape=[
            pltpu.VMEM((tok_dev, out_weight.shape[1]), jnp.float32),
            pltpu.VMEM((tok_dev, HDIM), jnp.float32),
        ],
        in_specs=[vmem] * 3,
        out_specs=[vmem] * 2,
        compiler_params=KERNEL_PARAMS,
        name="keep",
    )(*held(keep, partner_keep, weight_held))
    back, total, size = lax.optimization_barrier((back, total, size))
    partner_back = partner_2(back, "branch", 0)
    projected, saved = pl.pallas_call(
        project_kernel,
        out_shape=[
            jax.ShapeDtypeStruct((tok_dev, out_weight.shape[1]), jnp.bfloat16),
            jax.ShapeDtypeStruct((slot_count, seq_count, row_cap), jnp.float32),
        ],
        in_specs=[vmem] * 8,
        out_specs=[vmem] * 2,
        compiler_params=KERNEL_PARAMS,
        name="project",
    )(*held(total, size, back, partner_back, weight_held, table, pick, slot_head))
    saved = jnp.transpose(saved, (0, 2, 1))
    return (projected, saved.reshape(1, 1, slot_count, row_cap, seq_count))


def solution(mesh):
    seq_count = mesh.shape["seq"]
    hypercube = seq_count > SPLIT and seq_count & (seq_count - 1) == 0
    small = hypercube and seq_count <= HEADS
    return jax.shard_map(
        per_device_halves if small else per_device_exchange,
        mesh=mesh,
        in_specs=(
            P("branch", ("groups", "seq"), None),
            P("branch", ("groups", "seq"), None),
            P("branch", ("groups", "seq"), None),
            P("groups"),
            P(),
            P(None, "branch"),
        ),
        out_specs=(
            P(("groups", "seq"), "branch"),
            P("branch", ("groups", "seq"), None, None, None),
        ),
        check_vma=False,
    )
```

```python
import functools
import math

import jax
import jax.numpy as jnp
from jax import lax
from jax.experimental import pallas as pl
from jax.experimental.pallas import tpu as pltpu
from jax.sharding import PartitionSpec as P

HEADS = 12
HDIM = 128


GUIDE_SCALE = 3.0
EPSILON = 1e-06


def partner_2(array, axis, stride):
    return lax.ppermute(array, axis, [(i, i ^ 1 << stride) for i in range(lax.axis_size(axis))])


def slot_layout(head_of):
    flat_heads = head_of.reshape(-1)
    slot_order = jnp.arange(flat_heads.shape[0], dtype=jnp.int32)
    same_head = flat_heads[:, None] == flat_heads[None, :]
    group_size = jnp.sum(same_head.astype(jnp.int32), axis=1)
    earlier = same_head & (slot_order[None, :] < slot_order[:, None])
    group_rank = jnp.sum(earlier.astype(jnp.int32), axis=1)
    return (flat_heads, group_size, group_rank)


def key_grouping(seq_count, tok_dev):
    shard_limit = max(1, 2048 // tok_dev)
    grouping = 1
    for attempt in range(16):
        if grouping * 2 <= shard_limit and seq_count % (grouping * 2) == 0:
            grouping = grouping * 2
    return grouping


def attend_rows(query_block, key_slot, value_slot, key_valid, key_block):
    row_count = query_block.shape[0]
    head_size = query_block.shape[1]
    block_count = key_slot.shape[0] // key_block
    scale_factor = 1.0 / math.sqrt(head_size)

    def fold_block(block_id, state_in):
        top_score, weight_sum, summed = state_in
        scores = (
            jnp.einsum("qd,kd->qk", query_block, key_slot, preferred_element_type=jnp.float32)
            * scale_factor
        )
        scores = jnp.where(key_valid[None, :], scores, -jnp.inf)
        new_top = jnp.maximum(top_score, jnp.max(scores, axis=1))
        fading = jnp.exp(top_score - new_top)
        weights = jnp.exp(scores - new_top[:, None])
        weight_sum = weight_sum * fading + jnp.sum(weights, axis=1)
        summed = summed * fading[:, None] + jnp.dot(
            weights.astype(jnp.bfloat16), value_slot, preferred_element_type=jnp.float32
        )
        return (new_top, weight_sum, summed)

    start_state = (
        jnp.full((row_count,), -jnp.inf, jnp.float32),
        jnp.zeros((row_count,), jnp.float32),
        jnp.zeros((row_count, head_size), jnp.float32),
    )
    top_score, weight_sum, summed = lax.fori_loop(0, block_count, fold_block, start_state)
    return (summed / weight_sum[:, None], top_score + jnp.log(weight_sum))


def serve_slots(query_items, mask_items, key_recv, value_recv, key_valid, key_block):
    source_count, slot_count, item_count, head_size = query_items.shape
    all_tokens = key_recv.shape[0] * key_recv.shape[2]
    per_block = max(1, 512 // source_count)
    slot_outputs = []
    slot_logsum = []
    for slot_id in range(slot_count):
        key_slot = key_recv[:, slot_id].reshape(all_tokens, head_size)
        value_slot = value_recv[:, slot_id].reshape(all_tokens, head_size)
        taken_items = min(per_block, item_count)
        query_block = query_items[:, slot_id, 0:taken_items].reshape(
            source_count * taken_items, head_size
        )
        attended, logsum = attend_rows(query_block, key_slot, value_slot, key_valid, key_block)
        pieces_out = attended.reshape(source_count, taken_items, head_size)
        pieces_sum = logsum.reshape(source_count, taken_items)
        slot_outputs.append(pieces_out)
        slot_logsum.append(pieces_sum)
    attended = jnp.stack(slot_outputs, axis=1)
    logsum = jnp.stack(slot_logsum, axis=1)
    keep_rows = mask_items > 0
    attended = jnp.where(keep_rows[:, :, :, None], attended, 0.0).astype(jnp.bfloat16)
    logsum = jnp.where(keep_rows, logsum, 0.0)
    return (attended, logsum)


def per_device_exchange(queries, key_rows, value_rows, counts, head_of, out_weight):
    seq_count = lax.axis_size("seq")
    tok_dev = queries.shape[1]
    slot_count = head_of.shape[1]
    fewest = max(1, seq_count * slot_count // (2 * HEADS))
    row_cap = (tok_dev + fewest - 1) // fewest
    my_index = lax.axis_index("seq")
    flat_heads, group_size, group_rank = slot_layout(head_of)
    row_steps = jnp.arange(row_cap, dtype=jnp.int32)
    served_rows = group_rank[:, None] + group_size[:, None] * row_steps[None, :]
    my_count = counts[my_index]
    clipped = jnp.minimum(served_rows, tok_dev - 1)
    query_grid = queries[0].reshape(tok_dev, HEADS, HDIM)
    row_live = served_rows < my_count
    query_send = query_grid[clipped, flat_heads[:, None]]
    query_send = jnp.where(row_live[:, :, None], query_send, jnp.zeros((), jnp.bfloat16)).reshape(
        seq_count, slot_count, row_cap, HDIM
    )
    mask_send = row_live.astype(jnp.bfloat16).reshape(seq_count, slot_count, row_cap)
    token_ids = jnp.arange(tok_dev, dtype=jnp.int32)
    key_grid = key_rows[0].reshape(tok_dev, HEADS, HDIM)
    value_grid = value_rows[0].reshape(tok_dev, HEADS, HDIM)
    key_send = key_grid[token_ids[None, :], flat_heads[:, None]].reshape(
        seq_count, slot_count, tok_dev, HDIM
    )
    value_send = value_grid[token_ids[None, :], flat_heads[:, None]].reshape(
        seq_count, slot_count, tok_dev, HDIM
    )
    key_valid = (token_ids[None, :] < counts[:, None]).reshape(-1)
    key_block = tok_dev * key_grouping(seq_count, tok_dev)
    query_recv, mask_recv, key_recv, value_recv = (
        lax.all_to_all(query_send, "seq", split_axis=0, concat_axis=0, tiled=True),
        lax.all_to_all(mask_send, "seq", split_axis=0, concat_axis=0, tiled=True),
        lax.all_to_all(key_send, "seq", split_axis=0, concat_axis=0, tiled=True),
        lax.all_to_all(value_send, "seq", split_axis=0, concat_axis=0, tiled=True),
    )
    attended, logsum = serve_slots(
        query_recv, mask_recv, key_recv, value_recv, key_valid, key_block
    )
    returned = lax.all_to_all(attended, "seq", split_axis=0, concat_axis=0, tiled=True)
    head_ids = jnp.arange(HEADS, dtype=jnp.int32)
    head_group = jnp.sum((flat_heads[None, :] == head_ids[:, None]).astype(jnp.int32), axis=1)
    row_rank = token_ids[:, None] % head_group[None, :]
    row_step = token_ids[:, None] // head_group[None, :]
    slot_ids = jnp.arange(flat_heads.shape[0], dtype=jnp.int32)
    matched = (flat_heads[None, None, :] == head_ids[None, :, None]) & (
        group_rank[None, None, :] == row_rank[:, :, None]
    )
    owner_slot = jnp.sum(jnp.where(matched, slot_ids[None, None, :], 0), axis=2)
    flat_index = owner_slot * row_cap + row_step
    returned_rows = returned.reshape(-1, HDIM)
    attended_home = returned_rows[flat_index].reshape(tok_dev, HEADS * HDIM)
    partner = partner_2(attended_home, "branch", 0)
    on_positive = lax.axis_index("branch") == 0
    own_value = attended_home.astype(jnp.float32)
    partner_value = partner.astype(jnp.float32)
    positive = jnp.where(on_positive, own_value, partner_value)
    negative = jnp.where(on_positive, partner_value, own_value)
    guided = GUIDE_SCALE * positive - (GUIDE_SCALE - 1.0) * negative
    magnitude = jnp.mean(jnp.abs(guided), axis=1, keepdims=True)
    normed = (guided / (magnitude + EPSILON)).astype(jnp.bfloat16)
    projected = jnp.dot(normed, out_weight, preferred_element_type=jnp.float32).astype(jnp.bfloat16)
    saved_rows = jnp.transpose(logsum, (1, 2, 0)).reshape(1, 1, slot_count, row_cap, seq_count)
    return (projected, saved_rows)


KERNEL_PARAMS = pltpu.CompilerParams(vmem_limit_bytes=16 * 1024 * 1024)


SPLIT = 2
HOLD_COPIES = 4
TABLE_PIECES = 3
SPLITTER = 65537.0


def swap_shards(array, offset):
    pairs = [(i, i ^ offset) for i in range(lax.axis_size("seq"))]
    return lax.ppermute(array, "seq", pairs)


def place_offsets(shard_count):
    line = list(range(0, shard_count, SPLIT))
    return line + [offset + 1 for offset in line]


def pack_kernel(
    query_hbm,
    key_hbm,
    value_hbm,
    counts_hbm,
    head_hbm,
    own_ref,
    other_ref,
    limits_ref,
    pick_ref,
    slot_head_ref,
    counts_ref,
    head_ref,
    copy_sems,
):
    tok_dev = own_ref.shape[0] // 3
    half_width = own_ref.shape[1]
    slot_count, shard_count = head_ref.shape
    shard = lax.axis_index("seq")
    half = (shard // SPLIT) % 2
    copies = [
        pltpu.make_async_copy(counts_hbm, counts_ref, copy_sems.at[0]),
        pltpu.make_async_copy(head_hbm, head_ref, copy_sems.at[1]),
    ]
    for target, place in ((other_ref, 1 - half), (own_ref, half)):
        columns = pl.ds(pl.multiple_of(place * half_width, half_width), half_width)
        for part, source in enumerate((key_hbm, value_hbm, query_hbm)):
            rows = pl.ds(part * tok_dev, tok_dev)
            copies.append(
                pltpu.make_async_copy(
                    source.at[0, :, columns], target.at[rows, :], copy_sems.at[len(copies)]
                )
            )
    for copy in copies:
        copy.start()
    copies[0].wait()
    copies[1].wait()

    lane = lax.broadcasted_iota(jnp.int32, (1, limits_ref.shape[1]), 1)
    lane_limit = jnp.zeros(lane.shape, jnp.int32)
    for place, offset in enumerate(place_offsets(shard_count)):
        lane_limit = jnp.where(lane // tok_dev == place, counts_ref[shard ^ offset], lane_limit)
    limits_ref[0:1, :] = (lane % tok_dev < lane_limit).astype(jnp.int32)
    limits_ref[1:2, :] = jnp.full(lane.shape, counts_ref[shard], jnp.int32)
    limits_ref[2:3, :] = jnp.full(lane.shape, counts_ref[shard ^ SPLIT], jnp.int32)

    step = lax.broadcasted_iota(jnp.int32, (1, pick_ref.shape[2]), 1)
    for slot in range(slot_count):
        head = head_ref[slot, shard]
        group_size = jnp.int32(0)
        group_rank = jnp.int32(0)
        for other_shard in range(shard_count):
            for other_slot in range(slot_count):
                same = (head_ref[other_slot, other_shard] == head).astype(jnp.int32)
                before = other_shard * slot_count + other_slot < shard * slot_count + slot
                group_size = group_size + same
                group_rank = group_rank + same * before.astype(jnp.int32)
        served = group_rank + group_size * step
        for source in range(shard_count):
            pick_ref[slot, source : source + 1, :] = jnp.where(
                served < counts_ref[source], served + source * tok_dev, -1
            )
        slot_head_ref[slot] = jnp.full(slot_head_ref.shape[1:], head, jnp.int32)
    for copy in copies[2:]:
        copy.wait()


def hold_kernel(weight_hbm, after_ref, weight_ref, copy_sems):
    share = weight_ref.shape[0] // HOLD_COPIES
    copies = []
    for number in range(HOLD_COPIES):
        rows = pl.ds(number * share, share)
        copies.append(
            pltpu.make_async_copy(
                weight_hbm.at[rows, :], weight_ref.at[rows, :], copy_sems.at[number]
            )
        )
    for copy in copies:
        copy.start()
    for copy in copies:
        copy.wait()


def part_blocks(half_heads, tok_dev):
    return -(-half_heads * TABLE_PIECES // tok_dev)


def gathered(set_refs, part, columns):
    tok_dev = set_refs[0].shape[0] // 3
    rows = pl.ds(part * tok_dev, tok_dev)
    return jnp.concatenate([ref[rows, columns] for ref in set_refs], axis=0)


def head_scores(query_rows, key_all):
    return lax.dot_general(
        query_rows, key_all, (((1,), (1,)), ((), ())), preferred_element_type=jnp.float32
    )


def attend_kernel(set_count, limits_ref, *refs):
    set_refs = refs[:set_count]
    keep_ref, message_ref, table_ref, lines_ref = refs[set_count:]
    tok_dev, half_width = keep_ref.shape
    half_heads = half_width // HDIM
    shard = lax.axis_index("seq")
    head_columns = [pl.ds(head * HDIM, HDIM) for head in range(half_heads)]
    key_valid = limits_ref[0:1, :] > 0

    all_scores = [
        head_scores(gathered(set_refs, 2, columns), gathered(set_refs, 0, columns))
        for columns in head_columns
    ]
    lane = lax.broadcasted_iota(jnp.int32, all_scores[0].shape, 1)
    lines = jnp.zeros(lane.shape, jnp.float32)
    served = []
    for head, scores in enumerate(all_scores):
        scores = jnp.where(key_valid, scores * (1.0 / math.sqrt(HDIM)), -jnp.inf)
        top_score = jnp.max(scores, axis=1, keepdims=True)
        weights = jnp.exp(scores - top_score)
        weight_sum = jnp.sum(weights, axis=1, keepdims=True)
        lines = jnp.where(lane == head, top_score + jnp.log(weight_sum), lines)
        served.append((weights[: 2 * tok_dev].astype(jnp.bfloat16), weight_sum[: 2 * tok_dev]))
    row = lax.broadcasted_iota(jnp.int32, (tok_dev, HDIM), 0)
    for columns, (rounded, weight_sum) in zip(head_columns, served):
        mixed = jnp.dot(
            rounded, gathered(set_refs, 1, columns), preferred_element_type=jnp.float32
        )
        attended = mixed / weight_sum
        kept = jnp.where(row < limits_ref[1:2, :HDIM], attended[:tok_dev], 0.0)
        sent = jnp.where(row < limits_ref[2:3, :HDIM], attended[tok_dev:], 0.0)
        keep_ref[:, columns] = kept.astype(jnp.bfloat16)
        message_ref[:, columns] = sent.astype(jnp.bfloat16)

    for place, offset in enumerate(place_offsets(set_count)):
        rows = pl.ds(pl.multiple_of((shard ^ offset) * tok_dev, tok_dev), tok_dev)
        lines_ref[rows, :] = lines[place * tok_dev : (place + 1) * tok_dev]
    table = jnp.transpose(lines_ref[...])[: table_ref.shape[0]]
    table_ref[...] = table
    row = lax.broadcasted_iota(jnp.int32, (tok_dev, lines.shape[0]), 0)
    blocks = [jnp.zeros(row.shape, jnp.float32) for _ in range(part_blocks(half_heads, tok_dev))]
    for head in range(half_heads):
        rest = jnp.broadcast_to(table[head : head + 1], row.shape)
        for piece in range(TABLE_PIECES):
            scaled = rest * SPLITTER
            part = scaled - (scaled - rest)
            block, at_row = divmod(head * TABLE_PIECES + piece, tok_dev)
            blocks[block] = jnp.where(row == at_row, part, blocks[block])
            rest = rest - part
    message_ref[:, pl.ds(half_width, len(blocks) * lines.shape[0])] = jnp.concatenate(
        blocks, axis=1
    ).astype(jnp.bfloat16)


def guidance(own, partner):
    on_positive = lax.axis_index("branch") == 0
    own_scale = jnp.where(on_positive, GUIDE_SCALE, 1.0 - GUIDE_SCALE)
    partner_scale = jnp.where(on_positive, 1.0 - GUIDE_SCALE, GUIDE_SCALE)
    return own_scale * own.astype(jnp.float32) + partner_scale * partner.astype(jnp.float32)


def half_product(guided, weight_ref, place):
    half_width = guided.shape[1]
    rows = pl.ds(pl.multiple_of(place * half_width, half_width), half_width)
    return jnp.dot(
        guided.astype(jnp.bfloat16), weight_ref[rows, :], preferred_element_type=jnp.float32
    )


def keep_kernel(keep_ref, partner_keep_ref, weight_ref, total_ref, size_ref):
    half = (lax.axis_index("seq") // SPLIT) % 2
    guided = guidance(keep_ref[...], partner_keep_ref[...])
    size = jnp.sum(jnp.abs(guided), axis=1, keepdims=True)
    size_ref[...] = jnp.broadcast_to(size, size_ref.shape)
    total_ref[...] = half_product(guided, weight_ref, half)


def project_kernel(
    total_ref,
    size_ref,
    message_ref,
    partner_back_ref,
    weight_ref,
    table_ref,
    pick_ref,
    slot_head_ref,
    projected_ref,
    saved_ref,
):
    tok_dev = message_ref.shape[0]
    half_width = weight_ref.shape[0] // 2
    half_heads = half_width // HDIM
    tokens = table_ref.shape[1]
    half = (lax.axis_index("seq") // SPLIT) % 2
    rows = pl.ds(0, half_width)
    guided = guidance(message_ref[:, rows], partner_back_ref[:, rows])
    size = size_ref[:, 0:1] + jnp.sum(jnp.abs(guided), axis=1, keepdims=True)
    magnitude = size / (2 * half_width)
    total = total_ref[...] + half_product(guided, weight_ref, 1 - half)
    projected_ref[...] = (total / (magnitude + EPSILON)).astype(jnp.bfloat16)

    parts = message_ref[:, pl.ds(half_width, message_ref.shape[1] - half_width)].astype(jnp.float32)
    others = []
    for head in range(half_heads):
        other = jnp.zeros((1, tokens), jnp.float32)
        for piece in range(TABLE_PIECES):
            block, at_row = divmod(head * TABLE_PIECES + piece, tok_dev)
            other = other + parts[at_row : at_row + 1, block * tokens : (block + 1) * tokens]
        others.append(other)
    for slot in range(saved_ref.shape[0]):
        slot_head = slot_head_ref[slot, 0:1, :]
        line = jnp.zeros((1, tokens), jnp.float32)
        for head in range(half_heads):
            line = jnp.where(slot_head == half * half_heads + head, table_ref[head : head + 1], line)
            line = jnp.where(slot_head == (1 - half) * half_heads + head, others[head], line)
        pick = pick_ref[slot]
        spread = jnp.broadcast_to(line, pick.shape)
        taken = jnp.take_along_axis(spread, jnp.maximum(pick, 0), axis=1)
        saved_ref[slot] = jnp.where(pick >= 0, taken, 0.0)[:, : saved_ref.shape[2]]


def per_device_halves(queries, key_rows, value_rows, counts, head_of, out_weight):
    seq_count = lax.axis_size("seq")
    tok_dev, width = queries.shape[1:]
    half_width = width // 2
    tokens = seq_count * tok_dev
    slot_count = head_of.shape[1]
    fewest = max(1, seq_count * slot_count // (2 * HEADS))
    row_cap = (tok_dev + fewest - 1) // fewest
    message_width = half_width + part_blocks(half_width // HDIM, tok_dev) * tokens
    any_spec = pl.BlockSpec(memory_space=pl.ANY)
    vmem = pl.BlockSpec(memory_space=pltpu.VMEM)

    def held(*arrays):
        return [pltpu.with_memory_space_constraint(array, pltpu.VMEM) for array in arrays]

    def distant(*arrays):
        return [pltpu.with_memory_space_constraint(array, pltpu.HBM) for array in arrays]

    own, other, limits, pick, slot_head = pl.pallas_call(
        pack_kernel,
        out_shape=[
            pltpu.VMEM((3 * tok_dev, half_width), jnp.bfloat16),
            pltpu.VMEM((3 * tok_dev, half_width), jnp.bfloat16),
            pltpu.VMEM((8, tokens), jnp.int32),
            pltpu.VMEM((slot_count, seq_count, tokens), jnp.int32),
            pltpu.VMEM((slot_count, 8, tokens), jnp.int32),
        ],
        in_specs=[any_spec] * 5,
        out_specs=[vmem] * 5,
        scratch_shapes=[
            pltpu.SMEM((seq_count,), jnp.int32),
            pltpu.SMEM((slot_count, seq_count), jnp.int32),
            pltpu.SemaphoreType.DMA((8,)),
        ],
        compiler_params=KERNEL_PARAMS,
        name="pack",
    )(*distant(queries, key_rows, value_rows, counts, jnp.transpose(head_of)))

    weight_held = pl.pallas_call(
        hold_kernel,
        out_shape=pltpu.VMEM(out_weight.shape, jnp.bfloat16),
        in_specs=[any_spec, vmem],
        out_specs=vmem,
        scratch_shapes=[pltpu.SemaphoreType.DMA((HOLD_COPIES,))],
        compiler_params=KERNEL_PARAMS,
        cost_estimate=pl.CostEstimate(
            flops=0, bytes_accessed=4 * out_weight.size, transcendentals=0
        ),
        name="hold",
    )(*distant(out_weight), *held(limits))
    line = [own] + [
        swap_shards(other if offset & SPLIT else own, offset)
        for offset in range(SPLIT, seq_count, SPLIT)
    ]
    sets = line + [swap_shards(array, 1) for array in line]
    limits, weight_held = lax.optimization_barrier((limits, weight_held))
    keep, message, table = pl.pallas_call(
        functools.partial(attend_kernel, len(sets)),
        out_shape=[
            pltpu.VMEM((tok_dev, half_width), jnp.bfloat16),
            pltpu.VMEM((tok_dev, message_width), jnp.bfloat16),
            pltpu.VMEM((half_width // HDIM + 7 & -8, tokens), jnp.float32),
        ],
        in_specs=[vmem] * (1 + len(sets)),
        out_specs=[vmem] * 3,
        scratch_shapes=[pltpu.VMEM((tokens, HDIM), jnp.float32)],
        compiler_params=KERNEL_PARAMS,
        name="attend",
    )(*held(limits, *sets))
    across = [(2 * i + b, 2 * (i ^ SPLIT) + 1 - b) for i in range(seq_count) for b in range(2)]
    partner_back = lax.ppermute(message, ("seq", "branch"), across)
    partner_keep = partner_2(keep, "branch", 0)
    back = swap_shards(message, SPLIT)
    total, size = pl.pallas_call(
        keep_kernel,
        out_shape=[
            pltpu.VMEM((tok_dev, out_weight.shape[1]), jnp.float32),
            pltpu.VMEM((tok_dev, HDIM), jnp.float32),
        ],
        in_specs=[vmem] * 3,
        out_specs=[vmem] * 2,
        compiler_params=KERNEL_PARAMS,
        name="keep",
    )(*held(keep, partner_keep, weight_held))
    projected, saved = pl.pallas_call(
        project_kernel,
        out_shape=[
            jax.ShapeDtypeStruct((tok_dev, out_weight.shape[1]), jnp.bfloat16),
            jax.ShapeDtypeStruct((slot_count, seq_count, row_cap), jnp.float32),
        ],
        in_specs=[vmem] * 8,
        out_specs=[vmem] * 2,
        compiler_params=KERNEL_PARAMS,
        name="project",
    )(*held(total, size, back, partner_back, weight_held, table, pick, slot_head))
    saved = jnp.transpose(saved, (0, 2, 1))
    return (projected, saved.reshape(1, 1, slot_count, row_cap, seq_count))


def solution(mesh):
    seq_count = mesh.shape["seq"]
    hypercube = seq_count > SPLIT and seq_count & (seq_count - 1) == 0
    small = hypercube and seq_count <= HEADS
    return jax.shard_map(
        per_device_halves if small else per_device_exchange,
        mesh=mesh,
        in_specs=(
            P("branch", ("groups", "seq"), None),
            P("branch", ("groups", "seq"), None),
            P("branch", ("groups", "seq"), None),
            P("groups"),
            P(),
            P(None, "branch"),
        ),
        out_specs=(
            P(("groups", "seq"), "branch"),
            P("branch", ("groups", "seq"), None, None, None),
        ),
        check_vma=False,
    )
```

```python
import functools
import math

import jax
import jax.numpy as jnp
from jax import lax
from jax.experimental import pallas as pl
from jax.experimental.pallas import tpu as pltpu
from jax.sharding import PartitionSpec as P

HEADS = 12
HDIM = 128


GUIDE_SCALE = 3.0
EPSILON = 1e-06


def partner_2(array, axis, stride):
    return lax.ppermute(array, axis, [(i, i ^ 1 << stride) for i in range(lax.axis_size(axis))])


def slot_layout(head_of):
    flat_heads = head_of.reshape(-1)
    slot_order = jnp.arange(flat_heads.shape[0], dtype=jnp.int32)
    same_head = flat_heads[:, None] == flat_heads[None, :]
    group_size = jnp.sum(same_head.astype(jnp.int32), axis=1)
    earlier = same_head & (slot_order[None, :] < slot_order[:, None])
    group_rank = jnp.sum(earlier.astype(jnp.int32), axis=1)
    return (flat_heads, group_size, group_rank)


def key_grouping(seq_count, tok_dev):
    shard_limit = max(1, 2048 // tok_dev)
    grouping = 1
    for attempt in range(16):
        if grouping * 2 <= shard_limit and seq_count % (grouping * 2) == 0:
            grouping = grouping * 2
    return grouping


def attend_rows(query_block, key_slot, value_slot, key_valid, key_block):
    row_count = query_block.shape[0]
    head_size = query_block.shape[1]
    block_count = key_slot.shape[0] // key_block
    scale_factor = 1.0 / math.sqrt(head_size)

    def fold_block(block_id, state_in):
        top_score, weight_sum, summed = state_in
        scores = (
            jnp.einsum("qd,kd->qk", query_block, key_slot, preferred_element_type=jnp.float32)
            * scale_factor
        )
        scores = jnp.where(key_valid[None, :], scores, -jnp.inf)
        new_top = jnp.maximum(top_score, jnp.max(scores, axis=1))
        fading = jnp.exp(top_score - new_top)
        weights = jnp.exp(scores - new_top[:, None])
        weight_sum = weight_sum * fading + jnp.sum(weights, axis=1)
        summed = summed * fading[:, None] + jnp.dot(
            weights.astype(jnp.bfloat16), value_slot, preferred_element_type=jnp.float32
        )
        return (new_top, weight_sum, summed)

    start_state = (
        jnp.full((row_count,), -jnp.inf, jnp.float32),
        jnp.zeros((row_count,), jnp.float32),
        jnp.zeros((row_count, head_size), jnp.float32),
    )
    top_score, weight_sum, summed = lax.fori_loop(0, block_count, fold_block, start_state)
    return (summed / weight_sum[:, None], top_score + jnp.log(weight_sum))


def serve_slots(query_items, mask_items, key_recv, value_recv, key_valid, key_block):
    source_count, slot_count, item_count, head_size = query_items.shape
    all_tokens = key_recv.shape[0] * key_recv.shape[2]
    per_block = max(1, 512 // source_count)
    slot_outputs = []
    slot_logsum = []
    for slot_id in range(slot_count):
        key_slot = key_recv[:, slot_id].reshape(all_tokens, head_size)
        value_slot = value_recv[:, slot_id].reshape(all_tokens, head_size)
        taken_items = min(per_block, item_count)
        query_block = query_items[:, slot_id, 0:taken_items].reshape(
            source_count * taken_items, head_size
        )
        attended, logsum = attend_rows(query_block, key_slot, value_slot, key_valid, key_block)
        pieces_out = attended.reshape(source_count, taken_items, head_size)
        pieces_sum = logsum.reshape(source_count, taken_items)
        slot_outputs.append(pieces_out)
        slot_logsum.append(pieces_sum)
    attended = jnp.stack(slot_outputs, axis=1)
    logsum = jnp.stack(slot_logsum, axis=1)
    keep_rows = mask_items > 0
    attended = jnp.where(keep_rows[:, :, :, None], attended, 0.0).astype(jnp.bfloat16)
    logsum = jnp.where(keep_rows, logsum, 0.0)
    return (attended, logsum)


def per_device_exchange(queries, key_rows, value_rows, counts, head_of, out_weight):
    seq_count = lax.axis_size("seq")
    tok_dev = queries.shape[1]
    slot_count = head_of.shape[1]
    fewest = max(1, seq_count * slot_count // (2 * HEADS))
    row_cap = (tok_dev + fewest - 1) // fewest
    my_index = lax.axis_index("seq")
    flat_heads, group_size, group_rank = slot_layout(head_of)
    row_steps = jnp.arange(row_cap, dtype=jnp.int32)
    served_rows = group_rank[:, None] + group_size[:, None] * row_steps[None, :]
    my_count = counts[my_index]
    clipped = jnp.minimum(served_rows, tok_dev - 1)
    query_grid = queries[0].reshape(tok_dev, HEADS, HDIM)
    row_live = served_rows < my_count
    query_send = query_grid[clipped, flat_heads[:, None]]
    query_send = jnp.where(row_live[:, :, None], query_send, jnp.zeros((), jnp.bfloat16)).reshape(
        seq_count, slot_count, row_cap, HDIM
    )
    mask_send = row_live.astype(jnp.bfloat16).reshape(seq_count, slot_count, row_cap)
    token_ids = jnp.arange(tok_dev, dtype=jnp.int32)
    key_grid = key_rows[0].reshape(tok_dev, HEADS, HDIM)
    value_grid = value_rows[0].reshape(tok_dev, HEADS, HDIM)
    key_send = key_grid[token_ids[None, :], flat_heads[:, None]].reshape(
        seq_count, slot_count, tok_dev, HDIM
    )
    value_send = value_grid[token_ids[None, :], flat_heads[:, None]].reshape(
        seq_count, slot_count, tok_dev, HDIM
    )
    key_valid = (token_ids[None, :] < counts[:, None]).reshape(-1)
    key_block = tok_dev * key_grouping(seq_count, tok_dev)
    query_recv, mask_recv, key_recv, value_recv = (
        lax.all_to_all(query_send, "seq", split_axis=0, concat_axis=0, tiled=True),
        lax.all_to_all(mask_send, "seq", split_axis=0, concat_axis=0, tiled=True),
        lax.all_to_all(key_send, "seq", split_axis=0, concat_axis=0, tiled=True),
        lax.all_to_all(value_send, "seq", split_axis=0, concat_axis=0, tiled=True),
    )
    attended, logsum = serve_slots(
        query_recv, mask_recv, key_recv, value_recv, key_valid, key_block
    )
    returned = lax.all_to_all(attended, "seq", split_axis=0, concat_axis=0, tiled=True)
    head_ids = jnp.arange(HEADS, dtype=jnp.int32)
    head_group = jnp.sum((flat_heads[None, :] == head_ids[:, None]).astype(jnp.int32), axis=1)
    row_rank = token_ids[:, None] % head_group[None, :]
    row_step = token_ids[:, None] // head_group[None, :]
    slot_ids = jnp.arange(flat_heads.shape[0], dtype=jnp.int32)
    matched = (flat_heads[None, None, :] == head_ids[None, :, None]) & (
        group_rank[None, None, :] == row_rank[:, :, None]
    )
    owner_slot = jnp.sum(jnp.where(matched, slot_ids[None, None, :], 0), axis=2)
    flat_index = owner_slot * row_cap + row_step
    returned_rows = returned.reshape(-1, HDIM)
    attended_home = returned_rows[flat_index].reshape(tok_dev, HEADS * HDIM)
    partner = partner_2(attended_home, "branch", 0)
    on_positive = lax.axis_index("branch") == 0
    own_value = attended_home.astype(jnp.float32)
    partner_value = partner.astype(jnp.float32)
    positive = jnp.where(on_positive, own_value, partner_value)
    negative = jnp.where(on_positive, partner_value, own_value)
    guided = GUIDE_SCALE * positive - (GUIDE_SCALE - 1.0) * negative
    magnitude = jnp.mean(jnp.abs(guided), axis=1, keepdims=True)
    normed = (guided / (magnitude + EPSILON)).astype(jnp.bfloat16)
    projected = jnp.dot(normed, out_weight, preferred_element_type=jnp.float32).astype(jnp.bfloat16)
    saved_rows = jnp.transpose(logsum, (1, 2, 0)).reshape(1, 1, slot_count, row_cap, seq_count)
    return (projected, saved_rows)


KERNEL_PARAMS = pltpu.CompilerParams(vmem_limit_bytes=16 * 1024 * 1024)


SPLIT = 2
WEIGHT_COPIES = 4
TABLE_PIECES = 3
SPLITTER = 65537.0


def swap_shards(array, offset):
    pairs = [(i, i ^ offset) for i in range(lax.axis_size("seq"))]
    return lax.ppermute(array, "seq", pairs)


def place_offsets(shard_count):
    line = list(range(0, shard_count, SPLIT))
    return line + [offset + 1 for offset in line]


def pack_kernel(query_hbm, key_hbm, value_hbm, own_ref, other_ref, copy_sems):
    tok_dev = own_ref.shape[0] // 3
    half_width = own_ref.shape[1]
    half = (lax.axis_index("seq") // SPLIT) % 2
    copies = []
    for target, place in ((other_ref, 1 - half), (own_ref, half)):
        columns = pl.ds(pl.multiple_of(place * half_width, half_width), half_width)
        for part, source in enumerate((key_hbm, value_hbm, query_hbm)):
            rows = pl.ds(part * tok_dev, tok_dev)
            copies.append(
                pltpu.make_async_copy(
                    source.at[0, :, columns], target.at[rows, :], copy_sems.at[len(copies)]
                )
            )
    for copy in copies:
        copy.start()
    for copy in copies:
        copy.wait()


def plan_kernel(
    weight_hbm,
    counts_hbm,
    head_hbm,
    after_ref,
    weight_ref,
    limits_ref,
    pick_ref,
    slot_head_ref,
    counts_ref,
    head_ref,
    copy_sems,
):
    tok_dev = after_ref.shape[0] // 3
    slot_count, shard_count = head_ref.shape
    shard = lax.axis_index("seq")
    copies = [
        pltpu.make_async_copy(counts_hbm, counts_ref, copy_sems.at[0]),
        pltpu.make_async_copy(head_hbm, head_ref, copy_sems.at[1]),
    ]
    share = weight_ref.shape[0] // WEIGHT_COPIES
    for number in range(WEIGHT_COPIES):
        rows = pl.ds(number * share, share)
        copies.append(
            pltpu.make_async_copy(
                weight_hbm.at[rows, :], weight_ref.at[rows, :], copy_sems.at[len(copies)]
            )
        )
    for copy in copies:
        copy.start()
    copies[0].wait()
    copies[1].wait()

    lane = lax.broadcasted_iota(jnp.int32, (1, limits_ref.shape[1]), 1)
    lane_limit = jnp.zeros(lane.shape, jnp.int32)
    for place, offset in enumerate(place_offsets(shard_count)):
        lane_limit = jnp.where(lane // tok_dev == place, counts_ref[shard ^ offset], lane_limit)
    limits_ref[0:1, :] = (lane % tok_dev < lane_limit).astype(jnp.int32)
    limits_ref[1:2, :] = jnp.full(lane.shape, counts_ref[shard], jnp.int32)
    limits_ref[2:3, :] = jnp.full(lane.shape, counts_ref[shard ^ SPLIT], jnp.int32)

    step = lax.broadcasted_iota(jnp.int32, (1, pick_ref.shape[2]), 1)
    for slot in range(slot_count):
        head = head_ref[slot, shard]
        group_size = jnp.int32(0)
        group_rank = jnp.int32(0)
        for other_shard in range(shard_count):
            for other_slot in range(slot_count):
                same = (head_ref[other_slot, other_shard] == head).astype(jnp.int32)
                before = other_shard * slot_count + other_slot < shard * slot_count + slot
                group_size = group_size + same
                group_rank = group_rank + same * before.astype(jnp.int32)
        served = group_rank + group_size * step
        for source in range(shard_count):
            pick_ref[slot, source : source + 1, :] = jnp.where(
                served < counts_ref[source], served + source * tok_dev, -1
            )
        slot_head_ref[slot] = jnp.full(slot_head_ref.shape[1:], head, jnp.int32)
    for copy in copies[2:]:
        copy.wait()


def part_blocks(half_heads, tok_dev):
    return -(-half_heads * TABLE_PIECES // tok_dev)


def gathered(set_refs, part, columns):
    tok_dev = set_refs[0].shape[0] // 3
    rows = pl.ds(part * tok_dev, tok_dev)
    return jnp.concatenate([ref[rows, columns] for ref in set_refs], axis=0)


def head_scores(query_rows, key_all):
    return lax.dot_general(
        query_rows, key_all, (((1,), (1,)), ((), ())), preferred_element_type=jnp.float32
    )


def attend_kernel(set_count, limits_ref, *refs):
    set_refs = refs[:set_count]
    keep_ref, message_ref, table_ref, lines_ref = refs[set_count:]
    tok_dev, half_width = keep_ref.shape
    half_heads = half_width // HDIM
    shard = lax.axis_index("seq")
    head_columns = [pl.ds(head * HDIM, HDIM) for head in range(half_heads)]
    key_valid = limits_ref[0:1, :] > 0

    all_scores = [
        head_scores(gathered(set_refs, 2, columns), gathered(set_refs, 0, columns))
        for columns in head_columns
    ]
    lane = lax.broadcasted_iota(jnp.int32, all_scores[0].shape, 1)
    lines = jnp.zeros(lane.shape, jnp.float32)
    served = []
    for head, scores in enumerate(all_scores):
        scores = jnp.where(key_valid, scores * (1.0 / math.sqrt(HDIM)), -jnp.inf)
        top_score = jnp.max(scores, axis=1, keepdims=True)
        weights = jnp.exp(scores - top_score)
        weight_sum = jnp.sum(weights, axis=1, keepdims=True)
        lines = jnp.where(lane == head, top_score + jnp.log(weight_sum), lines)
        served.append((weights[: 2 * tok_dev].astype(jnp.bfloat16), weight_sum[: 2 * tok_dev]))
    row = lax.broadcasted_iota(jnp.int32, (tok_dev, HDIM), 0)
    for columns, (rounded, weight_sum) in zip(head_columns, served):
        mixed = jnp.dot(
            rounded, gathered(set_refs, 1, columns), preferred_element_type=jnp.float32
        )
        attended = mixed / weight_sum
        kept = jnp.where(row < limits_ref[1:2, :HDIM], attended[:tok_dev], 0.0)
        sent = jnp.where(row < limits_ref[2:3, :HDIM], attended[tok_dev:], 0.0)
        keep_ref[:, columns] = kept.astype(jnp.bfloat16)
        message_ref[:, columns] = sent.astype(jnp.bfloat16)

    for place, offset in enumerate(place_offsets(set_count)):
        rows = pl.ds(pl.multiple_of((shard ^ offset) * tok_dev, tok_dev), tok_dev)
        lines_ref[rows, :] = lines[place * tok_dev : (place + 1) * tok_dev]
    table = jnp.transpose(lines_ref[...])[: table_ref.shape[0]]
    table_ref[...] = table
    row = lax.broadcasted_iota(jnp.int32, (tok_dev, lines.shape[0]), 0)
    blocks = [jnp.zeros(row.shape, jnp.float32) for _ in range(part_blocks(half_heads, tok_dev))]
    for head in range(half_heads):
        rest = jnp.broadcast_to(table[head : head + 1], row.shape)
        for piece in range(TABLE_PIECES):
            scaled = rest * SPLITTER
            part = scaled - (scaled - rest)
            block, at_row = divmod(head * TABLE_PIECES + piece, tok_dev)
            blocks[block] = jnp.where(row == at_row, part, blocks[block])
            rest = rest - part
    message_ref[:, pl.ds(half_width, len(blocks) * lines.shape[0])] = jnp.concatenate(
        blocks, axis=1
    ).astype(jnp.bfloat16)


def guidance(own, partner):
    on_positive = lax.axis_index("branch") == 0
    own_scale = jnp.where(on_positive, GUIDE_SCALE, 1.0 - GUIDE_SCALE)
    partner_scale = jnp.where(on_positive, 1.0 - GUIDE_SCALE, GUIDE_SCALE)
    return own_scale * own.astype(jnp.float32) + partner_scale * partner.astype(jnp.float32)


def half_product(guided, weight_ref, place):
    half_width = guided.shape[1]
    rows = pl.ds(pl.multiple_of(place * half_width, half_width), half_width)
    return jnp.dot(
        guided.astype(jnp.bfloat16), weight_ref[rows, :], preferred_element_type=jnp.float32
    )


def keep_kernel(keep_ref, partner_keep_ref, weight_ref, total_ref, size_ref):
    half = (lax.axis_index("seq") // SPLIT) % 2
    guided = guidance(keep_ref[...], partner_keep_ref[...])
    size = jnp.sum(jnp.abs(guided), axis=1, keepdims=True)
    size_ref[...] = jnp.broadcast_to(size, size_ref.shape)
    total_ref[...] = half_product(guided, weight_ref, half)


def project_kernel(
    total_ref,
    size_ref,
    message_ref,
    partner_back_ref,
    weight_ref,
    table_ref,
    pick_ref,
    slot_head_ref,
    projected_ref,
    saved_ref,
):
    tok_dev = message_ref.shape[0]
    half_width = weight_ref.shape[0] // 2
    half_heads = half_width // HDIM
    tokens = table_ref.shape[1]
    half = (lax.axis_index("seq") // SPLIT) % 2
    rows = pl.ds(0, half_width)
    guided = guidance(message_ref[:, rows], partner_back_ref[:, rows])
    size = size_ref[:, 0:1] + jnp.sum(jnp.abs(guided), axis=1, keepdims=True)
    magnitude = size / (2 * half_width)
    total = total_ref[...] + half_product(guided, weight_ref, 1 - half)
    projected_ref[...] = (total / (magnitude + EPSILON)).astype(jnp.bfloat16)

    parts = message_ref[:, pl.ds(half_width, message_ref.shape[1] - half_width)].astype(jnp.float32)
    others = []
    for head in range(half_heads):
        other = jnp.zeros((1, tokens), jnp.float32)
        for piece in range(TABLE_PIECES):
            block, at_row = divmod(head * TABLE_PIECES + piece, tok_dev)
            other = other + parts[at_row : at_row + 1, block * tokens : (block + 1) * tokens]
        others.append(other)
    for slot in range(saved_ref.shape[0]):
        slot_head = slot_head_ref[slot, 0:1, :]
        line = jnp.zeros((1, tokens), jnp.float32)
        for head in range(half_heads):
            line = jnp.where(slot_head == half * half_heads + head, table_ref[head : head + 1], line)
            line = jnp.where(slot_head == (1 - half) * half_heads + head, others[head], line)
        pick = pick_ref[slot]
        spread = jnp.broadcast_to(line, pick.shape)
        taken = jnp.take_along_axis(spread, jnp.maximum(pick, 0), axis=1)
        saved_ref[slot] = jnp.where(pick >= 0, taken, 0.0)[:, : saved_ref.shape[2]]


def per_device_halves(queries, key_rows, value_rows, counts, head_of, out_weight):
    seq_count = lax.axis_size("seq")
    tok_dev, width = queries.shape[1:]
    half_width = width // 2
    tokens = seq_count * tok_dev
    slot_count = head_of.shape[1]
    fewest = max(1, seq_count * slot_count // (2 * HEADS))
    row_cap = (tok_dev + fewest - 1) // fewest
    message_width = half_width + part_blocks(half_width // HDIM, tok_dev) * tokens
    any_spec = pl.BlockSpec(memory_space=pl.ANY)
    vmem = pl.BlockSpec(memory_space=pltpu.VMEM)

    def held(*arrays):
        return [pltpu.with_memory_space_constraint(array, pltpu.VMEM) for array in arrays]

    def distant(*arrays):
        return [pltpu.with_memory_space_constraint(array, pltpu.HBM) for array in arrays]

    own, other = pl.pallas_call(
        pack_kernel,
        out_shape=[pltpu.VMEM((3 * tok_dev, half_width), jnp.bfloat16)] * 2,
        in_specs=[any_spec] * 3,
        out_specs=[vmem] * 2,
        scratch_shapes=[pltpu.SemaphoreType.DMA((6,))],
        compiler_params=KERNEL_PARAMS,
        name="pack",
    )(*distant(queries, key_rows, value_rows))
    weight_held, limits, pick, slot_head = pl.pallas_call(
        plan_kernel,
        out_shape=[
            pltpu.VMEM(out_weight.shape, jnp.bfloat16),
            pltpu.VMEM((8, tokens), jnp.int32),
            pltpu.VMEM((slot_count, seq_count, tokens), jnp.int32),
            pltpu.VMEM((slot_count, 8, tokens), jnp.int32),
        ],
        in_specs=[any_spec] * 3 + [vmem],
        out_specs=[vmem] * 4,
        scratch_shapes=[
            pltpu.SMEM((seq_count,), jnp.int32),
            pltpu.SMEM((slot_count, seq_count), jnp.int32),
            pltpu.SemaphoreType.DMA((2 + WEIGHT_COPIES,)),
        ],
        compiler_params=KERNEL_PARAMS,
        cost_estimate=pl.CostEstimate(
            flops=0, bytes_accessed=4 * out_weight.size, transcendentals=0
        ),
        name="plan",
    )(*distant(out_weight, counts, jnp.transpose(head_of)), *held(own))
    line = [own] + [
        swap_shards(other if offset & SPLIT else own, offset)
        for offset in range(SPLIT, seq_count, SPLIT)
    ]
    sets = line + [swap_shards(array, 1) for array in line]
    keep, message, table = pl.pallas_call(
        functools.partial(attend_kernel, len(sets)),
        out_shape=[
            pltpu.VMEM((tok_dev, half_width), jnp.bfloat16),
            pltpu.VMEM((tok_dev, message_width), jnp.bfloat16),
            pltpu.VMEM((half_width // HDIM + 7 & -8, tokens), jnp.float32),
        ],
        in_specs=[vmem] * (1 + len(sets)),
        out_specs=[vmem] * 3,
        scratch_shapes=[pltpu.VMEM((tokens, HDIM), jnp.float32)],
        compiler_params=KERNEL_PARAMS,
        name="attend",
    )(*held(limits, *sets))
    across = [(2 * i + b, 2 * (i ^ SPLIT) + 1 - b) for i in range(seq_count) for b in range(2)]
    partner_back = lax.ppermute(message, ("seq", "branch"), across)
    partner_keep = partner_2(keep, "branch", 0)
    back = swap_shards(message, SPLIT)
    total, size = pl.pallas_call(
        keep_kernel,
        out_shape=[
            pltpu.VMEM((tok_dev, out_weight.shape[1]), jnp.float32),
            pltpu.VMEM((tok_dev, HDIM), jnp.float32),
        ],
        in_specs=[vmem] * 3,
        out_specs=[vmem] * 2,
        compiler_params=KERNEL_PARAMS,
        name="keep",
    )(*held(keep, partner_keep, weight_held))
    projected, saved = pl.pallas_call(
        project_kernel,
        out_shape=[
            jax.ShapeDtypeStruct((tok_dev, out_weight.shape[1]), jnp.bfloat16),
            jax.ShapeDtypeStruct((slot_count, seq_count, row_cap), jnp.float32),
        ],
        in_specs=[vmem] * 8,
        out_specs=[vmem] * 2,
        compiler_params=KERNEL_PARAMS,
        name="project",
    )(*held(total, size, back, partner_back, weight_held, table, pick, slot_head))
    saved = jnp.transpose(saved, (0, 2, 1))
    return (projected, saved.reshape(1, 1, slot_count, row_cap, seq_count))


def solution(mesh):
    seq_count = mesh.shape["seq"]
    hypercube = seq_count > SPLIT and seq_count & (seq_count - 1) == 0
    small = hypercube and seq_count <= HEADS
    return jax.shard_map(
        per_device_halves if small else per_device_exchange,
        mesh=mesh,
        in_specs=(
            P("branch", ("groups", "seq"), None),
            P("branch", ("groups", "seq"), None),
            P("branch", ("groups", "seq"), None),
            P("groups"),
            P(),
            P(None, "branch"),
        ),
        out_specs=(
            P(("groups", "seq"), "branch"),
            P("branch", ("groups", "seq"), None, None, None),
        ),
        check_vma=False,
    )
```

```python
import functools
import math

import jax
import jax.numpy as jnp
from jax import lax
from jax.experimental import pallas as pl
from jax.experimental.pallas import tpu as pltpu
from jax.sharding import PartitionSpec as P

HEADS = 12
HDIM = 128


GUIDE_SCALE = 3.0
EPSILON = 1e-06


def partner_2(array, axis, stride):
    return lax.ppermute(array, axis, [(i, i ^ 1 << stride) for i in range(lax.axis_size(axis))])


def slot_layout(head_of):
    flat_heads = head_of.reshape(-1)
    slot_order = jnp.arange(flat_heads.shape[0], dtype=jnp.int32)
    same_head = flat_heads[:, None] == flat_heads[None, :]
    group_size = jnp.sum(same_head.astype(jnp.int32), axis=1)
    earlier = same_head & (slot_order[None, :] < slot_order[:, None])
    group_rank = jnp.sum(earlier.astype(jnp.int32), axis=1)
    return (flat_heads, group_size, group_rank)


def key_grouping(seq_count, tok_dev):
    shard_limit = max(1, 2048 // tok_dev)
    grouping = 1
    for attempt in range(16):
        if grouping * 2 <= shard_limit and seq_count % (grouping * 2) == 0:
            grouping = grouping * 2
    return grouping


def attend_rows(query_block, key_slot, value_slot, key_valid, key_block):
    row_count = query_block.shape[0]
    head_size = query_block.shape[1]
    block_count = key_slot.shape[0] // key_block
    scale_factor = 1.0 / math.sqrt(head_size)

    def fold_block(block_id, state_in):
        top_score, weight_sum, summed = state_in
        scores = (
            jnp.einsum("qd,kd->qk", query_block, key_slot, preferred_element_type=jnp.float32)
            * scale_factor
        )
        scores = jnp.where(key_valid[None, :], scores, -jnp.inf)
        new_top = jnp.maximum(top_score, jnp.max(scores, axis=1))
        fading = jnp.exp(top_score - new_top)
        weights = jnp.exp(scores - new_top[:, None])
        weight_sum = weight_sum * fading + jnp.sum(weights, axis=1)
        summed = summed * fading[:, None] + jnp.dot(
            weights.astype(jnp.bfloat16), value_slot, preferred_element_type=jnp.float32
        )
        return (new_top, weight_sum, summed)

    start_state = (
        jnp.full((row_count,), -jnp.inf, jnp.float32),
        jnp.zeros((row_count,), jnp.float32),
        jnp.zeros((row_count, head_size), jnp.float32),
    )
    top_score, weight_sum, summed = lax.fori_loop(0, block_count, fold_block, start_state)
    return (summed / weight_sum[:, None], top_score + jnp.log(weight_sum))


def serve_slots(query_items, mask_items, key_recv, value_recv, key_valid, key_block):
    source_count, slot_count, item_count, head_size = query_items.shape
    all_tokens = key_recv.shape[0] * key_recv.shape[2]
    per_block = max(1, 512 // source_count)
    slot_outputs = []
    slot_logsum = []
    for slot_id in range(slot_count):
        key_slot = key_recv[:, slot_id].reshape(all_tokens, head_size)
        value_slot = value_recv[:, slot_id].reshape(all_tokens, head_size)
        taken_items = min(per_block, item_count)
        query_block = query_items[:, slot_id, 0:taken_items].reshape(
            source_count * taken_items, head_size
        )
        attended, logsum = attend_rows(query_block, key_slot, value_slot, key_valid, key_block)
        pieces_out = attended.reshape(source_count, taken_items, head_size)
        pieces_sum = logsum.reshape(source_count, taken_items)
        slot_outputs.append(pieces_out)
        slot_logsum.append(pieces_sum)
    attended = jnp.stack(slot_outputs, axis=1)
    logsum = jnp.stack(slot_logsum, axis=1)
    keep_rows = mask_items > 0
    attended = jnp.where(keep_rows[:, :, :, None], attended, 0.0).astype(jnp.bfloat16)
    logsum = jnp.where(keep_rows, logsum, 0.0)
    return (attended, logsum)


def per_device_exchange(queries, key_rows, value_rows, counts, head_of, out_weight):
    seq_count = lax.axis_size("seq")
    tok_dev = queries.shape[1]
    slot_count = head_of.shape[1]
    fewest = max(1, seq_count * slot_count // (2 * HEADS))
    row_cap = (tok_dev + fewest - 1) // fewest
    my_index = lax.axis_index("seq")
    flat_heads, group_size, group_rank = slot_layout(head_of)
    row_steps = jnp.arange(row_cap, dtype=jnp.int32)
    served_rows = group_rank[:, None] + group_size[:, None] * row_steps[None, :]
    my_count = counts[my_index]
    clipped = jnp.minimum(served_rows, tok_dev - 1)
    query_grid = queries[0].reshape(tok_dev, HEADS, HDIM)
    row_live = served_rows < my_count
    query_send = query_grid[clipped, flat_heads[:, None]]
    query_send = jnp.where(row_live[:, :, None], query_send, jnp.zeros((), jnp.bfloat16)).reshape(
        seq_count, slot_count, row_cap, HDIM
    )
    mask_send = row_live.astype(jnp.bfloat16).reshape(seq_count, slot_count, row_cap)
    token_ids = jnp.arange(tok_dev, dtype=jnp.int32)
    key_grid = key_rows[0].reshape(tok_dev, HEADS, HDIM)
    value_grid = value_rows[0].reshape(tok_dev, HEADS, HDIM)
    key_send = key_grid[token_ids[None, :], flat_heads[:, None]].reshape(
        seq_count, slot_count, tok_dev, HDIM
    )
    value_send = value_grid[token_ids[None, :], flat_heads[:, None]].reshape(
        seq_count, slot_count, tok_dev, HDIM
    )
    key_valid = (token_ids[None, :] < counts[:, None]).reshape(-1)
    key_block = tok_dev * key_grouping(seq_count, tok_dev)
    query_recv, mask_recv, key_recv, value_recv = (
        lax.all_to_all(query_send, "seq", split_axis=0, concat_axis=0, tiled=True),
        lax.all_to_all(mask_send, "seq", split_axis=0, concat_axis=0, tiled=True),
        lax.all_to_all(key_send, "seq", split_axis=0, concat_axis=0, tiled=True),
        lax.all_to_all(value_send, "seq", split_axis=0, concat_axis=0, tiled=True),
    )
    attended, logsum = serve_slots(
        query_recv, mask_recv, key_recv, value_recv, key_valid, key_block
    )
    returned = lax.all_to_all(attended, "seq", split_axis=0, concat_axis=0, tiled=True)
    head_ids = jnp.arange(HEADS, dtype=jnp.int32)
    head_group = jnp.sum((flat_heads[None, :] == head_ids[:, None]).astype(jnp.int32), axis=1)
    row_rank = token_ids[:, None] % head_group[None, :]
    row_step = token_ids[:, None] // head_group[None, :]
    slot_ids = jnp.arange(flat_heads.shape[0], dtype=jnp.int32)
    matched = (flat_heads[None, None, :] == head_ids[None, :, None]) & (
        group_rank[None, None, :] == row_rank[:, :, None]
    )
    owner_slot = jnp.sum(jnp.where(matched, slot_ids[None, None, :], 0), axis=2)
    flat_index = owner_slot * row_cap + row_step
    returned_rows = returned.reshape(-1, HDIM)
    attended_home = returned_rows[flat_index].reshape(tok_dev, HEADS * HDIM)
    partner = partner_2(attended_home, "branch", 0)
    on_positive = lax.axis_index("branch") == 0
    own_value = attended_home.astype(jnp.float32)
    partner_value = partner.astype(jnp.float32)
    positive = jnp.where(on_positive, own_value, partner_value)
    negative = jnp.where(on_positive, partner_value, own_value)
    guided = GUIDE_SCALE * positive - (GUIDE_SCALE - 1.0) * negative
    magnitude = jnp.mean(jnp.abs(guided), axis=1, keepdims=True)
    normed = (guided / (magnitude + EPSILON)).astype(jnp.bfloat16)
    projected = jnp.dot(normed, out_weight, preferred_element_type=jnp.float32).astype(jnp.bfloat16)
    saved_rows = jnp.transpose(logsum, (1, 2, 0)).reshape(1, 1, slot_count, row_cap, seq_count)
    return (projected, saved_rows)


KERNEL_PARAMS = pltpu.CompilerParams(vmem_limit_bytes=16 * 1024 * 1024)


SPLIT = 2
HOLD_COPIES = 4
TABLE_PIECES = 3
SPLITTER = 65537.0


def swap_shards(array, offset):
    pairs = [(i, i ^ offset) for i in range(lax.axis_size("seq"))]
    return lax.ppermute(array, "seq", pairs)


FAR = 2 * SPLIT
NEXT = 1
THIRD = (NEXT, FAR)
FOURTH = (FAR, NEXT)


def swap_by_core(array, offsets):
    pairs = [
        (2 * i + core, 2 * (i ^ offsets[core]) + core)
        for i in range(lax.axis_size("seq"))
        for core in range(2)
    ]
    return lax.ppermute(array, ("seq", "branch"), pairs)


def by_core(first, second):
    return jnp.where(lax.axis_index("branch") == 0, first, second)


def place_offsets():
    received = [0, SPLIT, SPLIT + FAR, by_core(*THIRD), by_core(*FOURTH)]
    return received + [offset + NEXT for offset in (SPLIT, SPLIT + FAR, FAR)]


def pack_kernel(
    query_hbm,
    key_hbm,
    value_hbm,
    counts_hbm,
    head_hbm,
    own_ref,
    other_ref,
    limits_ref,
    pick_ref,
    slot_head_ref,
    counts_ref,
    head_ref,
    copy_sems,
):
    tok_dev = own_ref.shape[0] // 3
    half_width = own_ref.shape[1]
    slot_count, shard_count = head_ref.shape
    shard = lax.axis_index("seq")
    half = (shard // SPLIT) % 2
    copies = [
        pltpu.make_async_copy(counts_hbm, counts_ref, copy_sems.at[0]),
        pltpu.make_async_copy(head_hbm, head_ref, copy_sems.at[1]),
    ]
    for target, place in ((other_ref, 1 - half), (own_ref, half)):
        columns = pl.ds(pl.multiple_of(place * half_width, half_width), half_width)
        for part, source in enumerate((key_hbm, value_hbm, query_hbm)):
            rows = pl.ds(part * tok_dev, tok_dev)
            copies.append(
                pltpu.make_async_copy(
                    source.at[0, :, columns], target.at[rows, :], copy_sems.at[len(copies)]
                )
            )
    for copy in copies:
        copy.start()
    copies[0].wait()
    copies[1].wait()

    lane = lax.broadcasted_iota(jnp.int32, (1, limits_ref.shape[1]), 1)
    lane_limit = jnp.zeros(lane.shape, jnp.int32)
    for place, offset in enumerate(place_offsets()):
        lane_limit = jnp.where(lane // tok_dev == place, counts_ref[shard ^ offset], lane_limit)
    limits_ref[0:1, :] = (lane % tok_dev < lane_limit).astype(jnp.int32)
    limits_ref[1:2, :] = jnp.full(lane.shape, counts_ref[shard], jnp.int32)
    limits_ref[2:3, :] = jnp.full(lane.shape, counts_ref[shard ^ SPLIT], jnp.int32)

    step = lax.broadcasted_iota(jnp.int32, (1, pick_ref.shape[2]), 1)
    for slot in range(slot_count):
        head = head_ref[slot, shard]
        group_size = jnp.int32(0)
        group_rank = jnp.int32(0)
        for other_shard in range(shard_count):
            for other_slot in range(slot_count):
                same = (head_ref[other_slot, other_shard] == head).astype(jnp.int32)
                before = other_shard * slot_count + other_slot < shard * slot_count + slot
                group_size = group_size + same
                group_rank = group_rank + same * before.astype(jnp.int32)
        served = group_rank + group_size * step
        for source in range(shard_count):
            pick_ref[slot, source : source + 1, :] = jnp.where(
                served < counts_ref[source], served + source * tok_dev, -1
            )
        slot_head_ref[slot] = jnp.full(slot_head_ref.shape[1:], head, jnp.int32)
    for copy in copies[2:]:
        copy.wait()


def hold_kernel(weight_hbm, after_ref, weight_ref, copy_sems):
    share = weight_ref.shape[0] // HOLD_COPIES
    copies = []
    for number in range(HOLD_COPIES):
        rows = pl.ds(number * share, share)
        copies.append(
            pltpu.make_async_copy(
                weight_hbm.at[rows, :], weight_ref.at[rows, :], copy_sems.at[number]
            )
        )
    for copy in copies:
        copy.start()
    for copy in copies:
        copy.wait()


def part_blocks(half_heads, tok_dev):
    return -(-half_heads * TABLE_PIECES // tok_dev)


def gathered(set_refs, part, columns):
    tok_dev = set_refs[0].shape[0] // 3
    rows = pl.ds(part * tok_dev, tok_dev)
    return jnp.concatenate([ref[rows, columns] for ref in set_refs], axis=0)


def head_scores(query_rows, key_all):
    return lax.dot_general(
        query_rows, key_all, (((1,), (1,)), ((), ())), preferred_element_type=jnp.float32
    )


def attend_kernel(set_count, limits_ref, *refs):
    set_refs = refs[:set_count]
    keep_ref, message_ref, table_ref, lines_ref = refs[set_count:]
    tok_dev, half_width = keep_ref.shape
    half_heads = half_width // HDIM
    shard = lax.axis_index("seq")
    head_columns = [pl.ds(head * HDIM, HDIM) for head in range(half_heads)]
    key_valid = limits_ref[0:1, :] > 0

    all_scores = [
        head_scores(gathered(set_refs, 2, columns), gathered(set_refs, 0, columns))
        for columns in head_columns
    ]
    lane = lax.broadcasted_iota(jnp.int32, all_scores[0].shape, 1)
    lines = jnp.zeros(lane.shape, jnp.float32)
    served = []
    for head, scores in enumerate(all_scores):
        scores = jnp.where(key_valid, scores * (1.0 / math.sqrt(HDIM)), -jnp.inf)
        top_score = jnp.max(scores, axis=1, keepdims=True)
        weights = jnp.exp(scores - top_score)
        weight_sum = jnp.sum(weights, axis=1, keepdims=True)
        lines = jnp.where(lane == head, top_score + jnp.log(weight_sum), lines)
        served.append((weights[: 2 * tok_dev].astype(jnp.bfloat16), weight_sum[: 2 * tok_dev]))
    row = lax.broadcasted_iota(jnp.int32, (tok_dev, HDIM), 0)
    for columns, (rounded, weight_sum) in zip(head_columns, served):
        mixed = jnp.dot(
            rounded, gathered(set_refs, 1, columns), preferred_element_type=jnp.float32
        )
        attended = mixed / weight_sum
        kept = jnp.where(row < limits_ref[1:2, :HDIM], attended[:tok_dev], 0.0)
        sent = jnp.where(row < limits_ref[2:3, :HDIM], attended[tok_dev:], 0.0)
        keep_ref[:, columns] = kept.astype(jnp.bfloat16)
        message_ref[:, columns] = sent.astype(jnp.bfloat16)

    for place, offset in enumerate(place_offsets()):
        rows = pl.ds(pl.multiple_of((shard ^ offset) * tok_dev, tok_dev), tok_dev)
        lines_ref[rows, :] = lines[place * tok_dev : (place + 1) * tok_dev]
    table = jnp.transpose(lines_ref[...])[: table_ref.shape[0]]
    table_ref[...] = table
    row = lax.broadcasted_iota(jnp.int32, (tok_dev, lines.shape[0]), 0)
    blocks = [jnp.zeros(row.shape, jnp.float32) for _ in range(part_blocks(half_heads, tok_dev))]
    for head in range(half_heads):
        rest = jnp.broadcast_to(table[head : head + 1], row.shape)
        for piece in range(TABLE_PIECES):
            scaled = rest * SPLITTER
            part = scaled - (scaled - rest)
            block, at_row = divmod(head * TABLE_PIECES + piece, tok_dev)
            blocks[block] = jnp.where(row == at_row, part, blocks[block])
            rest = rest - part
    message_ref[:, pl.ds(half_width, len(blocks) * lines.shape[0])] = jnp.concatenate(
        blocks, axis=1
    ).astype(jnp.bfloat16)


def guidance(own, partner):
    on_positive = lax.axis_index("branch") == 0
    own_scale = jnp.where(on_positive, GUIDE_SCALE, 1.0 - GUIDE_SCALE)
    partner_scale = jnp.where(on_positive, 1.0 - GUIDE_SCALE, GUIDE_SCALE)
    return own_scale * own.astype(jnp.float32) + partner_scale * partner.astype(jnp.float32)


def half_product(guided, weight_ref, place):
    half_width = guided.shape[1]
    rows = pl.ds(pl.multiple_of(place * half_width, half_width), half_width)
    return jnp.dot(
        guided.astype(jnp.bfloat16), weight_ref[rows, :], preferred_element_type=jnp.float32
    )


def keep_kernel(keep_ref, partner_keep_ref, weight_ref, total_ref, size_ref):
    half = (lax.axis_index("seq") // SPLIT) % 2
    guided = guidance(keep_ref[...], partner_keep_ref[...])
    size = jnp.sum(jnp.abs(guided), axis=1, keepdims=True)
    size_ref[...] = jnp.broadcast_to(size, size_ref.shape)
    total_ref[...] = half_product(guided, weight_ref, half)


def project_kernel(
    total_ref,
    size_ref,
    message_ref,
    partner_back_ref,
    weight_ref,
    table_ref,
    pick_ref,
    slot_head_ref,
    projected_ref,
    saved_ref,
):
    tok_dev = message_ref.shape[0]
    half_width = weight_ref.shape[0] // 2
    half_heads = half_width // HDIM
    tokens = table_ref.shape[1]
    half = (lax.axis_index("seq") // SPLIT) % 2
    rows = pl.ds(0, half_width)
    guided = guidance(message_ref[:, rows], partner_back_ref[:, rows])
    size = size_ref[:, 0:1] + jnp.sum(jnp.abs(guided), axis=1, keepdims=True)
    magnitude = size / (2 * half_width)
    total = total_ref[...] + half_product(guided, weight_ref, 1 - half)
    projected_ref[...] = (total / (magnitude + EPSILON)).astype(jnp.bfloat16)

    parts = message_ref[:, pl.ds(half_width, message_ref.shape[1] - half_width)].astype(jnp.float32)
    others = []
    for head in range(half_heads):
        other = jnp.zeros((1, tokens), jnp.float32)
        for piece in range(TABLE_PIECES):
            block, at_row = divmod(head * TABLE_PIECES + piece, tok_dev)
            other = other + parts[at_row : at_row + 1, block * tokens : (block + 1) * tokens]
        others.append(other)
    for slot in range(saved_ref.shape[0]):
        slot_head = slot_head_ref[slot, 0:1, :]
        line = jnp.zeros((1, tokens), jnp.float32)
        for head in range(half_heads):
            line = jnp.where(slot_head == half * half_heads + head, table_ref[head : head + 1], line)
            line = jnp.where(slot_head == (1 - half) * half_heads + head, others[head], line)
        pick = pick_ref[slot]
        spread = jnp.broadcast_to(line, pick.shape)
        taken = jnp.take_along_axis(spread, jnp.maximum(pick, 0), axis=1)
        saved_ref[slot] = jnp.where(pick >= 0, taken, 0.0)[:, : saved_ref.shape[2]]


def per_device_halves(queries, key_rows, value_rows, counts, head_of, out_weight):
    seq_count = lax.axis_size("seq")
    tok_dev, width = queries.shape[1:]
    half_width = width // 2
    tokens = seq_count * tok_dev
    slot_count = head_of.shape[1]
    fewest = max(1, seq_count * slot_count // (2 * HEADS))
    row_cap = (tok_dev + fewest - 1) // fewest
    message_width = half_width + part_blocks(half_width // HDIM, tok_dev) * tokens
    any_spec = pl.BlockSpec(memory_space=pl.ANY)
    vmem = pl.BlockSpec(memory_space=pltpu.VMEM)

    def held(*arrays):
        return [pltpu.with_memory_space_constraint(array, pltpu.VMEM) for array in arrays]

    def distant(*arrays):
        return [pltpu.with_memory_space_constraint(array, pltpu.HBM) for array in arrays]

    own, other, limits, pick, slot_head = pl.pallas_call(
        pack_kernel,
        out_shape=[
            pltpu.VMEM((3 * tok_dev, half_width), jnp.bfloat16),
            pltpu.VMEM((3 * tok_dev, half_width), jnp.bfloat16),
            pltpu.VMEM((8, tokens), jnp.int32),
            pltpu.VMEM((slot_count, seq_count, tokens), jnp.int32),
            pltpu.VMEM((slot_count, 8, tokens), jnp.int32),
        ],
        in_specs=[any_spec] * 5,
        out_specs=[vmem] * 5,
        scratch_shapes=[
            pltpu.SMEM((seq_count,), jnp.int32),
            pltpu.SMEM((slot_count, seq_count), jnp.int32),
            pltpu.SemaphoreType.DMA((8,)),
        ],
        compiler_params=KERNEL_PARAMS,
        name="pack",
    )(*distant(queries, key_rows, value_rows, counts, jnp.transpose(head_of)))

    weight_held = pl.pallas_call(
        hold_kernel,
        out_shape=pltpu.VMEM(out_weight.shape, jnp.bfloat16),
        in_specs=[any_spec, vmem],
        out_specs=vmem,
        scratch_shapes=[pltpu.SemaphoreType.DMA((HOLD_COPIES,))],
        compiler_params=KERNEL_PARAMS,
        cost_estimate=pl.CostEstimate(
            flops=0, bytes_accessed=4 * out_weight.size, transcendentals=0
        ),
        name="hold",
    )(*distant(out_weight), *held(limits))
    near = swap_shards(other, SPLIT)
    across_line = swap_shards(other, SPLIT + FAR)
    third = swap_by_core(own, THIRD)
    fourth = swap_by_core(own, FOURTH)
    far = by_core(fourth, third)
    passed_on = [swap_shards(array, NEXT) for array in (near, across_line, far)]
    sets = [own, near, across_line, third, fourth] + passed_on
    limits, weight_held = lax.optimization_barrier((limits, weight_held))
    keep, message, table = pl.pallas_call(
        functools.partial(attend_kernel, len(sets)),
        out_shape=[
            pltpu.VMEM((tok_dev, half_width), jnp.bfloat16),
            pltpu.VMEM((tok_dev, message_width), jnp.bfloat16),
            pltpu.VMEM((half_width // HDIM + 7 & -8, tokens), jnp.float32),
        ],
        in_specs=[vmem] * (1 + len(sets)),
        out_specs=[vmem] * 3,
        scratch_shapes=[pltpu.VMEM((tokens, HDIM), jnp.float32)],
        compiler_params=KERNEL_PARAMS,
        name="attend",
    )(*held(limits, *sets))
    across = [(2 * i + b, 2 * (i ^ SPLIT) + 1 - b) for i in range(seq_count) for b in range(2)]
    partner_back = lax.ppermute(message, ("seq", "branch"), across)
    partner_keep = partner_2(keep, "branch", 0)
    back = swap_shards(message, SPLIT)
    total, size = pl.pallas_call(
        keep_kernel,
        out_shape=[
            pltpu.VMEM((tok_dev, out_weight.shape[1]), jnp.float32),
            pltpu.VMEM((tok_dev, HDIM), jnp.float32),
        ],
        in_specs=[vmem] * 3,
        out_specs=[vmem] * 2,
        compiler_params=KERNEL_PARAMS,
        name="keep",
    )(*held(keep, partner_keep, weight_held))
    projected, saved = pl.pallas_call(
        project_kernel,
        out_shape=[
            jax.ShapeDtypeStruct((tok_dev, out_weight.shape[1]), jnp.bfloat16),
            jax.ShapeDtypeStruct((slot_count, seq_count, row_cap), jnp.float32),
        ],
        in_specs=[vmem] * 8,
        out_specs=[vmem] * 2,
        compiler_params=KERNEL_PARAMS,
        name="project",
    )(*held(total, size, back, partner_back, weight_held, table, pick, slot_head))
    saved = jnp.transpose(saved, (0, 2, 1))
    return (projected, saved.reshape(1, 1, slot_count, row_cap, seq_count))


def solution(mesh):
    seq_count = mesh.shape["seq"]
    small = seq_count == 2 * FAR
    return jax.shard_map(
        per_device_halves if small else per_device_exchange,
        mesh=mesh,
        in_specs=(
            P("branch", ("groups", "seq"), None),
            P("branch", ("groups", "seq"), None),
            P("branch", ("groups", "seq"), None),
            P("groups"),
            P(),
            P(None, "branch"),
        ),
        out_specs=(
            P(("groups", "seq"), "branch"),
            P("branch", ("groups", "seq"), None, None, None),
        ),
        check_vma=False,
    )
```

```python
import functools
import math

import jax
import jax.numpy as jnp
from jax import lax
from jax.experimental import pallas as pl
from jax.experimental.pallas import tpu as pltpu
from jax.sharding import PartitionSpec as P

HEADS = 12
HDIM = 128


GUIDE_SCALE = 3.0
EPSILON = 1e-06


def partner_2(array, axis, stride):
    return lax.ppermute(array, axis, [(i, i ^ 1 << stride) for i in range(lax.axis_size(axis))])


def slot_layout(head_of):
    flat_heads = head_of.reshape(-1)
    slot_order = jnp.arange(flat_heads.shape[0], dtype=jnp.int32)
    same_head = flat_heads[:, None] == flat_heads[None, :]
    group_size = jnp.sum(same_head.astype(jnp.int32), axis=1)
    earlier = same_head & (slot_order[None, :] < slot_order[:, None])
    group_rank = jnp.sum(earlier.astype(jnp.int32), axis=1)
    return (flat_heads, group_size, group_rank)


def key_grouping(seq_count, tok_dev):
    shard_limit = max(1, 2048 // tok_dev)
    grouping = 1
    for attempt in range(16):
        if grouping * 2 <= shard_limit and seq_count % (grouping * 2) == 0:
            grouping = grouping * 2
    return grouping


def attend_rows(query_block, key_slot, value_slot, key_valid, key_block):
    row_count = query_block.shape[0]
    head_size = query_block.shape[1]
    block_count = key_slot.shape[0] // key_block
    scale_factor = 1.0 / math.sqrt(head_size)

    def fold_block(block_id, state_in):
        top_score, weight_sum, summed = state_in
        scores = (
            jnp.einsum("qd,kd->qk", query_block, key_slot, preferred_element_type=jnp.float32)
            * scale_factor
        )
        scores = jnp.where(key_valid[None, :], scores, -jnp.inf)
        new_top = jnp.maximum(top_score, jnp.max(scores, axis=1))
        fading = jnp.exp(top_score - new_top)
        weights = jnp.exp(scores - new_top[:, None])
        weight_sum = weight_sum * fading + jnp.sum(weights, axis=1)
        summed = summed * fading[:, None] + jnp.dot(
            weights.astype(jnp.bfloat16), value_slot, preferred_element_type=jnp.float32
        )
        return (new_top, weight_sum, summed)

    start_state = (
        jnp.full((row_count,), -jnp.inf, jnp.float32),
        jnp.zeros((row_count,), jnp.float32),
        jnp.zeros((row_count, head_size), jnp.float32),
    )
    top_score, weight_sum, summed = lax.fori_loop(0, block_count, fold_block, start_state)
    return (summed / weight_sum[:, None], top_score + jnp.log(weight_sum))


def serve_slots(query_items, mask_items, key_recv, value_recv, key_valid, key_block):
    source_count, slot_count, item_count, head_size = query_items.shape
    all_tokens = key_recv.shape[0] * key_recv.shape[2]
    per_block = max(1, 512 // source_count)
    slot_outputs = []
    slot_logsum = []
    for slot_id in range(slot_count):
        key_slot = key_recv[:, slot_id].reshape(all_tokens, head_size)
        value_slot = value_recv[:, slot_id].reshape(all_tokens, head_size)
        taken_items = min(per_block, item_count)
        query_block = query_items[:, slot_id, 0:taken_items].reshape(
            source_count * taken_items, head_size
        )
        attended, logsum = attend_rows(query_block, key_slot, value_slot, key_valid, key_block)
        pieces_out = attended.reshape(source_count, taken_items, head_size)
        pieces_sum = logsum.reshape(source_count, taken_items)
        slot_outputs.append(pieces_out)
        slot_logsum.append(pieces_sum)
    attended = jnp.stack(slot_outputs, axis=1)
    logsum = jnp.stack(slot_logsum, axis=1)
    keep_rows = mask_items > 0
    attended = jnp.where(keep_rows[:, :, :, None], attended, 0.0).astype(jnp.bfloat16)
    logsum = jnp.where(keep_rows, logsum, 0.0)
    return (attended, logsum)


def per_device_exchange(queries, key_rows, value_rows, counts, head_of, out_weight):
    seq_count = lax.axis_size("seq")
    tok_dev = queries.shape[1]
    slot_count = head_of.shape[1]
    fewest = max(1, seq_count * slot_count // (2 * HEADS))
    row_cap = (tok_dev + fewest - 1) // fewest
    my_index = lax.axis_index("seq")
    flat_heads, group_size, group_rank = slot_layout(head_of)
    row_steps = jnp.arange(row_cap, dtype=jnp.int32)
    served_rows = group_rank[:, None] + group_size[:, None] * row_steps[None, :]
    my_count = counts[my_index]
    clipped = jnp.minimum(served_rows, tok_dev - 1)
    query_grid = queries[0].reshape(tok_dev, HEADS, HDIM)
    row_live = served_rows < my_count
    query_send = query_grid[clipped, flat_heads[:, None]]
    query_send = jnp.where(row_live[:, :, None], query_send, jnp.zeros((), jnp.bfloat16)).reshape(
        seq_count, slot_count, row_cap, HDIM
    )
    mask_send = row_live.astype(jnp.bfloat16).reshape(seq_count, slot_count, row_cap)
    token_ids = jnp.arange(tok_dev, dtype=jnp.int32)
    key_grid = key_rows[0].reshape(tok_dev, HEADS, HDIM)
    value_grid = value_rows[0].reshape(tok_dev, HEADS, HDIM)
    key_send = key_grid[token_ids[None, :], flat_heads[:, None]].reshape(
        seq_count, slot_count, tok_dev, HDIM
    )
    value_send = value_grid[token_ids[None, :], flat_heads[:, None]].reshape(
        seq_count, slot_count, tok_dev, HDIM
    )
    key_valid = (token_ids[None, :] < counts[:, None]).reshape(-1)
    key_block = tok_dev * key_grouping(seq_count, tok_dev)
    query_recv, mask_recv, key_recv, value_recv = (
        lax.all_to_all(query_send, "seq", split_axis=0, concat_axis=0, tiled=True),
        lax.all_to_all(mask_send, "seq", split_axis=0, concat_axis=0, tiled=True),
        lax.all_to_all(key_send, "seq", split_axis=0, concat_axis=0, tiled=True),
        lax.all_to_all(value_send, "seq", split_axis=0, concat_axis=0, tiled=True),
    )
    attended, logsum = serve_slots(
        query_recv, mask_recv, key_recv, value_recv, key_valid, key_block
    )
    returned = lax.all_to_all(attended, "seq", split_axis=0, concat_axis=0, tiled=True)
    head_ids = jnp.arange(HEADS, dtype=jnp.int32)
    head_group = jnp.sum((flat_heads[None, :] == head_ids[:, None]).astype(jnp.int32), axis=1)
    row_rank = token_ids[:, None] % head_group[None, :]
    row_step = token_ids[:, None] // head_group[None, :]
    slot_ids = jnp.arange(flat_heads.shape[0], dtype=jnp.int32)
    matched = (flat_heads[None, None, :] == head_ids[None, :, None]) & (
        group_rank[None, None, :] == row_rank[:, :, None]
    )
    owner_slot = jnp.sum(jnp.where(matched, slot_ids[None, None, :], 0), axis=2)
    flat_index = owner_slot * row_cap + row_step
    returned_rows = returned.reshape(-1, HDIM)
    attended_home = returned_rows[flat_index].reshape(tok_dev, HEADS * HDIM)
    partner = partner_2(attended_home, "branch", 0)
    on_positive = lax.axis_index("branch") == 0
    own_value = attended_home.astype(jnp.float32)
    partner_value = partner.astype(jnp.float32)
    positive = jnp.where(on_positive, own_value, partner_value)
    negative = jnp.where(on_positive, partner_value, own_value)
    guided = GUIDE_SCALE * positive - (GUIDE_SCALE - 1.0) * negative
    magnitude = jnp.mean(jnp.abs(guided), axis=1, keepdims=True)
    normed = (guided / (magnitude + EPSILON)).astype(jnp.bfloat16)
    projected = jnp.dot(normed, out_weight, preferred_element_type=jnp.float32).astype(jnp.bfloat16)
    saved_rows = jnp.transpose(logsum, (1, 2, 0)).reshape(1, 1, slot_count, row_cap, seq_count)
    return (projected, saved_rows)


KERNEL_PARAMS = pltpu.CompilerParams(vmem_limit_bytes=16 * 1024 * 1024)


SPLIT = 2
SET_ORDER = (0, 3, 2, 1, 4, 7, 6, 5)
HOLD_COPIES = 4
TABLE_PIECES = 3
SPLITTER = 65537.0


def swap_shards(array, offset):
    pairs = [(i, i ^ offset) for i in range(lax.axis_size("seq"))]
    return lax.ppermute(array, "seq", pairs)


def place_offsets(shard_count):
    line = list(range(0, shard_count, SPLIT))
    return line + [offset + 1 for offset in line]


def pack_kernel(
    query_hbm,
    key_hbm,
    value_hbm,
    counts_hbm,
    head_hbm,
    own_ref,
    other_ref,
    own_copy_ref,
    other_copy_ref,
    limits_ref,
    pick_ref,
    slot_head_ref,
    counts_ref,
    head_ref,
    copy_sems,
):
    tok_dev = own_ref.shape[0] // 3
    half_width = own_ref.shape[1]
    slot_count, shard_count = head_ref.shape
    shard = lax.axis_index("seq")
    half = (shard // SPLIT) % 2
    copies = [
        pltpu.make_async_copy(counts_hbm, counts_ref, copy_sems.at[0]),
        pltpu.make_async_copy(head_hbm, head_ref, copy_sems.at[1]),
    ]
    for target, place in ((other_ref, 1 - half), (own_ref, half), (own_copy_ref, half), (other_copy_ref, 1 - half)):
        columns = pl.ds(pl.multiple_of(place * half_width, half_width), half_width)
        for part, source in enumerate((key_hbm, value_hbm, query_hbm)):
            rows = pl.ds(part * tok_dev, tok_dev)
            copies.append(
                pltpu.make_async_copy(
                    source.at[0, :, columns], target.at[rows, :], copy_sems.at[len(copies)]
                )
            )
    for copy in copies:
        copy.start()
    copies[0].wait()
    copies[1].wait()

    lane = lax.broadcasted_iota(jnp.int32, (1, limits_ref.shape[1]), 1)
    lane_limit = jnp.zeros(lane.shape, jnp.int32)
    for place, offset in enumerate(place_offsets(shard_count)):
        lane_limit = jnp.where(lane // tok_dev == place, counts_ref[shard ^ offset], lane_limit)
    limits_ref[0:1, :] = (lane % tok_dev < lane_limit).astype(jnp.int32)
    limits_ref[1:2, :] = jnp.full(lane.shape, counts_ref[shard], jnp.int32)
    limits_ref[2:3, :] = jnp.full(lane.shape, counts_ref[shard ^ SPLIT], jnp.int32)

    step = lax.broadcasted_iota(jnp.int32, (1, pick_ref.shape[2]), 1)
    for slot in range(slot_count):
        head = head_ref[slot, shard]
        group_size = jnp.int32(0)
        group_rank = jnp.int32(0)
        for other_shard in range(shard_count):
            for other_slot in range(slot_count):
                same = (head_ref[other_slot, other_shard] == head).astype(jnp.int32)
                before = other_shard * slot_count + other_slot < shard * slot_count + slot
                group_size = group_size + same
                group_rank = group_rank + same * before.astype(jnp.int32)
        served = group_rank + group_size * step
        for source in range(shard_count):
            pick_ref[slot, source : source + 1, :] = jnp.where(
                served < counts_ref[source], served + source * tok_dev, -1
            )
        slot_head_ref[slot] = jnp.full(slot_head_ref.shape[1:], head, jnp.int32)
    for copy in copies[2:]:
        copy.wait()


def hold_kernel(weight_hbm, after_ref, weight_ref, copy_sems):
    share = weight_ref.shape[0] // HOLD_COPIES
    copies = []
    for number in range(HOLD_COPIES):
        rows = pl.ds(number * share, share)
        copies.append(
            pltpu.make_async_copy(
                weight_hbm.at[rows, :], weight_ref.at[rows, :], copy_sems.at[number]
            )
        )
    for copy in copies:
        copy.start()
    for copy in copies:
        copy.wait()


def part_blocks(half_heads, tok_dev):
    return -(-half_heads * TABLE_PIECES // tok_dev)


def gathered(set_refs, part, columns):
    tok_dev = set_refs[0].shape[0] // 3
    rows = pl.ds(part * tok_dev, tok_dev)
    return jnp.concatenate([ref[rows, columns] for ref in set_refs], axis=0)


def head_scores(query_rows, key_all):
    return lax.dot_general(
        query_rows, key_all, (((1,), (1,)), ((), ())), preferred_element_type=jnp.float32
    )


def attend_kernel(set_count, limits_ref, *refs):
    set_refs = [refs[SET_ORDER.index(i)] for i in range(set_count)]
    keep_ref, message_ref, table_ref, lines_ref = refs[set_count:]
    tok_dev, half_width = keep_ref.shape
    half_heads = half_width // HDIM
    shard = lax.axis_index("seq")
    head_columns = [pl.ds(head * HDIM, HDIM) for head in range(half_heads)]
    key_valid = limits_ref[0:1, :] > 0

    all_scores = [
        head_scores(gathered(set_refs, 2, columns), gathered(set_refs, 0, columns))
        for columns in head_columns
    ]
    lane = lax.broadcasted_iota(jnp.int32, all_scores[0].shape, 1)
    lines = jnp.zeros(lane.shape, jnp.float32)
    served = []
    for head, scores in enumerate(all_scores):
        scores = jnp.where(key_valid, scores * (1.0 / math.sqrt(HDIM)), -jnp.inf)
        top_score = jnp.max(scores, axis=1, keepdims=True)
        weights = jnp.exp(scores - top_score)
        weight_sum = jnp.sum(weights, axis=1, keepdims=True)
        lines = jnp.where(lane == head, top_score + jnp.log(weight_sum), lines)
        served.append((weights[: 2 * tok_dev].astype(jnp.bfloat16), weight_sum[: 2 * tok_dev]))
    row = lax.broadcasted_iota(jnp.int32, (tok_dev, HDIM), 0)
    for columns, (rounded, weight_sum) in zip(head_columns, served):
        mixed = jnp.dot(
            rounded, gathered(set_refs, 1, columns), preferred_element_type=jnp.float32
        )
        attended = mixed / weight_sum
        kept = jnp.where(row < limits_ref[1:2, :HDIM], attended[:tok_dev], 0.0)
        sent = jnp.where(row < limits_ref[2:3, :HDIM], attended[tok_dev:], 0.0)
        keep_ref[:, columns] = kept.astype(jnp.bfloat16)
        message_ref[:, columns] = sent.astype(jnp.bfloat16)

    for place, offset in enumerate(place_offsets(set_count)):
        rows = pl.ds(pl.multiple_of((shard ^ offset) * tok_dev, tok_dev), tok_dev)
        lines_ref[rows, :] = lines[place * tok_dev : (place + 1) * tok_dev]
    table = jnp.transpose(lines_ref[...])[: table_ref.shape[0]]
    table_ref[...] = table
    row = lax.broadcasted_iota(jnp.int32, (tok_dev, lines.shape[0]), 0)
    blocks = [jnp.zeros(row.shape, jnp.float32) for _ in range(part_blocks(half_heads, tok_dev))]
    for head in range(half_heads):
        rest = jnp.broadcast_to(table[head : head + 1], row.shape)
        for piece in range(TABLE_PIECES):
            scaled = rest * SPLITTER
            part = scaled - (scaled - rest)
            block, at_row = divmod(head * TABLE_PIECES + piece, tok_dev)
            blocks[block] = jnp.where(row == at_row, part, blocks[block])
            rest = rest - part
    message_ref[:, pl.ds(half_width, len(blocks) * lines.shape[0])] = jnp.concatenate(
        blocks, axis=1
    ).astype(jnp.bfloat16)


def guidance(own, partner):
    on_positive = lax.axis_index("branch") == 0
    own_scale = jnp.where(on_positive, GUIDE_SCALE, 1.0 - GUIDE_SCALE)
    partner_scale = jnp.where(on_positive, 1.0 - GUIDE_SCALE, GUIDE_SCALE)
    return own_scale * own.astype(jnp.float32) + partner_scale * partner.astype(jnp.float32)


def half_product(guided, weight_ref, place):
    half_width = guided.shape[1]
    rows = pl.ds(pl.multiple_of(place * half_width, half_width), half_width)
    return jnp.dot(
        guided.astype(jnp.bfloat16), weight_ref[rows, :], preferred_element_type=jnp.float32
    )


def keep_kernel(keep_ref, partner_keep_ref, weight_ref, total_ref, size_ref):
    half = (lax.axis_index("seq") // SPLIT) % 2
    guided = guidance(keep_ref[...], partner_keep_ref[...])
    size = jnp.sum(jnp.abs(guided), axis=1, keepdims=True)
    size_ref[...] = jnp.broadcast_to(size, size_ref.shape)
    total_ref[...] = half_product(guided, weight_ref, half)


def project_kernel(
    total_ref,
    size_ref,
    message_ref,
    partner_back_ref,
    weight_ref,
    table_ref,
    pick_ref,
    slot_head_ref,
    projected_ref,
    saved_ref,
):
    tok_dev = message_ref.shape[0]
    half_width = weight_ref.shape[0] // 2
    half_heads = half_width // HDIM
    tokens = table_ref.shape[1]
    half = (lax.axis_index("seq") // SPLIT) % 2
    rows = pl.ds(0, half_width)
    guided = guidance(message_ref[:, rows], partner_back_ref[:, rows])
    size = size_ref[:, 0:1] + jnp.sum(jnp.abs(guided), axis=1, keepdims=True)
    magnitude = size / (2 * half_width)
    total = total_ref[...] + half_product(guided, weight_ref, 1 - half)
    projected_ref[...] = (total / (magnitude + EPSILON)).astype(jnp.bfloat16)

    parts = message_ref[:, pl.ds(half_width, message_ref.shape[1] - half_width)].astype(jnp.float32)
    others = []
    for head in range(half_heads):
        other = jnp.zeros((1, tokens), jnp.float32)
        for piece in range(TABLE_PIECES):
            block, at_row = divmod(head * TABLE_PIECES + piece, tok_dev)
            other = other + parts[at_row : at_row + 1, block * tokens : (block + 1) * tokens]
        others.append(other)
    for slot in range(saved_ref.shape[0]):
        slot_head = slot_head_ref[slot, 0:1, :]
        line = jnp.zeros((1, tokens), jnp.float32)
        for head in range(half_heads):
            line = jnp.where(slot_head == half * half_heads + head, table_ref[head : head + 1], line)
            line = jnp.where(slot_head == (1 - half) * half_heads + head, others[head], line)
        pick = pick_ref[slot]
        spread = jnp.broadcast_to(line, pick.shape)
        taken = jnp.take_along_axis(spread, jnp.maximum(pick, 0), axis=1)
        saved_ref[slot] = jnp.where(pick >= 0, taken, 0.0)[:, : saved_ref.shape[2]]


def per_device_halves(queries, key_rows, value_rows, counts, head_of, out_weight):
    seq_count = lax.axis_size("seq")
    tok_dev, width = queries.shape[1:]
    half_width = width // 2
    tokens = seq_count * tok_dev
    slot_count = head_of.shape[1]
    fewest = max(1, seq_count * slot_count // (2 * HEADS))
    row_cap = (tok_dev + fewest - 1) // fewest
    message_width = half_width + part_blocks(half_width // HDIM, tok_dev) * tokens
    any_spec = pl.BlockSpec(memory_space=pl.ANY)
    vmem = pl.BlockSpec(memory_space=pltpu.VMEM)

    def held(*arrays):
        return [pltpu.with_memory_space_constraint(array, pltpu.VMEM) for array in arrays]

    def distant(*arrays):
        return [pltpu.with_memory_space_constraint(array, pltpu.HBM) for array in arrays]

    own, other, own_copy, other_copy, limits, pick, slot_head = pl.pallas_call(
        pack_kernel,
        out_shape=[
            pltpu.VMEM((3 * tok_dev, half_width), jnp.bfloat16),
            pltpu.VMEM((3 * tok_dev, half_width), jnp.bfloat16),
            pltpu.VMEM((3 * tok_dev, half_width), jnp.bfloat16),
            pltpu.VMEM((3 * tok_dev, half_width), jnp.bfloat16),
            pltpu.VMEM((8, tokens), jnp.int32),
            pltpu.VMEM((slot_count, seq_count, tokens), jnp.int32),
            pltpu.VMEM((slot_count, 8, tokens), jnp.int32),
        ],
        in_specs=[any_spec] * 5,
        out_specs=[vmem] * 7,
        scratch_shapes=[
            pltpu.SMEM((seq_count,), jnp.int32),
            pltpu.SMEM((slot_count, seq_count), jnp.int32),
            pltpu.SemaphoreType.DMA((14,)),
        ],
        compiler_params=KERNEL_PARAMS,
        name="pack",
    )(*distant(queries, key_rows, value_rows, counts, jnp.transpose(head_of)))

    weight_held = pl.pallas_call(
        hold_kernel,
        out_shape=pltpu.VMEM(out_weight.shape, jnp.bfloat16),
        in_specs=[any_spec, vmem],
        out_specs=vmem,
        scratch_shapes=[pltpu.SemaphoreType.DMA((HOLD_COPIES,))],
        compiler_params=KERNEL_PARAMS,
        cost_estimate=pl.CostEstimate(
            flops=0, bytes_accessed=4 * out_weight.size, transcendentals=0
        ),
        name="hold",
    )(*distant(out_weight), *held(limits))
    line = [own] + [
        swap_shards({4: own_copy, 6: other_copy}.get(offset, other if offset & SPLIT else own), offset)
        for offset in range(SPLIT, seq_count, SPLIT)
    ]
    sets = line + [swap_shards(array, 1) for array in line]
    sets = [sets[i] for i in SET_ORDER]
    limits, weight_held = lax.optimization_barrier((limits, weight_held))
    keep, message, table = pl.pallas_call(
        functools.partial(attend_kernel, len(sets)),
        out_shape=[
            pltpu.VMEM((tok_dev, half_width), jnp.bfloat16),
            pltpu.VMEM((tok_dev, message_width), jnp.bfloat16),
            pltpu.VMEM((half_width // HDIM + 7 & -8, tokens), jnp.float32),
        ],
        in_specs=[vmem] * (1 + len(sets)),
        out_specs=[vmem] * 3,
        scratch_shapes=[pltpu.VMEM((tokens, HDIM), jnp.float32)],
        compiler_params=KERNEL_PARAMS,
        name="attend",
    )(*held(limits, *sets))
    across = [(2 * i + b, 2 * (i ^ SPLIT) + 1 - b) for i in range(seq_count) for b in range(2)]
    partner_back = lax.ppermute(message, ("seq", "branch"), across)
    partner_keep = partner_2(keep, "branch", 0)
    back = swap_shards(message, SPLIT)
    total, size = pl.pallas_call(
        keep_kernel,
        out_shape=[
            pltpu.VMEM((tok_dev, out_weight.shape[1]), jnp.float32),
            pltpu.VMEM((tok_dev, HDIM), jnp.float32),
        ],
        in_specs=[vmem] * 3,
        out_specs=[vmem] * 2,
        compiler_params=KERNEL_PARAMS,
        name="keep",
    )(*held(keep, partner_keep, weight_held))
    projected, saved = pl.pallas_call(
        project_kernel,
        out_shape=[
            jax.ShapeDtypeStruct((tok_dev, out_weight.shape[1]), jnp.bfloat16),
            jax.ShapeDtypeStruct((slot_count, seq_count, row_cap), jnp.float32),
        ],
        in_specs=[vmem] * 8,
        out_specs=[vmem] * 2,
        compiler_params=KERNEL_PARAMS,
        name="project",
    )(*held(total, size, back, partner_back, weight_held, table, pick, slot_head))
    saved = jnp.transpose(saved, (0, 2, 1))
    return (projected, saved.reshape(1, 1, slot_count, row_cap, seq_count))


def solution(mesh):
    seq_count = mesh.shape["seq"]
    hypercube = seq_count > SPLIT and seq_count & (seq_count - 1) == 0
    small = hypercube and seq_count <= HEADS
    return jax.shard_map(
        per_device_halves if small else per_device_exchange,
        mesh=mesh,
        in_specs=(
            P("branch", ("groups", "seq"), None),
            P("branch", ("groups", "seq"), None),
            P("branch", ("groups", "seq"), None),
            P("groups"),
            P(),
            P(None, "branch"),
        ),
        out_specs=(
            P(("groups", "seq"), "branch"),
            P("branch", ("groups", "seq"), None, None, None),
        ),
        check_vma=False,
    )
```

```python
import functools
import math

import jax
import jax.numpy as jnp
from jax import lax
from jax.experimental import pallas as pl
from jax.experimental.pallas import tpu as pltpu
from jax.sharding import PartitionSpec as P

HEADS = 12
HDIM = 128


GUIDE_SCALE = 3.0
EPSILON = 1e-06


def partner_2(array, axis, stride):
    return lax.ppermute(array, axis, [(i, i ^ 1 << stride) for i in range(lax.axis_size(axis))])


def slot_layout(head_of):
    flat_heads = head_of.reshape(-1)
    slot_order = jnp.arange(flat_heads.shape[0], dtype=jnp.int32)
    same_head = flat_heads[:, None] == flat_heads[None, :]
    group_size = jnp.sum(same_head.astype(jnp.int32), axis=1)
    earlier = same_head & (slot_order[None, :] < slot_order[:, None])
    group_rank = jnp.sum(earlier.astype(jnp.int32), axis=1)
    return (flat_heads, group_size, group_rank)


def key_grouping(seq_count, tok_dev):
    shard_limit = max(1, 2048 // tok_dev)
    grouping = 1
    for attempt in range(16):
        if grouping * 2 <= shard_limit and seq_count % (grouping * 2) == 0:
            grouping = grouping * 2
    return grouping


def attend_rows(query_block, key_slot, value_slot, key_valid, key_block):
    row_count = query_block.shape[0]
    head_size = query_block.shape[1]
    block_count = key_slot.shape[0] // key_block
    scale_factor = 1.0 / math.sqrt(head_size)

    def fold_block(block_id, state_in):
        top_score, weight_sum, summed = state_in
        scores = (
            jnp.einsum("qd,kd->qk", query_block, key_slot, preferred_element_type=jnp.float32)
            * scale_factor
        )
        scores = jnp.where(key_valid[None, :], scores, -jnp.inf)
        new_top = jnp.maximum(top_score, jnp.max(scores, axis=1))
        fading = jnp.exp(top_score - new_top)
        weights = jnp.exp(scores - new_top[:, None])
        weight_sum = weight_sum * fading + jnp.sum(weights, axis=1)
        summed = summed * fading[:, None] + jnp.dot(
            weights.astype(jnp.bfloat16), value_slot, preferred_element_type=jnp.float32
        )
        return (new_top, weight_sum, summed)

    start_state = (
        jnp.full((row_count,), -jnp.inf, jnp.float32),
        jnp.zeros((row_count,), jnp.float32),
        jnp.zeros((row_count, head_size), jnp.float32),
    )
    top_score, weight_sum, summed = lax.fori_loop(0, block_count, fold_block, start_state)
    return (summed / weight_sum[:, None], top_score + jnp.log(weight_sum))


def serve_slots(query_items, mask_items, key_recv, value_recv, key_valid, key_block):
    source_count, slot_count, item_count, head_size = query_items.shape
    all_tokens = key_recv.shape[0] * key_recv.shape[2]
    per_block = max(1, 512 // source_count)
    slot_outputs = []
    slot_logsum = []
    for slot_id in range(slot_count):
        key_slot = key_recv[:, slot_id].reshape(all_tokens, head_size)
        value_slot = value_recv[:, slot_id].reshape(all_tokens, head_size)
        taken_items = min(per_block, item_count)
        query_block = query_items[:, slot_id, 0:taken_items].reshape(
            source_count * taken_items, head_size
        )
        attended, logsum = attend_rows(query_block, key_slot, value_slot, key_valid, key_block)
        pieces_out = attended.reshape(source_count, taken_items, head_size)
        pieces_sum = logsum.reshape(source_count, taken_items)
        slot_outputs.append(pieces_out)
        slot_logsum.append(pieces_sum)
    attended = jnp.stack(slot_outputs, axis=1)
    logsum = jnp.stack(slot_logsum, axis=1)
    keep_rows = mask_items > 0
    attended = jnp.where(keep_rows[:, :, :, None], attended, 0.0).astype(jnp.bfloat16)
    logsum = jnp.where(keep_rows, logsum, 0.0)
    return (attended, logsum)


def per_device_exchange(queries, key_rows, value_rows, counts, head_of, out_weight):
    seq_count = lax.axis_size("seq")
    tok_dev = queries.shape[1]
    slot_count = head_of.shape[1]
    fewest = max(1, seq_count * slot_count // (2 * HEADS))
    row_cap = (tok_dev + fewest - 1) // fewest
    my_index = lax.axis_index("seq")
    flat_heads, group_size, group_rank = slot_layout(head_of)
    row_steps = jnp.arange(row_cap, dtype=jnp.int32)
    served_rows = group_rank[:, None] + group_size[:, None] * row_steps[None, :]
    my_count = counts[my_index]
    clipped = jnp.minimum(served_rows, tok_dev - 1)
    query_grid = queries[0].reshape(tok_dev, HEADS, HDIM)
    row_live = served_rows < my_count
    query_send = query_grid[clipped, flat_heads[:, None]]
    query_send = jnp.where(row_live[:, :, None], query_send, jnp.zeros((), jnp.bfloat16)).reshape(
        seq_count, slot_count, row_cap, HDIM
    )
    mask_send = row_live.astype(jnp.bfloat16).reshape(seq_count, slot_count, row_cap)
    token_ids = jnp.arange(tok_dev, dtype=jnp.int32)
    key_grid = key_rows[0].reshape(tok_dev, HEADS, HDIM)
    value_grid = value_rows[0].reshape(tok_dev, HEADS, HDIM)
    key_send = key_grid[token_ids[None, :], flat_heads[:, None]].reshape(
        seq_count, slot_count, tok_dev, HDIM
    )
    value_send = value_grid[token_ids[None, :], flat_heads[:, None]].reshape(
        seq_count, slot_count, tok_dev, HDIM
    )
    key_valid = (token_ids[None, :] < counts[:, None]).reshape(-1)
    key_block = tok_dev * key_grouping(seq_count, tok_dev)
    query_recv, mask_recv, key_recv, value_recv = (
        lax.all_to_all(query_send, "seq", split_axis=0, concat_axis=0, tiled=True),
        lax.all_to_all(mask_send, "seq", split_axis=0, concat_axis=0, tiled=True),
        lax.all_to_all(key_send, "seq", split_axis=0, concat_axis=0, tiled=True),
        lax.all_to_all(value_send, "seq", split_axis=0, concat_axis=0, tiled=True),
    )
    attended, logsum = serve_slots(
        query_recv, mask_recv, key_recv, value_recv, key_valid, key_block
    )
    returned = lax.all_to_all(attended, "seq", split_axis=0, concat_axis=0, tiled=True)
    head_ids = jnp.arange(HEADS, dtype=jnp.int32)
    head_group = jnp.sum((flat_heads[None, :] == head_ids[:, None]).astype(jnp.int32), axis=1)
    row_rank = token_ids[:, None] % head_group[None, :]
    row_step = token_ids[:, None] // head_group[None, :]
    slot_ids = jnp.arange(flat_heads.shape[0], dtype=jnp.int32)
    matched = (flat_heads[None, None, :] == head_ids[None, :, None]) & (
        group_rank[None, None, :] == row_rank[:, :, None]
    )
    owner_slot = jnp.sum(jnp.where(matched, slot_ids[None, None, :], 0), axis=2)
    flat_index = owner_slot * row_cap + row_step
    returned_rows = returned.reshape(-1, HDIM)
    attended_home = returned_rows[flat_index].reshape(tok_dev, HEADS * HDIM)
    partner = partner_2(attended_home, "branch", 0)
    on_positive = lax.axis_index("branch") == 0
    own_value = attended_home.astype(jnp.float32)
    partner_value = partner.astype(jnp.float32)
    positive = jnp.where(on_positive, own_value, partner_value)
    negative = jnp.where(on_positive, partner_value, own_value)
    guided = GUIDE_SCALE * positive - (GUIDE_SCALE - 1.0) * negative
    magnitude = jnp.mean(jnp.abs(guided), axis=1, keepdims=True)
    normed = (guided / (magnitude + EPSILON)).astype(jnp.bfloat16)
    projected = jnp.dot(normed, out_weight, preferred_element_type=jnp.float32).astype(jnp.bfloat16)
    saved_rows = jnp.transpose(logsum, (1, 2, 0)).reshape(1, 1, slot_count, row_cap, seq_count)
    return (projected, saved_rows)


KERNEL_PARAMS = pltpu.CompilerParams(vmem_limit_bytes=16 * 1024 * 1024)


SPLIT = 2
SET_ORDER = (0, 3, 2, 1, 4, 7, 6, 5)
HOLD_COPIES = 4
TABLE_PIECES = 3
SPLITTER = 65537.0


def swap_shards(array, offset):
    pairs = [(i, i ^ offset) for i in range(lax.axis_size("seq"))]
    return lax.ppermute(array, "seq", pairs)


def place_offsets(shard_count):
    line = list(range(0, shard_count, SPLIT))
    return line + [offset + 1 for offset in line]


def pack_kernel(
    query_hbm,
    key_hbm,
    value_hbm,
    counts_hbm,
    head_hbm,
    own_ref,
    other_ref,
    limits_ref,
    pick_ref,
    slot_head_ref,
    counts_ref,
    head_ref,
    copy_sems,
):
    tok_dev = own_ref.shape[0] // 3
    half_width = own_ref.shape[1]
    slot_count, shard_count = head_ref.shape
    shard = lax.axis_index("seq")
    half = (shard // SPLIT) % 2
    copies = [
        pltpu.make_async_copy(counts_hbm, counts_ref, copy_sems.at[0]),
        pltpu.make_async_copy(head_hbm, head_ref, copy_sems.at[1]),
    ]
    for target, place in ((other_ref, 1 - half), (own_ref, half)):
        columns = pl.ds(pl.multiple_of(place * half_width, half_width), half_width)
        for part, source in enumerate((key_hbm, value_hbm, query_hbm)):
            rows = pl.ds(part * tok_dev, tok_dev)
            copies.append(
                pltpu.make_async_copy(
                    source.at[0, :, columns], target.at[rows, :], copy_sems.at[len(copies)]
                )
            )
    for copy in copies:
        copy.start()
    copies[0].wait()
    copies[1].wait()

    lane = lax.broadcasted_iota(jnp.int32, (1, limits_ref.shape[1]), 1)
    lane_limit = jnp.zeros(lane.shape, jnp.int32)
    for place, offset in enumerate(place_offsets(shard_count)):
        lane_limit = jnp.where(lane // tok_dev == place, counts_ref[shard ^ offset], lane_limit)
    limits_ref[0:1, :] = (lane % tok_dev < lane_limit).astype(jnp.int32)
    limits_ref[1:2, :] = jnp.full(lane.shape, counts_ref[shard], jnp.int32)
    limits_ref[2:3, :] = jnp.full(lane.shape, counts_ref[shard ^ SPLIT], jnp.int32)

    step = lax.broadcasted_iota(jnp.int32, (1, pick_ref.shape[2]), 1)
    for slot in range(slot_count):
        head = head_ref[slot, shard]
        group_size = jnp.int32(0)
        group_rank = jnp.int32(0)
        for other_shard in range(shard_count):
            for other_slot in range(slot_count):
                same = (head_ref[other_slot, other_shard] == head).astype(jnp.int32)
                before = other_shard * slot_count + other_slot < shard * slot_count + slot
                group_size = group_size + same
                group_rank = group_rank + same * before.astype(jnp.int32)
        served = group_rank + group_size * step
        for source in range(shard_count):
            pick_ref[slot, source : source + 1, :] = jnp.where(
                served < counts_ref[source], served + source * tok_dev, -1
            )
        slot_head_ref[slot] = jnp.full(slot_head_ref.shape[1:], head, jnp.int32)
    for copy in copies[2:]:
        copy.wait()


def hold_kernel(weight_hbm, after_ref, weight_ref, copy_sems):
    share = weight_ref.shape[0] // HOLD_COPIES
    copies = []
    for number in range(HOLD_COPIES):
        rows = pl.ds(number * share, share)
        copies.append(
            pltpu.make_async_copy(
                weight_hbm.at[rows, :], weight_ref.at[rows, :], copy_sems.at[number]
            )
        )
    for copy in copies:
        copy.start()
    for copy in copies:
        copy.wait()


def part_blocks(half_heads, tok_dev):
    return -(-half_heads * TABLE_PIECES // tok_dev)


def gathered(set_refs, part, columns):
    tok_dev = set_refs[0].shape[0] // 3
    rows = pl.ds(part * tok_dev, tok_dev)
    return jnp.concatenate([ref[rows, columns] for ref in set_refs], axis=0)


def head_scores(query_rows, key_all):
    return lax.dot_general(
        query_rows, key_all, (((1,), (1,)), ((), ())), preferred_element_type=jnp.float32
    )


def attend_kernel(set_count, limits_ref, *refs):
    set_refs = [refs[SET_ORDER.index(i)] for i in range(set_count)]
    keep_ref, message_ref, table_ref, lines_ref = refs[set_count:]
    tok_dev, half_width = keep_ref.shape
    half_heads = half_width // HDIM
    shard = lax.axis_index("seq")
    head_columns = [pl.ds(head * HDIM, HDIM) for head in range(half_heads)]
    key_valid = limits_ref[0:1, :] > 0

    all_scores = [
        head_scores(gathered(set_refs, 2, columns), gathered(set_refs, 0, columns))
        for columns in head_columns
    ]
    lane = lax.broadcasted_iota(jnp.int32, all_scores[0].shape, 1)
    lines = jnp.zeros(lane.shape, jnp.float32)
    served = []
    for head, scores in enumerate(all_scores):
        scores = jnp.where(key_valid, scores * (1.0 / math.sqrt(HDIM)), -jnp.inf)
        top_score = jnp.max(scores, axis=1, keepdims=True)
        weights = jnp.exp(scores - top_score)
        weight_sum = jnp.sum(weights, axis=1, keepdims=True)
        lines = jnp.where(lane == head, top_score + jnp.log(weight_sum), lines)
        served.append((weights[: 2 * tok_dev].astype(jnp.bfloat16), weight_sum[: 2 * tok_dev]))
    row = lax.broadcasted_iota(jnp.int32, (tok_dev, HDIM), 0)
    for columns, (rounded, weight_sum) in zip(head_columns, served):
        mixed = jnp.dot(
            rounded, gathered(set_refs, 1, columns), preferred_element_type=jnp.float32
        )
        attended = mixed / weight_sum
        kept = jnp.where(row < limits_ref[1:2, :HDIM], attended[:tok_dev], 0.0)
        sent = jnp.where(row < limits_ref[2:3, :HDIM], attended[tok_dev:], 0.0)
        keep_ref[:, columns] = kept.astype(jnp.bfloat16)
        message_ref[:, columns] = sent.astype(jnp.bfloat16)

    for place, offset in enumerate(place_offsets(set_count)):
        rows = pl.ds(pl.multiple_of((shard ^ offset) * tok_dev, tok_dev), tok_dev)
        lines_ref[rows, :] = lines[place * tok_dev : (place + 1) * tok_dev]
    table = jnp.transpose(lines_ref[...])[: table_ref.shape[0]]
    table_ref[...] = table
    row = lax.broadcasted_iota(jnp.int32, (tok_dev, lines.shape[0]), 0)
    blocks = [jnp.zeros(row.shape, jnp.float32) for _ in range(part_blocks(half_heads, tok_dev))]
    for head in range(half_heads):
        rest = jnp.broadcast_to(table[head : head + 1], row.shape)
        for piece in range(TABLE_PIECES):
            scaled = rest * SPLITTER
            part = scaled - (scaled - rest)
            block, at_row = divmod(head * TABLE_PIECES + piece, tok_dev)
            blocks[block] = jnp.where(row == at_row, part, blocks[block])
            rest = rest - part
    message_ref[:, pl.ds(half_width, len(blocks) * lines.shape[0])] = jnp.concatenate(
        blocks, axis=1
    ).astype(jnp.bfloat16)


def guidance(own, partner):
    on_positive = lax.axis_index("branch") == 0
    own_scale = jnp.where(on_positive, GUIDE_SCALE, 1.0 - GUIDE_SCALE)
    partner_scale = jnp.where(on_positive, 1.0 - GUIDE_SCALE, GUIDE_SCALE)
    return own_scale * own.astype(jnp.float32) + partner_scale * partner.astype(jnp.float32)


def half_product(guided, weight_ref, place):
    half_width = guided.shape[1]
    rows = pl.ds(pl.multiple_of(place * half_width, half_width), half_width)
    return jnp.dot(
        guided.astype(jnp.bfloat16), weight_ref[rows, :], preferred_element_type=jnp.float32
    )


def keep_kernel(keep_ref, partner_keep_ref, weight_ref, total_ref, size_ref):
    half = (lax.axis_index("seq") // SPLIT) % 2
    guided = guidance(keep_ref[...], partner_keep_ref[...])
    size = jnp.sum(jnp.abs(guided), axis=1, keepdims=True)
    size_ref[...] = jnp.broadcast_to(size, size_ref.shape)
    total_ref[...] = half_product(guided, weight_ref, half)


def project_kernel(
    total_ref,
    size_ref,
    message_ref,
    partner_back_ref,
    weight_ref,
    table_ref,
    pick_ref,
    slot_head_ref,
    projected_ref,
    saved_ref,
):
    tok_dev = message_ref.shape[0]
    half_width = weight_ref.shape[0] // 2
    half_heads = half_width // HDIM
    tokens = table_ref.shape[1]
    half = (lax.axis_index("seq") // SPLIT) % 2
    rows = pl.ds(0, half_width)
    guided = guidance(message_ref[:, rows], partner_back_ref[:, rows])
    size = size_ref[:, 0:1] + jnp.sum(jnp.abs(guided), axis=1, keepdims=True)
    magnitude = size / (2 * half_width)
    total = total_ref[...] + half_product(guided, weight_ref, 1 - half)
    projected_ref[...] = (total / (magnitude + EPSILON)).astype(jnp.bfloat16)

    parts = message_ref[:, pl.ds(half_width, message_ref.shape[1] - half_width)].astype(jnp.float32)
    others = []
    for head in range(half_heads):
        other = jnp.zeros((1, tokens), jnp.float32)
        for piece in range(TABLE_PIECES):
            block, at_row = divmod(head * TABLE_PIECES + piece, tok_dev)
            other = other + parts[at_row : at_row + 1, block * tokens : (block + 1) * tokens]
        others.append(other)
    for slot in range(saved_ref.shape[0]):
        slot_head = slot_head_ref[slot, 0:1, :]
        line = jnp.zeros((1, tokens), jnp.float32)
        for head in range(half_heads):
            line = jnp.where(slot_head == half * half_heads + head, table_ref[head : head + 1], line)
            line = jnp.where(slot_head == (1 - half) * half_heads + head, others[head], line)
        pick = pick_ref[slot]
        spread = jnp.broadcast_to(line, pick.shape)
        taken = jnp.take_along_axis(spread, jnp.maximum(pick, 0), axis=1)
        saved_ref[slot] = jnp.where(pick >= 0, taken, 0.0)[:, : saved_ref.shape[2]]


def per_device_halves(queries, key_rows, value_rows, counts, head_of, out_weight):
    seq_count = lax.axis_size("seq")
    tok_dev, width = queries.shape[1:]
    half_width = width // 2
    tokens = seq_count * tok_dev
    slot_count = head_of.shape[1]
    fewest = max(1, seq_count * slot_count // (2 * HEADS))
    row_cap = (tok_dev + fewest - 1) // fewest
    message_width = half_width + part_blocks(half_width // HDIM, tok_dev) * tokens
    any_spec = pl.BlockSpec(memory_space=pl.ANY)
    vmem = pl.BlockSpec(memory_space=pltpu.VMEM)

    def held(*arrays):
        return [pltpu.with_memory_space_constraint(array, pltpu.VMEM) for array in arrays]

    def distant(*arrays):
        return [pltpu.with_memory_space_constraint(array, pltpu.HBM) for array in arrays]

    own, other, limits, pick, slot_head = pl.pallas_call(
        pack_kernel,
        out_shape=[
            pltpu.VMEM((3 * tok_dev, half_width), jnp.bfloat16),
            pltpu.VMEM((3 * tok_dev, half_width), jnp.bfloat16),
            pltpu.VMEM((8, tokens), jnp.int32),
            pltpu.VMEM((slot_count, seq_count, tokens), jnp.int32),
            pltpu.VMEM((slot_count, 8, tokens), jnp.int32),
        ],
        in_specs=[any_spec] * 5,
        out_specs=[vmem] * 5,
        scratch_shapes=[
            pltpu.SMEM((seq_count,), jnp.int32),
            pltpu.SMEM((slot_count, seq_count), jnp.int32),
            pltpu.SemaphoreType.DMA((8,)),
        ],
        compiler_params=KERNEL_PARAMS,
        name="pack",
    )(*distant(queries, key_rows, value_rows, counts, jnp.transpose(head_of)))

    weight_held = pl.pallas_call(
        hold_kernel,
        out_shape=pltpu.VMEM(out_weight.shape, jnp.bfloat16),
        in_specs=[any_spec, vmem],
        out_specs=vmem,
        scratch_shapes=[pltpu.SemaphoreType.DMA((HOLD_COPIES,))],
        compiler_params=KERNEL_PARAMS,
        cost_estimate=pl.CostEstimate(
            flops=0, bytes_accessed=4 * out_weight.size, transcendentals=0
        ),
        name="hold",
    )(*distant(out_weight), *held(limits))
    line = [own] + [
        swap_shards(other if offset & SPLIT else own, offset)
        for offset in range(SPLIT, seq_count, SPLIT)
    ]
    sets = line + [swap_shards(array, 1) for array in line]
    sets = [sets[i] for i in SET_ORDER]
    limits, weight_held = lax.optimization_barrier((limits, weight_held))
    keep, message, table = pl.pallas_call(
        functools.partial(attend_kernel, len(sets)),
        out_shape=[
            pltpu.VMEM((tok_dev, half_width), jnp.bfloat16),
            pltpu.VMEM((tok_dev, message_width), jnp.bfloat16),
            pltpu.VMEM((half_width // HDIM + 7 & -8, tokens), jnp.float32),
        ],
        in_specs=[vmem] * (1 + len(sets)),
        out_specs=[vmem] * 3,
        scratch_shapes=[pltpu.VMEM((tokens, HDIM), jnp.float32)],
        compiler_params=KERNEL_PARAMS,
        name="attend",
    )(*held(limits, *sets))
    across = [(2 * i + b, 2 * (i ^ SPLIT) + 1 - b) for i in range(seq_count) for b in range(2)]
    partner_back = lax.ppermute(message, ("seq", "branch"), across)
    partner_keep = partner_2(keep, "branch", 0)
    back = swap_shards(message, SPLIT)
    total, size = pl.pallas_call(
        keep_kernel,
        out_shape=[
            pltpu.VMEM((tok_dev, out_weight.shape[1]), jnp.float32),
            pltpu.VMEM((tok_dev, HDIM), jnp.float32),
        ],
        in_specs=[vmem] * 3,
        out_specs=[vmem] * 2,
        compiler_params=KERNEL_PARAMS,
        name="keep",
    )(*held(keep, partner_keep, weight_held))
    projected, saved = pl.pallas_call(
        project_kernel,
        out_shape=[
            jax.ShapeDtypeStruct((tok_dev, out_weight.shape[1]), jnp.bfloat16),
            jax.ShapeDtypeStruct((slot_count, seq_count, row_cap), jnp.float32),
        ],
        in_specs=[vmem] * 8,
        out_specs=[vmem] * 2,
        compiler_params=KERNEL_PARAMS,
        name="project",
    )(*held(total, size, back, partner_back, weight_held, table, pick, slot_head))
    saved = jnp.transpose(saved, (0, 2, 1))
    return (projected, saved.reshape(1, 1, slot_count, row_cap, seq_count))


def solution(mesh):
    seq_count = mesh.shape["seq"]
    hypercube = seq_count > SPLIT and seq_count & (seq_count - 1) == 0
    small = hypercube and seq_count <= HEADS
    return jax.shard_map(
        per_device_halves if small else per_device_exchange,
        mesh=mesh,
        in_specs=(
            P("branch", ("groups", "seq"), None),
            P("branch", ("groups", "seq"), None),
            P("branch", ("groups", "seq"), None),
            P("groups"),
            P(),
            P(None, "branch"),
        ),
        out_specs=(
            P(("groups", "seq"), "branch"),
            P("branch", ("groups", "seq"), None, None, None),
        ),
        check_vma=False,
    )
```

```python
import functools
import math

import jax
import jax.numpy as jnp
from jax import lax
from jax.experimental import pallas as pl
from jax.experimental.pallas import tpu as pltpu
from jax.sharding import PartitionSpec as P

HEADS = 12
HDIM = 128


GUIDE_SCALE = 3.0
EPSILON = 1e-06


def partner_2(array, axis, stride):
    return lax.ppermute(array, axis, [(i, i ^ 1 << stride) for i in range(lax.axis_size(axis))])


def slot_layout(head_of):
    flat_heads = head_of.reshape(-1)
    slot_order = jnp.arange(flat_heads.shape[0], dtype=jnp.int32)
    same_head = flat_heads[:, None] == flat_heads[None, :]
    group_size = jnp.sum(same_head.astype(jnp.int32), axis=1)
    earlier = same_head & (slot_order[None, :] < slot_order[:, None])
    group_rank = jnp.sum(earlier.astype(jnp.int32), axis=1)
    return (flat_heads, group_size, group_rank)


def key_grouping(seq_count, tok_dev):
    shard_limit = max(1, 2048 // tok_dev)
    grouping = 1
    for attempt in range(16):
        if grouping * 2 <= shard_limit and seq_count % (grouping * 2) == 0:
            grouping = grouping * 2
    return grouping


def attend_rows(query_block, key_slot, value_slot, key_valid, key_block):
    row_count = query_block.shape[0]
    head_size = query_block.shape[1]
    block_count = key_slot.shape[0] // key_block
    scale_factor = 1.0 / math.sqrt(head_size)

    def fold_block(block_id, state_in):
        top_score, weight_sum, summed = state_in
        scores = (
            jnp.einsum("qd,kd->qk", query_block, key_slot, preferred_element_type=jnp.float32)
            * scale_factor
        )
        scores = jnp.where(key_valid[None, :], scores, -jnp.inf)
        new_top = jnp.maximum(top_score, jnp.max(scores, axis=1))
        fading = jnp.exp(top_score - new_top)
        weights = jnp.exp(scores - new_top[:, None])
        weight_sum = weight_sum * fading + jnp.sum(weights, axis=1)
        summed = summed * fading[:, None] + jnp.dot(
            weights.astype(jnp.bfloat16), value_slot, preferred_element_type=jnp.float32
        )
        return (new_top, weight_sum, summed)

    start_state = (
        jnp.full((row_count,), -jnp.inf, jnp.float32),
        jnp.zeros((row_count,), jnp.float32),
        jnp.zeros((row_count, head_size), jnp.float32),
    )
    top_score, weight_sum, summed = lax.fori_loop(0, block_count, fold_block, start_state)
    return (summed / weight_sum[:, None], top_score + jnp.log(weight_sum))


def serve_slots(query_items, mask_items, key_recv, value_recv, key_valid, key_block):
    source_count, slot_count, item_count, head_size = query_items.shape
    all_tokens = key_recv.shape[0] * key_recv.shape[2]
    per_block = max(1, 512 // source_count)
    slot_outputs = []
    slot_logsum = []
    for slot_id in range(slot_count):
        key_slot = key_recv[:, slot_id].reshape(all_tokens, head_size)
        value_slot = value_recv[:, slot_id].reshape(all_tokens, head_size)
        taken_items = min(per_block, item_count)
        query_block = query_items[:, slot_id, 0:taken_items].reshape(
            source_count * taken_items, head_size
        )
        attended, logsum = attend_rows(query_block, key_slot, value_slot, key_valid, key_block)
        pieces_out = attended.reshape(source_count, taken_items, head_size)
        pieces_sum = logsum.reshape(source_count, taken_items)
        slot_outputs.append(pieces_out)
        slot_logsum.append(pieces_sum)
    attended = jnp.stack(slot_outputs, axis=1)
    logsum = jnp.stack(slot_logsum, axis=1)
    keep_rows = mask_items > 0
    attended = jnp.where(keep_rows[:, :, :, None], attended, 0.0).astype(jnp.bfloat16)
    logsum = jnp.where(keep_rows, logsum, 0.0)
    return (attended, logsum)


def per_device_exchange(queries, key_rows, value_rows, counts, head_of, out_weight):
    seq_count = lax.axis_size("seq")
    tok_dev = queries.shape[1]
    slot_count = head_of.shape[1]
    fewest = max(1, seq_count * slot_count // (2 * HEADS))
    row_cap = (tok_dev + fewest - 1) // fewest
    my_index = lax.axis_index("seq")
    flat_heads, group_size, group_rank = slot_layout(head_of)
    row_steps = jnp.arange(row_cap, dtype=jnp.int32)
    served_rows = group_rank[:, None] + group_size[:, None] * row_steps[None, :]
    my_count = counts[my_index]
    clipped = jnp.minimum(served_rows, tok_dev - 1)
    query_grid = queries[0].reshape(tok_dev, HEADS, HDIM)
    row_live = served_rows < my_count
    query_send = query_grid[clipped, flat_heads[:, None]]
    query_send = jnp.where(row_live[:, :, None], query_send, jnp.zeros((), jnp.bfloat16)).reshape(
        seq_count, slot_count, row_cap, HDIM
    )
    mask_send = row_live.astype(jnp.bfloat16).reshape(seq_count, slot_count, row_cap)
    token_ids = jnp.arange(tok_dev, dtype=jnp.int32)
    key_grid = key_rows[0].reshape(tok_dev, HEADS, HDIM)
    value_grid = value_rows[0].reshape(tok_dev, HEADS, HDIM)
    key_send = key_grid[token_ids[None, :], flat_heads[:, None]].reshape(
        seq_count, slot_count, tok_dev, HDIM
    )
    value_send = value_grid[token_ids[None, :], flat_heads[:, None]].reshape(
        seq_count, slot_count, tok_dev, HDIM
    )
    key_valid = (token_ids[None, :] < counts[:, None]).reshape(-1)
    key_block = tok_dev * key_grouping(seq_count, tok_dev)
    query_recv, mask_recv, key_recv, value_recv = (
        lax.all_to_all(query_send, "seq", split_axis=0, concat_axis=0, tiled=True),
        lax.all_to_all(mask_send, "seq", split_axis=0, concat_axis=0, tiled=True),
        lax.all_to_all(key_send, "seq", split_axis=0, concat_axis=0, tiled=True),
        lax.all_to_all(value_send, "seq", split_axis=0, concat_axis=0, tiled=True),
    )
    attended, logsum = serve_slots(
        query_recv, mask_recv, key_recv, value_recv, key_valid, key_block
    )
    returned = lax.all_to_all(attended, "seq", split_axis=0, concat_axis=0, tiled=True)
    head_ids = jnp.arange(HEADS, dtype=jnp.int32)
    head_group = jnp.sum((flat_heads[None, :] == head_ids[:, None]).astype(jnp.int32), axis=1)
    row_rank = token_ids[:, None] % head_group[None, :]
    row_step = token_ids[:, None] // head_group[None, :]
    slot_ids = jnp.arange(flat_heads.shape[0], dtype=jnp.int32)
    matched = (flat_heads[None, None, :] == head_ids[None, :, None]) & (
        group_rank[None, None, :] == row_rank[:, :, None]
    )
    owner_slot = jnp.sum(jnp.where(matched, slot_ids[None, None, :], 0), axis=2)
    flat_index = owner_slot * row_cap + row_step
    returned_rows = returned.reshape(-1, HDIM)
    attended_home = returned_rows[flat_index].reshape(tok_dev, HEADS * HDIM)
    partner = partner_2(attended_home, "branch", 0)
    on_positive = lax.axis_index("branch") == 0
    own_value = attended_home.astype(jnp.float32)
    partner_value = partner.astype(jnp.float32)
    positive = jnp.where(on_positive, own_value, partner_value)
    negative = jnp.where(on_positive, partner_value, own_value)
    guided = GUIDE_SCALE * positive - (GUIDE_SCALE - 1.0) * negative
    magnitude = jnp.mean(jnp.abs(guided), axis=1, keepdims=True)
    normed = (guided / (magnitude + EPSILON)).astype(jnp.bfloat16)
    projected = jnp.dot(normed, out_weight, preferred_element_type=jnp.float32).astype(jnp.bfloat16)
    saved_rows = jnp.transpose(logsum, (1, 2, 0)).reshape(1, 1, slot_count, row_cap, seq_count)
    return (projected, saved_rows)


KERNEL_PARAMS = pltpu.CompilerParams(vmem_limit_bytes=16 * 1024 * 1024)


SPLIT = 2
HOLD_COPIES = 4
TABLE_PIECES = 2
SPLITTER = 65537.0


def swap_shards(array, offset):
    pairs = [(i, i ^ offset) for i in range(lax.axis_size("seq"))]
    return lax.ppermute(array, "seq", pairs)


def place_offsets(shard_count):
    line = list(range(0, shard_count, SPLIT))
    return line + [offset + 1 for offset in line]


def pack_kernel(
    query_hbm,
    key_hbm,
    value_hbm,
    counts_hbm,
    head_hbm,
    own_ref,
    other_ref,
    limits_ref,
    pick_ref,
    slot_head_ref,
    counts_ref,
    head_ref,
    copy_sems,
):
    tok_dev = own_ref.shape[0] // 3
    half_width = own_ref.shape[1]
    slot_count, shard_count = head_ref.shape
    shard = lax.axis_index("seq")
    half = (shard // SPLIT) % 2
    copies = [
        pltpu.make_async_copy(counts_hbm, counts_ref, copy_sems.at[0]),
        pltpu.make_async_copy(head_hbm, head_ref, copy_sems.at[1]),
    ]
    for target, place in ((other_ref, 1 - half), (own_ref, half)):
        columns = pl.ds(pl.multiple_of(place * half_width, half_width), half_width)
        for part, source in enumerate((key_hbm, value_hbm, query_hbm)):
            rows = pl.ds(part * tok_dev, tok_dev)
            copies.append(
                pltpu.make_async_copy(
                    source.at[0, :, columns], target.at[rows, :], copy_sems.at[len(copies)]
                )
            )
    for copy in copies:
        copy.start()
    copies[0].wait()
    copies[1].wait()

    lane = lax.broadcasted_iota(jnp.int32, (1, limits_ref.shape[1]), 1)
    lane_limit = jnp.zeros(lane.shape, jnp.int32)
    for place, offset in enumerate(place_offsets(shard_count)):
        lane_limit = jnp.where(lane // tok_dev == place, counts_ref[shard ^ offset], lane_limit)
    limits_ref[0:1, :] = (lane % tok_dev < lane_limit).astype(jnp.int32)
    limits_ref[1:2, :] = jnp.full(lane.shape, counts_ref[shard], jnp.int32)
    limits_ref[2:3, :] = jnp.full(lane.shape, counts_ref[shard ^ SPLIT], jnp.int32)

    step = lax.broadcasted_iota(jnp.int32, (1, pick_ref.shape[2]), 1)
    for slot in range(slot_count):
        head = head_ref[slot, shard]
        group_size = jnp.int32(0)
        group_rank = jnp.int32(0)
        for other_shard in range(shard_count):
            for other_slot in range(slot_count):
                same = (head_ref[other_slot, other_shard] == head).astype(jnp.int32)
                before = other_shard * slot_count + other_slot < shard * slot_count + slot
                group_size = group_size + same
                group_rank = group_rank + same * before.astype(jnp.int32)
        served = group_rank + group_size * step
        for source in range(shard_count):
            pick_ref[slot, source : source + 1, :] = jnp.where(
                served < counts_ref[source], served + source * tok_dev, -1
            )
        slot_head_ref[slot] = jnp.full(slot_head_ref.shape[1:], head, jnp.int32)
    for copy in copies[2:]:
        copy.wait()


def hold_kernel(weight_hbm, after_ref, weight_ref, copy_sems):
    share = weight_ref.shape[0] // HOLD_COPIES
    copies = []
    for number in range(HOLD_COPIES):
        rows = pl.ds(number * share, share)
        copies.append(
            pltpu.make_async_copy(
                weight_hbm.at[rows, :], weight_ref.at[rows, :], copy_sems.at[number]
            )
        )
    for copy in copies:
        copy.start()
    for copy in copies:
        copy.wait()


def part_blocks(half_heads, tok_dev):
    return -(-half_heads * TABLE_PIECES // tok_dev)


def gathered(set_refs, part, columns):
    tok_dev = set_refs[0].shape[0] // 3
    rows = pl.ds(part * tok_dev, tok_dev)
    return jnp.concatenate([ref[rows, columns] for ref in set_refs], axis=0)


def head_scores(query_rows, key_all):
    return lax.dot_general(
        query_rows, key_all, (((1,), (1,)), ((), ())), preferred_element_type=jnp.float32
    )


def attend_kernel(set_count, limits_ref, *refs):
    set_refs = refs[:set_count]
    keep_ref, message_ref, table_ref, lines_ref = refs[set_count:]
    tok_dev, half_width = keep_ref.shape
    half_heads = half_width // HDIM
    shard = lax.axis_index("seq")
    head_columns = [pl.ds(head * HDIM, HDIM) for head in range(half_heads)]
    key_valid = limits_ref[0:1, :] > 0

    all_scores = [
        head_scores(gathered(set_refs, 2, columns), gathered(set_refs, 0, columns))
        for columns in head_columns
    ]
    lane = lax.broadcasted_iota(jnp.int32, all_scores[0].shape, 1)
    lines = jnp.zeros(lane.shape, jnp.float32)
    served = []
    for head, scores in enumerate(all_scores):
        scores = jnp.where(key_valid, scores * (1.0 / math.sqrt(HDIM)), -jnp.inf)
        top_score = jnp.max(scores, axis=1, keepdims=True)
        weights = jnp.exp(scores - top_score)
        weight_sum = jnp.sum(weights, axis=1, keepdims=True)
        lines = jnp.where(lane == head, top_score + jnp.log(weight_sum), lines)
        served.append((weights[: 2 * tok_dev].astype(jnp.bfloat16), weight_sum[: 2 * tok_dev]))
    row = lax.broadcasted_iota(jnp.int32, (tok_dev, HDIM), 0)
    for columns, (rounded, weight_sum) in zip(head_columns, served):
        mixed = jnp.dot(
            rounded, gathered(set_refs, 1, columns), preferred_element_type=jnp.float32
        )
        attended = mixed / weight_sum
        kept = jnp.where(row < limits_ref[1:2, :HDIM], attended[:tok_dev], 0.0)
        sent = jnp.where(row < limits_ref[2:3, :HDIM], attended[tok_dev:], 0.0)
        keep_ref[:, columns] = kept.astype(jnp.bfloat16)
        message_ref[:, columns] = sent.astype(jnp.bfloat16)

    for place, offset in enumerate(place_offsets(set_count)):
        rows = pl.ds(pl.multiple_of((shard ^ offset) * tok_dev, tok_dev), tok_dev)
        lines_ref[rows, :] = lines[place * tok_dev : (place + 1) * tok_dev]
    table = jnp.transpose(lines_ref[...])[: table_ref.shape[0]]
    table_ref[...] = table
    row = lax.broadcasted_iota(jnp.int32, (tok_dev, lines.shape[0]), 0)
    blocks = [jnp.zeros(row.shape, jnp.float32) for _ in range(part_blocks(half_heads, tok_dev))]
    for head in range(half_heads):
        rest = jnp.broadcast_to(table[head : head + 1], row.shape)
        for piece in range(TABLE_PIECES):
            scaled = rest * SPLITTER
            part = scaled - (scaled - rest)
            block, at_row = divmod(head * TABLE_PIECES + piece, tok_dev)
            blocks[block] = jnp.where(row == at_row, part, blocks[block])
            rest = rest - part
    message_ref[:, pl.ds(half_width, len(blocks) * lines.shape[0])] = jnp.concatenate(
        blocks, axis=1
    ).astype(jnp.bfloat16)


def guidance(own, partner):
    on_positive = lax.axis_index("branch") == 0
    own_scale = jnp.where(on_positive, GUIDE_SCALE, 1.0 - GUIDE_SCALE)
    partner_scale = jnp.where(on_positive, 1.0 - GUIDE_SCALE, GUIDE_SCALE)
    return own_scale * own.astype(jnp.float32) + partner_scale * partner.astype(jnp.float32)


def half_product(guided, weight_ref, place):
    half_width = guided.shape[1]
    rows = pl.ds(pl.multiple_of(place * half_width, half_width), half_width)
    return jnp.dot(
        guided.astype(jnp.bfloat16), weight_ref[rows, :], preferred_element_type=jnp.float32
    )


def keep_kernel(keep_ref, partner_keep_ref, weight_ref, total_ref, size_ref):
    half = (lax.axis_index("seq") // SPLIT) % 2
    guided = guidance(keep_ref[...], partner_keep_ref[...])
    size = jnp.sum(jnp.abs(guided), axis=1, keepdims=True)
    size_ref[...] = jnp.broadcast_to(size, size_ref.shape)
    total_ref[...] = half_product(guided, weight_ref, half)


def project_kernel(
    total_ref,
    size_ref,
    message_ref,
    partner_back_ref,
    weight_ref,
    table_ref,
    pick_ref,
    slot_head_ref,
    projected_ref,
    saved_ref,
):
    tok_dev = message_ref.shape[0]
    half_width = weight_ref.shape[0] // 2
    half_heads = half_width // HDIM
    tokens = table_ref.shape[1]
    half = (lax.axis_index("seq") // SPLIT) % 2
    rows = pl.ds(0, half_width)
    guided = guidance(message_ref[:, rows], partner_back_ref[:, rows])
    size = size_ref[:, 0:1] + jnp.sum(jnp.abs(guided), axis=1, keepdims=True)
    magnitude = size / (2 * half_width)
    total = total_ref[...] + half_product(guided, weight_ref, 1 - half)
    projected_ref[...] = (total / (magnitude + EPSILON)).astype(jnp.bfloat16)

    parts = message_ref[:, pl.ds(half_width, message_ref.shape[1] - half_width)].astype(jnp.float32)
    others = []
    for head in range(half_heads):
        other = jnp.zeros((1, tokens), jnp.float32)
        for piece in range(TABLE_PIECES):
            block, at_row = divmod(head * TABLE_PIECES + piece, tok_dev)
            other = other + parts[at_row : at_row + 1, block * tokens : (block + 1) * tokens]
        others.append(other)
    for slot in range(saved_ref.shape[0]):
        slot_head = slot_head_ref[slot, 0:1, :]
        line = jnp.zeros((1, tokens), jnp.float32)
        for head in range(half_heads):
            line = jnp.where(slot_head == half * half_heads + head, table_ref[head : head + 1], line)
            line = jnp.where(slot_head == (1 - half) * half_heads + head, others[head], line)
        pick = pick_ref[slot]
        spread = jnp.broadcast_to(line, pick.shape)
        taken = jnp.take_along_axis(spread, jnp.maximum(pick, 0), axis=1)
        saved_ref[slot] = jnp.where(pick >= 0, taken, 0.0)[:, : saved_ref.shape[2]]


def per_device_halves(queries, key_rows, value_rows, counts, head_of, out_weight):
    seq_count = lax.axis_size("seq")
    tok_dev, width = queries.shape[1:]
    half_width = width // 2
    tokens = seq_count * tok_dev
    slot_count = head_of.shape[1]
    fewest = max(1, seq_count * slot_count // (2 * HEADS))
    row_cap = (tok_dev + fewest - 1) // fewest
    message_width = half_width + part_blocks(half_width // HDIM, tok_dev) * tokens
    any_spec = pl.BlockSpec(memory_space=pl.ANY)
    vmem = pl.BlockSpec(memory_space=pltpu.VMEM)

    def held(*arrays):
        return [pltpu.with_memory_space_constraint(array, pltpu.VMEM) for array in arrays]

    def distant(*arrays):
        return [pltpu.with_memory_space_constraint(array, pltpu.HBM) for array in arrays]

    own, other, limits, pick, slot_head = pl.pallas_call(
        pack_kernel,
        out_shape=[
            pltpu.VMEM((3 * tok_dev, half_width), jnp.bfloat16),
            pltpu.VMEM((3 * tok_dev, half_width), jnp.bfloat16),
            pltpu.VMEM((8, tokens), jnp.int32),
            pltpu.VMEM((slot_count, seq_count, tokens), jnp.int32),
            pltpu.VMEM((slot_count, 8, tokens), jnp.int32),
        ],
        in_specs=[any_spec] * 5,
        out_specs=[vmem] * 5,
        scratch_shapes=[
            pltpu.SMEM((seq_count,), jnp.int32),
            pltpu.SMEM((slot_count, seq_count), jnp.int32),
            pltpu.SemaphoreType.DMA((8,)),
        ],
        compiler_params=KERNEL_PARAMS,
        name="pack",
    )(*distant(queries, key_rows, value_rows, counts, jnp.transpose(head_of)))

    weight_held = pl.pallas_call(
        hold_kernel,
        out_shape=pltpu.VMEM(out_weight.shape, jnp.bfloat16),
        in_specs=[any_spec, vmem],
        out_specs=vmem,
        scratch_shapes=[pltpu.SemaphoreType.DMA((HOLD_COPIES,))],
        compiler_params=KERNEL_PARAMS,
        cost_estimate=pl.CostEstimate(
            flops=0, bytes_accessed=4 * out_weight.size, transcendentals=0
        ),
        name="hold",
    )(*distant(out_weight), *held(limits))
    line = [own] + [
        swap_shards(other if offset & SPLIT else own, offset)
        for offset in range(SPLIT, seq_count, SPLIT)
    ]
    sets = line + [swap_shards(array, 1) for array in line]
    limits, weight_held = lax.optimization_barrier((limits, weight_held))
    keep, message, table = pl.pallas_call(
        functools.partial(attend_kernel, len(sets)),
        out_shape=[
            pltpu.VMEM((tok_dev, half_width), jnp.bfloat16),
            pltpu.VMEM((tok_dev, message_width), jnp.bfloat16),
            pltpu.VMEM((half_width // HDIM + 7 & -8, tokens), jnp.float32),
        ],
        in_specs=[vmem] * (1 + len(sets)),
        out_specs=[vmem] * 3,
        scratch_shapes=[pltpu.VMEM((tokens, HDIM), jnp.float32)],
        compiler_params=KERNEL_PARAMS,
        name="attend",
    )(*held(limits, *sets))
    across = [(2 * i + b, 2 * (i ^ SPLIT) + 1 - b) for i in range(seq_count) for b in range(2)]
    partner_back = lax.ppermute(message, ("seq", "branch"), across)
    partner_keep = partner_2(keep, "branch", 0)
    back = swap_shards(message, SPLIT)
    total, size = pl.pallas_call(
        keep_kernel,
        out_shape=[
            pltpu.VMEM((tok_dev, out_weight.shape[1]), jnp.float32),
            pltpu.VMEM((tok_dev, HDIM), jnp.float32),
        ],
        in_specs=[vmem] * 3,
        out_specs=[vmem] * 2,
        compiler_params=KERNEL_PARAMS,
        name="keep",
    )(*held(keep, partner_keep, weight_held))
    projected, saved = pl.pallas_call(
        project_kernel,
        out_shape=[
            jax.ShapeDtypeStruct((tok_dev, out_weight.shape[1]), jnp.bfloat16),
            jax.ShapeDtypeStruct((slot_count, seq_count, row_cap), jnp.float32),
        ],
        in_specs=[vmem] * 8,
        out_specs=[vmem] * 2,
        compiler_params=KERNEL_PARAMS,
        name="project",
    )(*held(total, size, back, partner_back, weight_held, table, pick, slot_head))
    saved = jnp.transpose(saved, (0, 2, 1))
    return (projected, saved.reshape(1, 1, slot_count, row_cap, seq_count))


def solution(mesh):
    seq_count = mesh.shape["seq"]
    hypercube = seq_count > SPLIT and seq_count & (seq_count - 1) == 0
    small = hypercube and seq_count <= HEADS
    return jax.shard_map(
        per_device_halves if small else per_device_exchange,
        mesh=mesh,
        in_specs=(
            P("branch", ("groups", "seq"), None),
            P("branch", ("groups", "seq"), None),
            P("branch", ("groups", "seq"), None),
            P("groups"),
            P(),
            P(None, "branch"),
        ),
        out_specs=(
            P(("groups", "seq"), "branch"),
            P("branch", ("groups", "seq"), None, None, None),
        ),
        check_vma=False,
    )
```

```python
import functools
import math

import jax
import jax.numpy as jnp
from jax import lax
from jax.experimental import pallas as pl
from jax.experimental.pallas import tpu as pltpu
from jax.sharding import PartitionSpec as P

HEADS = 12
HDIM = 128


GUIDE_SCALE = 3.0
EPSILON = 1e-06


def partner_2(array, axis, stride):
    return lax.ppermute(array, axis, [(i, i ^ 1 << stride) for i in range(lax.axis_size(axis))])


def slot_layout(head_of):
    flat_heads = head_of.reshape(-1)
    slot_order = jnp.arange(flat_heads.shape[0], dtype=jnp.int32)
    same_head = flat_heads[:, None] == flat_heads[None, :]
    group_size = jnp.sum(same_head.astype(jnp.int32), axis=1)
    earlier = same_head & (slot_order[None, :] < slot_order[:, None])
    group_rank = jnp.sum(earlier.astype(jnp.int32), axis=1)
    return (flat_heads, group_size, group_rank)


def key_grouping(seq_count, tok_dev):
    shard_limit = max(1, 2048 // tok_dev)
    grouping = 1
    for attempt in range(16):
        if grouping * 2 <= shard_limit and seq_count % (grouping * 2) == 0:
            grouping = grouping * 2
    return grouping


def attend_rows(query_block, key_slot, value_slot, key_valid, key_block):
    row_count = query_block.shape[0]
    head_size = query_block.shape[1]
    block_count = key_slot.shape[0] // key_block
    scale_factor = 1.0 / math.sqrt(head_size)

    def fold_block(block_id, state_in):
        top_score, weight_sum, summed = state_in
        scores = (
            jnp.einsum("qd,kd->qk", query_block, key_slot, preferred_element_type=jnp.float32)
            * scale_factor
        )
        scores = jnp.where(key_valid[None, :], scores, -jnp.inf)
        new_top = jnp.maximum(top_score, jnp.max(scores, axis=1))
        fading = jnp.exp(top_score - new_top)
        weights = jnp.exp(scores - new_top[:, None])
        weight_sum = weight_sum * fading + jnp.sum(weights, axis=1)
        summed = summed * fading[:, None] + jnp.dot(
            weights.astype(jnp.bfloat16), value_slot, preferred_element_type=jnp.float32
        )
        return (new_top, weight_sum, summed)

    start_state = (
        jnp.full((row_count,), -jnp.inf, jnp.float32),
        jnp.zeros((row_count,), jnp.float32),
        jnp.zeros((row_count, head_size), jnp.float32),
    )
    top_score, weight_sum, summed = lax.fori_loop(0, block_count, fold_block, start_state)
    return (summed / weight_sum[:, None], top_score + jnp.log(weight_sum))


def serve_slots(query_items, mask_items, key_recv, value_recv, key_valid, key_block):
    source_count, slot_count, item_count, head_size = query_items.shape
    all_tokens = key_recv.shape[0] * key_recv.shape[2]
    per_block = max(1, 512 // source_count)
    slot_outputs = []
    slot_logsum = []
    for slot_id in range(slot_count):
        key_slot = key_recv[:, slot_id].reshape(all_tokens, head_size)
        value_slot = value_recv[:, slot_id].reshape(all_tokens, head_size)
        taken_items = min(per_block, item_count)
        query_block = query_items[:, slot_id, 0:taken_items].reshape(
            source_count * taken_items, head_size
        )
        attended, logsum = attend_rows(query_block, key_slot, value_slot, key_valid, key_block)
        pieces_out = attended.reshape(source_count, taken_items, head_size)
        pieces_sum = logsum.reshape(source_count, taken_items)
        slot_outputs.append(pieces_out)
        slot_logsum.append(pieces_sum)
    attended = jnp.stack(slot_outputs, axis=1)
    logsum = jnp.stack(slot_logsum, axis=1)
    keep_rows = mask_items > 0
    attended = jnp.where(keep_rows[:, :, :, None], attended, 0.0).astype(jnp.bfloat16)
    logsum = jnp.where(keep_rows, logsum, 0.0)
    return (attended, logsum)


def per_device_exchange(queries, key_rows, value_rows, counts, head_of, out_weight):
    seq_count = lax.axis_size("seq")
    tok_dev = queries.shape[1]
    slot_count = head_of.shape[1]
    fewest = max(1, seq_count * slot_count // (2 * HEADS))
    row_cap = (tok_dev + fewest - 1) // fewest
    my_index = lax.axis_index("seq")
    flat_heads, group_size, group_rank = slot_layout(head_of)
    row_steps = jnp.arange(row_cap, dtype=jnp.int32)
    served_rows = group_rank[:, None] + group_size[:, None] * row_steps[None, :]
    my_count = counts[my_index]
    clipped = jnp.minimum(served_rows, tok_dev - 1)
    query_grid = queries[0].reshape(tok_dev, HEADS, HDIM)
    row_live = served_rows < my_count
    query_send = query_grid[clipped, flat_heads[:, None]]
    query_send = jnp.where(row_live[:, :, None], query_send, jnp.zeros((), jnp.bfloat16)).reshape(
        seq_count, slot_count, row_cap, HDIM
    )
    mask_send = row_live.astype(jnp.bfloat16).reshape(seq_count, slot_count, row_cap)
    token_ids = jnp.arange(tok_dev, dtype=jnp.int32)
    key_grid = key_rows[0].reshape(tok_dev, HEADS, HDIM)
    value_grid = value_rows[0].reshape(tok_dev, HEADS, HDIM)
    key_send = key_grid[token_ids[None, :], flat_heads[:, None]].reshape(
        seq_count, slot_count, tok_dev, HDIM
    )
    value_send = value_grid[token_ids[None, :], flat_heads[:, None]].reshape(
        seq_count, slot_count, tok_dev, HDIM
    )
    key_valid = (token_ids[None, :] < counts[:, None]).reshape(-1)
    key_block = tok_dev * key_grouping(seq_count, tok_dev)
    query_recv, mask_recv, key_recv, value_recv = (
        lax.all_to_all(query_send, "seq", split_axis=0, concat_axis=0, tiled=True),
        lax.all_to_all(mask_send, "seq", split_axis=0, concat_axis=0, tiled=True),
        lax.all_to_all(key_send, "seq", split_axis=0, concat_axis=0, tiled=True),
        lax.all_to_all(value_send, "seq", split_axis=0, concat_axis=0, tiled=True),
    )
    attended, logsum = serve_slots(
        query_recv, mask_recv, key_recv, value_recv, key_valid, key_block
    )
    returned = lax.all_to_all(attended, "seq", split_axis=0, concat_axis=0, tiled=True)
    head_ids = jnp.arange(HEADS, dtype=jnp.int32)
    head_group = jnp.sum((flat_heads[None, :] == head_ids[:, None]).astype(jnp.int32), axis=1)
    row_rank = token_ids[:, None] % head_group[None, :]
    row_step = token_ids[:, None] // head_group[None, :]
    slot_ids = jnp.arange(flat_heads.shape[0], dtype=jnp.int32)
    matched = (flat_heads[None, None, :] == head_ids[None, :, None]) & (
        group_rank[None, None, :] == row_rank[:, :, None]
    )
    owner_slot = jnp.sum(jnp.where(matched, slot_ids[None, None, :], 0), axis=2)
    flat_index = owner_slot * row_cap + row_step
    returned_rows = returned.reshape(-1, HDIM)
    attended_home = returned_rows[flat_index].reshape(tok_dev, HEADS * HDIM)
    partner = partner_2(attended_home, "branch", 0)
    on_positive = lax.axis_index("branch") == 0
    own_value = attended_home.astype(jnp.float32)
    partner_value = partner.astype(jnp.float32)
    positive = jnp.where(on_positive, own_value, partner_value)
    negative = jnp.where(on_positive, partner_value, own_value)
    guided = GUIDE_SCALE * positive - (GUIDE_SCALE - 1.0) * negative
    magnitude = jnp.mean(jnp.abs(guided), axis=1, keepdims=True)
    normed = (guided / (magnitude + EPSILON)).astype(jnp.bfloat16)
    projected = jnp.dot(normed, out_weight, preferred_element_type=jnp.float32).astype(jnp.bfloat16)
    saved_rows = jnp.transpose(logsum, (1, 2, 0)).reshape(1, 1, slot_count, row_cap, seq_count)
    return (projected, saved_rows)


KERNEL_PARAMS = pltpu.CompilerParams(vmem_limit_bytes=16 * 1024 * 1024)


SPLIT = 2
HOLD_COPIES = 4
TABLE_PIECES = 2
SPLITTER = 65537.0


def swap_shards(array, offset):
    pairs = [(i, i ^ offset) for i in range(lax.axis_size("seq"))]
    return lax.ppermute(array, "seq", pairs)


def place_offsets(shard_count):
    line = list(range(0, shard_count, SPLIT))
    return line + [offset + 1 for offset in line]


def pack_kernel(
    query_hbm,
    key_hbm,
    value_hbm,
    counts_hbm,
    head_hbm,
    own_ref,
    other_ref,
    limits_ref,
    pick_ref,
    slot_head_ref,
    counts_ref,
    head_ref,
    copy_sems,
):
    tok_dev = own_ref.shape[0] // 3
    half_width = own_ref.shape[1]
    slot_count, shard_count = head_ref.shape
    shard = lax.axis_index("seq")
    half = (shard // SPLIT) % 2
    copies = [
        pltpu.make_async_copy(counts_hbm, counts_ref, copy_sems.at[0]),
        pltpu.make_async_copy(head_hbm, head_ref, copy_sems.at[1]),
    ]
    for target, place in ((other_ref, 1 - half), (own_ref, half)):
        columns = pl.ds(pl.multiple_of(place * half_width, half_width), half_width)
        for part, source in enumerate((key_hbm, value_hbm, query_hbm)):
            rows = pl.ds(part * tok_dev, tok_dev)
            copies.append(
                pltpu.make_async_copy(
                    source.at[0, :, columns], target.at[rows, :], copy_sems.at[len(copies)]
                )
            )
    for copy in copies:
        copy.start()
    copies[0].wait()
    copies[1].wait()

    lane = lax.broadcasted_iota(jnp.int32, (1, limits_ref.shape[1]), 1)
    lane_limit = jnp.zeros(lane.shape, jnp.int32)
    for place, offset in enumerate(place_offsets(shard_count)):
        lane_limit = jnp.where(lane // tok_dev == place, counts_ref[shard ^ offset], lane_limit)
    limits_ref[0:1, :] = (lane % tok_dev < lane_limit).astype(jnp.int32)
    limits_ref[1:2, :] = jnp.full(lane.shape, counts_ref[shard], jnp.int32)
    limits_ref[2:3, :] = jnp.full(lane.shape, counts_ref[shard ^ SPLIT], jnp.int32)

    step = lax.broadcasted_iota(jnp.int32, (1, pick_ref.shape[2]), 1)
    for slot in range(slot_count):
        head = head_ref[slot, shard]
        group_size = jnp.int32(0)
        group_rank = jnp.int32(0)
        for other_shard in range(shard_count):
            for other_slot in range(slot_count):
                same = (head_ref[other_slot, other_shard] == head).astype(jnp.int32)
                before = other_shard * slot_count + other_slot < shard * slot_count + slot
                group_size = group_size + same
                group_rank = group_rank + same * before.astype(jnp.int32)
        served = group_rank + group_size * step
        for source in range(shard_count):
            pick_ref[slot, source : source + 1, :] = jnp.where(
                served < counts_ref[source], served + source * tok_dev, -1
            )
        slot_head_ref[slot] = jnp.full(slot_head_ref.shape[1:], head, jnp.int32)
    for copy in copies[2:]:
        copy.wait()


def hold_kernel(weight_hbm, after_ref, weight_ref, copy_sems):
    share = weight_ref.shape[0] // HOLD_COPIES
    copies = []
    for number in range(HOLD_COPIES):
        rows = pl.ds(number * share, share)
        copies.append(
            pltpu.make_async_copy(
                weight_hbm.at[rows, :], weight_ref.at[rows, :], copy_sems.at[number]
            )
        )
    for copy in copies:
        copy.start()
    for copy in copies:
        copy.wait()


def part_blocks(half_heads, tok_dev):
    return -(-half_heads * TABLE_PIECES // tok_dev)


def gathered(set_refs, part, columns):
    tok_dev = set_refs[0].shape[0] // 3
    rows = pl.ds(part * tok_dev, tok_dev)
    return jnp.concatenate([ref[rows, columns] for ref in set_refs], axis=0)


def head_scores(query_rows, key_all):
    return lax.dot_general(
        query_rows, key_all, (((1,), (1,)), ((), ())), preferred_element_type=jnp.float32
    )


def attend_kernel(set_count, limits_ref, *refs):
    set_refs = refs[:set_count]
    keep_ref, message_ref, table_ref, lines_ref = refs[set_count:]
    tok_dev, half_width = keep_ref.shape
    half_heads = half_width // HDIM
    shard = lax.axis_index("seq")
    head_columns = [pl.ds(head * HDIM, HDIM) for head in range(half_heads)]
    key_valid = limits_ref[0:1, :] > 0

    all_scores = [
        head_scores(gathered(set_refs, 2, columns), gathered(set_refs, 0, columns))
        for columns in head_columns
    ]
    lane = lax.broadcasted_iota(jnp.int32, all_scores[0].shape, 1)
    lines = jnp.zeros(lane.shape, jnp.float32)
    served = []
    for head, scores in enumerate(all_scores):
        scores = jnp.where(key_valid, scores * (1.0 / math.sqrt(HDIM)), -jnp.inf)
        top_score = jnp.max(scores, axis=1, keepdims=True)
        weights = jnp.exp(scores - top_score)
        weight_sum = jnp.sum(weights, axis=1, keepdims=True)
        lines = jnp.where(lane == head, top_score + jnp.log(weight_sum), lines)
        served.append((weights[: 2 * tok_dev].astype(jnp.bfloat16), weight_sum[: 2 * tok_dev]))
    row = lax.broadcasted_iota(jnp.int32, (tok_dev, HDIM), 0)
    for columns, (rounded, weight_sum) in zip(head_columns, served):
        mixed = jnp.dot(
            rounded, gathered(set_refs, 1, columns), preferred_element_type=jnp.float32
        )
        attended = mixed / weight_sum
        kept = jnp.where(row < limits_ref[1:2, :HDIM], attended[:tok_dev], 0.0)
        sent = jnp.where(row < limits_ref[2:3, :HDIM], attended[tok_dev:], 0.0)
        keep_ref[:, columns] = kept.astype(jnp.bfloat16)
        message_ref[:, columns] = sent.astype(jnp.bfloat16)

    for place, offset in enumerate(place_offsets(set_count)):
        rows = pl.ds(pl.multiple_of((shard ^ offset) * tok_dev, tok_dev), tok_dev)
        lines_ref[rows, :] = lines[place * tok_dev : (place + 1) * tok_dev]
    table = jnp.transpose(lines_ref[...])[: table_ref.shape[0]]
    table_ref[...] = table
    row = lax.broadcasted_iota(jnp.int32, (tok_dev, lines.shape[0]), 0)
    blocks = [jnp.zeros(row.shape, jnp.float32) for _ in range(part_blocks(half_heads, tok_dev))]
    for head in range(half_heads):
        rest = jnp.broadcast_to(table[head : head + 1], row.shape)
        for piece in range(TABLE_PIECES):
            scaled = rest * SPLITTER
            part = scaled - (scaled - rest)
            block, at_row = divmod(head * TABLE_PIECES + piece, tok_dev)
            blocks[block] = jnp.where(row == at_row, part, blocks[block])
            rest = rest - part
    message_ref[:, pl.ds(half_width, len(blocks) * lines.shape[0])] = jnp.concatenate(
        blocks, axis=1
    ).astype(jnp.bfloat16)


def guidance(own, partner):
    on_positive = lax.axis_index("branch") == 0
    own_scale = jnp.where(on_positive, GUIDE_SCALE, 1.0 - GUIDE_SCALE)
    partner_scale = jnp.where(on_positive, 1.0 - GUIDE_SCALE, GUIDE_SCALE)
    return own_scale * own.astype(jnp.float32) + partner_scale * partner.astype(jnp.float32)


def half_product(guided, weight_ref, place):
    half_width = guided.shape[1]
    rows = pl.ds(pl.multiple_of(place * half_width, half_width), half_width)
    return jnp.dot(
        guided.astype(jnp.bfloat16), weight_ref[rows, :], preferred_element_type=jnp.float32
    )


def keep_kernel(keep_ref, partner_keep_ref, weight_ref, total_ref, size_ref):
    half = (lax.axis_index("seq") // SPLIT) % 2
    guided = guidance(keep_ref[...], partner_keep_ref[...])
    size = jnp.sum(jnp.abs(guided), axis=1, keepdims=True)
    size_ref[...] = jnp.broadcast_to(size, size_ref.shape)
    total_ref[...] = half_product(guided, weight_ref, half)


def project_kernel(
    total_ref,
    size_ref,
    message_ref,
    partner_back_ref,
    weight_ref,
    table_ref,
    pick_ref,
    slot_head_ref,
    projected_hbm,
    saved_hbm,
    projected_ref,
    saved_ref,
    copy_sems,
):
    tok_dev = message_ref.shape[0]
    half_width = weight_ref.shape[0] // 2
    half_heads = half_width // HDIM
    tokens = table_ref.shape[1]
    half = (lax.axis_index("seq") // SPLIT) % 2
    rows = pl.ds(0, half_width)
    guided = guidance(message_ref[:, rows], partner_back_ref[:, rows])
    size = size_ref[:, 0:1] + jnp.sum(jnp.abs(guided), axis=1, keepdims=True)
    magnitude = size / (2 * half_width)
    parts = message_ref[:, pl.ds(half_width, message_ref.shape[1] - half_width)].astype(jnp.float32)
    others = []
    for head in range(half_heads):
        other = jnp.zeros((1, tokens), jnp.float32)
        for piece in range(TABLE_PIECES):
            block, at_row = divmod(head * TABLE_PIECES + piece, tok_dev)
            other = other + parts[at_row : at_row + 1, block * tokens : (block + 1) * tokens]
        others.append(other)
    for slot in range(saved_ref.shape[0]):
        slot_head = slot_head_ref[slot, 0:1, :]
        line = jnp.zeros((1, tokens), jnp.float32)
        for head in range(half_heads):
            line = jnp.where(slot_head == half * half_heads + head, table_ref[head : head + 1], line)
            line = jnp.where(slot_head == (1 - half) * half_heads + head, others[head], line)
        pick = pick_ref[slot]
        spread = jnp.broadcast_to(line, pick.shape)
        taken = jnp.take_along_axis(spread, jnp.maximum(pick, 0), axis=1)
        saved_ref[slot] = jnp.where(pick >= 0, taken, 0.0)[:, : saved_ref.shape[2]]
    copies = [pltpu.make_async_copy(saved_ref, saved_hbm, copy_sems.at[0])]
    copies[0].start()

    rounded = guided.astype(jnp.bfloat16)
    rows = pl.ds(pl.multiple_of((1 - half) * half_width, half_width), half_width)
    share = projected_ref.shape[1] // 2
    for number in range(2):
        columns = pl.ds(number * share, share)
        total = total_ref[:, columns] + jnp.dot(
            rounded, weight_ref[rows, columns], preferred_element_type=jnp.float32
        )
        projected_ref[:, columns] = (total / (magnitude + EPSILON)).astype(jnp.bfloat16)
        copies.append(
            pltpu.make_async_copy(
                projected_ref.at[:, columns],
                projected_hbm.at[:, columns],
                copy_sems.at[number + 1],
            )
        )
        copies[-1].start()
    for copy in copies:
        copy.wait()


def per_device_halves(queries, key_rows, value_rows, counts, head_of, out_weight):
    seq_count = lax.axis_size("seq")
    tok_dev, width = queries.shape[1:]
    half_width = width // 2
    tokens = seq_count * tok_dev
    slot_count = head_of.shape[1]
    fewest = max(1, seq_count * slot_count // (2 * HEADS))
    row_cap = (tok_dev + fewest - 1) // fewest
    message_width = half_width + part_blocks(half_width // HDIM, tok_dev) * tokens
    any_spec = pl.BlockSpec(memory_space=pl.ANY)
    vmem = pl.BlockSpec(memory_space=pltpu.VMEM)

    def held(*arrays):
        return [pltpu.with_memory_space_constraint(array, pltpu.VMEM) for array in arrays]

    def distant(*arrays):
        return [pltpu.with_memory_space_constraint(array, pltpu.HBM) for array in arrays]

    own, other, limits, pick, slot_head = pl.pallas_call(
        pack_kernel,
        out_shape=[
            pltpu.VMEM((3 * tok_dev, half_width), jnp.bfloat16),
            pltpu.VMEM((3 * tok_dev, half_width), jnp.bfloat16),
            pltpu.VMEM((8, tokens), jnp.int32),
            pltpu.VMEM((slot_count, seq_count, tokens), jnp.int32),
            pltpu.VMEM((slot_count, 8, tokens), jnp.int32),
        ],
        in_specs=[any_spec] * 5,
        out_specs=[vmem] * 5,
        scratch_shapes=[
            pltpu.SMEM((seq_count,), jnp.int32),
            pltpu.SMEM((slot_count, seq_count), jnp.int32),
            pltpu.SemaphoreType.DMA((8,)),
        ],
        compiler_params=KERNEL_PARAMS,
        name="pack",
    )(*distant(queries, key_rows, value_rows, counts, jnp.transpose(head_of)))

    weight_held = pl.pallas_call(
        hold_kernel,
        out_shape=pltpu.VMEM(out_weight.shape, jnp.bfloat16),
        in_specs=[any_spec, vmem],
        out_specs=vmem,
        scratch_shapes=[pltpu.SemaphoreType.DMA((HOLD_COPIES,))],
        compiler_params=KERNEL_PARAMS,
        cost_estimate=pl.CostEstimate(
            flops=0, bytes_accessed=4 * out_weight.size, transcendentals=0
        ),
        name="hold",
    )(*distant(out_weight), *held(limits))
    line = [own] + [
        swap_shards(other if offset & SPLIT else own, offset)
        for offset in range(SPLIT, seq_count, SPLIT)
    ]
    sets = line + [swap_shards(array, 1) for array in line]
    limits, weight_held = lax.optimization_barrier((limits, weight_held))
    keep, message, table = pl.pallas_call(
        functools.partial(attend_kernel, len(sets)),
        out_shape=[
            pltpu.VMEM((tok_dev, half_width), jnp.bfloat16),
            pltpu.VMEM((tok_dev, message_width), jnp.bfloat16),
            pltpu.VMEM((half_width // HDIM + 7 & -8, tokens), jnp.float32),
        ],
        in_specs=[vmem] * (1 + len(sets)),
        out_specs=[vmem] * 3,
        scratch_shapes=[pltpu.VMEM((tokens, HDIM), jnp.float32)],
        compiler_params=KERNEL_PARAMS,
        name="attend",
    )(*held(limits, *sets))
    across = [(2 * i + b, 2 * (i ^ SPLIT) + 1 - b) for i in range(seq_count) for b in range(2)]
    partner_back = lax.ppermute(message, ("seq", "branch"), across)
    partner_keep = partner_2(keep, "branch", 0)
    back = swap_shards(message, SPLIT)
    total, size = pl.pallas_call(
        keep_kernel,
        out_shape=[
            pltpu.VMEM((tok_dev, out_weight.shape[1]), jnp.float32),
            pltpu.VMEM((tok_dev, HDIM), jnp.float32),
        ],
        in_specs=[vmem] * 3,
        out_specs=[vmem] * 2,
        compiler_params=KERNEL_PARAMS,
        name="keep",
    )(*held(keep, partner_keep, weight_held))
    projected, saved = pl.pallas_call(
        project_kernel,
        out_shape=[
            jax.ShapeDtypeStruct((tok_dev, out_weight.shape[1]), jnp.bfloat16),
            jax.ShapeDtypeStruct((slot_count, seq_count, row_cap), jnp.float32),
        ],
        in_specs=[vmem] * 8,
        out_specs=[any_spec] * 2,
        scratch_shapes=[
            pltpu.VMEM((tok_dev, out_weight.shape[1]), jnp.bfloat16),
            pltpu.VMEM((slot_count, seq_count, row_cap), jnp.float32),
            pltpu.SemaphoreType.DMA((3,)),
        ],
        compiler_params=KERNEL_PARAMS,
        name="project",
    )(*held(total, size, back, partner_back, weight_held, table, pick, slot_head))
    saved = jnp.transpose(saved, (0, 2, 1))
    return (projected, saved.reshape(1, 1, slot_count, row_cap, seq_count))


def solution(mesh):
    seq_count = mesh.shape["seq"]
    hypercube = seq_count > SPLIT and seq_count & (seq_count - 1) == 0
    small = hypercube and seq_count <= HEADS
    return jax.shard_map(
        per_device_halves if small else per_device_exchange,
        mesh=mesh,
        in_specs=(
            P("branch", ("groups", "seq"), None),
            P("branch", ("groups", "seq"), None),
            P("branch", ("groups", "seq"), None),
            P("groups"),
            P(),
            P(None, "branch"),
        ),
        out_specs=(
            P(("groups", "seq"), "branch"),
            P("branch", ("groups", "seq"), None, None, None),
        ),
        check_vma=False,
    )
```

```python
import functools
import math

import jax
import jax.numpy as jnp
from jax import lax
from jax.experimental import pallas as pl
from jax.experimental.pallas import tpu as pltpu
from jax.sharding import PartitionSpec as P

HEADS = 12
HDIM = 128


GUIDE_SCALE = 3.0
EPSILON = 1e-06


def partner_2(array, axis, stride):
    return lax.ppermute(array, axis, [(i, i ^ 1 << stride) for i in range(lax.axis_size(axis))])


def slot_layout(head_of):
    flat_heads = head_of.reshape(-1)
    slot_order = jnp.arange(flat_heads.shape[0], dtype=jnp.int32)
    same_head = flat_heads[:, None] == flat_heads[None, :]
    group_size = jnp.sum(same_head.astype(jnp.int32), axis=1)
    earlier = same_head & (slot_order[None, :] < slot_order[:, None])
    group_rank = jnp.sum(earlier.astype(jnp.int32), axis=1)
    return (flat_heads, group_size, group_rank)


def key_grouping(seq_count, tok_dev):
    shard_limit = max(1, 2048 // tok_dev)
    grouping = 1
    for attempt in range(16):
        if grouping * 2 <= shard_limit and seq_count % (grouping * 2) == 0:
            grouping = grouping * 2
    return grouping


def attend_rows(query_block, key_slot, value_slot, key_valid, key_block):
    row_count = query_block.shape[0]
    head_size = query_block.shape[1]
    block_count = key_slot.shape[0] // key_block
    scale_factor = 1.0 / math.sqrt(head_size)

    def fold_block(block_id, state_in):
        top_score, weight_sum, summed = state_in
        scores = (
            jnp.einsum("qd,kd->qk", query_block, key_slot, preferred_element_type=jnp.float32)
            * scale_factor
        )
        scores = jnp.where(key_valid[None, :], scores, -jnp.inf)
        new_top = jnp.maximum(top_score, jnp.max(scores, axis=1))
        fading = jnp.exp(top_score - new_top)
        weights = jnp.exp(scores - new_top[:, None])
        weight_sum = weight_sum * fading + jnp.sum(weights, axis=1)
        summed = summed * fading[:, None] + jnp.dot(
            weights.astype(jnp.bfloat16), value_slot, preferred_element_type=jnp.float32
        )
        return (new_top, weight_sum, summed)

    start_state = (
        jnp.full((row_count,), -jnp.inf, jnp.float32),
        jnp.zeros((row_count,), jnp.float32),
        jnp.zeros((row_count, head_size), jnp.float32),
    )
    top_score, weight_sum, summed = lax.fori_loop(0, block_count, fold_block, start_state)
    return (summed / weight_sum[:, None], top_score + jnp.log(weight_sum))


def serve_slots(query_items, mask_items, key_recv, value_recv, key_valid, key_block):
    source_count, slot_count, item_count, head_size = query_items.shape
    all_tokens = key_recv.shape[0] * key_recv.shape[2]
    per_block = max(1, 512 // source_count)
    slot_outputs = []
    slot_logsum = []
    for slot_id in range(slot_count):
        key_slot = key_recv[:, slot_id].reshape(all_tokens, head_size)
        value_slot = value_recv[:, slot_id].reshape(all_tokens, head_size)
        taken_items = min(per_block, item_count)
        query_block = query_items[:, slot_id, 0:taken_items].reshape(
            source_count * taken_items, head_size
        )
        attended, logsum = attend_rows(query_block, key_slot, value_slot, key_valid, key_block)
        pieces_out = attended.reshape(source_count, taken_items, head_size)
        pieces_sum = logsum.reshape(source_count, taken_items)
        slot_outputs.append(pieces_out)
        slot_logsum.append(pieces_sum)
    attended = jnp.stack(slot_outputs, axis=1)
    logsum = jnp.stack(slot_logsum, axis=1)
    keep_rows = mask_items > 0
    attended = jnp.where(keep_rows[:, :, :, None], attended, 0.0).astype(jnp.bfloat16)
    logsum = jnp.where(keep_rows, logsum, 0.0)
    return (attended, logsum)


def per_device_exchange(queries, key_rows, value_rows, counts, head_of, out_weight):
    seq_count = lax.axis_size("seq")
    tok_dev = queries.shape[1]
    slot_count = head_of.shape[1]
    fewest = max(1, seq_count * slot_count // (2 * HEADS))
    row_cap = (tok_dev + fewest - 1) // fewest
    my_index = lax.axis_index("seq")
    flat_heads, group_size, group_rank = slot_layout(head_of)
    row_steps = jnp.arange(row_cap, dtype=jnp.int32)
    served_rows = group_rank[:, None] + group_size[:, None] * row_steps[None, :]
    my_count = counts[my_index]
    clipped = jnp.minimum(served_rows, tok_dev - 1)
    query_grid = queries[0].reshape(tok_dev, HEADS, HDIM)
    row_live = served_rows < my_count
    query_send = query_grid[clipped, flat_heads[:, None]]
    query_send = jnp.where(row_live[:, :, None], query_send, jnp.zeros((), jnp.bfloat16)).reshape(
        seq_count, slot_count, row_cap, HDIM
    )
    mask_send = row_live.astype(jnp.bfloat16).reshape(seq_count, slot_count, row_cap)
    token_ids = jnp.arange(tok_dev, dtype=jnp.int32)
    key_grid = key_rows[0].reshape(tok_dev, HEADS, HDIM)
    value_grid = value_rows[0].reshape(tok_dev, HEADS, HDIM)
    key_send = key_grid[token_ids[None, :], flat_heads[:, None]].reshape(
        seq_count, slot_count, tok_dev, HDIM
    )
    value_send = value_grid[token_ids[None, :], flat_heads[:, None]].reshape(
        seq_count, slot_count, tok_dev, HDIM
    )
    key_valid = (token_ids[None, :] < counts[:, None]).reshape(-1)
    key_block = tok_dev * key_grouping(seq_count, tok_dev)
    query_recv, mask_recv, key_recv, value_recv = (
        lax.all_to_all(query_send, "seq", split_axis=0, concat_axis=0, tiled=True),
        lax.all_to_all(mask_send, "seq", split_axis=0, concat_axis=0, tiled=True),
        lax.all_to_all(key_send, "seq", split_axis=0, concat_axis=0, tiled=True),
        lax.all_to_all(value_send, "seq", split_axis=0, concat_axis=0, tiled=True),
    )
    attended, logsum = serve_slots(
        query_recv, mask_recv, key_recv, value_recv, key_valid, key_block
    )
    returned = lax.all_to_all(attended, "seq", split_axis=0, concat_axis=0, tiled=True)
    head_ids = jnp.arange(HEADS, dtype=jnp.int32)
    head_group = jnp.sum((flat_heads[None, :] == head_ids[:, None]).astype(jnp.int32), axis=1)
    row_rank = token_ids[:, None] % head_group[None, :]
    row_step = token_ids[:, None] // head_group[None, :]
    slot_ids = jnp.arange(flat_heads.shape[0], dtype=jnp.int32)
    matched = (flat_heads[None, None, :] == head_ids[None, :, None]) & (
        group_rank[None, None, :] == row_rank[:, :, None]
    )
    owner_slot = jnp.sum(jnp.where(matched, slot_ids[None, None, :], 0), axis=2)
    flat_index = owner_slot * row_cap + row_step
    returned_rows = returned.reshape(-1, HDIM)
    attended_home = returned_rows[flat_index].reshape(tok_dev, HEADS * HDIM)
    partner = partner_2(attended_home, "branch", 0)
    on_positive = lax.axis_index("branch") == 0
    own_value = attended_home.astype(jnp.float32)
    partner_value = partner.astype(jnp.float32)
    positive = jnp.where(on_positive, own_value, partner_value)
    negative = jnp.where(on_positive, partner_value, own_value)
    guided = GUIDE_SCALE * positive - (GUIDE_SCALE - 1.0) * negative
    magnitude = jnp.mean(jnp.abs(guided), axis=1, keepdims=True)
    normed = (guided / (magnitude + EPSILON)).astype(jnp.bfloat16)
    projected = jnp.dot(normed, out_weight, preferred_element_type=jnp.float32).astype(jnp.bfloat16)
    saved_rows = jnp.transpose(logsum, (1, 2, 0)).reshape(1, 1, slot_count, row_cap, seq_count)
    return (projected, saved_rows)


KERNEL_PARAMS = pltpu.CompilerParams(vmem_limit_bytes=16 * 1024 * 1024)


SPLIT = 2
WEIGHT_COPIES = 4
TABLE_PIECES = 2
SPLITTER = 65537.0


def swap_shards(array, offset):
    pairs = [(i, i ^ offset) for i in range(lax.axis_size("seq"))]
    return lax.ppermute(array, "seq", pairs)


def place_offsets(shard_count):
    line = list(range(0, shard_count, SPLIT))
    return line + [offset + 1 for offset in line]


def pack_kernel(query_hbm, key_hbm, value_hbm, own_ref, other_ref, copy_sems):
    tok_dev = own_ref.shape[0] // 3
    half_width = own_ref.shape[1]
    half = (lax.axis_index("seq") // SPLIT) % 2
    copies = []
    for target, place in ((other_ref, 1 - half), (own_ref, half)):
        columns = pl.ds(pl.multiple_of(place * half_width, half_width), half_width)
        for part, source in enumerate((key_hbm, value_hbm, query_hbm)):
            rows = pl.ds(part * tok_dev, tok_dev)
            copies.append(
                pltpu.make_async_copy(
                    source.at[0, :, columns], target.at[rows, :], copy_sems.at[len(copies)]
                )
            )
    for copy in copies:
        copy.start()
    for copy in copies:
        copy.wait()


def plan_kernel(
    weight_hbm,
    counts_hbm,
    head_hbm,
    after_ref,
    weight_ref,
    limits_ref,
    pick_ref,
    slot_head_ref,
    counts_ref,
    head_ref,
    copy_sems,
):
    tok_dev = after_ref.shape[0] // 3
    slot_count, shard_count = head_ref.shape
    shard = lax.axis_index("seq")
    copies = [
        pltpu.make_async_copy(counts_hbm, counts_ref, copy_sems.at[0]),
        pltpu.make_async_copy(head_hbm, head_ref, copy_sems.at[1]),
    ]
    share = weight_ref.shape[0] // WEIGHT_COPIES
    for number in range(WEIGHT_COPIES):
        rows = pl.ds(number * share, share)
        copies.append(
            pltpu.make_async_copy(
                weight_hbm.at[rows, :], weight_ref.at[rows, :], copy_sems.at[len(copies)]
            )
        )
    for copy in copies:
        copy.start()
    copies[0].wait()
    copies[1].wait()

    lane = lax.broadcasted_iota(jnp.int32, (1, limits_ref.shape[1]), 1)
    lane_limit = jnp.zeros(lane.shape, jnp.int32)
    for place, offset in enumerate(place_offsets(shard_count)):
        lane_limit = jnp.where(lane // tok_dev == place, counts_ref[shard ^ offset], lane_limit)
    limits_ref[0:1, :] = (lane % tok_dev < lane_limit).astype(jnp.int32)
    limits_ref[1:2, :] = jnp.full(lane.shape, counts_ref[shard], jnp.int32)
    limits_ref[2:3, :] = jnp.full(lane.shape, counts_ref[shard ^ SPLIT], jnp.int32)

    step = lax.broadcasted_iota(jnp.int32, (1, pick_ref.shape[2]), 1)
    for slot in range(slot_count):
        head = head_ref[slot, shard]
        group_size = jnp.int32(0)
        group_rank = jnp.int32(0)
        for other_shard in range(shard_count):
            for other_slot in range(slot_count):
                same = (head_ref[other_slot, other_shard] == head).astype(jnp.int32)
                before = other_shard * slot_count + other_slot < shard * slot_count + slot
                group_size = group_size + same
                group_rank = group_rank + same * before.astype(jnp.int32)
        served = group_rank + group_size * step
        for source in range(shard_count):
            pick_ref[slot, source : source + 1, :] = jnp.where(
                served < counts_ref[source], served + source * tok_dev, -1
            )
        slot_head_ref[slot] = jnp.full(slot_head_ref.shape[1:], head, jnp.int32)
    for copy in copies[2:]:
        copy.wait()


def part_blocks(half_heads, tok_dev):
    return -(-half_heads * TABLE_PIECES // tok_dev)


def gathered(set_refs, part, columns):
    tok_dev = set_refs[0].shape[0] // 3
    rows = pl.ds(part * tok_dev, tok_dev)
    return jnp.concatenate([ref[rows, columns] for ref in set_refs], axis=0)


def head_scores(query_rows, key_all):
    return lax.dot_general(
        query_rows, key_all, (((1,), (1,)), ((), ())), preferred_element_type=jnp.float32
    )


def attend_kernel(set_count, limits_ref, *refs):
    set_refs = refs[:set_count]
    keep_ref, message_ref, table_ref, lines_ref = refs[set_count:]
    tok_dev, half_width = keep_ref.shape
    half_heads = half_width // HDIM
    shard = lax.axis_index("seq")
    head_columns = [pl.ds(head * HDIM, HDIM) for head in range(half_heads)]
    key_valid = limits_ref[0:1, :] > 0

    all_scores = [
        head_scores(gathered(set_refs, 2, columns), gathered(set_refs, 0, columns))
        for columns in head_columns
    ]
    lane = lax.broadcasted_iota(jnp.int32, all_scores[0].shape, 1)
    lines = jnp.zeros(lane.shape, jnp.float32)
    served = []
    for head, scores in enumerate(all_scores):
        scores = jnp.where(key_valid, scores * (1.0 / math.sqrt(HDIM)), -jnp.inf)
        top_score = jnp.max(scores, axis=1, keepdims=True)
        weights = jnp.exp(scores - top_score)
        weight_sum = jnp.sum(weights, axis=1, keepdims=True)
        lines = jnp.where(lane == head, top_score + jnp.log(weight_sum), lines)
        served.append((weights[: 2 * tok_dev].astype(jnp.bfloat16), weight_sum[: 2 * tok_dev]))
    row = lax.broadcasted_iota(jnp.int32, (tok_dev, HDIM), 0)
    for columns, (rounded, weight_sum) in zip(head_columns, served):
        mixed = jnp.dot(
            rounded, gathered(set_refs, 1, columns), preferred_element_type=jnp.float32
        )
        attended = mixed / weight_sum
        kept = jnp.where(row < limits_ref[1:2, :HDIM], attended[:tok_dev], 0.0)
        sent = jnp.where(row < limits_ref[2:3, :HDIM], attended[tok_dev:], 0.0)
        keep_ref[:, columns] = kept.astype(jnp.bfloat16)
        message_ref[:, columns] = sent.astype(jnp.bfloat16)

    for place, offset in enumerate(place_offsets(set_count)):
        rows = pl.ds(pl.multiple_of((shard ^ offset) * tok_dev, tok_dev), tok_dev)
        lines_ref[rows, :] = lines[place * tok_dev : (place + 1) * tok_dev]
    table = jnp.transpose(lines_ref[...])[: table_ref.shape[0]]
    table_ref[...] = table
    row = lax.broadcasted_iota(jnp.int32, (tok_dev, lines.shape[0]), 0)
    blocks = [jnp.zeros(row.shape, jnp.float32) for _ in range(part_blocks(half_heads, tok_dev))]
    for head in range(half_heads):
        rest = jnp.broadcast_to(table[head : head + 1], row.shape)
        for piece in range(TABLE_PIECES):
            scaled = rest * SPLITTER
            part = scaled - (scaled - rest)
            block, at_row = divmod(head * TABLE_PIECES + piece, tok_dev)
            blocks[block] = jnp.where(row == at_row, part, blocks[block])
            rest = rest - part
    message_ref[:, pl.ds(half_width, len(blocks) * lines.shape[0])] = jnp.concatenate(
        blocks, axis=1
    ).astype(jnp.bfloat16)


def guidance(own, partner):
    on_positive = lax.axis_index("branch") == 0
    own_scale = jnp.where(on_positive, GUIDE_SCALE, 1.0 - GUIDE_SCALE)
    partner_scale = jnp.where(on_positive, 1.0 - GUIDE_SCALE, GUIDE_SCALE)
    return own_scale * own.astype(jnp.float32) + partner_scale * partner.astype(jnp.float32)


def half_product(guided, weight_ref, place):
    half_width = guided.shape[1]
    rows = pl.ds(pl.multiple_of(place * half_width, half_width), half_width)
    return jnp.dot(
        guided.astype(jnp.bfloat16), weight_ref[rows, :], preferred_element_type=jnp.float32
    )


def keep_kernel(keep_ref, partner_keep_ref, weight_ref, total_ref, size_ref):
    half = (lax.axis_index("seq") // SPLIT) % 2
    guided = guidance(keep_ref[...], partner_keep_ref[...])
    size = jnp.sum(jnp.abs(guided), axis=1, keepdims=True)
    size_ref[...] = jnp.broadcast_to(size, size_ref.shape)
    total_ref[...] = half_product(guided, weight_ref, half)


def project_kernel(
    total_ref,
    size_ref,
    message_ref,
    partner_back_ref,
    weight_ref,
    table_ref,
    pick_ref,
    slot_head_ref,
    projected_ref,
    saved_ref,
):
    tok_dev = message_ref.shape[0]
    half_width = weight_ref.shape[0] // 2
    half_heads = half_width // HDIM
    tokens = table_ref.shape[1]
    half = (lax.axis_index("seq") // SPLIT) % 2
    rows = pl.ds(0, half_width)
    guided = guidance(message_ref[:, rows], partner_back_ref[:, rows])
    size = size_ref[:, 0:1] + jnp.sum(jnp.abs(guided), axis=1, keepdims=True)
    magnitude = size / (2 * half_width)
    total = total_ref[...] + half_product(guided, weight_ref, 1 - half)
    projected_ref[...] = (total / (magnitude + EPSILON)).astype(jnp.bfloat16)

    parts = message_ref[:, pl.ds(half_width, message_ref.shape[1] - half_width)].astype(jnp.float32)
    others = []
    for head in range(half_heads):
        other = jnp.zeros((1, tokens), jnp.float32)
        for piece in range(TABLE_PIECES):
            block, at_row = divmod(head * TABLE_PIECES + piece, tok_dev)
            other = other + parts[at_row : at_row + 1, block * tokens : (block + 1) * tokens]
        others.append(other)
    for slot in range(saved_ref.shape[0]):
        slot_head = slot_head_ref[slot, 0:1, :]
        line = jnp.zeros((1, tokens), jnp.float32)
        for head in range(half_heads):
            line = jnp.where(slot_head == half * half_heads + head, table_ref[head : head + 1], line)
            line = jnp.where(slot_head == (1 - half) * half_heads + head, others[head], line)
        pick = pick_ref[slot]
        spread = jnp.broadcast_to(line, pick.shape)
        taken = jnp.take_along_axis(spread, jnp.maximum(pick, 0), axis=1)
        saved_ref[slot] = jnp.where(pick >= 0, taken, 0.0)[:, : saved_ref.shape[2]]


def per_device_halves(queries, key_rows, value_rows, counts, head_of, out_weight):
    seq_count = lax.axis_size("seq")
    tok_dev, width = queries.shape[1:]
    half_width = width // 2
    tokens = seq_count * tok_dev
    slot_count = head_of.shape[1]
    fewest = max(1, seq_count * slot_count // (2 * HEADS))
    row_cap = (tok_dev + fewest - 1) // fewest
    message_width = half_width + part_blocks(half_width // HDIM, tok_dev) * tokens
    any_spec = pl.BlockSpec(memory_space=pl.ANY)
    vmem = pl.BlockSpec(memory_space=pltpu.VMEM)

    def held(*arrays):
        return [pltpu.with_memory_space_constraint(array, pltpu.VMEM) for array in arrays]

    def distant(*arrays):
        return [pltpu.with_memory_space_constraint(array, pltpu.HBM) for array in arrays]

    own, other = pl.pallas_call(
        pack_kernel,
        out_shape=[pltpu.VMEM((3 * tok_dev, half_width), jnp.bfloat16)] * 2,
        in_specs=[any_spec] * 3,
        out_specs=[vmem] * 2,
        scratch_shapes=[pltpu.SemaphoreType.DMA((6,))],
        compiler_params=KERNEL_PARAMS,
        name="pack",
    )(*distant(queries, key_rows, value_rows))
    weight_held, limits, pick, slot_head = pl.pallas_call(
        plan_kernel,
        out_shape=[
            pltpu.VMEM(out_weight.shape, jnp.bfloat16),
            pltpu.VMEM((8, tokens), jnp.int32),
            pltpu.VMEM((slot_count, seq_count, tokens), jnp.int32),
            pltpu.VMEM((slot_count, 8, tokens), jnp.int32),
        ],
        in_specs=[any_spec] * 3 + [vmem],
        out_specs=[vmem] * 4,
        scratch_shapes=[
            pltpu.SMEM((seq_count,), jnp.int32),
            pltpu.SMEM((slot_count, seq_count), jnp.int32),
            pltpu.SemaphoreType.DMA((2 + WEIGHT_COPIES,)),
        ],
        compiler_params=KERNEL_PARAMS,
        cost_estimate=pl.CostEstimate(
            flops=0, bytes_accessed=4 * out_weight.size, transcendentals=0
        ),
        name="plan",
    )(*distant(out_weight, counts, jnp.transpose(head_of)), *held(own))
    line = [own] + [
        swap_shards(other if offset & SPLIT else own, offset)
        for offset in range(SPLIT, seq_count, SPLIT)
    ]
    sets = line + [swap_shards(array, 1) for array in line]
    keep, message, table = pl.pallas_call(
        functools.partial(attend_kernel, len(sets)),
        out_shape=[
            pltpu.VMEM((tok_dev, half_width), jnp.bfloat16),
            pltpu.VMEM((tok_dev, message_width), jnp.bfloat16),
            pltpu.VMEM((half_width // HDIM + 7 & -8, tokens), jnp.float32),
        ],
        in_specs=[vmem] * (1 + len(sets)),
        out_specs=[vmem] * 3,
        scratch_shapes=[pltpu.VMEM((tokens, HDIM), jnp.float32)],
        compiler_params=KERNEL_PARAMS,
        name="attend",
    )(*held(limits, *sets))
    across = [(2 * i + b, 2 * (i ^ SPLIT) + 1 - b) for i in range(seq_count) for b in range(2)]
    partner_back = lax.ppermute(message, ("seq", "branch"), across)
    partner_keep = partner_2(keep, "branch", 0)
    back = swap_shards(message, SPLIT)
    total, size = pl.pallas_call(
        keep_kernel,
        out_shape=[
            pltpu.VMEM((tok_dev, out_weight.shape[1]), jnp.float32),
            pltpu.VMEM((tok_dev, HDIM), jnp.float32),
        ],
        in_specs=[vmem] * 3,
        out_specs=[vmem] * 2,
        compiler_params=KERNEL_PARAMS,
        name="keep",
    )(*held(keep, partner_keep, weight_held))
    projected, saved = pl.pallas_call(
        project_kernel,
        out_shape=[
            jax.ShapeDtypeStruct((tok_dev, out_weight.shape[1]), jnp.bfloat16),
            jax.ShapeDtypeStruct((slot_count, seq_count, row_cap), jnp.float32),
        ],
        in_specs=[vmem] * 8,
        out_specs=[vmem] * 2,
        compiler_params=KERNEL_PARAMS,
        name="project",
    )(*held(total, size, back, partner_back, weight_held, table, pick, slot_head))
    saved = jnp.transpose(saved, (0, 2, 1))
    return (projected, saved.reshape(1, 1, slot_count, row_cap, seq_count))


def solution(mesh):
    seq_count = mesh.shape["seq"]
    hypercube = seq_count > SPLIT and seq_count & (seq_count - 1) == 0
    small = hypercube and seq_count <= HEADS
    return jax.shard_map(
        per_device_halves if small else per_device_exchange,
        mesh=mesh,
        in_specs=(
            P("branch", ("groups", "seq"), None),
            P("branch", ("groups", "seq"), None),
            P("branch", ("groups", "seq"), None),
            P("groups"),
            P(),
            P(None, "branch"),
        ),
        out_specs=(
            P(("groups", "seq"), "branch"),
            P("branch", ("groups", "seq"), None, None, None),
        ),
        check_vma=False,
    )
```
